32 devices in a mesh: lat: 8 (over y, x, core), mem: 4 (over z).
Axes of the slice: x: 2, y: 2, z: 4, core: 2. Of those that a mesh axis runs over, the one named last changes fastest.
Arguments:
- latent: bfloat16 [1, 64, 23040], P(None, 'lat'), may hold values from -6 to 6
- member_seeds: int32 [8], replicated, may hold values from 0 to 1048575
- noise_scale: float32 [64], replicated, may hold values from 0.3 to 1.5
- kernel_one: bfloat16 [3, 3, 64, 32], replicated, may hold values from -0.5 to 0.5
- kernel_two: bfloat16 [3, 3, 32, 16], replicated, may hold values from -0.75 to 0.75
- targets: bfloat16 [1, 256, 23040], P(None, 'lat'), may hold values from -6 to 6
- land_words: int32 [256, 48], P('lat'), may hold values from 0 to 1073741823
- channel_weight: float32 [16], replicated, may hold values from 0.5 to 2
Outputs:
- latent_grad: float32 [1, 64, 23040], P(None, 'lat')
- grad_one: float32 [3, 3, 64, 32], replicated
- grad_two: float32 [3, 3, 32, 16], replicated
The draws below stay inside these ranges and needn't reach their ends.
All inputs are finite; a program needn't handle non-finite values.
Results may differ from the reference program's by a relative error of at most 0.0031.
The reference program's roundings to bfloat16 on the way count: a program that leaves them out, or rounds other values in their place, can miss the bound.
Values may be sent and summed in bfloat16 or wider, within the bound.
No kernel may reach another device: no remote copies, remote signals or barrier semaphores. Data moves between devices by JAX's collectives and lax.ppermute only.
A program may use at most 256 MiB of HBM per device.

```python
import math
import jax
import jax.numpy as jnp
from jax import lax

C0 = 64
C1 = 32
LEVEL_CHANNELS = 16
W0 = 360
SAMPLES = 1
MEMBERS = 8
NR0 = 64
OUTPUT_LAT_ROWS = 256
OUTPUT_LON_CELLS = 1440


def touch_ends(values, key, smallest, top_value):
    longest = values.shape.index(max(values.shape))
    spots = []
    for shift in (0, 1):
        where = [jax.random.randint(jax.random.fold_in(key, axis), (), 0, length) for axis, length in enumerate(values.shape)]
        where[longest] = (where[longest] + shift) % values.shape[longest]
        spots.append(tuple(where))
    return values.at[spots[0]].set(smallest).at[spots[1]].set(top_value)


def levels(rng, shape, pieces, low, largest):
    loudness, own = 1.0, jax.random.fold_in(rng, 6)
    for axis_at, parts in pieces:
        heights = jnp.exp(jax.random.uniform(jax.random.fold_in(own, axis_at), (parts,), jnp.float32, low / len(pieces), largest / len(pieces)))
        loudness = loudness * jnp.repeat(heights, shape[axis_at] // parts).reshape([-1 if axis == axis_at else 1 for axis in range(len(shape))])
    return loudness


def normal_values(own_key, shape, spread, reach, cuts=(), kind=jnp.bfloat16):
    values = spread * jax.random.normal(own_key, shape, jnp.float32)
    if cuts:
        values = values * levels(own_key, shape, cuts, -0.22, 0.18)
    return jnp.clip(values, -reach, reach).astype(kind)


def setup_inputs(seed: int = 0) -> dict:
    splits = jax.random.split(jax.random.key(seed), 9)
    latent = normal_values(splits[0], (SAMPLES, NR0, W0 * C0), 1.0, 6.0, ((1, 8),))
    member_seeds = touch_ends(jax.random.randint(splits[1], (MEMBERS,), 0, 1048576), jax.random.fold_in(splits[1], 1), 0, 1048575).astype(jnp.int32)
    noise_scale = jnp.clip(jnp.exp(jax.random.uniform(splits[2], (C0,), jnp.float32, math.log(0.3), math.log(1.5))), 0.3, 1.5)
    kernel_one = normal_values(splits[3], (3, 3, C0, C1), (9 * C0 // 4) ** -0.5, 0.5)
    kernel_two = normal_values(splits[4], (3, 3, C1, LEVEL_CHANNELS), (9 * C1 // 4) ** -0.5, 0.75)
    targets = normal_values(splits[5], (SAMPLES, OUTPUT_LAT_ROWS, OUTPUT_LON_CELLS * LEVEL_CHANNELS), 1.0, 6.0, ((1, 8),))
    land_words = touch_ends(jax.random.randint(splits[6], (OUTPUT_LAT_ROWS, OUTPUT_LON_CELLS // 30), 0, 1073741824), jax.random.fold_in(splits[6], 1), 0, 1073741823).astype(jnp.int32)
    channel_weight = jnp.clip(jnp.exp(jax.random.uniform(splits[7], (LEVEL_CHANNELS,), jnp.float32, math.log(0.5), math.log(2.0))), 0.5, 2.0)
    return dict(latent=latent, member_seeds=member_seeds, noise_scale=noise_scale, kernel_one=kernel_one, kernel_two=kernel_two, targets=targets, land_words=land_words, channel_weight=channel_weight)


SMOOTH = 0.01
HASH_CELL = 1103515245
HASH_SEED = 747796405
HASH_MIX = 277803737

def member_noise(seeds, sample_count, row_ids, span_cols, total_rows):
    sample_ids = jnp.arange(sample_count, dtype=jnp.int32)
    cell_ids = (sample_ids[:, None, None, None] * total_rows + row_ids[None, None, :, None]) * span_cols
    cell_ids = cell_ids + jnp.arange(span_cols, dtype=jnp.int32)[None, None, None, :]
    hashed = cell_ids * HASH_CELL + seeds[None, :, None, None] * HASH_SEED
    hashed = jnp.bitwise_xor(hashed, jnp.right_shift(hashed, 15))
    hashed = hashed * HASH_MIX
    hashed = jnp.bitwise_xor(hashed, jnp.right_shift(hashed, 13))
    uniform_val = jnp.bitwise_and(hashed, 65535).astype(jnp.float32) / 65536.0 - 0.5
    return uniform_val * 3.4641016

def unpack_land(words):
    shifts = jnp.arange(30, dtype=jnp.int32)
    bits = jnp.bitwise_and(jnp.right_shift(words[:, :, None], shifts[None, None, :]), 1)
    return bits.reshape(words.shape[0], words.shape[1] * 30).astype(jnp.float32)

def loss_weight(land_words, channel_weight, row_ids, grid_total):
    latitude = math.pi / 2 - math.pi * (row_ids.astype(jnp.float32) + 0.5) / grid_total
    cosine = jnp.cos(latitude)
    land = unpack_land(land_words)
    weight_tensor = (cosine[:, None] * (1.0 + land))[:, :, None] * channel_weight[None, None, :]
    return weight_tensor.reshape(row_ids.shape[0], -1)

def smooth_sign(diff):
    return diff / jnp.sqrt(diff * diff + SMOOTH)

def member_gradients(own, all_members_total, observed_field, weight_tensor):
    count = all_members_total.shape[1]
    own_float = own.astype(jnp.float32)
    summed = jnp.zeros_like(own_float)
    for other_idx in range(count):
        summed = summed + smooth_sign(own_float - all_members_total[:, other_idx:other_idx + 1].astype(jnp.float32))
    gradient_field = weight_tensor * (smooth_sign(own_float - observed_field.astype(jnp.float32)[:, None]) / count - summed / (count * (count - 1)))
    return gradient_field.astype(jnp.bfloat16)

def upsample_convolve(source_field, kernel):
    height, span_cols, chan_in = source_field.shape
    canvas = jnp.zeros((2 * height + 1, 2 * span_cols + 1, kernel.shape[3]), jnp.float32)
    for row_tap in range(3):
        for col_tap in range(3):
            contrib = jnp.einsum('hwi,io->hwo', source_field, kernel[row_tap, col_tap], precision=lax.Precision.HIGHEST)
            canvas = canvas.at[row_tap:row_tap + 2 * height:2, col_tap:col_tap + 2 * span_cols:2].add(contrib)
    result = canvas[1:, 1:]
    return result.at[:, -1].add(canvas[1:, 0])

def reference(latent, member_seeds, noise_scale, kernel_one, kernel_two, targets, land_words, channel_weight):
    member_list = member_seeds.shape[0]
    first_k = kernel_one.astype(jnp.float32)
    second_kernel = kernel_two.astype(jnp.float32)
    noise = member_noise(member_seeds, SAMPLES, jnp.arange(NR0, dtype=jnp.int32), W0 * C0, NR0)
    scale_cols = jnp.tile(noise_scale, W0)
    weight_tensor = loss_weight(land_words, channel_weight, jnp.arange(OUTPUT_LAT_ROWS, dtype=jnp.int32), OUTPUT_LAT_ROWS)
    latent_grad = jnp.zeros((SAMPLES, NR0, W0 * C0), jnp.float32)
    grad_one = jnp.zeros((3, 3, C0, C1), jnp.float32)
    grad_two = jnp.zeros((3, 3, C1, LEVEL_CHANNELS), jnp.float32)

    def forward_pass(sample_draw, member_entry):
        source_field = (latent[sample_draw].astype(jnp.float32) + noise[sample_draw, member_entry] * scale_cols).astype(jnp.bfloat16)
        preactivation_field = upsample_convolve(source_field.astype(jnp.float32).reshape(NR0, W0, C0), first_k)
        activated_field = jax.nn.gelu(preactivation_field).astype(jnp.bfloat16)
        predicted_field = upsample_convolve(activated_field.astype(jnp.float32), second_kernel).astype(jnp.bfloat16)
        return (source_field, preactivation_field, activated_field, predicted_field.reshape(OUTPUT_LAT_ROWS, OUTPUT_LON_CELLS * LEVEL_CHANNELS))
    for sample_draw in range(SAMPLES):
        predicted_fields = jnp.stack([forward_pass(sample_draw, member_entry)[3] for member_entry in range(member_list)])[None]
        observed_field = targets[sample_draw:sample_draw + 1]
        for member_entry in range(member_list):
            source_field, preactivation_field, activated_field, predicted_field = forward_pass(sample_draw, member_entry)
            gradient_field = member_gradients(predicted_fields[:, member_entry:member_entry + 1], predicted_fields, observed_field, weight_tensor)[0, 0]
            _, pull_two = jax.vjp(upsample_convolve, activated_field.astype(jnp.float32), second_kernel)
            act_grad, two_term = pull_two(gradient_field.astype(jnp.float32).reshape(OUTPUT_LAT_ROWS, OUTPUT_LON_CELLS, LEVEL_CHANNELS))
            _, gelu_pull = jax.vjp(jax.nn.gelu, preactivation_field)
            pre_grad = gelu_pull(act_grad)[0].astype(jnp.bfloat16)
            _, pull_one = jax.vjp(upsample_convolve, source_field.astype(jnp.float32).reshape(NR0, W0, C0), first_k)
            source_grad, one_term = pull_one(pre_grad.astype(jnp.float32))
            latent_grad = latent_grad.at[sample_draw].add(source_grad.reshape(NR0, W0 * C0))
            grad_one = grad_one + one_term
            grad_two = grad_two + two_term
    norm_factor = 1.0 / math.sqrt(SAMPLES * OUTPUT_LAT_ROWS * OUTPUT_LON_CELLS * LEVEL_CHANNELS)
    return (latent_grad, grad_one * norm_factor, grad_two * norm_factor)
```

```python
import functools
import math

import jax
import jax.numpy as jnp
from jax import lax
from jax.experimental import pallas as pl
from jax.experimental.pallas import tpu as pltpu
from jax.sharding import PartitionSpec as P

SMOOTH = 0.01
HASH_CELL = 1103515245
HASH_SEED = 747796405
HASH_MIX = 277803737
LANES = 128
MEM = 8
GELU_A = math.sqrt(2.0 / math.pi)
GELU_B = 0.044715


def shifted(array, axis, by):
    peers = lax.axis_size(axis)
    pairs = [(i, i + by) for i in range(peers) if 0 <= i + by < peers]
    return lax.ppermute(array, axis, pairs)


def iota(shape, axis):
    return lax.broadcasted_iota(jnp.int32, shape, axis)


def lane_table(ref, count):
    lane = iota((8, LANES), 1) % count
    total = jnp.zeros((8, LANES), jnp.float32)
    for k in range(count):
        total = jnp.where(lane == k, ref[k], total)
    return total


def build_band(kernel_ref, band_ref, back_ref):
    chan_in, chan_out = kernel_ref.shape[2], kernel_ref.shape[3]
    cells = LANES // chan_in
    repeat = (iota((chan_out, LANES), 1) % chan_out == iota((chan_out, LANES), 0)).astype(jnp.bfloat16)
    wide = {}
    for a in range(3):
        for b in range(3):
            wide[a, b] = jnp.dot(kernel_ref[a, b], repeat, preferred_element_type=jnp.float32)
    column = iota((chan_in, LANES), 1) // chan_out
    zero = jnp.zeros((chan_in, LANES), jnp.float32)
    for block in range(2):
        for row in range(2):
            for cell in range(cells):
                at = block * 256 + row * LANES + cell * chan_in
                for sub in range(2):
                    a = sub - 2 * row + 1
                    part = zero
                    for q in range(2 * cells):
                        b = q - 2 * (cell + block * cells) + 1
                        if 0 <= a <= 2 and 0 <= b <= 2:
                            part = jnp.where(column == q, wide[a, b], part)
                    band_ref[at : at + chan_in, sub * LANES : (sub + 1) * LANES] = part.astype(jnp.bfloat16)
    for block in range(2):
        square = band_ref[block * 256 : (block + 1) * 256, :].astype(jnp.float32)
        back_ref[block * 256 : (block + 1) * 256, :] = square.T.astype(jnp.bfloat16)


def tap_sums(total, chan_in, chan_out):
    cells = LANES // chan_in
    column = iota((chan_in, LANES), 1) // chan_out
    sums = {}
    for a in range(3):
        row, sub = ((1, 1), (0, 0), (0, 1))[a]
        for b in range(3):
            part = jnp.zeros((chan_in, LANES), jnp.float32)
            for reach in range(cells + 1):
                q = 2 * reach + b - 1
                if 0 <= q < 2 * cells:
                    block, cell = reach // cells, reach % cells
                    at = block * 256 + row * LANES + cell * chan_in
                    piece = total[at : at + chan_in, sub * LANES : (sub + 1) * LANES]
                    part = jnp.where(column == q, piece, part)
            sums[a, b] = part
    return sums


def fold_to(part, chan_out, at):
    fold = (iota((LANES, LANES), 0) % chan_out == iota((LANES, LANES), 1) - at).astype(jnp.float32)
    return jnp.dot(part, fold, precision=lax.Precision.HIGHEST, preferred_element_type=jnp.float32)


def band_kernel(
    half,
    norm,
    seeds,
    scale,
    channel_weight,
    land,
    land_above,
    latent,
    above,
    below,
    targets,
    targets_above,
    kernel_one,
    kernel_two,
    out_lat,
    out_taps,
    lat_rows,
    tgt_rows,
    weight_rows,
    band_one,
    back_one,
    band_two,
    back_two,
    source,
    pre,
    act,
    slope,
    cast,
    fgrad,
    carry,
    pgrad,
    sums,
    acc_one,
    acc_two,
):
    rows = latent.shape[1]
    span = latent.shape[2]
    blocks = span // LANES
    lat_count = lax.axis_size("lat")
    own = blocks // lax.axis_size("mem")
    total_rows = rows * lat_count
    grid_rows = 4 * rows
    grid_total = grid_rows * lat_count
    lat_pos = lax.axis_index("lat")
    mem_pos = lax.axis_index("mem")
    wide = half + 2
    front = half + 1
    chan0, chan1, chan2 = kernel_one.shape[2], kernel_one.shape[3], kernel_two.shape[3]
    f32, bf16 = jnp.float32, jnp.bfloat16

    def block_of(part, t):
        at = mem_pos * own + part * half + t + (blocks - 1)
        at = jnp.where(at >= blocks, at - blocks, at)
        return jnp.where(at >= blocks, at - blocks, at)

    def load_blocks(t, _):
        for part in range(2):
            off = pl.multiple_of(block_of(part, t) * LANES, LANES)
            slot = t * 2 + part
            lat_rows[slot, 0:rows] = latent[0, :, pl.ds(off, LANES)].astype(f32)
            lat_rows[slot, rows : rows + 1] = below[0, :, pl.ds(off, LANES)].astype(f32)
            lat_rows[slot, rows + 1 : rows + 2] = above[0, :, pl.ds(off, LANES)].astype(f32)

            @pl.when(t < front)
            def _():
                tgt_rows[slot, 0:grid_rows] = targets[0, :, pl.ds(off, LANES)].astype(f32)
                tgt_rows[slot, grid_rows : grid_rows + 4] = targets_above[0, :, pl.ds(off, LANES)].astype(f32)

        return 0

    lax.fori_loop(0, wide, load_blocks, 0)

    pad_rows = weight_rows.shape[0]
    grid_row = iota((pad_rows, LANES), 0) + (lat_pos * grid_rows - 4)
    latitude = math.pi / 2 - math.pi * (grid_row.astype(f32) + 0.5) / grid_total
    channels = lane_table(channel_weight, chan2)
    cosine = jnp.where(grid_row >= 0, jnp.cos(latitude), 0.0)
    weight_rows[...] = cosine * (jnp.tile(channels, (pad_rows // 8, 1)) * (1.0 / (MEM * (MEM - 1))))

    build_band(kernel_one, band_one, back_one)
    build_band(kernel_two, band_two, back_two)

    source[rows + 2] = jnp.zeros(source.shape[1:], bf16)
    source[:, wide] = jnp.zeros((source.shape[0],) + source.shape[2:], bf16)
    fgrad[:, 0] = jnp.zeros((2,) + fgrad.shape[2:], bf16)
    carry[...] = jnp.zeros(carry.shape, f32)
    acc_one[...] = jnp.zeros(acc_one.shape, f32)
    acc_two[...] = jnp.zeros(acc_two.shape, f32)

    sublane = iota((8, LANES), 0)
    seed_table = jnp.zeros((8, LANES), jnp.int32)
    for m in range(MEM):
        seed_table = jnp.where(sublane == m, seeds[m], seed_table)
    hash_table = iota((8, LANES), 1) * HASH_CELL + seed_table * HASH_SEED
    scale_table = lane_table(scale, chan0)

    def make_source(i, _):
        row = lat_pos * rows - 1 + i
        inside = jnp.where(row < total_rows, 1.0, 0.0).astype(f32)
        at = jnp.where(i == 0, rows + 1, i - 1)
        for t in range(wide):
            parts = []
            for part in range(2):
                first = (row * span + block_of(part, t) * LANES) * HASH_CELL
                h = hash_table + first
                h = jnp.bitwise_xor(h, jnp.right_shift(h, 15))
                h = h * HASH_MIX
                h = jnp.bitwise_xor(h, jnp.right_shift(h, 13))
                noise = jnp.bitwise_and(h, 65535).astype(f32) * (1.0 / 65536.0) - 0.5
                noise = noise * 3.4641016
                cell = lat_rows[t * 2 + part, pl.ds(at, 1), :]
                parts.append((cell + noise * scale_table) * inside)
            source[i, t] = jnp.concatenate(parts, axis=0).astype(bf16)
        return 0

    lax.fori_loop(0, rows + 2, make_source, 0)

    def operand(ref, i, start, count):
        def piece(r, at):
            return ref[r, pl.ds(at, count)].reshape(count * 16, LANES)

        return jnp.concatenate(
            [piece(i, start), piece(i + 1, start), piece(i, start + 1), piece(i + 1, start + 1)], axis=1
        )

    def first_segment(i, _):
        pre[...] = jnp.dot(operand(source, i, 0, wide), band_one[...], preferred_element_type=f32)
        for t in range(wide):
            for sub in range(2):
                x = pre[t * 16 : (t + 1) * 16, sub * LANES : (sub + 1) * LANES]
                square = x * x
                th = jnp.tanh(x * (GELU_A + (GELU_A * GELU_B) * square))
                plus = 0.5 + 0.5 * th
                act[2 * i + sub, t] = (x * plus).astype(bf16)
                if t < front:
                    d = plus + (x * plus) * (1.0 - th) * (GELU_A + (3.0 * GELU_A * GELU_B) * square)
                    if t == half:
                        d = jnp.where(iota((16, LANES), 0) < 8, d, 0.0)
                    slope[2 * i + sub, t] = d
        return 0

    lax.fori_loop(0, rows + 2, first_segment, 0)

    bit_table = jnp.left_shift(1, iota((8, LANES), 1) // chan2)
    members = front * 16
    owner = iota((48, members), 0)
    group = iota((48, members), 1) // 8
    place = (group % 2) * half + group // 2
    real = (group // 2 > 0) & (place - 1 < own)
    pick_own = (real & (place - 1 == owner)).astype(bf16)
    pick_prev = ((group // 2 < half) & (place == owner)).astype(bf16)
    pick = jnp.concatenate([pick_own, pick_prev], axis=0)

    def land_bits(p, part, t):
        cell = block_of(part, t) * (LANES // chan2)
        word = lax.shift_right_logical(cell * 2185, 16)
        bit = cell - 30 * word
        after = jnp.minimum(word + 1, land.shape[1] - 1)
        inner = p >= 4
        line = jnp.where(inner, p - 4, 0)
        edge = jnp.where(inner, 0, p)
        low = jnp.where(inner, land[line, word], land_above[edge, word])
        high = jnp.where(inner, land[line, after], land_above[edge, after])
        return jnp.bitwise_or(lax.shift_right_logical(low, bit), lax.shift_left(high, 30 - bit))

    def second_segment(j, _):
        taken = operand(act, j, 0, front)
        cast[...] = jnp.dot(taken, band_two[...], preferred_element_type=f32)
        for sub in range(2):
            p = 2 * j + sub
            line = jnp.where(p >= 4, p - 4, p + grid_rows)
            base = jnp.broadcast_to(weight_rows[pl.ds(p, 1), :], (8, LANES))
            twice = base + base
            for t in range(front):
                parts = []
                for part in range(2):
                    if t == half and part == 1:
                        parts.append(jnp.zeros((8, LANES), f32))
                        continue
                    at = t * 16 + part * 8
                    f = cast[at : at + 8, sub * LANES : (sub + 1) * LANES].astype(bf16).astype(f32)
                    y = tgt_rows[t * 2 + part, pl.ds(line, 1), :]
                    d = f - y
                    goal = d * lax.rsqrt(d * d + SMOOTH)
                    gs = []
                    for k in range(1, 5):
                        d = f - pltpu.roll(f, k, 0)
                        gs.append(d * lax.rsqrt(d * d + SMOOTH))
                    back = gs[2]
                    for k in (1, 0):
                        back = gs[k] + pltpu.roll(back, MEM - 1, 0)
                    back = pltpu.roll(back, MEM - 1, 0)
                    spread = (gs[0] + gs[1]) + (gs[2] + gs[3]) - back
                    land_hit = jnp.bitwise_and(land_bits(p, part, t), bit_table) != 0
                    weight = jnp.where(land_hit, twice, base)
                    parts.append(weight * ((MEM - 1.0) * goal - spread))
                fgrad[sub, t + 1] = jnp.concatenate(parts, axis=0).astype(bf16)

        def flat(sub, at, count):
            return fgrad[sub, at : at + count].reshape(count * 16, LANES)

        @pl.when(j >= 2)
        def _():
            g = jnp.concatenate([flat(0, 2, half), flat(1, 2, half)], axis=1)
            x = operand(act, j, 1, half)
            acc_two[...] += lax.dot_general(g, x, (((0,), (0,)), ((), ())), preferred_element_type=f32)

        g = jnp.concatenate([flat(0, 1, front), flat(1, 1, front), flat(0, 0, front), flat(1, 0, front)], axis=1)
        pulled = jnp.dot(g, back_two[...], preferred_element_type=f32)
        grad = pulled[:, :LANES] + carry[...]
        carry[...] = pulled[:, LANES:]
        grad = (grad * slope[j].reshape(members, LANES)).astype(bf16)
        pgrad[j] = grad.reshape(front, 16, LANES)
        sums[j] = jnp.dot(pick, grad, preferred_element_type=f32)
        return 0

    lax.fori_loop(0, 2 * rows + 2, second_segment, 0)

    def first_taps(i, _):
        g = jnp.concatenate(
            [pgrad[2 * i + sub, pl.ds(1, half)].reshape(half * 16, LANES) for sub in range(2)], axis=1
        )
        x = operand(source, i, 1, half)
        acc_one[...] += lax.dot_general(g, x, (((0,), (0,)), ((), ())), preferred_element_type=f32)
        return 0

    lax.fori_loop(1, rows + 1, first_taps, 0)

    z = sums[...].reshape(rows + 1, 2, 96, LANES)
    z = [z[:, sub, at : at + 48].reshape((rows + 1) * 48, LANES) for at in (0, 48) for sub in range(2)]
    z = jnp.concatenate(z, axis=1)
    high = z.astype(bf16)
    low = (z - high.astype(f32)).astype(bf16)
    pulled = jnp.dot(high, back_one[...], preferred_element_type=f32)
    pulled = pulled + jnp.dot(low, back_one[...], preferred_element_type=f32)
    pulled = pulled.reshape(rows + 1, 48, 2 * LANES)
    result = pulled[1:, :, :LANES] + pulled[:-1, :, LANES:]
    out_lat[...] = result[:, :own, :].astype(out_lat.dtype)

    one = tap_sums(acc_one[...].T, chan0, chan1)
    two = tap_sums(acc_two[...].T, chan1, chan2)
    for a in range(3):
        block = fold_to(one[a, 0], chan1, 0) + fold_to(one[a, 1], chan1, chan1) + fold_to(one[a, 2], chan1, 2 * chan1)
        top = fold_to(two[a, 0], chan2, 3 * chan1) + fold_to(two[a, 1], chan2, 3 * chan1 + chan2)
        bottom = fold_to(two[a, 2], chan2, 3 * chan1)
        block = (block + jnp.concatenate([top, bottom], axis=0)) * norm
        out_taps[a * chan0 : (a + 1) * chan0, :] = block


def local(
    latent, member_seeds, noise_scale, kernel_one, kernel_two, targets, land_words, channel_weight
):
    sample_count, rows, span = latent.shape
    chan0, chan1, chan2 = kernel_one.shape[2], kernel_one.shape[3], kernel_two.shape[3]
    lat_count = lax.axis_size("lat")
    own = span // LANES // lax.axis_size("mem")
    half = (own + 1) // 2
    assert sample_count == 1 and member_seeds.shape[0] == MEM and own % 2 == 1
    assert 4 * chan2 == 2 * chan1 == chan0 and chan0 == 64
    below = shifted(latent[:, :1], "lat", -1)
    above = shifted(latent[:, rows - 1 :], "lat", 1)
    targets_above = shifted(targets[:, 4 * rows - 4 :], "lat", 1)
    land_above = shifted(land_words[4 * rows - 4 :], "lat", 1)
    norm = 1.0 / math.sqrt(sample_count * 4 * rows * lat_count * targets.shape[2])
    vmem = pl.BlockSpec(memory_space=pltpu.VMEM)
    smem = pl.BlockSpec(memory_space=pltpu.SMEM)
    f32, bf16 = jnp.float32, jnp.bfloat16
    wide, front = half + 2, half + 1
    lat_grad, taps = pl.pallas_call(
        functools.partial(band_kernel, half, norm),
        in_specs=[smem] * 5 + [vmem] * 7,
        out_specs=[vmem, vmem],
        out_shape=[
            jax.ShapeDtypeStruct((rows, own, LANES), bf16),
            jax.ShapeDtypeStruct((3 * chan0, LANES), f32),
        ],
        scratch_shapes=[
            pltpu.VMEM((2 * wide, rows + 8, LANES), f32),
            pltpu.VMEM((2 * front, 4 * rows + 8, LANES), f32),
            pltpu.VMEM((4 * rows + 8, LANES), f32),
            pltpu.VMEM((512, 256), bf16),
            pltpu.VMEM((512, 256), bf16),
            pltpu.VMEM((512, 256), bf16),
            pltpu.VMEM((512, 256), bf16),
            pltpu.VMEM((rows + 3, wide + 1, 16, LANES), bf16),
            pltpu.VMEM((wide * 16, 2 * LANES), f32),
            pltpu.VMEM((2 * rows + 4, wide, 16, LANES), bf16),
            pltpu.VMEM((2 * rows + 4, front, 16, LANES), f32),
            pltpu.VMEM((front * 16, 2 * LANES), f32),
            pltpu.VMEM((2, front + 1, 16, LANES), bf16),
            pltpu.VMEM((front * 16, LANES), f32),
            pltpu.VMEM((2 * rows + 2, front, 16, LANES), bf16),
            pltpu.VMEM((2 * rows + 2, 96, LANES), f32),
            pltpu.VMEM((256, 512), f32),
            pltpu.VMEM((256, 512), f32),
        ],
        compiler_params=pltpu.CompilerParams(vmem_limit_bytes=56 * 1024 * 1024),
        name="band",
    )(
        member_seeds,
        noise_scale,
        channel_weight,
        land_words,
        land_above,
        latent,
        above,
        below,
        targets,
        targets_above,
        kernel_one,
        kernel_two,
    )
    taps = lax.psum(taps, ("lat", "mem"))
    whole = lax.all_gather(lat_grad, "mem", axis=1, tiled=True)
    latent_grad = whole.astype(f32).reshape(1, rows, span)
    one = taps[:, : 3 * chan1].reshape(3, chan0, 3, chan1).transpose(0, 2, 1, 3)
    two = taps[:, 3 * chan1 :].reshape(3, 2, chan1, 2, chan2)
    two = jnp.stack([two[:, 0, :, 0], two[:, 0, :, 1], two[:, 1, :, 0]], axis=1)
    return (latent_grad, one, two)


def solution(mesh):
    in_specs = (P(None, "lat", None), P(), P(), P(), P(), P(None, "lat", None), P("lat", None), P())
    out_specs = (P(None, "lat", None), P(), P())
    return jax.shard_map(local, mesh=mesh, in_specs=in_specs, out_specs=out_specs, check_vma=False)
```

```python
import functools
import math

import jax
import jax.numpy as jnp
from jax import lax
from jax.experimental import pallas as pl
from jax.experimental.pallas import tpu as pltpu
from jax.sharding import PartitionSpec as P

SMOOTH = 0.01
HASH_CELL = 1103515245
HASH_SEED = 747796405
HASH_MIX = 277803737
LANES = 128
MEM = 8
GELU_A = math.sqrt(2.0 / math.pi)
GELU_B = 0.044715


def shifted(array, axis, by):
    peers = lax.axis_size(axis)
    pairs = [(i, i + by) for i in range(peers) if 0 <= i + by < peers]
    return lax.ppermute(array, axis, pairs)


def iota(shape, axis):
    return lax.broadcasted_iota(jnp.int32, shape, axis)


def lane_table(ref, count):
    lane = iota((8, LANES), 1) % count
    total = jnp.zeros((8, LANES), jnp.float32)
    for k in range(count):
        total = jnp.where(lane == k, ref[k], total)
    return total


def build_band(kernel_ref, band_ref, back_ref):
    chan_out, chan_in = kernel_ref.shape[2], kernel_ref.shape[3]
    cells = LANES // chan_in
    repeat = (iota((chan_out, LANES), 1) % chan_out == iota((chan_out, LANES), 0)).astype(jnp.bfloat16)
    wide = {}
    for a in range(3):
        for b in range(3):
            wide[a, b] = lax.dot_general(
                kernel_ref[a, b], repeat, (((0,), (0,)), ((), ())), preferred_element_type=jnp.float32
            )
    column = iota((chan_in, LANES), 1) // chan_out
    zero = jnp.zeros((chan_in, LANES), jnp.float32)
    for block in range(2):
        for row in range(2):
            for cell in range(cells):
                at = block * 256 + row * LANES + cell * chan_in
                for sub in range(2):
                    a = sub - 2 * row + 1
                    part = zero
                    for q in range(2 * cells):
                        b = q - 2 * (cell + block * cells) + 1
                        if 0 <= a <= 2 and 0 <= b <= 2:
                            part = jnp.where(column == q, wide[a, b], part)
                    band_ref[at : at + chan_in, sub * LANES : (sub + 1) * LANES] = part.astype(jnp.bfloat16)
    for block in range(2):
        square = band_ref[block * 256 : (block + 1) * 256, :].astype(jnp.float32)
        back_ref[block * 256 : (block + 1) * 256, :] = square.T.astype(jnp.bfloat16)


def pack_taps(acc_ref, out_ref, first, chan_in, chan_out, norm):
    cells = LANES // chan_in
    group = iota((chan_out, LANES), 1) // chan_in
    packed = None
    for k in range(9):
        a, b = divmod(k, 3)
        row, sub = ((1, 1), (0, 0), (0, 1))[a]
        slot = k % cells
        part = None
        for reach in range(cells + 1):
            q = 2 * reach + b - 1
            if 0 <= q < 2 * cells:
                block, cell = reach // cells, reach % cells
                lines = sub * LANES + q * chan_out
                lanes = block * 256 + row * LANES
                piece = acc_ref[lines : lines + chan_out, lanes : lanes + LANES]
                turn = (slot - cell) % cells * chan_in
                piece = pltpu.roll(piece, turn, 1) if turn else piece
                part = piece if part is None else part + piece
        packed = part if slot == 0 else jnp.where(group == slot, part, packed)
        if slot == cells - 1 or k == 8:
            at = first + k // cells * chan_out
            out_ref[at : at + chan_out, :] = packed * norm


def window_block(mem_pos, own, half, blocks, part, t):
    at = mem_pos * own + part * half + t + (blocks - 1)
    at = jnp.where(at >= blocks, at - blocks, at)
    return jnp.where(at >= blocks, at - blocks, at)


def land_of(words, block, chan):
    cell = block * (LANES // chan) + iota(words.shape, 1) // chan
    word = jnp.right_shift(cell * 2185, 16)
    picked = jnp.take_along_axis(words, word, axis=1, mode="promise_in_bounds")
    return jnp.bitwise_and(jnp.right_shift(picked, cell - 30 * word), 1).astype(jnp.float32)


def edge_kernel(half, chan, latent, targets, land, down, up, words):
    rows = latent.shape[1]
    blocks = latent.shape[2] // LANES
    own = blocks // lax.axis_size("mem")
    mem_pos = lax.axis_index("mem")
    words[...] = jnp.zeros(words.shape, jnp.int32)
    words[:, : land.shape[1]] = land[...]
    line = iota((8, LANES), 0)
    for t in range(half + 2):
        for part in range(2):
            block = window_block(mem_pos, own, half, blocks, part, t)
            off = pl.multiple_of(block * LANES, LANES)
            slot = t * 2 + part
            cells = latent[0, :, pl.ds(off, LANES)].astype(jnp.float32)
            aims = targets[0, :, pl.ds(off, LANES)].astype(jnp.float32)
            mask = land_of(words[...], block, chan)
            pack = pltpu.roll(cells, 1, 0)
            pack = jnp.where((line >= 1) & (line <= 3), pltpu.roll(aims, 4, 0), pack)
            pack = jnp.where((line >= 4) & (line <= 6), pltpu.roll(mask, 7, 0), pack)
            down[slot] = pack.astype(jnp.bfloat16)
            up[:, slot * LANES : (slot + 1) * LANES] = cells[0:1].astype(jnp.bfloat16)


def place_kernel(own, part0, part1, part2, part3, taps, latent_grad, grad_one, grad_two):
    mem_pos = lax.axis_index("mem")
    for k, part in enumerate((part0, part1, part2, part3)):
        off = pl.multiple_of(jnp.bitwise_xor(mem_pos, k) * own * LANES, LANES)
        latent_grad[0, :, pl.ds(off, own * LANES)] = part[...].astype(jnp.float32)
    first = 0
    for out in (grad_one, grad_two):
        chan_out, chan_in = out.shape[2], out.shape[3]
        cells = LANES // chan_in
        for k in range(9):
            at = first + k // cells * chan_out
            block = taps[at : at + chan_out, :]
            turn = (-(k % cells)) % cells * chan_in
            block = pltpu.roll(block, turn, 1) if turn else block
            out[k // 3, k % 3] = block[:, :chan_in]
        first += -(-9 // cells) * chan_out


def band_kernel(
    half,
    norm,
    seeds,
    scale,
    channel_weight,
    latent,
    above,
    below,
    targets,
    land,
    kernel_one,
    kernel_two,
    out_lat,
    out_taps,
    lat_rows,
    tgt_rows,
    weight_rows,
    words,
    band_one,
    back_one,
    band_two,
    back_two,
    source,
    pre,
    act,
    slope,
    cast,
    fgrad,
    carry,
    pgrad,
    sums,
    acc_one,
    acc_two,
):
    rows = latent.shape[1]
    span = latent.shape[2]
    blocks = span // LANES
    lat_count = lax.axis_size("lat")
    own = blocks // lax.axis_size("mem")
    total_rows = rows * lat_count
    grid_rows = 4 * rows
    grid_total = grid_rows * lat_count
    lat_pos = lax.axis_index("lat")
    mem_pos = lax.axis_index("mem")
    wide = half + 2
    front = half + 1
    chan0, chan1, chan2 = kernel_one.shape[3], kernel_two.shape[3], kernel_two.shape[2]
    f32, bf16 = jnp.float32, jnp.bfloat16

    def block_of(part, t):
        return window_block(mem_pos, own, half, blocks, part, t)

    pad_rows = grid_rows + 8
    grid_row = iota((pad_rows, LANES), 0)
    grid_row = jnp.where(grid_row < grid_rows, grid_row, grid_row - (grid_rows + 4)) + lat_pos * grid_rows
    latitude = math.pi / 2 - math.pi * (grid_row.astype(f32) + 0.5) / grid_total
    channels = lane_table(channel_weight, chan2)
    cosine = jnp.where(grid_row >= 0, jnp.cos(latitude), 0.0)
    base_rows = cosine * (jnp.tile(channels, (pad_rows // 8, 1)) * (1.0 / (MEM * (MEM - 1))))

    words[...] = jnp.zeros(words.shape, jnp.int32)
    words[:, : land.shape[1]] = land[...]
    for t in range(wide):
        for part in range(2):
            block = block_of(part, t)
            off = pl.multiple_of(block * LANES, LANES)
            slot = t * 2 + part
            edge = above[slot].astype(f32)
            lat_rows[slot, 0:rows] = latent[0, :, pl.ds(off, LANES)].astype(f32)
            lat_rows[slot, rows : rows + 1] = below[:, slot * LANES : (slot + 1) * LANES].astype(f32)
            lat_rows[slot, rows + 1 : rows + 2] = edge[0:1]
            if t < front:
                tgt_rows[slot, 0:grid_rows] = targets[0, :, pl.ds(off, LANES)].astype(f32)
                tgt_rows[slot, grid_rows:] = edge
                mask = jnp.concatenate([land_of(words[...], block, chan2), pltpu.roll(edge, 5, 0)], axis=0)
                weight_rows[slot] = base_rows + base_rows * mask

    build_band(kernel_one, band_one, back_one)
    build_band(kernel_two, band_two, back_two)

    source[rows + 2] = jnp.zeros(source.shape[1:], bf16)
    source[:, wide] = jnp.zeros((source.shape[0],) + source.shape[2:], bf16)
    fgrad[:, 0] = jnp.zeros((2,) + fgrad.shape[2:], bf16)
    carry[...] = jnp.zeros(carry.shape, f32)
    acc_one[...] = jnp.zeros(acc_one.shape, f32)
    acc_two[...] = jnp.zeros(acc_two.shape, f32)

    sublane = iota((8, LANES), 0)
    seed_table = jnp.zeros((8, LANES), jnp.int32)
    for m in range(MEM):
        seed_table = jnp.where(sublane == m, seeds[m], seed_table)
    hash_table = iota((8, LANES), 1) * HASH_CELL + seed_table * HASH_SEED
    scale_table = lane_table(scale, chan0)

    def make_source(i, _):
        row = lat_pos * rows - 1 + i
        inside = jnp.where(row < total_rows, 1.0, 0.0).astype(f32)
        at = jnp.where(i == 0, rows + 1, i - 1)
        for t in range(wide):
            parts = []
            for part in range(2):
                first = (row * span + block_of(part, t) * LANES) * HASH_CELL
                h = hash_table + first
                h = jnp.bitwise_xor(h, jnp.right_shift(h, 15))
                h = h * HASH_MIX
                h = jnp.bitwise_xor(h, jnp.right_shift(h, 13))
                noise = jnp.bitwise_and(h, 65535).astype(f32) * (1.0 / 65536.0) - 0.5
                noise = noise * 3.4641016
                cell = lat_rows[t * 2 + part, pl.ds(at, 1), :]
                parts.append((cell + noise * scale_table) * inside)
            source[i, t] = jnp.concatenate(parts, axis=0).astype(bf16)
        return 0

    lax.fori_loop(0, rows + 2, make_source, 0)

    def operand(ref, i, start, count):
        def piece(r, at):
            return ref[r, pl.ds(at, count)].reshape(count * 16, LANES)

        return jnp.concatenate(
            [piece(i, start), piece(i + 1, start), piece(i, start + 1), piece(i + 1, start + 1)], axis=1
        )

    def first_segment(i, _):
        pre[...] = jnp.dot(operand(source, i, 0, wide), band_one[...], preferred_element_type=f32)
        for t in range(wide):
            for sub in range(2):
                x = pre[t * 16 : (t + 1) * 16, sub * LANES : (sub + 1) * LANES]
                square = x * x
                th = jnp.tanh(x * (GELU_A + (GELU_A * GELU_B) * square))
                plus = 0.5 + 0.5 * th
                act[2 * i + sub, t] = (x * plus).astype(bf16)
                if t < front:
                    d = plus + (x * plus) * (1.0 - th) * (GELU_A + (3.0 * GELU_A * GELU_B) * square)
                    if t == half:
                        d = jnp.where(iota((16, LANES), 0) < 8, d, 0.0)
                    slope[2 * i + sub, t] = d
        return 0

    lax.fori_loop(0, rows + 2, first_segment, 0)

    members = front * 16
    owner = iota((48, members), 0)
    group = iota((48, members), 1) // 8
    place = (group % 2) * half + group // 2
    real = (group // 2 > 0) & (place - 1 < own)
    pick_own = (real & (place - 1 == owner)).astype(bf16)
    pick_prev = ((group // 2 < half) & (place == owner)).astype(bf16)
    pick = jnp.concatenate([pick_own, pick_prev], axis=0)

    def second_segment(j, _):
        taken = operand(act, j, 0, front)
        cast[...] = jnp.dot(taken, band_two[...], preferred_element_type=f32)
        for sub in range(2):
            p = 2 * j + sub
            line = jnp.where(p >= 4, p - 4, p + grid_rows)
            for t in range(front):
                parts = []
                for part in range(2):
                    if t == half and part == 1:
                        parts.append(jnp.zeros((8, LANES), f32))
                        continue
                    at = t * 16 + part * 8
                    f = cast[at : at + 8, sub * LANES : (sub + 1) * LANES].astype(bf16).astype(f32)
                    y = tgt_rows[t * 2 + part, pl.ds(line, 1), :]
                    d = f - y
                    goal = d * lax.rsqrt(d * d + SMOOTH)
                    gs = []
                    for k in range(1, 5):
                        d = f - pltpu.roll(f, k, 0)
                        gs.append(d * lax.rsqrt(d * d + SMOOTH))
                    back = gs[2]
                    for k in (1, 0):
                        back = gs[k] + pltpu.roll(back, MEM - 1, 0)
                    back = pltpu.roll(back, MEM - 1, 0)
                    spread = (gs[0] + gs[1]) + (gs[2] + gs[3]) - back
                    weight = weight_rows[t * 2 + part, pl.ds(line, 1), :]
                    parts.append(weight * ((MEM - 1.0) * goal - spread))
                fgrad[sub, t + 1] = jnp.concatenate(parts, axis=0).astype(bf16)

        def flat(sub, at, count):
            return fgrad[sub, at : at + count].reshape(count * 16, LANES)

        @pl.when(j >= 2)
        def _():
            g = jnp.concatenate([flat(0, 2, half), flat(1, 2, half)], axis=1)
            x = operand(act, j, 1, half)
            acc_two[...] += lax.dot_general(g, x, (((0,), (0,)), ((), ())), preferred_element_type=f32)

        g = jnp.concatenate([flat(0, 1, front), flat(1, 1, front), flat(0, 0, front), flat(1, 0, front)], axis=1)
        pulled = jnp.dot(g, back_two[...], preferred_element_type=f32)
        grad = pulled[:, :LANES] + carry[...]
        carry[...] = pulled[:, LANES:]
        grad = (grad * slope[j].reshape(members, LANES)).astype(bf16)
        pgrad[j] = grad.reshape(front, 16, LANES)
        sums[j] = jnp.dot(pick, grad, preferred_element_type=f32)
        return 0

    lax.fori_loop(0, 2 * rows + 2, second_segment, 0)

    def first_taps(i, _):
        g = jnp.concatenate(
            [pgrad[2 * i + sub, pl.ds(1, half)].reshape(half * 16, LANES) for sub in range(2)], axis=1
        )
        x = operand(source, i, 1, half)
        acc_one[...] += lax.dot_general(g, x, (((0,), (0,)), ((), ())), preferred_element_type=f32)
        return 0

    lax.fori_loop(1, rows + 1, first_taps, 0)

    z = sums[...].reshape(rows + 1, 2, 96, LANES)
    z = [z[:, sub, at : at + 48].reshape((rows + 1) * 48, LANES) for at in (0, 48) for sub in range(2)]
    z = jnp.concatenate(z, axis=1)
    high = z.astype(bf16)
    low = (z - high.astype(f32)).astype(bf16)
    pulled = jnp.dot(high, back_one[...], preferred_element_type=f32)
    pulled = pulled + jnp.dot(low, back_one[...], preferred_element_type=f32)
    pulled = pulled.reshape(rows + 1, 48, 2 * LANES)
    result = (pulled[1:, :, :LANES] + pulled[:-1, :, LANES:]).astype(bf16)
    swap_to, swap_from = iota((own * rows, rows * 48), 0), iota((own * rows, rows * 48), 1)
    swap = (swap_to // rows == swap_from % 48) & (swap_to % rows == swap_from // 48)
    result = jnp.dot(swap.astype(bf16), result.reshape(rows * 48, LANES), preferred_element_type=f32)
    for t in range(own):
        out_lat[:, t * LANES : (t + 1) * LANES] = result[t * rows : (t + 1) * rows].astype(bf16)

    pack_taps(acc_one, out_taps, 0, chan0, chan1, norm)
    pack_taps(acc_two, out_taps, -(-9 // (LANES // chan0)) * chan1, chan1, chan2, norm)


def swapped(array, axis, bit):
    return lax.ppermute(array, axis, [(i, i ^ bit) for i in range(lax.axis_size(axis))])


def local(
    latent, member_seeds, noise_scale, kernel_one, kernel_two, targets, land_words, channel_weight
):
    sample_count, rows, span = latent.shape
    chan0, chan1, chan2 = kernel_one.shape[2], kernel_one.shape[3], kernel_two.shape[3]
    lat_count = lax.axis_size("lat")
    own = span // LANES // lax.axis_size("mem")
    half = (own + 1) // 2
    assert sample_count == 1 and member_seeds.shape[0] == MEM and own % 2 == 1 and lax.axis_size("mem") == 4
    assert 4 * chan2 == 2 * chan1 == chan0 and chan0 == 64
    vmem = pl.BlockSpec(memory_space=pltpu.VMEM)
    smem = pl.BlockSpec(memory_space=pltpu.SMEM)
    f32, bf16 = jnp.float32, jnp.bfloat16
    wide, front = half + 2, half + 1
    params = pltpu.CompilerParams(vmem_limit_bytes=56 * 1024 * 1024)
    kernel_one = kernel_one.transpose(0, 1, 3, 2)
    kernel_two = kernel_two.transpose(0, 1, 3, 2)
    down, up = pl.pallas_call(
        functools.partial(edge_kernel, half, chan2),
        grid=(1,),
        in_specs=[
            pl.BlockSpec((1, 8, span), lambda i: (0, 0, 0)),
            pl.BlockSpec((1, 8, span), lambda i: (0, rows // 2 - 1, 0)),
            pl.BlockSpec((8, land_words.shape[1]), lambda i: (rows // 2 - 1, 0)),
        ],
        out_specs=[
            pl.BlockSpec((2 * wide, 8, LANES), lambda i: (0, 0, 0)),
            pl.BlockSpec((1, 2 * wide * LANES), lambda i: (0, 0)),
        ],
        out_shape=[
            jax.ShapeDtypeStruct((2 * wide, 8, LANES), bf16),
            jax.ShapeDtypeStruct((1, 2 * wide * LANES), bf16),
        ],
        scratch_shapes=[pltpu.VMEM((8, LANES), jnp.int32)],
        name="edges",
    )(latent, targets, land_words)
    above = shifted(down, "lat", 1)
    below = shifted(up, "lat", -1)
    norm = 1.0 / math.sqrt(sample_count * 4 * rows * lat_count * targets.shape[2])
    lat_grad, taps = pl.pallas_call(
        functools.partial(band_kernel, half, norm),
        in_specs=[smem] * 3 + [vmem] * 7,
        out_specs=[vmem, vmem],
        out_shape=[
            jax.ShapeDtypeStruct((rows, own * LANES), bf16),
            jax.ShapeDtypeStruct((5 * chan1 + 3 * chan2, LANES), f32),
        ],
        scratch_shapes=[
            pltpu.VMEM((2 * wide, rows + 8, LANES), f32),
            pltpu.VMEM((2 * front, 4 * rows + 8, LANES), f32),
            pltpu.VMEM((2 * front, 4 * rows + 8, LANES), f32),
            pltpu.VMEM((4 * rows, LANES), jnp.int32),
            pltpu.VMEM((512, 256), bf16),
            pltpu.VMEM((512, 256), bf16),
            pltpu.VMEM((512, 256), bf16),
            pltpu.VMEM((512, 256), bf16),
            pltpu.VMEM((rows + 3, wide + 1, 16, LANES), bf16),
            pltpu.VMEM((wide * 16, 2 * LANES), f32),
            pltpu.VMEM((2 * rows + 4, wide, 16, LANES), bf16),
            pltpu.VMEM((2 * rows + 4, front, 16, LANES), f32),
            pltpu.VMEM((front * 16, 2 * LANES), f32),
            pltpu.VMEM((2, front + 1, 16, LANES), bf16),
            pltpu.VMEM((front * 16, LANES), f32),
            pltpu.VMEM((2 * rows + 2, front, 16, LANES), bf16),
            pltpu.VMEM((2 * rows + 2, 96, LANES), f32),
            pltpu.VMEM((256, 512), f32),
            pltpu.VMEM((256, 512), f32),
        ],
        compiler_params=params,
        name="band",
    )(
        member_seeds,
        noise_scale,
        channel_weight,
        latent,
        above,
        below,
        targets,
        land_words,
        kernel_one,
        kernel_two,
    )
    quarters = [lat_grad] + [swapped(lat_grad, "mem", k) for k in range(1, 4)]
    for axis in ("lat", "mem"):
        bit = 1
        while bit < lax.axis_size(axis):
            taps = taps + swapped(taps, axis, bit)
            bit *= 2
    latent_grad, one, two = pl.pallas_call(
        functools.partial(place_kernel, own),
        in_specs=[vmem] * 5,
        out_specs=[vmem] * 3,
        out_shape=[
            jax.ShapeDtypeStruct((1, rows, span), f32),
            jax.ShapeDtypeStruct(kernel_one.shape, f32),
            jax.ShapeDtypeStruct(kernel_two.shape, f32),
        ],
        name="place",
    )(*quarters, taps)
    return (latent_grad, one.transpose(0, 1, 3, 2), two.transpose(0, 1, 3, 2))


def solution(mesh):
    in_specs = (P(None, "lat", None), P(), P(), P(), P(), P(None, "lat", None), P("lat", None), P())
    out_specs = (P(None, "lat", None), P(), P())
    return jax.shard_map(local, mesh=mesh, in_specs=in_specs, out_specs=out_specs, check_vma=False)
```

```python
import functools
import math

import jax
import jax.numpy as jnp
from jax import lax
from jax.experimental import pallas as pl
from jax.experimental.pallas import tpu as pltpu
from jax.sharding import PartitionSpec as P

SMOOTH = 0.01
HASH_CELL = 1103515245
HASH_SEED = 747796405
HASH_MIX = 277803737
LANES = 128
MEM = 8
GELU_A = math.sqrt(2.0 / math.pi)
GELU_B = 0.044715


def shifted(array, axis, by):
    peers = lax.axis_size(axis)
    pairs = [(i, i + by) for i in range(peers) if 0 <= i + by < peers]
    return lax.ppermute(array, axis, pairs)


def iota(shape, axis):
    return lax.broadcasted_iota(jnp.int32, shape, axis)


def lane_table(ref, count):
    lane = iota((8, LANES), 1) % count
    total = jnp.zeros((8, LANES), jnp.float32)
    for k in range(count):
        total = jnp.where(lane == k, ref[k], total)
    return total


def build_band(kernel_ref, band_ref):
    chan_out, chan_in = kernel_ref.shape[2], kernel_ref.shape[3]
    cells = LANES // chan_in
    repeat = (iota((chan_out, LANES), 1) % chan_out == iota((chan_out, LANES), 0)).astype(jnp.bfloat16)
    wide = {}
    for a in range(3):
        for b in range(3):
            wide[a, b] = lax.dot_general(
                kernel_ref[a, b], repeat, (((0,), (0,)), ((), ())), preferred_element_type=jnp.float32
            )
    column = iota((chan_in, LANES), 1) // chan_out
    zero = jnp.zeros((chan_in, LANES), jnp.float32)
    for block in range(2):
        for row in range(2):
            for cell in range(cells):
                at = block * 256 + row * LANES + cell * chan_in
                for sub in range(2):
                    a = sub - 2 * row + 1
                    part = zero
                    for q in range(2 * cells):
                        b = q - 2 * (cell + block * cells) + 1
                        if 0 <= a <= 2 and 0 <= b <= 2:
                            part = jnp.where(column == q, wide[a, b], part)
                    band_ref[at : at + chan_in, sub * LANES : (sub + 1) * LANES] = part.astype(jnp.bfloat16)


def build_back(kernel_ref, back_ref):
    chan_out, chan_in = kernel_ref.shape[2], kernel_ref.shape[3]
    cells = LANES // chan_in
    repeat = (iota((chan_in, LANES), 1) % chan_in == iota((chan_in, LANES), 0)).astype(jnp.bfloat16)
    flat = kernel_ref[...].reshape(9 * chan_out, chan_in)
    wide = jnp.dot(flat, repeat, preferred_element_type=jnp.float32)
    column = iota((chan_out, LANES), 1) // chan_in
    zero = jnp.zeros((chan_out, LANES), jnp.float32)
    for block in range(2):
        for sub in range(2):
            for q in range(2 * cells):
                at = block * 256 + sub * LANES + q * chan_out
                for row in range(2):
                    a = sub - 2 * row + 1
                    part = zero
                    for cell in range(cells):
                        b = q - 2 * (cell + block * cells) + 1
                        if 0 <= a <= 2 and 0 <= b <= 2:
                            tap = (3 * a + b) * chan_out
                            part = jnp.where(column == cell, wide[tap : tap + chan_out], part)
                    back_ref[at : at + chan_out, row * LANES : (row + 1) * LANES] = part.astype(jnp.bfloat16)


def pack_taps(acc_ref, out_ref, first, chan_in, chan_out, norm):
    cells = LANES // chan_in
    group = iota((chan_out, LANES), 1) // chan_in
    packed = None
    for k in range(9):
        a, b = divmod(k, 3)
        row, sub = ((1, 1), (0, 0), (0, 1))[a]
        slot = k % cells
        part = None
        for reach in range(cells + 1):
            q = 2 * reach + b - 1
            if 0 <= q < 2 * cells:
                block, cell = reach // cells, reach % cells
                lines = sub * LANES + q * chan_out
                lanes = block * 256 + row * LANES
                piece = acc_ref[lines : lines + chan_out, lanes : lanes + LANES]
                turn = (slot - cell) % cells * chan_in
                piece = pltpu.roll(piece, turn, 1) if turn else piece
                part = piece if part is None else part + piece
        packed = part if slot == 0 else jnp.where(group == slot, part, packed)
        if slot == cells - 1 or k == 8:
            at = first + k // cells * chan_out
            out_ref[at : at + chan_out, :] = packed * norm


def window_block(mem_pos, own, half, blocks, part, t):
    at = mem_pos * own + part * half + t + (blocks - 1)
    at = jnp.where(at >= blocks, at - blocks, at)
    return jnp.where(at >= blocks, at - blocks, at)


def land_of(words, block, chan):
    cell = block * (LANES // chan) + iota(words.shape, 1) // chan
    word = jnp.right_shift(cell * 2185, 16)
    picked = jnp.take_along_axis(words, word, axis=1, mode="promise_in_bounds")
    return jnp.bitwise_and(jnp.right_shift(picked, cell - 30 * word), 1).astype(jnp.float32)


def edge_kernel(half, chan, latent, targets, land, down, up, words):
    rows = latent.shape[1]
    blocks = latent.shape[2] // LANES
    own = blocks // lax.axis_size("mem")
    mem_pos = lax.axis_index("mem")
    words[...] = jnp.zeros(words.shape, jnp.int32)
    words[:, : land.shape[1]] = land[...]
    line = iota((8, LANES), 0)
    for t in range(half + 2):
        for part in range(2):
            block = window_block(mem_pos, own, half, blocks, part, t)
            off = pl.multiple_of(block * LANES, LANES)
            slot = t * 2 + part
            cells = latent[0, :, pl.ds(off, LANES)].astype(jnp.float32)
            aims = targets[0, :, pl.ds(off, LANES)].astype(jnp.float32)
            mask = land_of(words[...], block, chan)
            pack = pltpu.roll(cells, 1, 0)
            pack = jnp.where((line >= 1) & (line <= 3), pltpu.roll(aims, 4, 0), pack)
            pack = jnp.where((line >= 4) & (line <= 6), pltpu.roll(mask, 7, 0), pack)
            down[slot] = pack.astype(jnp.bfloat16)
            up[:, slot * LANES : (slot + 1) * LANES] = cells[0:1].astype(jnp.bfloat16)


def place_kernel(own, part0, part1, part2, part3, latent_grad):
    mem_pos = lax.axis_index("mem")
    for k, part in enumerate((part0, part1, part2, part3)):
        off = pl.multiple_of(jnp.bitwise_xor(mem_pos, k) * own * LANES, LANES)
        latent_grad[0, :, pl.ds(off, own * LANES)] = part[...].astype(jnp.float32)


def taps_kernel(mine, other, grad_one, grad_two, taps):
    count = mine.shape[0]
    odd = jnp.bitwise_and(lax.axis_index("lat"), 1)
    taps[pl.ds(pl.multiple_of(odd * count, 8), count), :] = mine[...]
    taps[pl.ds(pl.multiple_of((1 - odd) * count, 8), count), :] = other[...]
    first = 0
    for out in (grad_one, grad_two):
        chan_out, chan_in = out.shape[2], out.shape[3]
        cells = LANES // chan_in
        for k in range(9):
            at = first + k // cells * chan_out
            block = taps[at : at + chan_out, :]
            turn = (-(k % cells)) % cells * chan_in
            block = pltpu.roll(block, turn, 1) if turn else block
            out[k // 3, k % 3] = block[:, :chan_in]
        first += -(-9 // cells) * chan_out


def latent_kernel(rows, own, sums, kernel_one, out_lat, back_one):
    bf16, f32 = jnp.bfloat16, jnp.float32
    build_back(kernel_one, back_one)
    z = sums[...].reshape(rows + 1, 2, 96, LANES)
    z = [z[:, sub, at : at + 48].reshape((rows + 1) * 48, LANES) for at in (0, 48) for sub in range(2)]
    z = jnp.concatenate(z, axis=1)
    high = z.astype(bf16)
    low = (z - high.astype(f32)).astype(bf16)
    pulled = jnp.dot(high, back_one[...], preferred_element_type=f32)
    pulled = pulled + jnp.dot(low, back_one[...], preferred_element_type=f32)
    pulled = pulled.reshape(rows + 1, 48, 2 * LANES)
    result = (pulled[1:, :, :LANES] + pulled[:-1, :, LANES:]).astype(bf16)
    swap_to, swap_from = iota((own * rows, rows * 48), 0), iota((own * rows, rows * 48), 1)
    swap = (swap_to // rows == swap_from % 48) & (swap_to % rows == swap_from // 48)
    result = jnp.dot(swap.astype(bf16), result.reshape(rows * 48, LANES), preferred_element_type=f32)
    for t in range(own):
        out_lat[:, t * LANES : (t + 1) * LANES] = result[t * rows : (t + 1) * rows].astype(bf16)


def band_kernel(
    half,
    norm,
    seeds,
    scale,
    channel_weight,
    latent,
    above,
    below,
    targets,
    land,
    kernel_one,
    kernel_two,
    sums,
    taps_keep,
    taps_send,
    lat_rows,
    tgt_rows,
    weight_rows,
    words,
    band_one,
    band_two,
    back_two,
    source,
    pre,
    act,
    slope,
    cast,
    fgrad,
    carry,
    pgrad,
    taps,
    acc_one,
    acc_two,
):
    rows = latent.shape[1]
    span = latent.shape[2]
    blocks = span // LANES
    lat_count = lax.axis_size("lat")
    own = blocks // lax.axis_size("mem")
    total_rows = rows * lat_count
    grid_rows = 4 * rows
    grid_total = grid_rows * lat_count
    lat_pos = lax.axis_index("lat")
    mem_pos = lax.axis_index("mem")
    wide = half + 2
    front = half + 1
    chan0, chan1, chan2 = kernel_one.shape[3], kernel_two.shape[3], kernel_two.shape[2]
    f32, bf16 = jnp.float32, jnp.bfloat16

    def block_of(part, t):
        return window_block(mem_pos, own, half, blocks, part, t)

    pad_rows = grid_rows + 8
    grid_row = iota((pad_rows, LANES), 0)
    grid_row = jnp.where(grid_row < grid_rows, grid_row, grid_row - (grid_rows + 4)) + lat_pos * grid_rows
    latitude = math.pi / 2 - math.pi * (grid_row.astype(f32) + 0.5) / grid_total
    channels = lane_table(channel_weight, chan2)
    cosine = jnp.where(grid_row >= 0, jnp.cos(latitude), 0.0)
    base_rows = cosine * (jnp.tile(channels, (pad_rows // 8, 1)) * (1.0 / (MEM * (MEM - 1))))

    words[...] = jnp.zeros(words.shape, jnp.int32)
    words[:, : land.shape[1]] = land[...]
    for t in range(wide):
        for part in range(2):
            block = block_of(part, t)
            off = pl.multiple_of(block * LANES, LANES)
            slot = t * 2 + part
            edge = above[slot].astype(f32)
            lat_rows[slot, 0:rows] = latent[0, :, pl.ds(off, LANES)].astype(f32)
            lat_rows[slot, rows : rows + 1] = below[:, slot * LANES : (slot + 1) * LANES].astype(f32)
            lat_rows[slot, rows + 1 : rows + 2] = edge[0:1]
            if t < front:
                tgt_rows[slot, 0:grid_rows] = targets[0, :, pl.ds(off, LANES)].astype(f32)
                tgt_rows[slot, grid_rows:] = edge
                mask = jnp.concatenate([land_of(words[...], block, chan2), pltpu.roll(edge, 5, 0)], axis=0)
                weight_rows[slot] = base_rows + base_rows * mask

    build_band(kernel_one, band_one)
    build_band(kernel_two, band_two)
    build_back(kernel_two, back_two)

    source[rows + 2] = jnp.zeros(source.shape[1:], bf16)
    source[:, wide] = jnp.zeros((source.shape[0],) + source.shape[2:], bf16)
    fgrad[:, 0] = jnp.zeros((2,) + fgrad.shape[2:], bf16)
    carry[...] = jnp.zeros(carry.shape, f32)
    acc_one[...] = jnp.zeros(acc_one.shape, f32)
    acc_two[...] = jnp.zeros(acc_two.shape, f32)

    sublane = iota((8, LANES), 0)
    seed_table = jnp.zeros((8, LANES), jnp.int32)
    for m in range(MEM):
        seed_table = jnp.where(sublane == m, seeds[m], seed_table)
    hash_table = iota((8, LANES), 1) * HASH_CELL + seed_table * HASH_SEED
    scale_table = lane_table(scale, chan0)

    def make_source(i, _):
        row = lat_pos * rows - 1 + i
        inside = jnp.where(row < total_rows, 1.0, 0.0).astype(f32)
        at = jnp.where(i == 0, rows + 1, i - 1)
        for t in range(wide):
            parts = []
            for part in range(2):
                first = (row * span + block_of(part, t) * LANES) * HASH_CELL
                h = hash_table + first
                h = jnp.bitwise_xor(h, jnp.right_shift(h, 15))
                h = h * HASH_MIX
                h = jnp.bitwise_xor(h, jnp.right_shift(h, 13))
                noise = jnp.bitwise_and(h, 65535).astype(f32) * (1.0 / 65536.0) - 0.5
                noise = noise * 3.4641016
                cell = lat_rows[t * 2 + part, pl.ds(at, 1), :]
                parts.append((cell + noise * scale_table) * inside)
            source[i, t] = jnp.concatenate(parts, axis=0).astype(bf16)
        return 0

    lax.fori_loop(0, rows + 2, make_source, 0)

    def operand(ref, i, start, count):
        def piece(r, at):
            return ref[r, pl.ds(at, count)].reshape(count * 16, LANES)

        return jnp.concatenate(
            [piece(i, start), piece(i + 1, start), piece(i, start + 1), piece(i + 1, start + 1)], axis=1
        )

    def first_segment(i, _):
        pre[...] = jnp.dot(operand(source, i, 0, wide), band_one[...], preferred_element_type=f32)
        for t in range(wide):
            for sub in range(2):
                x = pre[t * 16 : (t + 1) * 16, sub * LANES : (sub + 1) * LANES]
                square = x * x
                th = jnp.tanh(x * (GELU_A + (GELU_A * GELU_B) * square))
                plus = 0.5 + 0.5 * th
                act[2 * i + sub, t] = (x * plus).astype(bf16)
                if t < front:
                    d = plus + (x * plus) * (1.0 - th) * (GELU_A + (3.0 * GELU_A * GELU_B) * square)
                    if t == half:
                        d = jnp.where(iota((16, LANES), 0) < 8, d, 0.0)
                    slope[2 * i + sub, t] = d
        return 0

    lax.fori_loop(0, rows + 2, first_segment, 0)

    members = front * 16
    owner = iota((48, members), 0)
    group = iota((48, members), 1) // 8
    place = (group % 2) * half + group // 2
    real = (group // 2 > 0) & (place - 1 < own)
    pick_own = (real & (place - 1 == owner)).astype(bf16)
    pick_prev = ((group // 2 < half) & (place == owner)).astype(bf16)
    pick = jnp.concatenate([pick_own, pick_prev], axis=0)

    def second_segment(j, _):
        taken = operand(act, j, 0, front)
        cast[...] = jnp.dot(taken, band_two[...], preferred_element_type=f32)
        for sub in range(2):
            p = 2 * j + sub
            line = jnp.where(p >= 4, p - 4, p + grid_rows)
            for t in range(front):
                parts = []
                for part in range(2):
                    if t == half and part == 1:
                        parts.append(jnp.zeros((8, LANES), f32))
                        continue
                    at = t * 16 + part * 8
                    f = cast[at : at + 8, sub * LANES : (sub + 1) * LANES].astype(bf16).astype(f32)
                    y = tgt_rows[t * 2 + part, pl.ds(line, 1), :]
                    d = f - y
                    goal = d * lax.rsqrt(d * d + SMOOTH)
                    gs = []
                    for k in range(1, 5):
                        d = f - pltpu.roll(f, k, 0)
                        gs.append(d * lax.rsqrt(d * d + SMOOTH))
                    back = gs[2]
                    for k in (1, 0):
                        back = gs[k] + pltpu.roll(back, MEM - 1, 0)
                    back = pltpu.roll(back, MEM - 1, 0)
                    spread = (gs[0] + gs[1]) + (gs[2] + gs[3]) - back
                    weight = weight_rows[t * 2 + part, pl.ds(line, 1), :]
                    parts.append(weight * ((MEM - 1.0) * goal - spread))
                fgrad[sub, t + 1] = jnp.concatenate(parts, axis=0).astype(bf16)

        def flat(sub, at, count):
            return fgrad[sub, at : at + count].reshape(count * 16, LANES)

        @pl.when(j >= 2)
        def _():
            g = jnp.concatenate([flat(0, 2, half), flat(1, 2, half)], axis=1)
            x = operand(act, j, 1, half)
            acc_two[...] += lax.dot_general(g, x, (((0,), (0,)), ((), ())), preferred_element_type=f32)

        g = jnp.concatenate([flat(0, 1, front), flat(1, 1, front), flat(0, 0, front), flat(1, 0, front)], axis=1)
        pulled = jnp.dot(g, back_two[...], preferred_element_type=f32)
        grad = pulled[:, :LANES] + carry[...]
        carry[...] = pulled[:, LANES:]
        grad = (grad * slope[j].reshape(members, LANES)).astype(bf16)
        pgrad[j] = grad.reshape(front, 16, LANES)
        sums[j] = jnp.dot(pick, grad, preferred_element_type=f32)
        return 0

    lax.fori_loop(0, 2 * rows + 2, second_segment, 0)

    def first_taps(i, _):
        g = jnp.concatenate(
            [pgrad[2 * i + sub, pl.ds(1, half)].reshape(half * 16, LANES) for sub in range(2)], axis=1
        )
        x = operand(source, i, 1, half)
        acc_one[...] += lax.dot_general(g, x, (((0,), (0,)), ((), ())), preferred_element_type=f32)
        return 0

    lax.fori_loop(1, rows + 1, first_taps, 0)

    pack_taps(acc_one, taps, 0, chan0, chan1, norm)
    pack_taps(acc_two, taps, -(-9 // (LANES // chan0)) * chan1, chan1, chan2, norm)
    count = taps_keep.shape[0]
    odd = jnp.bitwise_and(lat_pos, 1)
    taps_keep[...] = taps[pl.ds(pl.multiple_of(odd * count, 8), count), :]
    taps_send[...] = taps[pl.ds(pl.multiple_of((1 - odd) * count, 8), count), :]


def swapped(array, axis, bit):
    return lax.ppermute(array, axis, [(i, i ^ bit) for i in range(lax.axis_size(axis))])


def total(array, axis, bits):
    if len(bits) == 1:
        return array + swapped(array, axis, bits[0])
    first, second = bits
    one, two, three = (swapped(array, axis, k) for k in (first, second, first ^ second))
    return (array + one) + (two + three)


def local(
    latent, member_seeds, noise_scale, kernel_one, kernel_two, targets, land_words, channel_weight
):
    sample_count, rows, span = latent.shape
    chan0, chan1, chan2 = kernel_one.shape[2], kernel_one.shape[3], kernel_two.shape[3]
    lat_count = lax.axis_size("lat")
    own = span // LANES // lax.axis_size("mem")
    half = (own + 1) // 2
    assert sample_count == 1 and member_seeds.shape[0] == MEM and own % 2 == 1 and lax.axis_size("mem") == 4
    assert 4 * chan2 == 2 * chan1 == chan0 and chan0 == 64
    vmem = pl.BlockSpec(memory_space=pltpu.VMEM)
    smem = pl.BlockSpec(memory_space=pltpu.SMEM)
    f32, bf16 = jnp.float32, jnp.bfloat16
    wide, front = half + 2, half + 1
    params = pltpu.CompilerParams(vmem_limit_bytes=32 * 1024 * 1024)
    kernel_one = kernel_one.transpose(0, 1, 3, 2)
    kernel_two = kernel_two.transpose(0, 1, 3, 2)
    down, up = pl.pallas_call(
        functools.partial(edge_kernel, half, chan2),
        grid=(1,),
        in_specs=[
            pl.BlockSpec((1, 8, span), lambda i: (0, 0, 0)),
            pl.BlockSpec((1, 8, span), lambda i: (0, rows // 2 - 1, 0)),
            pl.BlockSpec((8, land_words.shape[1]), lambda i: (rows // 2 - 1, 0)),
        ],
        out_specs=[
            pl.BlockSpec((2 * wide, 8, LANES), lambda i: (0, 0, 0)),
            pl.BlockSpec((1, 2 * wide * LANES), lambda i: (0, 0)),
        ],
        out_shape=[
            jax.ShapeDtypeStruct((2 * wide, 8, LANES), bf16),
            jax.ShapeDtypeStruct((1, 2 * wide * LANES), bf16),
        ],
        scratch_shapes=[pltpu.VMEM((8, LANES), jnp.int32)],
        name="edges",
    )(latent, targets, land_words)
    above = shifted(down, "lat", 1)
    below = shifted(up, "lat", -1)
    norm = 1.0 / math.sqrt(sample_count * 4 * rows * lat_count * targets.shape[2])
    tap_rows = 5 * chan1 + 3 * chan2
    sums, taps, taps_send = pl.pallas_call(
        functools.partial(band_kernel, half, norm),
        in_specs=[smem] * 3 + [vmem] * 7,
        out_specs=[vmem] * 3,
        out_shape=[
            jax.ShapeDtypeStruct((2 * rows + 2, 96, LANES), f32),
            jax.ShapeDtypeStruct((tap_rows // 2, LANES), f32),
            jax.ShapeDtypeStruct((tap_rows // 2, LANES), f32),
        ],
        scratch_shapes=[
            pltpu.VMEM((2 * wide, rows + 8, LANES), f32),
            pltpu.VMEM((2 * front, 4 * rows + 8, LANES), f32),
            pltpu.VMEM((2 * front, 4 * rows + 8, LANES), f32),
            pltpu.VMEM((4 * rows, LANES), jnp.int32),
            pltpu.VMEM((512, 256), bf16),
            pltpu.VMEM((512, 256), bf16),
            pltpu.VMEM((512, 256), bf16),
            pltpu.VMEM((rows + 3, wide + 1, 16, LANES), bf16),
            pltpu.VMEM((wide * 16, 2 * LANES), f32),
            pltpu.VMEM((2 * rows + 4, wide, 16, LANES), bf16),
            pltpu.VMEM((2 * rows + 4, front, 16, LANES), f32),
            pltpu.VMEM((front * 16, 2 * LANES), f32),
            pltpu.VMEM((2, front + 1, 16, LANES), bf16),
            pltpu.VMEM((front * 16, LANES), f32),
            pltpu.VMEM((2 * rows + 2, front, 16, LANES), bf16),
            pltpu.VMEM((tap_rows, LANES), f32),
            pltpu.VMEM((256, 512), f32),
            pltpu.VMEM((256, 512), f32),
        ],
        compiler_params=params,
        name="band",
    )(
        member_seeds,
        noise_scale,
        channel_weight,
        latent,
        above,
        below,
        targets,
        land_words,
        kernel_one,
        kernel_two,
    )
    lat_grad = pl.pallas_call(
        functools.partial(latent_kernel, rows, own),
        in_specs=[vmem] * 2,
        out_specs=vmem,
        out_shape=jax.ShapeDtypeStruct((rows, own * LANES), bf16),
        scratch_shapes=[pltpu.VMEM((512, 256), bf16)],
        name="latent",
    )(sums, kernel_one)
    quarters = [swapped(lat_grad, "mem", k) for k in range(1, 4)]
    taps = taps + swapped(taps_send, "lat", 1)
    bits = [1 << k for k in range(1, lat_count.bit_length() - 1)]
    for k in range(0, len(bits), 2):
        taps = total(taps, "lat", bits[k : k + 2])
    taps, quarters = lax.optimization_barrier((taps, quarters))
    latent_grad = pl.pallas_call(
        functools.partial(place_kernel, own),
        in_specs=[vmem] * 4,
        out_specs=vmem,
        out_shape=jax.ShapeDtypeStruct((1, rows, span), f32),
        name="place",
    )(lat_grad, *quarters)
    taps = total(taps, "mem", [1, 2])
    other = swapped(taps, "lat", 1)
    one, two = pl.pallas_call(
        taps_kernel,
        in_specs=[vmem] * 2,
        out_specs=[vmem] * 2,
        out_shape=[
            jax.ShapeDtypeStruct(kernel_one.shape, f32),
            jax.ShapeDtypeStruct(kernel_two.shape, f32),
        ],
        scratch_shapes=[pltpu.VMEM((tap_rows, LANES), f32)],
        name="taps",
    )(taps, other)
    return (latent_grad, one.transpose(0, 1, 3, 2), two.transpose(0, 1, 3, 2))


def solution(mesh):
    in_specs = (P(None, "lat", None), P(), P(), P(), P(), P(None, "lat", None), P("lat", None), P())
    out_specs = (P(None, "lat", None), P(), P())
    return jax.shard_map(local, mesh=mesh, in_specs=in_specs, out_specs=out_specs, check_vma=False)
```

```python
import functools
import math

import jax
import jax.numpy as jnp
from jax import lax
from jax.experimental import pallas as pl
from jax.experimental.pallas import tpu as pltpu
from jax.sharding import PartitionSpec as P

SMOOTH = 0.01
HASH_CELL = 1103515245
HASH_SEED = 747796405
HASH_MIX = 277803737
LANES = 128
MEM = 8
GELU_A = math.sqrt(2.0 / math.pi)
GELU_B = 0.044715


def shifted(array, axis, by):
    peers = lax.axis_size(axis)
    pairs = [(i, i + by) for i in range(peers) if 0 <= i + by < peers]
    return lax.ppermute(array, axis, pairs)


def iota(shape, axis):
    return lax.broadcasted_iota(jnp.int32, shape, axis)


def lane_table(ref, count):
    lane = iota((8, LANES), 1) % count
    total = jnp.zeros((8, LANES), jnp.float32)
    for k in range(count):
        total = jnp.where(lane == k, ref[k], total)
    return total


def build_band(kernel_ref, band_ref):
    chan_out, chan_in = kernel_ref.shape[2], kernel_ref.shape[3]
    cells = LANES // chan_in
    repeat = (iota((chan_out, LANES), 1) % chan_out == iota((chan_out, LANES), 0)).astype(jnp.bfloat16)
    wide = {}
    for a in range(3):
        for b in range(3):
            wide[a, b] = lax.dot_general(
                kernel_ref[a, b], repeat, (((0,), (0,)), ((), ())), preferred_element_type=jnp.float32
            )
    column = iota((chan_in, LANES), 1) // chan_out
    zero = jnp.zeros((chan_in, LANES), jnp.float32)
    for block in range(2):
        for row in range(2):
            for cell in range(cells):
                at = block * 256 + row * LANES + cell * chan_in
                for sub in range(2):
                    a = sub - 2 * row + 1
                    part = zero
                    for q in range(2 * cells):
                        b = q - 2 * (cell + block * cells) + 1
                        if 0 <= a <= 2 and 0 <= b <= 2:
                            part = jnp.where(column == q, wide[a, b], part)
                    band_ref[at : at + chan_in, sub * LANES : (sub + 1) * LANES] = part.astype(jnp.bfloat16)


def build_back(kernel_ref, back_ref):
    chan_out, chan_in = kernel_ref.shape[2], kernel_ref.shape[3]
    cells = LANES // chan_in
    repeat = (iota((chan_in, LANES), 1) % chan_in == iota((chan_in, LANES), 0)).astype(jnp.bfloat16)
    flat = kernel_ref[...].reshape(9 * chan_out, chan_in)
    wide = jnp.dot(flat, repeat, preferred_element_type=jnp.float32)
    column = iota((chan_out, LANES), 1) // chan_in
    zero = jnp.zeros((chan_out, LANES), jnp.float32)
    for block in range(2):
        for sub in range(2):
            for q in range(2 * cells):
                at = block * 256 + sub * LANES + q * chan_out
                for row in range(2):
                    a = sub - 2 * row + 1
                    part = zero
                    for cell in range(cells):
                        b = q - 2 * (cell + block * cells) + 1
                        if 0 <= a <= 2 and 0 <= b <= 2:
                            tap = (3 * a + b) * chan_out
                            part = jnp.where(column == cell, wide[tap : tap + chan_out], part)
                    back_ref[at : at + chan_out, row * LANES : (row + 1) * LANES] = part.astype(jnp.bfloat16)


def pack_taps(acc_ref, out_ref, first, chan_in, chan_out, norm):
    cells = LANES // chan_in
    group = iota((chan_out, LANES), 1) // chan_in
    packed = None
    for k in range(9):
        a, b = divmod(k, 3)
        row, sub = ((1, 1), (0, 0), (0, 1))[a]
        slot = k % cells
        part = None
        for reach in range(cells + 1):
            q = 2 * reach + b - 1
            if 0 <= q < 2 * cells:
                block, cell = reach // cells, reach % cells
                lines = sub * LANES + q * chan_out
                lanes = block * 256 + row * LANES
                piece = acc_ref[lines : lines + chan_out, lanes : lanes + LANES]
                turn = (slot - cell) % cells * chan_in
                piece = pltpu.roll(piece, turn, 1) if turn else piece
                part = piece if part is None else part + piece
        packed = part if slot == 0 else jnp.where(group == slot, part, packed)
        if slot == cells - 1 or k == 8:
            at = first + k // cells * chan_out
            out_ref[at : at + chan_out, :] = packed * norm


def spread_line(ref, slot, at):
    return ref[slot, pl.ds(at, 8, stride=0), :]


def window_block(mem_pos, own, half, blocks, part, t):
    at = mem_pos * own + part * half + t + (blocks - 1)
    at = jnp.where(at >= blocks, at - blocks, at)
    return jnp.where(at >= blocks, at - blocks, at)


def land_of(words, block, chan):
    cell = block * (LANES // chan) + iota(words.shape, 1) // chan
    word = jnp.right_shift(cell * 2185, 16)
    picked = jnp.take_along_axis(words, word, axis=1, mode="promise_in_bounds")
    return jnp.bitwise_and(jnp.right_shift(picked, cell - 30 * word), 1).astype(jnp.float32)


def edge_kernel(half, chan, latent, targets, land, down, up, words):
    rows = latent.shape[1]
    blocks = latent.shape[2] // LANES
    own = blocks // lax.axis_size("mem")
    mem_pos = lax.axis_index("mem")
    words[...] = jnp.zeros(words.shape, jnp.int32)
    words[:, : land.shape[1]] = land[...]
    line = iota((8, LANES), 0)
    for t in range(half + 2):
        for part in range(2):
            block = window_block(mem_pos, own, half, blocks, part, t)
            off = pl.multiple_of(block * LANES, LANES)
            slot = t * 2 + part
            cells = latent[0, :, pl.ds(off, LANES)].astype(jnp.float32)
            aims = targets[0, :, pl.ds(off, LANES)].astype(jnp.float32)
            mask = land_of(words[...], block, chan)
            pack = pltpu.roll(cells, 1, 0)
            pack = jnp.where((line >= 1) & (line <= 3), pltpu.roll(aims, 4, 0), pack)
            pack = jnp.where((line >= 4) & (line <= 6), pltpu.roll(mask, 7, 0), pack)
            down[slot] = pack.astype(jnp.bfloat16)
            up[:, slot * LANES : (slot + 1) * LANES] = cells[0:1].astype(jnp.bfloat16)


def place_kernel(own, part0, part1, part2, part3, latent_grad):
    mem_pos = lax.axis_index("mem")
    for k, part in enumerate((part0, part1, part2, part3)):
        off = pl.multiple_of(jnp.bitwise_xor(mem_pos, k) * own * LANES, LANES)
        latent_grad[0, :, pl.ds(off, own * LANES)] = part[...].astype(jnp.float32)


def taps_kernel(mine, other, grad_one, grad_two, taps):
    count = mine.shape[0]
    odd = jnp.bitwise_and(lax.axis_index("lat"), 1)
    taps[pl.ds(pl.multiple_of(odd * count, 8), count), :] = mine[...]
    taps[pl.ds(pl.multiple_of((1 - odd) * count, 8), count), :] = other[...]
    first = 0
    for out in (grad_one, grad_two):
        chan_out, chan_in = out.shape[2], out.shape[3]
        cells = LANES // chan_in
        for k in range(9):
            at = first + k // cells * chan_out
            block = taps[at : at + chan_out, :]
            turn = (-(k % cells)) % cells * chan_in
            block = pltpu.roll(block, turn, 1) if turn else block
            out[k // 3, k % 3] = block[:, :chan_in]
        first += -(-9 // cells) * chan_out


def latent_kernel(rows, own, sums, kernel_one, out_lat, back_one):
    bf16, f32 = jnp.bfloat16, jnp.float32
    build_back(kernel_one, back_one)
    z = sums[...].reshape(rows + 1, 2, 96, LANES)
    z = [z[:, sub, at : at + 48].reshape((rows + 1) * 48, LANES) for at in (0, 48) for sub in range(2)]
    z = jnp.concatenate(z, axis=1)
    high = z.astype(bf16)
    low = (z - high.astype(f32)).astype(bf16)
    pulled = jnp.dot(high, back_one[...], preferred_element_type=f32)
    pulled = pulled + jnp.dot(low, back_one[...], preferred_element_type=f32)
    pulled = pulled.reshape(rows + 1, 48, 2 * LANES)
    result = (pulled[1:, :, :LANES] + pulled[:-1, :, LANES:]).astype(bf16)
    swap_to, swap_from = iota((own * rows, rows * 48), 0), iota((own * rows, rows * 48), 1)
    swap = (swap_to // rows == swap_from % 48) & (swap_to % rows == swap_from // 48)
    result = jnp.dot(swap.astype(bf16), result.reshape(rows * 48, LANES), preferred_element_type=f32)
    for t in range(own):
        out_lat[:, t * LANES : (t + 1) * LANES] = result[t * rows : (t + 1) * rows].astype(bf16)


def band_kernel(
    half,
    norm,
    seeds,
    scale,
    channel_weight,
    latent,
    above,
    below,
    targets,
    land,
    kernel_one,
    kernel_two,
    sums,
    taps_keep,
    taps_send,
    lat_rows,
    tgt_rows,
    weight_rows,
    words,
    band_one,
    band_two,
    back_two,
    source,
    pre_even,
    pre_odd,
    act,
    slope,
    cast_even,
    cast_odd,
    fgrad_even,
    fgrad_odd,
    carry,
    taps,
    acc_one,
    acc_two,
):
    rows = latent.shape[1]
    span = latent.shape[2]
    blocks = span // LANES
    lat_count = lax.axis_size("lat")
    own = blocks // lax.axis_size("mem")
    total_rows = rows * lat_count
    grid_rows = 4 * rows
    grid_total = grid_rows * lat_count
    lat_pos = lax.axis_index("lat")
    mem_pos = lax.axis_index("mem")
    wide = half + 2
    front = half + 1
    chan0, chan1, chan2 = kernel_one.shape[3], kernel_two.shape[3], kernel_two.shape[2]
    f32, bf16 = jnp.float32, jnp.bfloat16

    def block_of(part, t):
        return window_block(mem_pos, own, half, blocks, part, t)

    pad_rows = grid_rows + 8
    grid_row = iota((pad_rows, LANES), 0)
    grid_row = jnp.where(grid_row < grid_rows, grid_row, grid_row - (grid_rows + 4)) + lat_pos * grid_rows
    latitude = math.pi / 2 - math.pi * (grid_row.astype(f32) + 0.5) / grid_total
    channels = lane_table(channel_weight, chan2)
    cosine = jnp.where(grid_row >= 0, jnp.cos(latitude), 0.0)
    base_rows = cosine * (jnp.tile(channels, (pad_rows // 8, 1)) * (1.0 / (MEM * (MEM - 1))))

    words[...] = jnp.zeros(words.shape, jnp.int32)
    words[:, : land.shape[1]] = land[...]
    for t in range(wide):
        for part in range(2):
            block = block_of(part, t)
            off = pl.multiple_of(block * LANES, LANES)
            slot = t * 2 + part
            edge = above[slot].astype(f32)
            lat_rows[slot, 0:rows] = latent[0, :, pl.ds(off, LANES)].astype(f32)
            lat_rows[slot, rows : rows + 1] = below[:, slot * LANES : (slot + 1) * LANES].astype(f32)
            lat_rows[slot, rows + 1 : rows + 2] = edge[0:1]
            if t < front:
                tgt_rows[slot, 0:grid_rows] = targets[0, :, pl.ds(off, LANES)].astype(f32)
                tgt_rows[slot, grid_rows:] = edge
                mask = jnp.concatenate([land_of(words[...], block, chan2), pltpu.roll(edge, 5, 0)], axis=0)
                weight_rows[slot] = base_rows + base_rows * mask

    build_band(kernel_one, band_one)
    build_band(kernel_two, band_two)
    build_back(kernel_two, back_two)

    source[rows + 2 :] = jnp.zeros((2,) + source.shape[1:], bf16)
    source[:, wide] = jnp.zeros((source.shape[0],) + source.shape[2:], bf16)
    fgrad_even[:, 0] = jnp.zeros((4,) + fgrad_even.shape[2:], bf16)
    fgrad_odd[...] = jnp.zeros(fgrad_odd.shape, bf16)
    carry[...] = jnp.zeros(carry.shape, f32)
    acc_one[...] = jnp.zeros(acc_one.shape, f32)
    acc_two[...] = jnp.zeros(acc_two.shape, f32)

    sublane = iota((8, LANES), 0)
    seed_table = jnp.zeros((8, LANES), jnp.int32)
    for m in range(MEM):
        seed_table = jnp.where(sublane == m, seeds[m], seed_table)
    hash_table = iota((8, LANES), 1) * HASH_CELL + seed_table * HASH_SEED
    scale_table = lane_table(scale, chan0)

    def make_source(i, _):
        row = lat_pos * rows - 1 + i
        inside = jnp.where(row < total_rows, 1.0, 0.0).astype(f32)
        at = jnp.where(i == 0, rows + 1, i - 1)
        for t in range(wide):
            parts = []
            for part in range(2):
                first = (row * span + block_of(part, t) * LANES) * HASH_CELL
                h = hash_table + first
                h = jnp.bitwise_xor(h, jnp.right_shift(h, 15))
                h = h * HASH_MIX
                h = jnp.bitwise_xor(h, jnp.right_shift(h, 13))
                noise = jnp.bitwise_and(h, 65535).astype(f32) * (1.0 / 65536.0) - 0.5
                noise = noise * 3.4641016
                cell = spread_line(lat_rows, t * 2 + part, at)
                parts.append((cell + noise * scale_table) * inside)
            source[i, t] = jnp.concatenate(parts, axis=0).astype(bf16)
        return 0

    lax.fori_loop(0, rows + 2, make_source, 0)

    def operand(ref, i, start, count):
        def piece(r, at):
            return ref[r, pl.ds(at, count)].reshape(count * 16, LANES)

        return jnp.concatenate(
            [piece(i, start), piece(i + 1, start), piece(i, start + 1), piece(i + 1, start + 1)], axis=1
        )

    def first_product(i, pre):
        pre[...] = jnp.dot(operand(source, i, 0, wide), band_one[...], preferred_element_type=f32)

    def first_gelu(i, pre):
        for t in range(wide):
            for sub in range(2):
                x = pre[t * 16 : (t + 1) * 16, sub * LANES : (sub + 1) * LANES]
                square = x * x
                th = jnp.tanh(x * (GELU_A + (GELU_A * GELU_B) * square))
                plus = 0.5 + 0.5 * th
                act[2 * i + sub, t] = (x * plus).astype(bf16)
                if t < front:
                    d = plus + (x * plus) * (1.0 - th) * (GELU_A + (3.0 * GELU_A * GELU_B) * square)
                    if t == half:
                        d = jnp.where(iota((16, LANES), 0) < 8, d, 0.0)
                    slope[2 * i + sub, t] = d

    def first_segment(m, _):
        first_product(2 * m + 1, pre_odd)
        first_gelu(2 * m, pre_even)
        first_product(2 * m + 2, pre_even)
        first_gelu(2 * m + 1, pre_odd)
        return 0

    first_product(0, pre_even)
    lax.fori_loop(0, rows // 2 + 1, first_segment, 0)

    members = front * 16
    owner = iota((48, members), 0)
    group = iota((48, members), 1) // 8
    place = (group % 2) * half + group // 2
    real = (group // 2 > 0) & (place - 1 < own)
    pick_own = (real & (place - 1 == owner)).astype(bf16)
    pick_prev = ((group // 2 < half) & (place == owner)).astype(bf16)
    pick = jnp.concatenate([pick_own, pick_prev], axis=0)

    def second_product(n, cast):
        taken = jnp.concatenate([operand(act, 2 * n + k, 0, front) for k in range(2)], axis=0)
        out = jnp.dot(taken, band_two[...], preferred_element_type=f32).astype(bf16)
        for k in range(2):
            for sub in range(2):
                part = out[k * members : (k + 1) * members, sub * LANES : (sub + 1) * LANES]
                cast[2 * k + sub] = part.reshape(front, 16, LANES)

    def loss_gradient(n, cast, fgrad):
        first = jnp.where(n >= 1, 4 * (n - 1), grid_rows)
        for line in range(4):
            for t in range(front):
                both = cast[line, t].astype(f32)
                parts = []
                for part in range(2):
                    if t == half and part == 1:
                        parts.append(jnp.zeros((8, LANES), f32))
                        continue
                    f = both[part * 8 : part * 8 + 8]
                    d = f - spread_line(tgt_rows, t * 2 + part, first + line)
                    goal = d * lax.rsqrt(d * d + SMOOTH)
                    gs = []
                    for k in range(1, 5):
                        d = f - pltpu.roll(f, k, 0)
                        gs.append(d * lax.rsqrt(d * d + SMOOTH))
                    back = gs[2]
                    for k in (1, 0):
                        back = gs[k] + pltpu.roll(back, MEM - 1, 0)
                    back = pltpu.roll(back, MEM - 1, 0)
                    spread = (gs[0] + gs[1]) + (gs[2] + gs[3]) - back
                    weight = spread_line(weight_rows, t * 2 + part, first + line)
                    parts.append(weight * ((MEM - 1.0) * goal - spread))
                fgrad[line, t + 1] = jnp.concatenate(parts, axis=0).astype(bf16)

    def pull_back(n, fgrad):
        at = jnp.maximum(n, 0)
        keep = jnp.where(n >= 1, 1.0, 0.0).astype(bf16)

        def flat(line, start, count):
            return fgrad[line, start : start + count].reshape(count * 16, LANES)

        def product(g, x):
            return lax.dot_general(g, x, (((0,), (0,)), ((), ())), preferred_element_type=f32)

        g = [
            jnp.concatenate(
                [flat(2 * k, 1, front), flat(2 * k + 1, 1, front), flat(2 * k, 0, front), flat(2 * k + 1, 0, front)],
                axis=1,
            )
            for k in range(2)
        ]
        pulled = jnp.dot(jnp.concatenate(g, axis=0), back_two[...], preferred_element_type=f32)
        g = [jnp.concatenate([flat(2 * k, 2, half), flat(2 * k + 1, 2, half)], axis=1) for k in range(2)]
        x = [operand(act, 2 * at + k, 1, half) for k in range(2)]
        acc_two[...] += product(jnp.concatenate(g, axis=0) * keep, jnp.concatenate(x, axis=0))
        grads = [
            pulled[:members, :LANES] + carry[...],
            pulled[members:, :LANES] + pulled[:members, LANES:],
        ]
        carry[...] = pulled[members:, LANES:]
        grads = [(grads[k] * slope[2 * at + k].reshape(members, LANES)).astype(bf16) for k in range(2)]
        grads = jnp.concatenate(grads, axis=1)
        total_grad = jnp.dot(pick, grads, preferred_element_type=f32)
        for k in range(2):
            sums[2 * at + k] = total_grad[:, k * LANES : (k + 1) * LANES]
        acc_one[...] += product(grads[16:] * keep, operand(source, at, 1, half))

    def second_segment(m, _):
        second_product(2 * m + 1, cast_odd)
        loss_gradient(2 * m, cast_even, fgrad_even)
        pull_back(2 * m - 1, fgrad_odd)
        second_product(2 * m + 2, cast_even)
        loss_gradient(2 * m + 1, cast_odd, fgrad_odd)
        pull_back(2 * m, fgrad_even)
        return 0

    second_product(0, cast_even)
    lax.fori_loop(0, rows // 2, second_segment, 0)
    loss_gradient(rows, cast_even, fgrad_even)
    pull_back(rows - 1, fgrad_odd)
    pull_back(rows, fgrad_even)

    pack_taps(acc_one, taps, 0, chan0, chan1, norm)
    pack_taps(acc_two, taps, -(-9 // (LANES // chan0)) * chan1, chan1, chan2, norm)
    count = taps_keep.shape[0]
    odd = jnp.bitwise_and(lat_pos, 1)
    taps_keep[...] = taps[pl.ds(pl.multiple_of(odd * count, 8), count), :]
    taps_send[...] = taps[pl.ds(pl.multiple_of((1 - odd) * count, 8), count), :]


def swapped(array, axis, bit):
    return lax.ppermute(array, axis, [(i, i ^ bit) for i in range(lax.axis_size(axis))])


def total(array, axis, bits):
    if len(bits) == 1:
        return array + swapped(array, axis, bits[0])
    first, second = bits
    one, two, three = (swapped(array, axis, k) for k in (first, second, first ^ second))
    return (array + one) + (two + three)


def local(
    latent, member_seeds, noise_scale, kernel_one, kernel_two, targets, land_words, channel_weight
):
    sample_count, rows, span = latent.shape
    chan0, chan1, chan2 = kernel_one.shape[2], kernel_one.shape[3], kernel_two.shape[3]
    lat_count = lax.axis_size("lat")
    own = span // LANES // lax.axis_size("mem")
    half = (own + 1) // 2
    assert sample_count == 1 and member_seeds.shape[0] == MEM and rows % 2 == 0 and own % 2 == 1 and lax.axis_size("mem") == 4
    assert 4 * chan2 == 2 * chan1 == chan0 and chan0 == 64
    vmem = pl.BlockSpec(memory_space=pltpu.VMEM)
    smem = pl.BlockSpec(memory_space=pltpu.SMEM)
    f32, bf16 = jnp.float32, jnp.bfloat16
    wide, front = half + 2, half + 1
    params = pltpu.CompilerParams(vmem_limit_bytes=32 * 1024 * 1024)
    kernel_one = kernel_one.transpose(0, 1, 3, 2)
    kernel_two = kernel_two.transpose(0, 1, 3, 2)
    down, up = pl.pallas_call(
        functools.partial(edge_kernel, half, chan2),
        grid=(1,),
        in_specs=[
            pl.BlockSpec((1, 8, span), lambda i: (0, 0, 0)),
            pl.BlockSpec((1, 8, span), lambda i: (0, rows // 2 - 1, 0)),
            pl.BlockSpec((8, land_words.shape[1]), lambda i: (rows // 2 - 1, 0)),
        ],
        out_specs=[
            pl.BlockSpec((2 * wide, 8, LANES), lambda i: (0, 0, 0)),
            pl.BlockSpec((1, 2 * wide * LANES), lambda i: (0, 0)),
        ],
        out_shape=[
            jax.ShapeDtypeStruct((2 * wide, 8, LANES), bf16),
            jax.ShapeDtypeStruct((1, 2 * wide * LANES), bf16),
        ],
        scratch_shapes=[pltpu.VMEM((8, LANES), jnp.int32)],
        name="edges",
    )(latent, targets, land_words)
    above = shifted(down, "lat", 1)
    below = shifted(up, "lat", -1)
    norm = 1.0 / math.sqrt(sample_count * 4 * rows * lat_count * targets.shape[2])
    tap_rows = 5 * chan1 + 3 * chan2
    sums, taps, taps_send = pl.pallas_call(
        functools.partial(band_kernel, half, norm),
        in_specs=[smem] * 3 + [vmem] * 7,
        out_specs=[vmem] * 3,
        out_shape=[
            jax.ShapeDtypeStruct((2 * rows + 2, 96, LANES), f32),
            jax.ShapeDtypeStruct((tap_rows // 2, LANES), f32),
            jax.ShapeDtypeStruct((tap_rows // 2, LANES), f32),
        ],
        scratch_shapes=[
            pltpu.VMEM((2 * wide, rows + 8, LANES), f32),
            pltpu.VMEM((2 * front, 4 * rows + 8, LANES), f32),
            pltpu.VMEM((2 * front, 4 * rows + 8, LANES), f32),
            pltpu.VMEM((4 * rows, LANES), jnp.int32),
            pltpu.VMEM((512, 256), bf16),
            pltpu.VMEM((512, 256), bf16),
            pltpu.VMEM((512, 256), bf16),
            pltpu.VMEM((rows + 4, wide + 1, 16, LANES), bf16),
            pltpu.VMEM((wide * 16, 2 * LANES), f32),
            pltpu.VMEM((wide * 16, 2 * LANES), f32),
            pltpu.VMEM((2 * rows + 4, wide, 16, LANES), bf16),
            pltpu.VMEM((2 * rows + 4, front, 16, LANES), f32),
            pltpu.VMEM((4, front, 16, LANES), bf16),
            pltpu.VMEM((4, front, 16, LANES), bf16),
            pltpu.VMEM((4, front + 1, 16, LANES), bf16),
            pltpu.VMEM((4, front + 1, 16, LANES), bf16),
            pltpu.VMEM((front * 16, LANES), f32),
            pltpu.VMEM((tap_rows, LANES), f32),
            pltpu.VMEM((256, 512), f32),
            pltpu.VMEM((256, 512), f32),
        ],
        compiler_params=params,
        name="band",
    )(
        member_seeds,
        noise_scale,
        channel_weight,
        latent,
        above,
        below,
        targets,
        land_words,
        kernel_one,
        kernel_two,
    )
    lat_grad = pl.pallas_call(
        functools.partial(latent_kernel, rows, own),
        in_specs=[vmem] * 2,
        out_specs=vmem,
        out_shape=jax.ShapeDtypeStruct((rows, own * LANES), bf16),
        scratch_shapes=[pltpu.VMEM((512, 256), bf16)],
        name="latent",
    )(sums, kernel_one)
    quarters = [swapped(lat_grad, "mem", k) for k in range(1, 4)]
    taps = taps + swapped(taps_send, "lat", 1)
    bits = [1 << k for k in range(1, lat_count.bit_length() - 1)]
    for k in range(0, len(bits), 2):
        taps = total(taps, "lat", bits[k : k + 2])
    taps, quarters = lax.optimization_barrier((taps, quarters))
    latent_grad = pl.pallas_call(
        functools.partial(place_kernel, own),
        in_specs=[vmem] * 4,
        out_specs=vmem,
        out_shape=jax.ShapeDtypeStruct((1, rows, span), f32),
        name="place",
    )(lat_grad, *quarters)
    taps = total(taps, "mem", [1, 2])
    other = swapped(taps, "lat", 1)
    one, two = pl.pallas_call(
        taps_kernel,
        in_specs=[vmem] * 2,
        out_specs=[vmem] * 2,
        out_shape=[
            jax.ShapeDtypeStruct(kernel_one.shape, f32),
            jax.ShapeDtypeStruct(kernel_two.shape, f32),
        ],
        scratch_shapes=[pltpu.VMEM((tap_rows, LANES), f32)],
        name="taps",
    )(taps, other)
    return (latent_grad, one.transpose(0, 1, 3, 2), two.transpose(0, 1, 3, 2))


def solution(mesh):
    in_specs = (P(None, "lat", None), P(), P(), P(), P(), P(None, "lat", None), P("lat", None), P())
    out_specs = (P(None, "lat", None), P(), P())
    return jax.shard_map(local, mesh=mesh, in_specs=in_specs, out_specs=out_specs, check_vma=False)
```

```python
import functools
import math

import jax
import jax.numpy as jnp
from jax import lax
from jax.experimental import pallas as pl
from jax.experimental.pallas import tpu as pltpu
from jax.sharding import PartitionSpec as P

SMOOTH = 0.01
HASH_CELL = 1103515245
HASH_SEED = 747796405
HASH_MIX = 277803737
LANES = 128
MEM = 8
GELU_A = math.sqrt(2.0 / math.pi)
GELU_B = 0.044715


def shifted(array, axis, by):
    peers = lax.axis_size(axis)
    pairs = [(i, i + by) for i in range(peers) if 0 <= i + by < peers]
    return lax.ppermute(array, axis, pairs)


def iota(shape, axis):
    return lax.broadcasted_iota(jnp.int32, shape, axis)


def lane_table(ref, count):
    lane = iota((8, LANES), 1) % count
    total = jnp.zeros((8, LANES), jnp.float32)
    for k in range(count):
        total = jnp.where(lane == k, ref[k], total)
    return total


def build_band(kernel_ref, band_ref):
    chan_out, chan_in = kernel_ref.shape[2], kernel_ref.shape[3]
    cells = LANES // chan_in
    repeat = (iota((chan_out, LANES), 1) % chan_out == iota((chan_out, LANES), 0)).astype(jnp.bfloat16)
    wide = {}
    for a in range(3):
        for b in range(3):
            wide[a, b] = lax.dot_general(
                kernel_ref[a, b], repeat, (((0,), (0,)), ((), ())), preferred_element_type=jnp.float32
            )
    column = iota((chan_in, LANES), 1) // chan_out
    zero = jnp.zeros((chan_in, LANES), jnp.float32)
    for block in range(2):
        for row in range(2):
            for cell in range(cells):
                at = block * 256 + row * LANES + cell * chan_in
                for sub in range(2):
                    a = sub - 2 * row + 1
                    part = zero
                    for q in range(2 * cells):
                        b = q - 2 * (cell + block * cells) + 1
                        if 0 <= a <= 2 and 0 <= b <= 2:
                            part = jnp.where(column == q, wide[a, b], part)
                    band_ref[at : at + chan_in, sub * LANES : (sub + 1) * LANES] = part.astype(jnp.bfloat16)


def build_back(kernel_ref, back_ref):
    chan_out, chan_in = kernel_ref.shape[2], kernel_ref.shape[3]
    cells = LANES // chan_in
    repeat = (iota((chan_in, LANES), 1) % chan_in == iota((chan_in, LANES), 0)).astype(jnp.bfloat16)
    flat = kernel_ref[...].reshape(9 * chan_out, chan_in)
    wide = jnp.dot(flat, repeat, preferred_element_type=jnp.float32)
    column = iota((chan_out, LANES), 1) // chan_in
    zero = jnp.zeros((chan_out, LANES), jnp.float32)
    for block in range(2):
        for sub in range(2):
            for q in range(2 * cells):
                at = block * 256 + sub * LANES + q * chan_out
                for row in range(2):
                    a = sub - 2 * row + 1
                    part = zero
                    for cell in range(cells):
                        b = q - 2 * (cell + block * cells) + 1
                        if 0 <= a <= 2 and 0 <= b <= 2:
                            tap = (3 * a + b) * chan_out
                            part = jnp.where(column == cell, wide[tap : tap + chan_out], part)
                    back_ref[at : at + chan_out, row * LANES : (row + 1) * LANES] = part.astype(jnp.bfloat16)


def pack_taps(acc_ref, out_ref, first, chan_in, chan_out, norm):
    cells = LANES // chan_in
    group = iota((chan_out, LANES), 1) // chan_in
    packed = None
    for k in range(9):
        a, b = divmod(k, 3)
        row, sub = ((1, 1), (0, 0), (0, 1))[a]
        slot = k % cells
        part = None
        for reach in range(cells + 1):
            q = 2 * reach + b - 1
            if 0 <= q < 2 * cells:
                block, cell = reach // cells, reach % cells
                lines = sub * LANES + q * chan_out
                lanes = block * 256 + row * LANES
                piece = acc_ref[lines : lines + chan_out, lanes : lanes + LANES]
                turn = (slot - cell) % cells * chan_in
                piece = pltpu.roll(piece, turn, 1) if turn else piece
                part = piece if part is None else part + piece
        packed = part if slot == 0 else jnp.where(group == slot, part, packed)
        if slot == cells - 1 or k == 8:
            at = first + k // cells * chan_out
            out_ref[at : at + chan_out, :] = packed * norm


def spread_line(ref, slot, at):
    return ref[slot, pl.ds(at, 8, stride=0), :]


def window_block(mem_pos, own, half, blocks, part, t):
    at = mem_pos * own + part * half + t + (blocks - 1)
    at = jnp.where(at >= blocks, at - blocks, at)
    return jnp.where(at >= blocks, at - blocks, at)


def land_of(words, block, chan):
    cell = block * (LANES // chan) + iota(words.shape, 1) // chan
    word = jnp.right_shift(cell * 2185, 16)
    picked = jnp.take_along_axis(words, word, axis=1, mode="promise_in_bounds")
    return jnp.bitwise_and(jnp.right_shift(picked, cell - 30 * word), 1).astype(jnp.float32)


def edge_kernel(half, chan, latent, targets, land, down, up, words):
    rows = latent.shape[1]
    blocks = latent.shape[2] // LANES
    own = blocks // lax.axis_size("mem")
    mem_pos = lax.axis_index("mem")
    words[...] = jnp.zeros(words.shape, jnp.int32)
    words[:, : land.shape[1]] = land[...]
    line = iota((8, LANES), 0)
    for t in range(half + 2):
        for part in range(2):
            block = window_block(mem_pos, own, half, blocks, part, t)
            off = pl.multiple_of(block * LANES, LANES)
            slot = t * 2 + part
            cells = latent[0, :, pl.ds(off, LANES)].astype(jnp.float32)
            aims = targets[0, :, pl.ds(off, LANES)].astype(jnp.float32)
            mask = land_of(words[...], block, chan)
            pack = pltpu.roll(cells, 1, 0)
            pack = jnp.where((line >= 1) & (line <= 3), pltpu.roll(aims, 4, 0), pack)
            pack = jnp.where((line >= 4) & (line <= 6), pltpu.roll(mask, 7, 0), pack)
            down[slot] = pack.astype(jnp.bfloat16)
            up[:, slot * LANES : (slot + 1) * LANES] = cells[0:1].astype(jnp.bfloat16)


def place_kernel(own, part0, part1, part2, part3, latent_grad):
    mem_pos = lax.axis_index("mem")
    for k, part in enumerate((part0, part1, part2, part3)):
        off = pl.multiple_of(jnp.bitwise_xor(mem_pos, k) * own * LANES, LANES)
        latent_grad[0, :, pl.ds(off, own * LANES)] = part[...].astype(jnp.float32)


def taps_kernel(mine, other, grad_one, grad_two, taps):
    count = mine.shape[0]
    odd = jnp.bitwise_and(lax.axis_index("lat"), 1)
    taps[pl.ds(pl.multiple_of(odd * count, 8), count), :] = mine[...]
    taps[pl.ds(pl.multiple_of((1 - odd) * count, 8), count), :] = other[...]
    first = 0
    for out in (grad_one, grad_two):
        chan_out, chan_in = out.shape[2], out.shape[3]
        cells = LANES // chan_in
        for k in range(9):
            at = first + k // cells * chan_out
            block = taps[at : at + chan_out, :]
            turn = (-(k % cells)) % cells * chan_in
            block = pltpu.roll(block, turn, 1) if turn else block
            out[k // 3, k % 3] = block[:, :chan_in]
        first += -(-9 // cells) * chan_out


def make_source(i, row, total_rows, span, own, half, seeds, scale, chan, line, store):
    blocks = span // LANES
    mem_pos = lax.axis_index("mem")
    sublane = iota((8, LANES), 0)
    seed_table = jnp.zeros((8, LANES), jnp.int32)
    for m in range(MEM):
        seed_table = jnp.where(sublane == m, seeds[m], seed_table)
    hash_table = iota((8, LANES), 1) * HASH_CELL + seed_table * HASH_SEED
    scale_table = lane_table(scale, chan)
    inside = jnp.where(row < total_rows, 1.0, 0.0).astype(jnp.float32)
    for t in range(half + 2):
        parts = []
        for part in range(2):
            first = (row * span + window_block(mem_pos, own, half, blocks, part, t) * LANES) * HASH_CELL
            h = hash_table + first
            h = jnp.bitwise_xor(h, jnp.right_shift(h, 15))
            h = h * HASH_MIX
            h = jnp.bitwise_xor(h, jnp.right_shift(h, 13))
            noise = jnp.bitwise_and(h, 65535).astype(jnp.float32) * (1.0 / 65536.0) - 0.5
            noise = noise * 3.4641016
            parts.append((line(t * 2 + part, i) + noise * scale_table) * inside)
        store(i, t, jnp.concatenate(parts, axis=0).astype(jnp.bfloat16))


def prepare_kernel(half, seeds, scale, latent, kernel_one, kernel_two, source, band_one, band_two, back_one, back_two, lines):
    rows, span = latent.shape[1], latent.shape[2]
    blocks = span // LANES
    own = blocks // lax.axis_size("mem")
    total_rows = rows * lax.axis_size("lat")
    lat_pos, mem_pos = lax.axis_index("lat"), lax.axis_index("mem")
    for t in range(half + 2):
        for part in range(2):
            off = pl.multiple_of(window_block(mem_pos, own, half, blocks, part, t) * LANES, LANES)
            lines[t * 2 + part] = latent[0, :, pl.ds(off, LANES)].astype(jnp.float32)

    def line(slot, i):
        return spread_line(lines, slot, i)

    def store(i, t, value):
        source[i, t] = value

    def step(i, _):
        make_source(
            i, lat_pos * rows + i, total_rows, span, own, half, seeds, scale, kernel_one.shape[3], line, store
        )
        return 0

    lax.fori_loop(0, rows, step, 0)
    build_band(kernel_one, band_one)
    build_band(kernel_two, band_two)
    build_back(kernel_one, back_one)
    build_back(kernel_two, back_two)


def band_kernel(
    half,
    chans,
    norm,
    seeds,
    scale,
    channel_weight,
    own_source,
    above,
    below,
    targets,
    land,
    band_one,
    band_two,
    back_one,
    back_two,
    out_lat,
    taps_keep,
    taps_send,
    lat_rows,
    tgt_rows,
    weight_rows,
    words,
    source,
    pre_even,
    pre_odd,
    act,
    slope,
    cast_even,
    cast_odd,
    fgrad_even,
    fgrad_odd,
    carry,
    carry_lat,
    lat_lines,
    taps,
    acc_one,
    acc_two,
):
    rows = own_source.shape[0]
    span = targets.shape[2]
    blocks = span // LANES
    lat_count = lax.axis_size("lat")
    own = blocks // lax.axis_size("mem")
    total_rows = rows * lat_count
    grid_rows = 4 * rows
    grid_total = grid_rows * lat_count
    lat_pos = lax.axis_index("lat")
    mem_pos = lax.axis_index("mem")
    wide = half + 2
    front = half + 1
    chan0, chan1, chan2 = chans
    f32, bf16 = jnp.float32, jnp.bfloat16

    def block_of(part, t):
        return window_block(mem_pos, own, half, blocks, part, t)

    pad_rows = grid_rows + 8
    grid_row = iota((pad_rows, LANES), 0)
    grid_row = jnp.where(grid_row < grid_rows, grid_row, grid_row - (grid_rows + 4)) + lat_pos * grid_rows
    latitude = math.pi / 2 - math.pi * (grid_row.astype(f32) + 0.5) / grid_total
    channels = lane_table(channel_weight, chan2)
    cosine = jnp.where(grid_row >= 0, jnp.cos(latitude), 0.0)
    base_rows = cosine * (jnp.tile(channels, (pad_rows // 8, 1)) * (1.0 / (MEM * (MEM - 1))))

    words[...] = jnp.zeros(words.shape, jnp.int32)
    words[:, : land.shape[1]] = land[...]
    for t in range(wide):
        for part in range(2):
            block = block_of(part, t)
            off = pl.multiple_of(block * LANES, LANES)
            slot = t * 2 + part
            edge = above[slot].astype(f32)
            lat_rows[slot, 0:1] = edge[0:1]
            lat_rows[slot, 1:2] = below[:, slot * LANES : (slot + 1) * LANES].astype(f32)
            if t < front:
                tgt_rows[slot, 0:grid_rows] = targets[0, :, pl.ds(off, LANES)].astype(f32)
                tgt_rows[slot, grid_rows:] = edge
                mask = jnp.concatenate([land_of(words[...], block, chan2), pltpu.roll(edge, 5, 0)], axis=0)
                weight_rows[slot] = base_rows + base_rows * mask

    source[rows + 2 :] = jnp.zeros((2,) + source.shape[1:], bf16)
    source[:, wide] = jnp.zeros((source.shape[0],) + source.shape[2:], bf16)
    fgrad_even[:, 0] = jnp.zeros((4,) + fgrad_even.shape[2:], bf16)
    fgrad_odd[...] = jnp.zeros(fgrad_odd.shape, bf16)
    carry[...] = jnp.zeros(carry.shape, f32)
    carry_lat[...] = jnp.zeros(carry_lat.shape, f32)
    acc_one[...] = jnp.zeros(acc_one.shape, f32)
    acc_two[...] = jnp.zeros(acc_two.shape, f32)

    def line(slot, i):
        return spread_line(lat_rows, slot, i)

    def store(i, t, value):
        source[i * (rows + 1), t] = value

    def edge_source(i, _):
        row = lat_pos * rows - 1 + i * (rows + 1)
        make_source(i, row, total_rows, span, own, half, seeds, scale, chan0, line, store)
        return 0

    lax.fori_loop(0, 2, edge_source, 0)
    source[1 : rows + 1, 0:wide] = own_source[...]

    def operand(ref, i, start, count):
        def piece(r, at):
            return ref[r, pl.ds(at, count)].reshape(count * 16, LANES)

        return jnp.concatenate(
            [piece(i, start), piece(i + 1, start), piece(i, start + 1), piece(i + 1, start + 1)], axis=1
        )

    def first_product(i, pre):
        pre[...] = jnp.dot(operand(source, i, 0, wide), band_one[...], preferred_element_type=f32)

    def first_gelu(i, pre):
        for t in range(wide):
            for sub in range(2):
                x = pre[t * 16 : (t + 1) * 16, sub * LANES : (sub + 1) * LANES]
                square = x * x
                th = jnp.tanh(x * (GELU_A + (GELU_A * GELU_B) * square))
                plus = 0.5 + 0.5 * th
                act[2 * i + sub, t] = (x * plus).astype(bf16)
                if t < front:
                    d = plus + (x * plus) * (1.0 - th) * (GELU_A + (3.0 * GELU_A * GELU_B) * square)
                    if t == half:
                        d = jnp.where(iota((16, LANES), 0) < 8, d, 0.0)
                    slope[2 * i + sub, t] = d

    def first_segment(m, _):
        first_product(2 * m + 1, pre_odd)
        first_gelu(2 * m, pre_even)
        first_product(2 * m + 2, pre_even)
        first_gelu(2 * m + 1, pre_odd)
        return 0

    first_product(0, pre_even)
    lax.fori_loop(0, rows // 2 + 1, first_segment, 0)

    members = front * 16
    owner = iota((48, members), 0)
    group = iota((48, members), 1) // 8
    place = (group % 2) * half + group // 2
    real = (group // 2 > 0) & (place - 1 < own)
    pick_own = (real & (place - 1 == owner)).astype(bf16)
    pick_prev = ((group // 2 < half) & (place == owner)).astype(bf16)
    pick = jnp.concatenate([pick_own, pick_prev], axis=0)

    def second_product(n, cast):
        taken = jnp.concatenate([operand(act, 2 * n + k, 0, front) for k in range(2)], axis=0)
        out = jnp.dot(taken, band_two[...], preferred_element_type=f32).astype(bf16)
        for k in range(2):
            for sub in range(2):
                part = out[k * members : (k + 1) * members, sub * LANES : (sub + 1) * LANES]
                cast[2 * k + sub] = part.reshape(front, 16, LANES)

    def loss_gradient(n, cast, fgrad):
        first = jnp.where(n >= 1, 4 * (n - 1), grid_rows)
        for line in range(4):
            for t in range(front):
                both = cast[line, t].astype(f32)
                parts = []
                for part in range(2):
                    if t == half and part == 1:
                        parts.append(jnp.zeros((8, LANES), f32))
                        continue
                    f = both[part * 8 : part * 8 + 8]
                    d = f - spread_line(tgt_rows, t * 2 + part, first + line)
                    goal = d * lax.rsqrt(d * d + SMOOTH)
                    gs = []
                    for k in range(1, 5):
                        d = f - pltpu.roll(f, k, 0)
                        gs.append(d * lax.rsqrt(d * d + SMOOTH))
                    back = gs[2]
                    for k in (1, 0):
                        back = gs[k] + pltpu.roll(back, MEM - 1, 0)
                    back = pltpu.roll(back, MEM - 1, 0)
                    spread = (gs[0] + gs[1]) + (gs[2] + gs[3]) - back
                    weight = spread_line(weight_rows, t * 2 + part, first + line)
                    parts.append(weight * ((MEM - 1.0) * goal - spread))
                fgrad[line, t + 1] = jnp.concatenate(parts, axis=0).astype(bf16)

    def pull_back(n, fgrad):
        at = jnp.maximum(n, 0)
        keep = jnp.where(n >= 1, 1.0, 0.0).astype(bf16)

        def flat(line, start, count):
            return fgrad[line, start : start + count].reshape(count * 16, LANES)

        def product(g, x):
            return lax.dot_general(g, x, (((0,), (0,)), ((), ())), preferred_element_type=f32)

        g = [
            jnp.concatenate(
                [flat(2 * k, 1, front), flat(2 * k + 1, 1, front), flat(2 * k, 0, front), flat(2 * k + 1, 0, front)],
                axis=1,
            )
            for k in range(2)
        ]
        pulled = jnp.dot(jnp.concatenate(g, axis=0), back_two[...], preferred_element_type=f32)
        g = [jnp.concatenate([flat(2 * k, 2, half), flat(2 * k + 1, 2, half)], axis=1) for k in range(2)]
        x = [operand(act, 2 * at + k, 1, half) for k in range(2)]
        acc_two[...] += product(jnp.concatenate(g, axis=0) * keep, jnp.concatenate(x, axis=0))
        grads = [
            pulled[:members, :LANES] + carry[...],
            pulled[members:, :LANES] + pulled[:members, LANES:],
        ]
        carry[...] = pulled[members:, LANES:]
        grads = [(grads[k] * slope[2 * at + k].reshape(members, LANES)).astype(bf16) for k in range(2)]
        grads = jnp.concatenate(grads, axis=1)
        z = jnp.dot(pick, grads, preferred_element_type=f32)
        z = jnp.concatenate([z[:48], z[48:]], axis=1)
        high = z.astype(bf16)
        z = jnp.concatenate([high, (z - high.astype(f32)).astype(bf16)], axis=0)
        z = jnp.dot(z, back_one[...], preferred_element_type=f32)
        z = z[:48] + z[48:]
        lat_lines[pl.ds(jnp.maximum(n - 1, 0), 48, stride=rows), :] = z[:, :LANES] + carry_lat[...]
        carry_lat[...] = z[:, LANES:]
        acc_one[...] += product(grads[16:] * keep, operand(source, at, 1, half))

    def second_segment(m, _):
        second_product(2 * m + 1, cast_odd)
        loss_gradient(2 * m, cast_even, fgrad_even)
        pull_back(2 * m - 1, fgrad_odd)
        second_product(2 * m + 2, cast_even)
        loss_gradient(2 * m + 1, cast_odd, fgrad_odd)
        pull_back(2 * m, fgrad_even)
        return 0

    second_product(0, cast_even)
    lax.fori_loop(0, rows // 2, second_segment, 0)
    loss_gradient(rows, cast_even, fgrad_even)
    pull_back(rows - 1, fgrad_odd)
    pull_back(rows, fgrad_even)

    for t in range(own):
        out_lat[:, t * LANES : (t + 1) * LANES] = lat_lines[t * rows : (t + 1) * rows].astype(bf16)
    pack_taps(acc_one, taps, 0, chan0, chan1, norm)
    pack_taps(acc_two, taps, -(-9 // (LANES // chan0)) * chan1, chan1, chan2, norm)
    count = taps_keep.shape[0]
    odd = jnp.bitwise_and(lat_pos, 1)
    taps_keep[...] = taps[pl.ds(pl.multiple_of(odd * count, 8), count), :]
    taps_send[...] = taps[pl.ds(pl.multiple_of((1 - odd) * count, 8), count), :]


def swapped(array, axis, bit):
    return lax.ppermute(array, axis, [(i, i ^ bit) for i in range(lax.axis_size(axis))])


def total(array, axis, first, second):
    one, two, three = (swapped(array, axis, k) for k in (first, second, first ^ second))
    return (array + one) + (two + three)


def local(
    latent, member_seeds, noise_scale, kernel_one, kernel_two, targets, land_words, channel_weight
):
    sample_count, rows, span = latent.shape
    chan0, chan1, chan2 = kernel_one.shape[2], kernel_one.shape[3], kernel_two.shape[3]
    lat_count = lax.axis_size("lat")
    own = span // LANES // lax.axis_size("mem")
    half = (own + 1) // 2
    assert sample_count == 1 and member_seeds.shape[0] == MEM and rows % 2 == 0 and own % 2 == 1 and lax.axis_size("mem") == 4
    assert 4 * chan2 == 2 * chan1 == chan0 and chan0 == 64
    vmem = pl.BlockSpec(memory_space=pltpu.VMEM)
    smem = pl.BlockSpec(memory_space=pltpu.SMEM)
    f32, bf16 = jnp.float32, jnp.bfloat16
    wide, front = half + 2, half + 1
    params = pltpu.CompilerParams(vmem_limit_bytes=32 * 1024 * 1024)
    small = pltpu.CompilerParams(vmem_limit_bytes=8 * 1024 * 1024)
    kernel_one = kernel_one.transpose(0, 1, 3, 2)
    kernel_two = kernel_two.transpose(0, 1, 3, 2)
    down, up = pl.pallas_call(
        functools.partial(edge_kernel, half, chan2),
        grid=(1,),
        in_specs=[
            pl.BlockSpec((1, 8, span), lambda i: (0, 0, 0)),
            pl.BlockSpec((1, 8, span), lambda i: (0, rows // 2 - 1, 0)),
            pl.BlockSpec((8, land_words.shape[1]), lambda i: (rows // 2 - 1, 0)),
        ],
        out_specs=[
            pl.BlockSpec((2 * wide, 8, LANES), lambda i: (0, 0, 0)),
            pl.BlockSpec((1, 2 * wide * LANES), lambda i: (0, 0)),
        ],
        out_shape=[
            jax.ShapeDtypeStruct((2 * wide, 8, LANES), bf16),
            jax.ShapeDtypeStruct((1, 2 * wide * LANES), bf16),
        ],
        scratch_shapes=[pltpu.VMEM((8, LANES), jnp.int32)],
        compiler_params=small,
        name="edges",
    )(latent, targets, land_words)
    above = shifted(down, "lat", 1)
    below = shifted(up, "lat", -1)
    band = jax.ShapeDtypeStruct((512, 256), bf16)
    source, *bands = pl.pallas_call(
        functools.partial(prepare_kernel, half),
        in_specs=[smem] * 2 + [vmem] * 3,
        out_specs=[vmem] * 5,
        out_shape=[jax.ShapeDtypeStruct((rows, wide, 16, LANES), bf16)] + [band] * 4,
        scratch_shapes=[pltpu.VMEM((2 * wide, rows, LANES), f32)],
        compiler_params=small,
        cost_estimate=pl.CostEstimate(flops=10**8, bytes_accessed=10**7, transcendentals=0),
        name="prepare",
    )(member_seeds, noise_scale, latent, kernel_one, kernel_two)
    norm = 1.0 / math.sqrt(sample_count * 4 * rows * lat_count * targets.shape[2])
    tap_rows = 5 * chan1 + 3 * chan2
    lat_grad, taps, taps_send = pl.pallas_call(
        functools.partial(band_kernel, half, (chan0, chan1, chan2), norm),
        in_specs=[smem] * 3 + [vmem] * 9,
        out_specs=[vmem] * 3,
        out_shape=[
            jax.ShapeDtypeStruct((rows, own * LANES), bf16),
            jax.ShapeDtypeStruct((tap_rows // 2, LANES), f32),
            jax.ShapeDtypeStruct((tap_rows // 2, LANES), f32),
        ],
        scratch_shapes=[
            pltpu.VMEM((2 * wide, 8, LANES), f32),
            pltpu.VMEM((2 * front, 4 * rows + 8, LANES), f32),
            pltpu.VMEM((2 * front, 4 * rows + 8, LANES), f32),
            pltpu.VMEM((4 * rows, LANES), jnp.int32),
            pltpu.VMEM((rows + 4, wide + 1, 16, LANES), bf16),
            pltpu.VMEM((wide * 16, 2 * LANES), f32),
            pltpu.VMEM((wide * 16, 2 * LANES), f32),
            pltpu.VMEM((2 * rows + 4, wide, 16, LANES), bf16),
            pltpu.VMEM((2 * rows + 4, front, 16, LANES), f32),
            pltpu.VMEM((4, front, 16, LANES), bf16),
            pltpu.VMEM((4, front, 16, LANES), bf16),
            pltpu.VMEM((4, front + 1, 16, LANES), bf16),
            pltpu.VMEM((4, front + 1, 16, LANES), bf16),
            pltpu.VMEM((front * 16, LANES), f32),
            pltpu.VMEM((48, LANES), f32),
            pltpu.VMEM((48 * rows, LANES), f32),
            pltpu.VMEM((tap_rows, LANES), f32),
            pltpu.VMEM((256, 512), f32),
            pltpu.VMEM((256, 512), f32),
        ],
        compiler_params=params,
        name="band",
    )(
        member_seeds,
        noise_scale,
        channel_weight,
        source,
        above,
        below,
        targets,
        land_words,
        *bands,
    )
    one, two, three = (swapped(lat_grad, "mem", k) for k in range(1, 4))
    taps = taps + swapped(taps_send, "lat", 1)
    bits = [1 << k for k in range(1, lat_count.bit_length() - 1)]
    for bit in bits:
        if bit == bits[-1]:
            taps, three = lax.optimization_barrier((taps, three))
        taps = taps + swapped(taps, "lat", bit)
    taps, two = lax.optimization_barrier((taps, two))
    latent_grad = pl.pallas_call(
        functools.partial(place_kernel, own),
        in_specs=[vmem] * 4,
        out_specs=vmem,
        out_shape=jax.ShapeDtypeStruct((1, rows, span), f32),
        compiler_params=small,
        name="place",
    )(lat_grad, one, two, three)
    taps = total(taps, "mem", 1, 2)
    taps, latent_grad = lax.optimization_barrier((taps, latent_grad))
    other = swapped(taps, "lat", 1)
    one, two = pl.pallas_call(
        taps_kernel,
        in_specs=[vmem] * 2,
        out_specs=[vmem] * 2,
        out_shape=[
            jax.ShapeDtypeStruct(kernel_one.shape, f32),
            jax.ShapeDtypeStruct(kernel_two.shape, f32),
        ],
        scratch_shapes=[pltpu.VMEM((tap_rows, LANES), f32)],
        compiler_params=small,
        name="taps",
    )(taps, other)
    return (latent_grad, one.transpose(0, 1, 3, 2), two.transpose(0, 1, 3, 2))


def solution(mesh):
    in_specs = (P(None, "lat", None), P(), P(), P(), P(), P(None, "lat", None), P("lat", None), P())
    out_specs = (P(None, "lat", None), P(), P())
    return jax.shard_map(local, mesh=mesh, in_specs=in_specs, out_specs=out_specs, check_vma=False)
```

```python
import functools
import math

import jax
import jax.numpy as jnp
from jax import lax
from jax.experimental import pallas as pl
from jax.experimental.pallas import tpu as pltpu
from jax.sharding import PartitionSpec as P

SMOOTH = 0.01
HASH_CELL = 1103515245
HASH_SEED = 747796405
HASH_MIX = 277803737
LANES = 128
MEM = 8
GELU_A = math.sqrt(2.0 / math.pi)
GELU_B = 0.044715


def shifted(array, axis, by):
    peers = lax.axis_size(axis)
    pairs = [(i, i + by) for i in range(peers) if 0 <= i + by < peers]
    return lax.ppermute(array, axis, pairs)


def iota(shape, axis):
    return lax.broadcasted_iota(jnp.int32, shape, axis)


def lane_table(ref, count):
    lane = iota((8, LANES), 1) % count
    total = jnp.zeros((8, LANES), jnp.float32)
    for k in range(count):
        total = jnp.where(lane == k, ref[k], total)
    return total


def build_band(kernel_ref, band_ref):
    chan_out, chan_in = kernel_ref.shape[2], kernel_ref.shape[3]
    cells = LANES // chan_in
    repeat = (iota((chan_out, LANES), 1) % chan_out == iota((chan_out, LANES), 0)).astype(jnp.bfloat16)
    wide = {}
    for a in range(3):
        for b in range(3):
            wide[a, b] = lax.dot_general(
                kernel_ref[a, b], repeat, (((0,), (0,)), ((), ())), preferred_element_type=jnp.float32
            )
    column = iota((chan_in, LANES), 1) // chan_out
    zero = jnp.zeros((chan_in, LANES), jnp.float32)
    for block in range(2):
        for row in range(2):
            for cell in range(cells):
                at = block * 256 + row * LANES + cell * chan_in
                for sub in range(2):
                    a = sub - 2 * row + 1
                    part = zero
                    for q in range(2 * cells):
                        b = q - 2 * (cell + block * cells) + 1
                        if 0 <= a <= 2 and 0 <= b <= 2:
                            part = jnp.where(column == q, wide[a, b], part)
                    band_ref[at : at + chan_in, sub * LANES : (sub + 1) * LANES] = part.astype(jnp.bfloat16)


def build_back(kernel_ref, back_ref):
    chan_out, chan_in = kernel_ref.shape[2], kernel_ref.shape[3]
    cells = LANES // chan_in
    repeat = (iota((chan_in, LANES), 1) % chan_in == iota((chan_in, LANES), 0)).astype(jnp.bfloat16)
    flat = kernel_ref[...].reshape(9 * chan_out, chan_in)
    wide = jnp.dot(flat, repeat, preferred_element_type=jnp.float32)
    column = iota((chan_out, LANES), 1) // chan_in
    zero = jnp.zeros((chan_out, LANES), jnp.float32)
    for block in range(2):
        for sub in range(2):
            for q in range(2 * cells):
                at = block * 256 + sub * LANES + q * chan_out
                for row in range(2):
                    a = sub - 2 * row + 1
                    part = zero
                    for cell in range(cells):
                        b = q - 2 * (cell + block * cells) + 1
                        if 0 <= a <= 2 and 0 <= b <= 2:
                            tap = (3 * a + b) * chan_out
                            part = jnp.where(column == cell, wide[tap : tap + chan_out], part)
                    back_ref[at : at + chan_out, row * LANES : (row + 1) * LANES] = part.astype(jnp.bfloat16)


def pack_taps(acc_ref, out_ref, first, chan_in, chan_out, norm):
    cells = LANES // chan_in
    group = iota((chan_out, LANES), 1) // chan_in
    packed = None
    for k in range(9):
        a, b = divmod(k, 3)
        row, sub = ((1, 1), (0, 0), (0, 1))[a]
        slot = k % cells
        part = None
        for reach in range(cells + 1):
            q = 2 * reach + b - 1
            if 0 <= q < 2 * cells:
                block, cell = reach // cells, reach % cells
                lines = sub * LANES + q * chan_out
                lanes = block * 256 + row * LANES
                piece = acc_ref[lines : lines + chan_out, lanes : lanes + LANES]
                turn = (slot - cell) % cells * chan_in
                piece = pltpu.roll(piece, turn, 1) if turn else piece
                part = piece if part is None else part + piece
        packed = part if slot == 0 else jnp.where(group == slot, part, packed)
        if slot == cells - 1 or k == 8:
            at = first + k // cells * chan_out
            out_ref[at : at + chan_out, :] = packed * norm


def spread_line(ref, slot, at):
    return ref[slot, pl.ds(at, 8, stride=0), :]


def window_block(mem_pos, own, half, blocks, part, t):
    at = mem_pos * own + part * half + t + (blocks - 1)
    at = jnp.where(at >= blocks, at - blocks, at)
    return jnp.where(at >= blocks, at - blocks, at)


def land_of(words, block, chan):
    cell = block * (LANES // chan) + iota(words.shape, 1) // chan
    word = jnp.right_shift(cell * 2185, 16)
    picked = jnp.take_along_axis(words, word, axis=1, mode="promise_in_bounds")
    return jnp.bitwise_and(jnp.right_shift(picked, cell - 30 * word), 1).astype(jnp.float32)


def edge_kernel(half, chan, latent, targets, land, down, up, words):
    rows = latent.shape[1]
    blocks = latent.shape[2] // LANES
    own = blocks // lax.axis_size("mem")
    mem_pos = lax.axis_index("mem")
    words[...] = jnp.zeros(words.shape, jnp.int32)
    words[:, : land.shape[1]] = land[...]
    line = iota((8, LANES), 0)
    for t in range(half + 2):
        for part in range(2):
            block = window_block(mem_pos, own, half, blocks, part, t)
            off = pl.multiple_of(block * LANES, LANES)
            slot = t * 2 + part
            cells = latent[0, :, pl.ds(off, LANES)].astype(jnp.float32)
            aims = targets[0, :, pl.ds(off, LANES)].astype(jnp.float32)
            mask = land_of(words[...], block, chan)
            pack = pltpu.roll(cells, 1, 0)
            pack = jnp.where((line >= 1) & (line <= 3), pltpu.roll(aims, 4, 0), pack)
            pack = jnp.where((line >= 4) & (line <= 6), pltpu.roll(mask, 7, 0), pack)
            down[slot] = pack.astype(jnp.bfloat16)
            up[:, slot * LANES : (slot + 1) * LANES] = cells[0:1].astype(jnp.bfloat16)


def place_kernel(own, part0, part1, part2, part3, latent_grad):
    mem_pos = lax.axis_index("mem")
    for k, part in enumerate((part0, part1, part2, part3)):
        off = pl.multiple_of(jnp.bitwise_xor(mem_pos, k) * own * LANES, LANES)
        latent_grad[0, :, pl.ds(off, own * LANES)] = part[...].astype(jnp.float32)


def taps_kernel(mine, other, grad_one, grad_two, taps):
    count = mine.shape[0]
    odd = jnp.bitwise_and(lax.axis_index("lat"), 1)
    taps[pl.ds(pl.multiple_of(odd * count, 8), count), :] = mine[...]
    taps[pl.ds(pl.multiple_of((1 - odd) * count, 8), count), :] = other[...]
    first = 0
    for out in (grad_one, grad_two):
        chan_out, chan_in = out.shape[2], out.shape[3]
        cells = LANES // chan_in
        for k in range(9):
            at = first + k // cells * chan_out
            block = taps[at : at + chan_out, :]
            turn = (-(k % cells)) % cells * chan_in
            block = pltpu.roll(block, turn, 1) if turn else block
            out[k // 3, k % 3] = block[:, :chan_in]
        first += -(-9 // cells) * chan_out


def make_source(i, row, total_rows, span, own, half, seeds, scale, chan, line, store):
    blocks = span // LANES
    mem_pos = lax.axis_index("mem")
    sublane = iota((8, LANES), 0)
    seed_table = jnp.zeros((8, LANES), jnp.int32)
    for m in range(MEM):
        seed_table = jnp.where(sublane == m, seeds[m], seed_table)
    hash_table = iota((8, LANES), 1) * HASH_CELL + seed_table * HASH_SEED
    scale_table = lane_table(scale, chan)
    inside = jnp.where(row < total_rows, 1.0, 0.0).astype(jnp.float32)
    for t in range(half + 2):
        parts = []
        for part in range(2):
            first = (row * span + window_block(mem_pos, own, half, blocks, part, t) * LANES) * HASH_CELL
            h = hash_table + first
            h = jnp.bitwise_xor(h, jnp.right_shift(h, 15))
            h = h * HASH_MIX
            h = jnp.bitwise_xor(h, jnp.right_shift(h, 13))
            noise = jnp.bitwise_and(h, 65535).astype(jnp.float32) * (1.0 / 65536.0) - 0.5
            noise = noise * 3.4641016
            parts.append((line(t * 2 + part, i) + noise * scale_table) * inside)
        store(i, t, jnp.concatenate(parts, axis=0).astype(jnp.bfloat16))


def prepare_kernel(half, seeds, scale, latent, kernel_one, kernel_two, source, band_one, band_two, back_one, back_two, lines):
    rows, span = latent.shape[1], latent.shape[2]
    blocks = span // LANES
    own = blocks // lax.axis_size("mem")
    total_rows = rows * lax.axis_size("lat")
    lat_pos, mem_pos = lax.axis_index("lat"), lax.axis_index("mem")
    for t in range(half + 2):
        for part in range(2):
            off = pl.multiple_of(window_block(mem_pos, own, half, blocks, part, t) * LANES, LANES)
            lines[t * 2 + part] = latent[0, :, pl.ds(off, LANES)].astype(jnp.float32)

    def line(slot, i):
        return spread_line(lines, slot, i)

    def store(i, t, value):
        source[i, t] = value

    def step(i, _):
        make_source(
            i, lat_pos * rows + i, total_rows, span, own, half, seeds, scale, kernel_one.shape[3], line, store
        )
        return 0

    lax.fori_loop(0, rows, step, 0)
    build_band(kernel_one, band_one)
    build_band(kernel_two, band_two)
    build_back(kernel_one, back_one)
    build_back(kernel_two, back_two)


def band_kernel(
    half,
    chans,
    norm,
    seeds,
    scale,
    channel_weight,
    own_source,
    above,
    below,
    targets,
    land,
    band_one,
    band_two,
    back_one,
    back_two,
    out_lat,
    taps_keep,
    taps_send,
    lat_rows,
    tgt_rows,
    weight_rows,
    words,
    source,
    pre_even,
    pre_odd,
    act,
    slope,
    cast_even,
    cast_odd,
    fgrad_even,
    fgrad_odd,
    carry,
    carry_lat,
    lat_lines,
    taps,
    acc_one,
    acc_two,
):
    rows = own_source.shape[0]
    span = targets.shape[2]
    blocks = span // LANES
    lat_count = lax.axis_size("lat")
    own = blocks // lax.axis_size("mem")
    total_rows = rows * lat_count
    grid_rows = 4 * rows
    grid_total = grid_rows * lat_count
    lat_pos = lax.axis_index("lat")
    mem_pos = lax.axis_index("mem")
    wide = half + 2
    front = half + 1
    chan0, chan1, chan2 = chans
    f32, bf16 = jnp.float32, jnp.bfloat16

    def block_of(part, t):
        return window_block(mem_pos, own, half, blocks, part, t)

    pad_rows = grid_rows + 8
    grid_row = iota((pad_rows, LANES), 0)
    grid_row = jnp.where(grid_row < grid_rows, grid_row, grid_row - (grid_rows + 4)) + lat_pos * grid_rows
    latitude = math.pi / 2 - math.pi * (grid_row.astype(f32) + 0.5) / grid_total
    channels = lane_table(channel_weight, chan2)
    cosine = jnp.where(grid_row >= 0, jnp.cos(latitude), 0.0)
    base_rows = cosine * (jnp.tile(channels, (pad_rows // 8, 1)) * (1.0 / (MEM * (MEM - 1))))

    words[...] = jnp.zeros(words.shape, jnp.int32)
    words[:, : land.shape[1]] = land[...]
    for t in range(wide):
        for part in range(2):
            block = block_of(part, t)
            off = pl.multiple_of(block * LANES, LANES)
            slot = t * 2 + part
            edge = above[slot].astype(f32)
            lat_rows[slot, 0:1] = edge[0:1]
            lat_rows[slot, 1:2] = below[:, slot * LANES : (slot + 1) * LANES].astype(f32)
            if t < front:
                tgt_rows[slot, 0:grid_rows] = targets[0, :, pl.ds(off, LANES)].astype(f32)
                tgt_rows[slot, grid_rows:] = edge
                mask = jnp.concatenate([land_of(words[...], block, chan2), pltpu.roll(edge, 5, 0)], axis=0)
                weight_rows[slot] = base_rows + base_rows * mask

    source[rows + 2 :] = jnp.zeros((2,) + source.shape[1:], bf16)
    source[:, wide] = jnp.zeros((source.shape[0],) + source.shape[2:], bf16)
    fgrad_even[:, 0] = jnp.zeros((4,) + fgrad_even.shape[2:], bf16)
    fgrad_odd[...] = jnp.zeros(fgrad_odd.shape, bf16)
    carry[...] = jnp.zeros(carry.shape, f32)
    carry_lat[...] = jnp.zeros(carry_lat.shape, f32)
    acc_one[...] = jnp.zeros(acc_one.shape, f32)
    acc_two[...] = jnp.zeros(acc_two.shape, f32)

    def line(slot, i):
        return spread_line(lat_rows, slot, i)

    def store(i, t, value):
        source[i * (rows + 1), t] = value

    def edge_source(i, _):
        row = lat_pos * rows - 1 + i * (rows + 1)
        make_source(i, row, total_rows, span, own, half, seeds, scale, chan0, line, store)
        return 0

    lax.fori_loop(0, 2, edge_source, 0)
    source[1 : rows + 1, 0:wide] = own_source[...]

    def operand(ref, i, start, count):
        def piece(r, at):
            return ref[r, pl.ds(at, count)].reshape(count * 16, LANES)

        return jnp.concatenate(
            [piece(i, start), piece(i + 1, start), piece(i, start + 1), piece(i + 1, start + 1)], axis=1
        )

    def first_product(i, pre):
        pre[...] = jnp.dot(operand(source, i, 0, wide), band_one[...], preferred_element_type=f32)

    def first_gelu(i, pre):
        for t in range(wide):
            for sub in range(2):
                x = pre[t * 16 : (t + 1) * 16, sub * LANES : (sub + 1) * LANES]
                square = x * x
                th = jnp.tanh(x * (GELU_A + (GELU_A * GELU_B) * square))
                plus = 0.5 + 0.5 * th
                act[2 * i + sub, t] = (x * plus).astype(bf16)
                if t < front:
                    d = plus + (x * plus) * (1.0 - th) * (GELU_A + (3.0 * GELU_A * GELU_B) * square)
                    if t == half:
                        d = jnp.where(iota((16, LANES), 0) < 8, d, 0.0)
                    slope[2 * i + sub, t] = d

    def first_segment(m, _):
        first_product(2 * m + 1, pre_odd)
        first_gelu(2 * m, pre_even)
        first_product(2 * m + 2, pre_even)
        first_gelu(2 * m + 1, pre_odd)
        return 0

    first_product(0, pre_even)
    lax.fori_loop(0, rows // 2 + 1, first_segment, 0)

    members = front * 16
    owner = iota((48, members), 0)
    group = iota((48, members), 1) // 8
    place = (group % 2) * half + group // 2
    real = (group // 2 > 0) & (place - 1 < own)
    pick_own = (real & (place - 1 == owner)).astype(bf16)
    pick_prev = ((group // 2 < half) & (place == owner)).astype(bf16)
    pick = jnp.concatenate([pick_own, pick_prev], axis=0)

    unit = (iota((256, 256), 0) == iota((256, 256), 1)).astype(bf16)

    def second_product(n, cast):
        taken = jnp.concatenate([operand(act, 2 * n + k, 0, front) for k in range(2)], axis=0)
        out = jnp.dot(taken, band_two[...], preferred_element_type=f32).astype(bf16)
        for k in range(2):
            for sub in range(2):
                part = out[k * members : (k + 1) * members, sub * LANES : (sub + 1) * LANES]
                cast[2 * k + sub] = part.reshape(front, 16, LANES)

    def loss_gradient(n, cast, fgrad):
        first = jnp.where(n >= 1, 4 * (n - 1), grid_rows)
        for line in range(4):
            for t in range(front):
                both = cast[line, t].astype(f32)
                parts = []
                for part in range(2):
                    if t == half and part == 1:
                        parts.append(jnp.zeros((8, LANES), f32))
                        continue
                    f = both[part * 8 : part * 8 + 8]
                    d = f - spread_line(tgt_rows, t * 2 + part, first + line)
                    goal = d * lax.rsqrt(d * d + SMOOTH)
                    gs = []
                    for k in range(1, 5):
                        d = f - pltpu.roll(f, k, 0)
                        gs.append(d * lax.rsqrt(d * d + SMOOTH))
                    back = gs[2]
                    for k in (1, 0):
                        back = gs[k] + pltpu.roll(back, MEM - 1, 0)
                    back = pltpu.roll(back, MEM - 1, 0)
                    spread = (gs[0] + gs[1]) + (gs[2] + gs[3]) - back
                    weight = spread_line(weight_rows, t * 2 + part, first + line)
                    parts.append(weight * ((MEM - 1.0) * goal - spread))
                fgrad[line, t + 1] = jnp.concatenate(parts, axis=0).astype(bf16)

    def pull_back(n, fgrad):
        at = jnp.maximum(n, 0)
        keep = jnp.where(n >= 1, 1.0, 0.0).astype(bf16)

        def flat(line, start, count):
            return fgrad[line, start : start + count].reshape(count * 16, LANES)

        def product(g, x):
            turned = lax.dot_general(unit, g, (((1,), (1,)), ((), ())), preferred_element_type=f32)
            return jnp.dot(turned.astype(bf16), x, preferred_element_type=f32)

        g = [
            jnp.concatenate(
                [flat(2 * k, 1, front), flat(2 * k + 1, 1, front), flat(2 * k, 0, front), flat(2 * k + 1, 0, front)],
                axis=1,
            )
            for k in range(2)
        ]
        pulled = jnp.dot(jnp.concatenate(g, axis=0), back_two[...], preferred_element_type=f32)
        g = [jnp.concatenate([flat(2 * k, 2, half), flat(2 * k + 1, 2, half)], axis=1) for k in range(2)]
        x = [operand(act, 2 * at + k, 1, half) for k in range(2)]
        acc_two[...] += product(jnp.concatenate(g, axis=0) * keep, jnp.concatenate(x, axis=0))
        grads = [
            pulled[:members, :LANES] + carry[...],
            pulled[members:, :LANES] + pulled[:members, LANES:],
        ]
        carry[...] = pulled[members:, LANES:]
        grads = [(grads[k] * slope[2 * at + k].reshape(members, LANES)).astype(bf16) for k in range(2)]
        grads = jnp.concatenate(grads, axis=1)
        z = jnp.dot(pick, grads, preferred_element_type=f32)
        z = jnp.concatenate([z[:48], z[48:]], axis=1)
        high = z.astype(bf16)
        z = jnp.concatenate([high, (z - high.astype(f32)).astype(bf16)], axis=0)
        z = jnp.dot(z, back_one[...], preferred_element_type=f32)
        z = z[:48] + z[48:]
        lat_lines[pl.ds(jnp.maximum(n - 1, 0), 48, stride=rows), :] = z[:, :LANES] + carry_lat[...]
        carry_lat[...] = z[:, LANES:]
        acc_one[...] += product(grads[16:] * keep, operand(source, at, 1, half))

    def second_segment(m, _):
        second_product(2 * m + 1, cast_odd)
        loss_gradient(2 * m, cast_even, fgrad_even)
        pull_back(2 * m - 1, fgrad_odd)
        second_product(2 * m + 2, cast_even)
        loss_gradient(2 * m + 1, cast_odd, fgrad_odd)
        pull_back(2 * m, fgrad_even)
        return 0

    second_product(0, cast_even)
    lax.fori_loop(0, rows // 2, second_segment, 0)
    loss_gradient(rows, cast_even, fgrad_even)
    pull_back(rows - 1, fgrad_odd)
    pull_back(rows, fgrad_even)

    for t in range(own):
        out_lat[:, t * LANES : (t + 1) * LANES] = lat_lines[t * rows : (t + 1) * rows].astype(bf16)
    pack_taps(acc_one, taps, 0, chan0, chan1, norm)
    pack_taps(acc_two, taps, -(-9 // (LANES // chan0)) * chan1, chan1, chan2, norm)
    count = taps_keep.shape[0]
    odd = jnp.bitwise_and(lat_pos, 1)
    taps_keep[...] = taps[pl.ds(pl.multiple_of(odd * count, 8), count), :]
    taps_send[...] = taps[pl.ds(pl.multiple_of((1 - odd) * count, 8), count), :]


def swapped(array, axis, bit):
    return lax.ppermute(array, axis, [(i, i ^ bit) for i in range(lax.axis_size(axis))])


def total(array, axis, first, second):
    one, two, three = (swapped(array, axis, k) for k in (first, second, first ^ second))
    return (array + one) + (two + three)


def local(
    latent, member_seeds, noise_scale, kernel_one, kernel_two, targets, land_words, channel_weight
):
    sample_count, rows, span = latent.shape
    chan0, chan1, chan2 = kernel_one.shape[2], kernel_one.shape[3], kernel_two.shape[3]
    lat_count = lax.axis_size("lat")
    own = span // LANES // lax.axis_size("mem")
    half = (own + 1) // 2
    assert sample_count == 1 and member_seeds.shape[0] == MEM and rows % 2 == 0 and own % 2 == 1 and lax.axis_size("mem") == 4
    assert 4 * chan2 == 2 * chan1 == chan0 and chan0 == 64
    vmem = pl.BlockSpec(memory_space=pltpu.VMEM)
    smem = pl.BlockSpec(memory_space=pltpu.SMEM)
    f32, bf16 = jnp.float32, jnp.bfloat16
    wide, front = half + 2, half + 1
    params = pltpu.CompilerParams(vmem_limit_bytes=32 * 1024 * 1024)
    small = pltpu.CompilerParams(vmem_limit_bytes=8 * 1024 * 1024)
    kernel_one = kernel_one.transpose(0, 1, 3, 2)
    kernel_two = kernel_two.transpose(0, 1, 3, 2)
    down, up = pl.pallas_call(
        functools.partial(edge_kernel, half, chan2),
        grid=(1,),
        in_specs=[
            pl.BlockSpec((1, 8, span), lambda i: (0, 0, 0)),
            pl.BlockSpec((1, 8, span), lambda i: (0, rows // 2 - 1, 0)),
            pl.BlockSpec((8, land_words.shape[1]), lambda i: (rows // 2 - 1, 0)),
        ],
        out_specs=[
            pl.BlockSpec((2 * wide, 8, LANES), lambda i: (0, 0, 0)),
            pl.BlockSpec((1, 2 * wide * LANES), lambda i: (0, 0)),
        ],
        out_shape=[
            jax.ShapeDtypeStruct((2 * wide, 8, LANES), bf16),
            jax.ShapeDtypeStruct((1, 2 * wide * LANES), bf16),
        ],
        scratch_shapes=[pltpu.VMEM((8, LANES), jnp.int32)],
        compiler_params=pltpu.CompilerParams(vmem_limit_bytes=56 * 1024 * 1024),
        name="edges",
    )(latent, targets, land_words)
    above = shifted(down, "lat", 1)
    below = shifted(up, "lat", -1)
    band = jax.ShapeDtypeStruct((512, 256), bf16)
    source, *bands = pl.pallas_call(
        functools.partial(prepare_kernel, half),
        in_specs=[smem] * 2 + [vmem] * 3,
        out_specs=[vmem] * 5,
        out_shape=[jax.ShapeDtypeStruct((rows, wide, 16, LANES), bf16)] + [band] * 4,
        scratch_shapes=[pltpu.VMEM((2 * wide, rows, LANES), f32)],
        compiler_params=small,
        cost_estimate=pl.CostEstimate(flops=10**8, bytes_accessed=10**7, transcendentals=0),
        name="prepare",
    )(member_seeds, noise_scale, latent, kernel_one, kernel_two)
    norm = 1.0 / math.sqrt(sample_count * 4 * rows * lat_count * targets.shape[2])
    tap_rows = 5 * chan1 + 3 * chan2
    lat_grad, taps, taps_send = pl.pallas_call(
        functools.partial(band_kernel, half, (chan0, chan1, chan2), norm),
        in_specs=[smem] * 3 + [vmem] * 9,
        out_specs=[vmem] * 3,
        out_shape=[
            jax.ShapeDtypeStruct((rows, own * LANES), bf16),
            jax.ShapeDtypeStruct((tap_rows // 2, LANES), f32),
            jax.ShapeDtypeStruct((tap_rows // 2, LANES), f32),
        ],
        scratch_shapes=[
            pltpu.VMEM((2 * wide, 8, LANES), f32),
            pltpu.VMEM((2 * front, 4 * rows + 8, LANES), f32),
            pltpu.VMEM((2 * front, 4 * rows + 8, LANES), f32),
            pltpu.VMEM((4 * rows, LANES), jnp.int32),
            pltpu.VMEM((rows + 4, wide + 1, 16, LANES), bf16),
            pltpu.VMEM((wide * 16, 2 * LANES), f32),
            pltpu.VMEM((wide * 16, 2 * LANES), f32),
            pltpu.VMEM((2 * rows + 4, wide, 16, LANES), bf16),
            pltpu.VMEM((2 * rows + 4, front, 16, LANES), f32),
            pltpu.VMEM((4, front, 16, LANES), bf16),
            pltpu.VMEM((4, front, 16, LANES), bf16),
            pltpu.VMEM((4, front + 1, 16, LANES), bf16),
            pltpu.VMEM((4, front + 1, 16, LANES), bf16),
            pltpu.VMEM((front * 16, LANES), f32),
            pltpu.VMEM((48, LANES), f32),
            pltpu.VMEM((48 * rows, LANES), f32),
            pltpu.VMEM((tap_rows, LANES), f32),
            pltpu.VMEM((256, 512), f32),
            pltpu.VMEM((256, 512), f32),
        ],
        compiler_params=params,
        name="band",
    )(
        member_seeds,
        noise_scale,
        channel_weight,
        source,
        above,
        below,
        targets,
        land_words,
        *bands,
    )
    one, two, three = (swapped(lat_grad, "mem", k) for k in range(1, 4))
    taps = taps + swapped(taps_send, "lat", 1)
    bits = [1 << k for k in range(1, lat_count.bit_length() - 1)]
    for bit in bits:
        if bit == bits[-1]:
            taps, three = lax.optimization_barrier((taps, three))
        taps = taps + swapped(taps, "lat", bit)
    taps, two = lax.optimization_barrier((taps, two))
    latent_grad = pl.pallas_call(
        functools.partial(place_kernel, own),
        in_specs=[vmem] * 4,
        out_specs=vmem,
        out_shape=jax.ShapeDtypeStruct((1, rows, span), f32),
        compiler_params=small,
        name="place",
    )(lat_grad, one, two, three)
    taps = total(taps, "mem", 1, 2)
    taps, latent_grad = lax.optimization_barrier((taps, latent_grad))
    other = swapped(taps, "lat", 1)
    one, two = pl.pallas_call(
        taps_kernel,
        in_specs=[vmem] * 2,
        out_specs=[vmem] * 2,
        out_shape=[
            jax.ShapeDtypeStruct(kernel_one.shape, f32),
            jax.ShapeDtypeStruct(kernel_two.shape, f32),
        ],
        scratch_shapes=[pltpu.VMEM((tap_rows, LANES), f32)],
        compiler_params=small,
        name="taps",
    )(taps, other)
    return (latent_grad, one.transpose(0, 1, 3, 2), two.transpose(0, 1, 3, 2))


def solution(mesh):
    in_specs = (P(None, "lat", None), P(), P(), P(), P(), P(None, "lat", None), P("lat", None), P())
    out_specs = (P(None, "lat", None), P(), P())
    return jax.shard_map(local, mesh=mesh, in_specs=in_specs, out_specs=out_specs, check_vma=False)
```

```python
import functools
import math

import jax
import jax.numpy as jnp
from jax import lax
from jax.experimental import pallas as pl
from jax.experimental.pallas import tpu as pltpu
from jax.sharding import PartitionSpec as P

SMOOTH = 0.01
HASH_CELL = 1103515245
HASH_SEED = 747796405
HASH_MIX = 277803737
LANES = 128
MEM = 8
GELU_A = math.sqrt(2.0 / math.pi)
GELU_B = 0.044715


def shifted(array, axis, by):
    peers = lax.axis_size(axis)
    pairs = [(i, i + by) for i in range(peers) if 0 <= i + by < peers]
    return lax.ppermute(array, axis, pairs)


def iota(shape, axis):
    return lax.broadcasted_iota(jnp.int32, shape, axis)


def lane_table(ref, count):
    lane = iota((8, LANES), 1) % count
    total = jnp.zeros((8, LANES), jnp.float32)
    for k in range(count):
        total = jnp.where(lane == k, ref[k], total)
    return total


def build_band(kernel_ref, band_ref):
    chan_out, chan_in = kernel_ref.shape[2], kernel_ref.shape[3]
    cells = LANES // chan_in
    repeat = (iota((chan_out, LANES), 1) % chan_out == iota((chan_out, LANES), 0)).astype(jnp.bfloat16)
    wide = {}
    for a in range(3):
        for b in range(3):
            wide[a, b] = lax.dot_general(
                kernel_ref[a, b], repeat, (((0,), (0,)), ((), ())), preferred_element_type=jnp.float32
            )
    column = iota((chan_in, LANES), 1) // chan_out
    zero = jnp.zeros((chan_in, LANES), jnp.float32)
    for block in range(2):
        for row in range(2):
            for cell in range(cells):
                at = block * 256 + row * LANES + cell * chan_in
                for sub in range(2):
                    a = sub - 2 * row + 1
                    part = zero
                    for q in range(2 * cells):
                        b = q - 2 * (cell + block * cells) + 1
                        if 0 <= a <= 2 and 0 <= b <= 2:
                            part = jnp.where(column == q, wide[a, b], part)
                    band_ref[at : at + chan_in, sub * LANES : (sub + 1) * LANES] = part.astype(jnp.bfloat16)


def build_back(kernel_ref, back_ref):
    chan_out, chan_in = kernel_ref.shape[2], kernel_ref.shape[3]
    cells = LANES // chan_in
    repeat = (iota((chan_in, LANES), 1) % chan_in == iota((chan_in, LANES), 0)).astype(jnp.bfloat16)
    flat = kernel_ref[...].reshape(9 * chan_out, chan_in)
    wide = jnp.dot(flat, repeat, preferred_element_type=jnp.float32)
    column = iota((chan_out, LANES), 1) // chan_in
    zero = jnp.zeros((chan_out, LANES), jnp.float32)
    for block in range(2):
        for sub in range(2):
            for q in range(2 * cells):
                at = block * 256 + sub * LANES + q * chan_out
                for row in range(2):
                    a = sub - 2 * row + 1
                    part = zero
                    for cell in range(cells):
                        b = q - 2 * (cell + block * cells) + 1
                        if 0 <= a <= 2 and 0 <= b <= 2:
                            tap = (3 * a + b) * chan_out
                            part = jnp.where(column == cell, wide[tap : tap + chan_out], part)
                    back_ref[at : at + chan_out, row * LANES : (row + 1) * LANES] = part.astype(jnp.bfloat16)


def pack_taps(acc_ref, next_ref, out_ref, first, chan_in, chan_out, norm):
    cells = LANES // chan_in
    group = iota((chan_out, LANES), 1) // chan_in
    packed = None
    for k in range(9):
        a, b = divmod(k, 3)
        row, sub = ((1, 1), (0, 0), (0, 1))[a]
        slot = k % cells
        part = None
        for reach in range(cells + 1):
            q = 2 * reach + b - 1
            if 0 <= q < 2 * cells:
                block, cell = reach // cells, reach % cells
                lines = sub * LANES + q * chan_out if block == 0 else sub * chan_out
                ref = acc_ref if block == 0 else next_ref
                piece = ref[lines : lines + chan_out, row * LANES : (row + 1) * LANES]
                turn = (slot - cell) % cells * chan_in
                piece = pltpu.roll(piece, turn, 1) if turn else piece
                part = piece if part is None else part + piece
        packed = part if slot == 0 else jnp.where(group == slot, part, packed)
        if slot == cells - 1 or k == 8:
            at = first + k // cells * chan_out
            out_ref[at : at + chan_out, :] = packed * norm


def spread_line(ref, slot, at):
    return ref[slot, pl.ds(at, 8, stride=0), :]


def window_block(mem_pos, own, half, blocks, part, t):
    at = mem_pos * own + part * half + t + (blocks - 1)
    at = jnp.where(at >= blocks, at - blocks, at)
    return jnp.where(at >= blocks, at - blocks, at)


def land_of(words, block, chan):
    cell = block * (LANES // chan) + iota(words.shape, 1) // chan
    word = jnp.right_shift(cell * 2185, 16)
    picked = jnp.take_along_axis(words, word, axis=1, mode="promise_in_bounds")
    return jnp.bitwise_and(jnp.right_shift(picked, cell - 30 * word), 1).astype(jnp.float32)


def edge_kernel(half, chan, latent, targets, land, down, up, words):
    rows = latent.shape[1]
    blocks = latent.shape[2] // LANES
    own = blocks // lax.axis_size("mem")
    mem_pos = lax.axis_index("mem")
    words[...] = jnp.zeros(words.shape, jnp.int32)
    words[:, : land.shape[1]] = land[...]
    line = iota((8, LANES), 0)
    for t in range(half + 2):
        for part in range(2):
            block = window_block(mem_pos, own, half, blocks, part, t)
            off = pl.multiple_of(block * LANES, LANES)
            slot = t * 2 + part
            cells = latent[0, :, pl.ds(off, LANES)].astype(jnp.float32)
            aims = targets[0, :, pl.ds(off, LANES)].astype(jnp.float32)
            mask = land_of(words[...], block, chan)
            pack = pltpu.roll(cells, 1, 0)
            pack = jnp.where((line >= 1) & (line <= 3), pltpu.roll(aims, 4, 0), pack)
            pack = jnp.where((line >= 4) & (line <= 6), pltpu.roll(mask, 7, 0), pack)
            down[slot] = pack.astype(jnp.bfloat16)
            up[:, slot * LANES : (slot + 1) * LANES] = cells[0:1].astype(jnp.bfloat16)


def place_kernel(own, part0, part1, part2, part3, latent_grad):
    mem_pos = lax.axis_index("mem")
    for k, part in enumerate((part0, part1, part2, part3)):
        off = pl.multiple_of(jnp.bitwise_xor(mem_pos, k) * own * LANES, LANES)
        latent_grad[0, :, pl.ds(off, own * LANES)] = part[...].astype(jnp.float32)


def taps_kernel(mine, other, grad_one, grad_two, taps):
    count = mine.shape[0]
    odd = jnp.bitwise_and(lax.axis_index("lat"), 1)
    taps[pl.ds(pl.multiple_of(odd * count, 8), count), :] = mine[...]
    taps[pl.ds(pl.multiple_of((1 - odd) * count, 8), count), :] = other[...]
    first = 0
    for out in (grad_one, grad_two):
        chan_out, chan_in = out.shape[2], out.shape[3]
        cells = LANES // chan_in
        for k in range(9):
            at = first + k // cells * chan_out
            block = taps[at : at + chan_out, :]
            turn = (-(k % cells)) % cells * chan_in
            block = pltpu.roll(block, turn, 1) if turn else block
            out[k // 3, k % 3] = block[:, :chan_in]
        first += -(-9 // cells) * chan_out


def make_source(i, row, total_rows, span, own, half, seeds, scale, chan, line, store):
    blocks = span // LANES
    mem_pos = lax.axis_index("mem")
    sublane = iota((8, LANES), 0)
    seed_table = jnp.zeros((8, LANES), jnp.int32)
    for m in range(MEM):
        seed_table = jnp.where(sublane == m, seeds[m], seed_table)
    hash_table = iota((8, LANES), 1) * HASH_CELL + seed_table * HASH_SEED
    scale_table = lane_table(scale, chan)
    inside = jnp.where(row < total_rows, 1.0, 0.0).astype(jnp.float32)
    for t in range(half + 2):
        parts = []
        for part in range(2):
            first = (row * span + window_block(mem_pos, own, half, blocks, part, t) * LANES) * HASH_CELL
            h = hash_table + first
            h = jnp.bitwise_xor(h, jnp.right_shift(h, 15))
            h = h * HASH_MIX
            h = jnp.bitwise_xor(h, jnp.right_shift(h, 13))
            noise = jnp.bitwise_and(h, 65535).astype(jnp.float32) * (1.0 / 65536.0) - 0.5
            noise = noise * 3.4641016
            parts.append((line(t * 2 + part, i) + noise * scale_table) * inside)
        store(i, t, jnp.concatenate(parts, axis=0).astype(jnp.bfloat16))


def prepare_kernel(half, seeds, scale, latent, kernel_one, kernel_two, source, band_one, band_two, back_one, back_two, lines):
    rows, span = latent.shape[1], latent.shape[2]
    blocks = span // LANES
    own = blocks // lax.axis_size("mem")
    total_rows = rows * lax.axis_size("lat")
    lat_pos, mem_pos = lax.axis_index("lat"), lax.axis_index("mem")
    for t in range(half + 2):
        for part in range(2):
            off = pl.multiple_of(window_block(mem_pos, own, half, blocks, part, t) * LANES, LANES)
            lines[t * 2 + part] = latent[0, :, pl.ds(off, LANES)].astype(jnp.float32)

    def line(slot, i):
        return spread_line(lines, slot, i)

    def store(i, t, value):
        source[i, t] = value

    def step(i, _):
        make_source(
            i, lat_pos * rows + i, total_rows, span, own, half, seeds, scale, kernel_one.shape[3], line, store
        )
        return 0

    lax.fori_loop(0, rows, step, 0)
    build_band(kernel_one, band_one)
    build_band(kernel_two, band_two)
    build_back(kernel_one, back_one)
    build_back(kernel_two, back_two)


def band_kernel(
    half,
    chans,
    norm,
    seeds,
    scale,
    channel_weight,
    own_source,
    above,
    below,
    targets,
    land,
    band_one,
    band_two,
    back_one,
    back_two,
    out_lat,
    taps_keep,
    taps_send,
    lat_rows,
    tgt_rows,
    weight_rows,
    words,
    source,
    pre_even,
    pre_odd,
    act,
    slope,
    cast_even,
    cast_odd,
    fgrad_even,
    fgrad_odd,
    carry,
    carry_lat,
    lat_lines,
    taps,
    acc_one,
    acc_one_next,
    acc_two,
    acc_two_next,
):
    rows = own_source.shape[0]
    span = targets.shape[2]
    blocks = span // LANES
    lat_count = lax.axis_size("lat")
    own = blocks // lax.axis_size("mem")
    total_rows = rows * lat_count
    grid_rows = 4 * rows
    grid_total = grid_rows * lat_count
    lat_pos = lax.axis_index("lat")
    mem_pos = lax.axis_index("mem")
    wide = half + 2
    front = half + 1
    chan0, chan1, chan2 = chans
    f32, bf16 = jnp.float32, jnp.bfloat16

    def block_of(part, t):
        return window_block(mem_pos, own, half, blocks, part, t)

    pad_rows = grid_rows + 8
    grid_row = iota((pad_rows, LANES), 0)
    grid_row = jnp.where(grid_row < grid_rows, grid_row, grid_row - (grid_rows + 4)) + lat_pos * grid_rows
    latitude = math.pi / 2 - math.pi * (grid_row.astype(f32) + 0.5) / grid_total
    channels = lane_table(channel_weight, chan2)
    cosine = jnp.where(grid_row >= 0, jnp.cos(latitude), 0.0)
    base_rows = cosine * (jnp.tile(channels, (pad_rows // 8, 1)) * (1.0 / (MEM * (MEM - 1))))

    words[...] = jnp.zeros(words.shape, jnp.int32)
    words[:, : land.shape[1]] = land[...]
    for t in range(wide):
        for part in range(2):
            block = block_of(part, t)
            off = pl.multiple_of(block * LANES, LANES)
            slot = t * 2 + part
            edge = above[slot].astype(f32)
            lat_rows[slot, 0:1] = edge[0:1]
            lat_rows[slot, 1:2] = below[:, slot * LANES : (slot + 1) * LANES].astype(f32)
            if t < front:
                tgt_rows[slot, 0:grid_rows] = targets[0, :, pl.ds(off, LANES)].astype(f32)
                tgt_rows[slot, grid_rows:] = edge
                mask = jnp.concatenate([land_of(words[...], block, chan2), pltpu.roll(edge, 5, 0)], axis=0)
                weight_rows[slot] = base_rows + base_rows * mask

    source[rows + 2 :] = jnp.zeros((2,) + source.shape[1:], bf16)
    source[:, wide] = jnp.zeros((source.shape[0],) + source.shape[2:], bf16)
    fgrad_even[:, 0] = jnp.zeros((4,) + fgrad_even.shape[2:], bf16)
    fgrad_odd[...] = jnp.zeros(fgrad_odd.shape, bf16)
    carry[...] = jnp.zeros(carry.shape, f32)
    carry_lat[...] = jnp.zeros(carry_lat.shape, f32)
    for acc in (acc_one, acc_one_next, acc_two, acc_two_next):
        acc[...] = jnp.zeros(acc.shape, f32)

    def line(slot, i):
        return spread_line(lat_rows, slot, i)

    def store(i, t, value):
        source[i * (rows + 1), t] = value

    def edge_source(i, _):
        row = lat_pos * rows - 1 + i * (rows + 1)
        make_source(i, row, total_rows, span, own, half, seeds, scale, chan0, line, store)
        return 0

    lax.fori_loop(0, 2, edge_source, 0)
    source[1 : rows + 1, 0:wide] = own_source[...]

    def operand(ref, i, start, count):
        def piece(r, at):
            return ref[r, pl.ds(at, count)].reshape(count * 16, LANES)

        return jnp.concatenate(
            [piece(i, start), piece(i + 1, start), piece(i, start + 1), piece(i + 1, start + 1)], axis=1
        )

    def first_product(i, pre):
        pre[...] = jnp.dot(operand(source, i, 0, wide), band_one[...], preferred_element_type=f32)

    def first_gelu(i, pre):
        for t in range(wide):
            for sub in range(2):
                x = pre[t * 16 : (t + 1) * 16, sub * LANES : (sub + 1) * LANES]
                square = x * x
                th = jnp.tanh(x * (GELU_A + (GELU_A * GELU_B) * square))
                plus = 0.5 + 0.5 * th
                act[2 * i + sub, t] = (x * plus).astype(bf16)
                if t < front:
                    d = plus + (x * plus) * (1.0 - th) * (GELU_A + (3.0 * GELU_A * GELU_B) * square)
                    if t == half:
                        d = jnp.where(iota((16, LANES), 0) < 8, d, 0.0)
                    slope[2 * i + sub, t] = d

    def first_segment(m, _):
        first_product(2 * m + 1, pre_odd)
        first_gelu(2 * m, pre_even)
        first_product(2 * m + 2, pre_even)
        first_gelu(2 * m + 1, pre_odd)
        return 0

    first_product(0, pre_even)
    lax.fori_loop(0, rows // 2 + 1, first_segment, 0)

    members = front * 16
    owner = iota((48, members), 0)
    group = iota((48, members), 1) // 8
    place = (group % 2) * half + group // 2
    real = (group // 2 > 0) & (place - 1 < own)
    pick_own = (real & (place - 1 == owner)).astype(bf16)
    pick_prev = ((group // 2 < half) & (place == owner)).astype(bf16)
    pick = jnp.concatenate([pick_own, pick_prev], axis=0)

    def second_product(n, cast):
        taken = jnp.concatenate([operand(act, 2 * n + k, 0, front) for k in range(2)], axis=0)
        out = jnp.dot(taken, band_two[...], preferred_element_type=f32).astype(bf16)
        for k in range(2):
            for sub in range(2):
                part = out[k * members : (k + 1) * members, sub * LANES : (sub + 1) * LANES]
                cast[2 * k + sub] = part.reshape(front, 16, LANES)

    def loss_gradient(n, cast, fgrad):
        first = jnp.where(n >= 1, 4 * (n - 1), grid_rows)
        for line in range(4):
            for t in range(front):
                both = cast[line, t].astype(f32)
                parts = []
                for part in range(2):
                    if t == half and part == 1:
                        parts.append(jnp.zeros((8, LANES), f32))
                        continue
                    f = both[part * 8 : part * 8 + 8]
                    d = f - spread_line(tgt_rows, t * 2 + part, first + line)
                    goal = d * lax.rsqrt(d * d + SMOOTH)
                    gs = []
                    for k in range(1, 5):
                        d = f - pltpu.roll(f, k, 0)
                        gs.append(d * lax.rsqrt(d * d + SMOOTH))
                    back = gs[2]
                    for k in (1, 0):
                        back = gs[k] + pltpu.roll(back, MEM - 1, 0)
                    back = pltpu.roll(back, MEM - 1, 0)
                    spread = (gs[0] + gs[1]) + (gs[2] + gs[3]) - back
                    weight = spread_line(weight_rows, t * 2 + part, first + line)
                    parts.append(weight * ((MEM - 1.0) * goal - spread))
                fgrad[line, t + 1] = jnp.concatenate(parts, axis=0).astype(bf16)

    def pull_back(n, fgrad):
        at = jnp.maximum(n, 0)
        keep = jnp.where(n >= 1, 1.0, 0.0).astype(bf16)

        def flat(line, start, count):
            return fgrad[line, start : start + count].reshape(count * 16, LANES)

        def add_taps(g, x, acc, acc_next, chan_out):
            turned = g.T
            acc[...] += jnp.dot(turned, x[:, :256], preferred_element_type=f32)
            last = [turned[k * LANES - chan_out : k * LANES] for k in (1, 2)]
            last = jnp.concatenate(last, axis=0)
            acc_next[...] += jnp.dot(last, x[:, 256:], preferred_element_type=f32)

        g = [
            jnp.concatenate(
                [flat(2 * k, 1, front), flat(2 * k + 1, 1, front), flat(2 * k, 0, front), flat(2 * k + 1, 0, front)],
                axis=1,
            )
            for k in range(2)
        ]
        pulled = jnp.dot(jnp.concatenate(g, axis=0), back_two[...], preferred_element_type=f32)
        g = [jnp.concatenate([flat(2 * k, 2, half), flat(2 * k + 1, 2, half)], axis=1) for k in range(2)]
        x = [operand(act, 2 * at + k, 1, half) for k in range(2)]
        add_taps(jnp.concatenate(g, axis=0) * keep, jnp.concatenate(x, axis=0), acc_two, acc_two_next, chan2)
        grads = [
            pulled[:members, :LANES] + carry[...],
            pulled[members:, :LANES] + pulled[:members, LANES:],
        ]
        carry[...] = pulled[members:, LANES:]
        grads = [(grads[k] * slope[2 * at + k].reshape(members, LANES)).astype(bf16) for k in range(2)]
        grads = jnp.concatenate(grads, axis=1)
        z = jnp.dot(pick, grads, preferred_element_type=f32)
        z = jnp.concatenate([z[:48], z[48:]], axis=1)
        high = z.astype(bf16)
        z = jnp.concatenate([high, (z - high.astype(f32)).astype(bf16)], axis=0)
        z = jnp.dot(z, back_one[...], preferred_element_type=f32)
        z = z[:48] + z[48:]
        lat_lines[pl.ds(jnp.maximum(n - 1, 0), 48, stride=rows), :] = z[:, :LANES] + carry_lat[...]
        carry_lat[...] = z[:, LANES:]
        add_taps(grads[16:] * keep, operand(source, at, 1, half), acc_one, acc_one_next, chan1)

    def second_segment(m, _):
        second_product(2 * m + 1, cast_odd)
        loss_gradient(2 * m, cast_even, fgrad_even)
        pull_back(2 * m - 1, fgrad_odd)
        second_product(2 * m + 2, cast_even)
        loss_gradient(2 * m + 1, cast_odd, fgrad_odd)
        pull_back(2 * m, fgrad_even)
        return 0

    second_product(0, cast_even)
    lax.fori_loop(0, rows // 2, second_segment, 0)
    loss_gradient(rows, cast_even, fgrad_even)
    pull_back(rows - 1, fgrad_odd)
    pull_back(rows, fgrad_even)

    for t in range(own):
        out_lat[:, t * LANES : (t + 1) * LANES] = lat_lines[t * rows : (t + 1) * rows].astype(bf16)
    pack_taps(acc_one, acc_one_next, taps, 0, chan0, chan1, norm)
    pack_taps(acc_two, acc_two_next, taps, -(-9 // (LANES // chan0)) * chan1, chan1, chan2, norm)
    count = taps_keep.shape[0]
    odd = jnp.bitwise_and(lat_pos, 1)
    taps_keep[...] = taps[pl.ds(pl.multiple_of(odd * count, 8), count), :]
    taps_send[...] = taps[pl.ds(pl.multiple_of((1 - odd) * count, 8), count), :]


def swapped(array, axis, bit):
    return lax.ppermute(array, axis, [(i, i ^ bit) for i in range(lax.axis_size(axis))])


def total(array, axis, first, second):
    one, two, three = (swapped(array, axis, k) for k in (first, second, first ^ second))
    return (array + one) + (two + three)


def local(
    latent, member_seeds, noise_scale, kernel_one, kernel_two, targets, land_words, channel_weight
):
    sample_count, rows, span = latent.shape
    chan0, chan1, chan2 = kernel_one.shape[2], kernel_one.shape[3], kernel_two.shape[3]
    lat_count = lax.axis_size("lat")
    own = span // LANES // lax.axis_size("mem")
    half = (own + 1) // 2
    assert sample_count == 1 and member_seeds.shape[0] == MEM and rows % 2 == 0 and own % 2 == 1 and lax.axis_size("mem") == 4
    assert 4 * chan2 == 2 * chan1 == chan0 and chan0 == 64
    vmem = pl.BlockSpec(memory_space=pltpu.VMEM)
    smem = pl.BlockSpec(memory_space=pltpu.SMEM)
    f32, bf16 = jnp.float32, jnp.bfloat16
    wide, front = half + 2, half + 1
    params = pltpu.CompilerParams(vmem_limit_bytes=32 * 1024 * 1024)
    small = pltpu.CompilerParams(vmem_limit_bytes=8 * 1024 * 1024)
    kernel_one = kernel_one.transpose(0, 1, 3, 2)
    kernel_two = kernel_two.transpose(0, 1, 3, 2)
    down, up = pl.pallas_call(
        functools.partial(edge_kernel, half, chan2),
        grid=(1,),
        in_specs=[
            pl.BlockSpec((1, 8, span), lambda i: (0, 0, 0)),
            pl.BlockSpec((1, 8, span), lambda i: (0, rows // 2 - 1, 0)),
            pl.BlockSpec((8, land_words.shape[1]), lambda i: (rows // 2 - 1, 0)),
        ],
        out_specs=[
            pl.BlockSpec((2 * wide, 8, LANES), lambda i: (0, 0, 0)),
            pl.BlockSpec((1, 2 * wide * LANES), lambda i: (0, 0)),
        ],
        out_shape=[
            jax.ShapeDtypeStruct((2 * wide, 8, LANES), bf16),
            jax.ShapeDtypeStruct((1, 2 * wide * LANES), bf16),
        ],
        scratch_shapes=[pltpu.VMEM((8, LANES), jnp.int32)],
        compiler_params=pltpu.CompilerParams(vmem_limit_bytes=56 * 1024 * 1024),
        name="edges",
    )(latent, targets, land_words)
    above = shifted(down, "lat", 1)
    below = shifted(up, "lat", -1)
    band = jax.ShapeDtypeStruct((512, 256), bf16)
    source, *bands = pl.pallas_call(
        functools.partial(prepare_kernel, half),
        in_specs=[smem] * 2 + [vmem] * 3,
        out_specs=[vmem] * 5,
        out_shape=[jax.ShapeDtypeStruct((rows, wide, 16, LANES), bf16)] + [band] * 4,
        scratch_shapes=[pltpu.VMEM((2 * wide, rows, LANES), f32)],
        compiler_params=small,
        cost_estimate=pl.CostEstimate(flops=10**8, bytes_accessed=10**7, transcendentals=0),
        name="prepare",
    )(member_seeds, noise_scale, latent, kernel_one, kernel_two)
    norm = 1.0 / math.sqrt(sample_count * 4 * rows * lat_count * targets.shape[2])
    tap_rows = 5 * chan1 + 3 * chan2
    lat_grad, taps, taps_send = pl.pallas_call(
        functools.partial(band_kernel, half, (chan0, chan1, chan2), norm),
        in_specs=[smem] * 3 + [vmem] * 9,
        out_specs=[vmem] * 3,
        out_shape=[
            jax.ShapeDtypeStruct((rows, own * LANES), bf16),
            jax.ShapeDtypeStruct((tap_rows // 2, LANES), f32),
            jax.ShapeDtypeStruct((tap_rows // 2, LANES), f32),
        ],
        scratch_shapes=[
            pltpu.VMEM((2 * wide, 8, LANES), f32),
            pltpu.VMEM((2 * front, 4 * rows + 8, LANES), f32),
            pltpu.VMEM((2 * front, 4 * rows + 8, LANES), f32),
            pltpu.VMEM((4 * rows, LANES), jnp.int32),
            pltpu.VMEM((rows + 4, wide + 1, 16, LANES), bf16),
            pltpu.VMEM((wide * 16, 2 * LANES), f32),
            pltpu.VMEM((wide * 16, 2 * LANES), f32),
            pltpu.VMEM((2 * rows + 4, wide, 16, LANES), bf16),
            pltpu.VMEM((2 * rows + 4, front, 16, LANES), f32),
            pltpu.VMEM((4, front, 16, LANES), bf16),
            pltpu.VMEM((4, front, 16, LANES), bf16),
            pltpu.VMEM((4, front + 1, 16, LANES), bf16),
            pltpu.VMEM((4, front + 1, 16, LANES), bf16),
            pltpu.VMEM((front * 16, LANES), f32),
            pltpu.VMEM((48, LANES), f32),
            pltpu.VMEM((48 * rows, LANES), f32),
            pltpu.VMEM((tap_rows, LANES), f32),
            pltpu.VMEM((256, 256), f32),
            pltpu.VMEM((2 * chan1, 256), f32),
            pltpu.VMEM((256, 256), f32),
            pltpu.VMEM((2 * chan2, 256), f32),
        ],
        compiler_params=params,
        name="band",
    )(
        member_seeds,
        noise_scale,
        channel_weight,
        source,
        above,
        below,
        targets,
        land_words,
        *bands,
    )
    one, two, three = (swapped(lat_grad, "mem", k) for k in range(1, 4))
    taps = taps + swapped(taps_send, "lat", 1)
    bits = [1 << k for k in range(1, lat_count.bit_length() - 1)]
    for bit in bits:
        if bit == bits[-1]:
            taps, three = lax.optimization_barrier((taps, three))
        taps = taps + swapped(taps, "lat", bit)
    taps, two = lax.optimization_barrier((taps, two))
    latent_grad = pl.pallas_call(
        functools.partial(place_kernel, own),
        in_specs=[vmem] * 4,
        out_specs=vmem,
        out_shape=jax.ShapeDtypeStruct((1, rows, span), f32),
        compiler_params=small,
        name="place",
    )(lat_grad, one, two, three)
    taps = total(taps, "mem", 1, 2)
    taps, latent_grad = lax.optimization_barrier((taps, latent_grad))
    other = swapped(taps, "lat", 1)
    one, two = pl.pallas_call(
        taps_kernel,
        in_specs=[vmem] * 2,
        out_specs=[vmem] * 2,
        out_shape=[
            jax.ShapeDtypeStruct(kernel_one.shape, f32),
            jax.ShapeDtypeStruct(kernel_two.shape, f32),
        ],
        scratch_shapes=[pltpu.VMEM((tap_rows, LANES), f32)],
        compiler_params=small,
        name="taps",
    )(taps, other)
    return (latent_grad, one.transpose(0, 1, 3, 2), two.transpose(0, 1, 3, 2))


def solution(mesh):
    in_specs = (P(None, "lat", None), P(), P(), P(), P(), P(None, "lat", None), P("lat", None), P())
    out_specs = (P(None, "lat", None), P(), P())
    return jax.shard_map(local, mesh=mesh, in_specs=in_specs, out_specs=out_specs, check_vma=False)
```

```python
import functools
import math

import jax
import jax.numpy as jnp
from jax import lax
from jax.experimental import pallas as pl
from jax.experimental.pallas import tpu as pltpu
from jax.sharding import PartitionSpec as P

SMOOTH = 0.01
HASH_CELL = 1103515245
HASH_SEED = 747796405
HASH_MIX = 277803737
LANES = 128
MEM = 8
GELU_A = math.sqrt(2.0 / math.pi)
GELU_B = 0.044715


def shifted(array, axis, by):
    peers = lax.axis_size(axis)
    pairs = [(i, i + by) for i in range(peers) if 0 <= i + by < peers]
    return lax.ppermute(array, axis, pairs)


def iota(shape, axis):
    return lax.broadcasted_iota(jnp.int32, shape, axis)


def lane_table(ref, count):
    lane = iota((8, LANES), 1) % count
    total = jnp.zeros((8, LANES), jnp.float32)
    for k in range(count):
        total = jnp.where(lane == k, ref[k], total)
    return total


def build_band(kernel_ref, band_ref):
    chan_out, chan_in = kernel_ref.shape[2], kernel_ref.shape[3]
    cells = LANES // chan_in
    repeat = (iota((chan_out, LANES), 1) % chan_out == iota((chan_out, LANES), 0)).astype(jnp.bfloat16)
    wide = {}
    for a in range(3):
        for b in range(3):
            wide[a, b] = lax.dot_general(
                kernel_ref[a, b], repeat, (((0,), (0,)), ((), ())), preferred_element_type=jnp.float32
            )
    column = iota((chan_in, LANES), 1) // chan_out
    zero = jnp.zeros((chan_in, LANES), jnp.float32)
    for block in range(2):
        for row in range(2):
            for cell in range(cells):
                at = block * 256 + row * LANES + cell * chan_in
                for sub in range(2):
                    a = sub - 2 * row + 1
                    part = zero
                    for q in range(2 * cells):
                        b = q - 2 * (cell + block * cells) + 1
                        if 0 <= a <= 2 and 0 <= b <= 2:
                            part = jnp.where(column == q, wide[a, b], part)
                    band_ref[at : at + chan_in, sub * LANES : (sub + 1) * LANES] = part.astype(jnp.bfloat16)


def build_back(kernel_ref, back_ref):
    chan_out, chan_in = kernel_ref.shape[2], kernel_ref.shape[3]
    cells = LANES // chan_in
    repeat = (iota((chan_in, LANES), 1) % chan_in == iota((chan_in, LANES), 0)).astype(jnp.bfloat16)
    flat = kernel_ref[...].reshape(9 * chan_out, chan_in)
    wide = jnp.dot(flat, repeat, preferred_element_type=jnp.float32)
    column = iota((chan_out, LANES), 1) // chan_in
    zero = jnp.zeros((chan_out, LANES), jnp.float32)
    for block in range(2):
        for sub in range(2):
            for q in range(2 * cells):
                at = block * 256 + sub * LANES + q * chan_out
                for row in range(2):
                    a = sub - 2 * row + 1
                    part = zero
                    for cell in range(cells):
                        b = q - 2 * (cell + block * cells) + 1
                        if 0 <= a <= 2 and 0 <= b <= 2:
                            tap = (3 * a + b) * chan_out
                            part = jnp.where(column == cell, wide[tap : tap + chan_out], part)
                    back_ref[at : at + chan_out, row * LANES : (row + 1) * LANES] = part.astype(jnp.bfloat16)


def tap_place(k, first, chan_in, chan_out):
    cells = LANES // chan_in
    if k == 8 and first > 0:
        return 4 * 2 * chan_out, 2 * chan_in
    return first + k // cells * chan_out, k % cells * chan_in


def pack_taps(acc_ref, next_ref, out_ref, first, chan_in, chan_out, norm):
    cells = LANES // chan_in
    group = iota((chan_out, LANES), 1) // chan_in
    for k in range(9):
        a, b = divmod(k, 3)
        row, sub = ((1, 1), (0, 0), (0, 1))[a]
        at, lane = tap_place(k, first, chan_in, chan_out)
        part = None
        for reach in range(cells + 1):
            q = 2 * reach + b - 1
            if 0 <= q < 2 * cells:
                block, cell = reach // cells, reach % cells
                lines = sub * LANES + q * chan_out if block == 0 else sub * chan_out
                ref = acc_ref if block == 0 else next_ref
                piece = ref[lines : lines + chan_out, row * LANES : (row + 1) * LANES]
                turn = (lane - cell * chan_in) % LANES
                piece = pltpu.roll(piece, turn, 1) if turn else piece
                part = piece if part is None else part + piece
        part = part * norm
        if lane:
            part = jnp.where(group == lane // chan_in, part, out_ref[at : at + chan_out, :])
        out_ref[at : at + chan_out, :] = part


def spread_line(ref, slot, at):
    return ref[slot, pl.ds(at, 8, stride=0), :]


def window_block(mem_pos, own, half, blocks, part, t):
    at = mem_pos * own + part * half + t + (blocks - 1)
    at = jnp.where(at >= blocks, at - blocks, at)
    return jnp.where(at >= blocks, at - blocks, at)


def land_of(words, block, chan):
    cell = block * (LANES // chan) + iota(words.shape, 1) // chan
    word = jnp.right_shift(cell * 2185, 16)
    picked = jnp.take_along_axis(words, word, axis=1, mode="promise_in_bounds")
    return jnp.bitwise_and(jnp.right_shift(picked, cell - 30 * word), 1).astype(jnp.float32)


def edge_kernel(half, chan, latent, targets, land, down, up, words):
    rows = latent.shape[1]
    blocks = latent.shape[2] // LANES
    own = blocks // lax.axis_size("mem")
    mem_pos = lax.axis_index("mem")
    words[...] = jnp.zeros(words.shape, jnp.int32)
    words[:, : land.shape[1]] = land[...]
    line = iota((8, LANES), 0)
    for t in range(half + 2):
        for part in range(2):
            block = window_block(mem_pos, own, half, blocks, part, t)
            off = pl.multiple_of(block * LANES, LANES)
            slot = t * 2 + part
            cells = latent[0, :, pl.ds(off, LANES)].astype(jnp.float32)
            aims = targets[0, :, pl.ds(off, LANES)].astype(jnp.float32)
            mask = land_of(words[...], block, chan)
            pack = pltpu.roll(cells, 1, 0)
            pack = jnp.where((line >= 1) & (line <= 3), pltpu.roll(aims, 4, 0), pack)
            pack = jnp.where((line >= 4) & (line <= 6), pltpu.roll(mask, 7, 0), pack)
            down[slot] = pack.astype(jnp.bfloat16)
            up[:, slot * LANES : (slot + 1) * LANES] = cells[0:1].astype(jnp.bfloat16)


def place_kernel(own, part0, part1, part2, part3, latent_grad):
    mem_pos = lax.axis_index("mem")
    for k, part in enumerate((part0, part1, part2, part3)):
        off = pl.multiple_of(jnp.bitwise_xor(mem_pos, k) * own * LANES, LANES)
        latent_grad[0, :, pl.ds(off, own * LANES)] = part[...].astype(jnp.float32)


def taps_kernel(taps, grad_one, grad_two):
    first = 0
    for out in (grad_one, grad_two):
        chan_out, chan_in = out.shape[2], out.shape[3]
        for k in range(9):
            at, lane = tap_place(k, first, chan_in, chan_out)
            block = taps[at : at + chan_out, :]
            block = pltpu.roll(block, LANES - lane, 1) if lane else block
            out[k // 3, k % 3] = block[:, :chan_in]
        first += 5 * chan_out


def make_source(i, row, total_rows, span, own, half, seeds, scale, chan, line, store):
    blocks = span // LANES
    mem_pos = lax.axis_index("mem")
    sublane = iota((8, LANES), 0)
    seed_table = jnp.zeros((8, LANES), jnp.int32)
    for m in range(MEM):
        seed_table = jnp.where(sublane == m, seeds[m], seed_table)
    hash_table = iota((8, LANES), 1) * HASH_CELL + seed_table * HASH_SEED
    scale_table = lane_table(scale, chan)
    inside = jnp.where(row < total_rows, 1.0, 0.0).astype(jnp.float32)
    for t in range(half + 2):
        parts = []
        for part in range(2):
            first = (row * span + window_block(mem_pos, own, half, blocks, part, t) * LANES) * HASH_CELL
            h = hash_table + first
            h = jnp.bitwise_xor(h, jnp.right_shift(h, 15))
            h = h * HASH_MIX
            h = jnp.bitwise_xor(h, jnp.right_shift(h, 13))
            noise = jnp.bitwise_and(h, 65535).astype(jnp.float32) * (1.0 / 65536.0) - 0.5
            noise = noise * 3.4641016
            parts.append((line(t * 2 + part, i) + noise * scale_table) * inside)
        store(i, t, jnp.concatenate(parts, axis=0).astype(jnp.bfloat16))


def prepare_kernel(half, seeds, scale, latent, kernel_one, kernel_two, source, band_one, band_two, back_one, back_two, lines):
    rows, span = latent.shape[1], latent.shape[2]
    blocks = span // LANES
    own = blocks // lax.axis_size("mem")
    total_rows = rows * lax.axis_size("lat")
    lat_pos, mem_pos = lax.axis_index("lat"), lax.axis_index("mem")
    for t in range(half + 2):
        for part in range(2):
            off = pl.multiple_of(window_block(mem_pos, own, half, blocks, part, t) * LANES, LANES)
            lines[t * 2 + part] = latent[0, :, pl.ds(off, LANES)].astype(jnp.float32)

    def line(slot, i):
        return spread_line(lines, slot, i)

    def store(i, t, value):
        source[i, t] = value

    def step(i, _):
        make_source(
            i, lat_pos * rows + i, total_rows, span, own, half, seeds, scale, kernel_one.shape[3], line, store
        )
        return 0

    lax.fori_loop(0, rows, step, 0)
    build_band(kernel_one, band_one)
    build_band(kernel_two, band_two)
    build_back(kernel_one, back_one)
    build_back(kernel_two, back_two)


def band_kernel(
    half,
    chans,
    norm,
    seeds,
    scale,
    channel_weight,
    own_source,
    above,
    below,
    targets,
    land,
    band_one,
    band_two,
    back_one,
    back_two,
    out_lat,
    taps,
    lat_rows,
    tgt_rows,
    weight_rows,
    words,
    source,
    pre_even,
    pre_odd,
    act,
    slope,
    cast_even,
    cast_odd,
    fgrad_even,
    fgrad_odd,
    carry,
    carry_lat,
    lat_lines,
    acc_one,
    acc_one_next,
    acc_two,
    acc_two_next,
):
    rows = own_source.shape[0]
    span = targets.shape[2]
    blocks = span // LANES
    lat_count = lax.axis_size("lat")
    own = blocks // lax.axis_size("mem")
    total_rows = rows * lat_count
    grid_rows = 4 * rows
    grid_total = grid_rows * lat_count
    lat_pos = lax.axis_index("lat")
    mem_pos = lax.axis_index("mem")
    wide = half + 2
    front = half + 1
    chan0, chan1, chan2 = chans
    f32, bf16 = jnp.float32, jnp.bfloat16

    def block_of(part, t):
        return window_block(mem_pos, own, half, blocks, part, t)

    pad_rows = grid_rows + 8
    grid_row = iota((pad_rows, LANES), 0)
    grid_row = jnp.where(grid_row < grid_rows, grid_row, grid_row - (grid_rows + 4)) + lat_pos * grid_rows
    latitude = math.pi / 2 - math.pi * (grid_row.astype(f32) + 0.5) / grid_total
    channels = lane_table(channel_weight, chan2)
    cosine = jnp.where(grid_row >= 0, jnp.cos(latitude), 0.0)
    base_rows = cosine * (jnp.tile(channels, (pad_rows // 8, 1)) * (1.0 / (MEM * (MEM - 1))))

    words[...] = jnp.zeros(words.shape, jnp.int32)
    words[:, : land.shape[1]] = land[...]
    for t in range(wide):
        for part in range(2):
            block = block_of(part, t)
            off = pl.multiple_of(block * LANES, LANES)
            slot = t * 2 + part
            edge = above[slot].astype(f32)
            lat_rows[slot, 0:1] = edge[0:1]
            lat_rows[slot, 1:2] = below[:, slot * LANES : (slot + 1) * LANES].astype(f32)
            if t < front:
                tgt_rows[slot, 0:grid_rows] = targets[0, :, pl.ds(off, LANES)].astype(f32)
                tgt_rows[slot, grid_rows:] = edge
                mask = jnp.concatenate([land_of(words[...], block, chan2), pltpu.roll(edge, 5, 0)], axis=0)
                weight_rows[slot] = base_rows + base_rows * mask

    source[rows + 2 :] = jnp.zeros((2,) + source.shape[1:], bf16)
    source[:, wide] = jnp.zeros((source.shape[0],) + source.shape[2:], bf16)
    fgrad_even[:, 0] = jnp.zeros((4,) + fgrad_even.shape[2:], bf16)
    fgrad_odd[...] = jnp.zeros(fgrad_odd.shape, bf16)
    carry[...] = jnp.zeros(carry.shape, f32)
    carry_lat[...] = jnp.zeros(carry_lat.shape, f32)
    for acc in (acc_one, acc_one_next, acc_two, acc_two_next):
        acc[...] = jnp.zeros(acc.shape, f32)

    def line(slot, i):
        return spread_line(lat_rows, slot, i)

    def store(i, t, value):
        source[i * (rows + 1), t] = value

    def edge_source(i, _):
        row = lat_pos * rows - 1 + i * (rows + 1)
        make_source(i, row, total_rows, span, own, half, seeds, scale, chan0, line, store)
        return 0

    lax.fori_loop(0, 2, edge_source, 0)
    source[1 : rows + 1, 0:wide] = own_source[...]

    def operand(ref, i, start, count):
        def piece(r, at):
            return ref[r, pl.ds(at, count)].reshape(count * 16, LANES)

        return jnp.concatenate(
            [piece(i, start), piece(i + 1, start), piece(i, start + 1), piece(i + 1, start + 1)], axis=1
        )

    def first_product(i, pre):
        pre[...] = jnp.dot(operand(source, i, 0, wide), band_one[...], preferred_element_type=f32)

    def first_gelu(i, pre):
        for t in range(wide):
            for sub in range(2):
                x = pre[t * 16 : (t + 1) * 16, sub * LANES : (sub + 1) * LANES]
                square = x * x
                th = jnp.tanh(x * (GELU_A + (GELU_A * GELU_B) * square))
                plus = 0.5 + 0.5 * th
                act[2 * i + sub, t] = (x * plus).astype(bf16)
                if t < front:
                    d = plus + (x * plus) * (1.0 - th) * (GELU_A + (3.0 * GELU_A * GELU_B) * square)
                    if t == half:
                        d = jnp.where(iota((16, LANES), 0) < 8, d, 0.0)
                    slope[2 * i + sub, t] = d

    def first_segment(m, _):
        first_product(2 * m + 1, pre_odd)
        first_gelu(2 * m, pre_even)
        first_product(2 * m + 2, pre_even)
        first_gelu(2 * m + 1, pre_odd)
        return 0

    first_product(0, pre_even)
    lax.fori_loop(0, rows // 2 + 1, first_segment, 0)

    members = front * 16
    owner = iota((48, members), 0)
    group = iota((48, members), 1) // 8
    place = (group % 2) * half + group // 2
    real = (group // 2 > 0) & (place - 1 < own)
    pick_own = (real & (place - 1 == owner)).astype(bf16)
    pick_prev = ((group // 2 < half) & (place == owner)).astype(bf16)
    pick = jnp.concatenate([pick_own, pick_prev], axis=0)

    def second_product(n, cast):
        taken = jnp.concatenate([operand(act, 2 * n + k, 0, front) for k in range(2)], axis=0)
        out = jnp.dot(taken, band_two[...], preferred_element_type=f32).astype(bf16)
        for k in range(2):
            for sub in range(2):
                part = out[k * members : (k + 1) * members, sub * LANES : (sub + 1) * LANES]
                cast[2 * k + sub] = part.reshape(front, 16, LANES)

    def loss_gradient(n, cast, fgrad):
        first = jnp.where(n >= 1, 4 * (n - 1), grid_rows)
        for line in range(4):
            for t in range(front):
                both = cast[line, t].astype(f32)
                parts = []
                for part in range(2):
                    if t == half and part == 1:
                        parts.append(jnp.zeros((8, LANES), f32))
                        continue
                    f = both[part * 8 : part * 8 + 8]
                    d = f - spread_line(tgt_rows, t * 2 + part, first + line)
                    goal = d * lax.rsqrt(d * d + SMOOTH)
                    gs = []
                    for k in range(1, 5):
                        d = f - pltpu.roll(f, k, 0)
                        gs.append(d * lax.rsqrt(d * d + SMOOTH))
                    back = gs[2]
                    for k in (1, 0):
                        back = gs[k] + pltpu.roll(back, MEM - 1, 0)
                    back = pltpu.roll(back, MEM - 1, 0)
                    spread = (gs[0] + gs[1]) + (gs[2] + gs[3]) - back
                    weight = spread_line(weight_rows, t * 2 + part, first + line)
                    parts.append(weight * ((MEM - 1.0) * goal - spread))
                fgrad[line, t + 1] = jnp.concatenate(parts, axis=0).astype(bf16)

    def pull_back(n, fgrad):
        at = jnp.maximum(n, 0)
        keep = jnp.where(n >= 1, 1.0, 0.0).astype(bf16)

        def flat(line, start, count):
            return fgrad[line, start : start + count].reshape(count * 16, LANES)

        def add_taps(g, x, acc, acc_next, chan_out):
            turned = g.T
            acc[...] += jnp.dot(turned, x[:, :256], preferred_element_type=f32)
            last = [turned[k * LANES - chan_out : k * LANES] for k in (1, 2)]
            last = jnp.concatenate(last, axis=0)
            acc_next[...] += jnp.dot(last, x[:, 256:], preferred_element_type=f32)

        g = [
            jnp.concatenate(
                [flat(2 * k, 1, front), flat(2 * k + 1, 1, front), flat(2 * k, 0, front), flat(2 * k + 1, 0, front)],
                axis=1,
            )
            for k in range(2)
        ]
        pulled = jnp.dot(jnp.concatenate(g, axis=0), back_two[...], preferred_element_type=f32)
        g = [jnp.concatenate([flat(2 * k, 2, half), flat(2 * k + 1, 2, half)], axis=1) for k in range(2)]
        x = [operand(act, 2 * at + k, 1, half) for k in range(2)]
        add_taps(jnp.concatenate(g, axis=0) * keep, jnp.concatenate(x, axis=0), acc_two, acc_two_next, chan2)
        grads = [
            pulled[:members, :LANES] + carry[...],
            pulled[members:, :LANES] + pulled[:members, LANES:],
        ]
        carry[...] = pulled[members:, LANES:]
        grads = [(grads[k] * slope[2 * at + k].reshape(members, LANES)).astype(bf16) for k in range(2)]
        grads = jnp.concatenate(grads, axis=1)
        z = jnp.dot(pick, grads, preferred_element_type=f32)
        z = jnp.concatenate([z[:48], z[48:]], axis=1)
        high = z.astype(bf16)
        z = jnp.concatenate([high, (z - high.astype(f32)).astype(bf16)], axis=0)
        z = jnp.dot(z, back_one[...], preferred_element_type=f32)
        z = z[:48] + z[48:]
        lat_lines[pl.ds(jnp.maximum(n - 1, 0), 48, stride=rows), :] = z[:, :LANES] + carry_lat[...]
        carry_lat[...] = z[:, LANES:]
        add_taps(grads[16:] * keep, operand(source, at, 1, half), acc_one, acc_one_next, chan1)

    def second_segment(m, _):
        second_product(2 * m + 1, cast_odd)
        loss_gradient(2 * m, cast_even, fgrad_even)
        pull_back(2 * m - 1, fgrad_odd)
        second_product(2 * m + 2, cast_even)
        loss_gradient(2 * m + 1, cast_odd, fgrad_odd)
        pull_back(2 * m, fgrad_even)
        return 0

    second_product(0, cast_even)
    lax.fori_loop(0, rows // 2, second_segment, 0)
    loss_gradient(rows, cast_even, fgrad_even)
    pull_back(rows - 1, fgrad_odd)
    pull_back(rows, fgrad_even)

    for t in range(own):
        out_lat[:, t * LANES : (t + 1) * LANES] = lat_lines[t * rows : (t + 1) * rows].astype(bf16)
    pack_taps(acc_one, acc_one_next, taps, 0, chan0, chan1, norm)
    pack_taps(acc_two, acc_two_next, taps, 5 * chan1, chan1, chan2, norm)


def swapped(array, axis, bit):
    return lax.ppermute(array, axis, [(i, i ^ bit) for i in range(lax.axis_size(axis))])


def local(
    latent, member_seeds, noise_scale, kernel_one, kernel_two, targets, land_words, channel_weight
):
    sample_count, rows, span = latent.shape
    chan0, chan1, chan2 = kernel_one.shape[2], kernel_one.shape[3], kernel_two.shape[3]
    lat_count = lax.axis_size("lat")
    own = span // LANES // lax.axis_size("mem")
    half = (own + 1) // 2
    assert sample_count == 1 and member_seeds.shape[0] == MEM and rows % 2 == 0 and own % 2 == 1 and lax.axis_size("mem") == 4
    assert 4 * chan2 == 2 * chan1 == chan0 and chan0 == 64
    vmem = pl.BlockSpec(memory_space=pltpu.VMEM)
    smem = pl.BlockSpec(memory_space=pltpu.SMEM)
    f32, bf16 = jnp.float32, jnp.bfloat16
    wide, front = half + 2, half + 1
    params = pltpu.CompilerParams(vmem_limit_bytes=32 * 1024 * 1024)
    small = pltpu.CompilerParams(vmem_limit_bytes=8 * 1024 * 1024)
    kernel_one = kernel_one.transpose(0, 1, 3, 2)
    kernel_two = kernel_two.transpose(0, 1, 3, 2)
    down, up = pl.pallas_call(
        functools.partial(edge_kernel, half, chan2),
        grid=(1,),
        in_specs=[
            pl.BlockSpec((1, 8, span), lambda i: (0, 0, 0)),
            pl.BlockSpec((1, 8, span), lambda i: (0, rows // 2 - 1, 0)),
            pl.BlockSpec((8, land_words.shape[1]), lambda i: (rows // 2 - 1, 0)),
        ],
        out_specs=[
            pl.BlockSpec((2 * wide, 8, LANES), lambda i: (0, 0, 0)),
            pl.BlockSpec((1, 2 * wide * LANES), lambda i: (0, 0)),
        ],
        out_shape=[
            jax.ShapeDtypeStruct((2 * wide, 8, LANES), bf16),
            jax.ShapeDtypeStruct((1, 2 * wide * LANES), bf16),
        ],
        scratch_shapes=[pltpu.VMEM((8, LANES), jnp.int32)],
        compiler_params=pltpu.CompilerParams(vmem_limit_bytes=56 * 1024 * 1024),
        name="edges",
    )(latent, targets, land_words)
    above = shifted(down, "lat", 1)
    below = shifted(up, "lat", -1)
    band = jax.ShapeDtypeStruct((512, 256), bf16)
    source, *bands = pl.pallas_call(
        functools.partial(prepare_kernel, half),
        in_specs=[smem] * 2 + [vmem] * 3,
        out_specs=[vmem] * 5,
        out_shape=[jax.ShapeDtypeStruct((rows, wide, 16, LANES), bf16)] + [band] * 4,
        scratch_shapes=[pltpu.VMEM((2 * wide, rows, LANES), f32)],
        compiler_params=small,
        cost_estimate=pl.CostEstimate(flops=10**8, bytes_accessed=10**7, transcendentals=0),
        name="prepare",
    )(member_seeds, noise_scale, latent, kernel_one, kernel_two)
    norm = 1.0 / math.sqrt(sample_count * 4 * rows * lat_count * targets.shape[2])
    tap_rows = 5 * chan1 + 2 * chan2
    lat_grad, taps = pl.pallas_call(
        functools.partial(band_kernel, half, (chan0, chan1, chan2), norm),
        in_specs=[smem] * 3 + [vmem] * 9,
        out_specs=[vmem] * 2,
        out_shape=[
            jax.ShapeDtypeStruct((rows, own * LANES), bf16),
            jax.ShapeDtypeStruct((tap_rows, LANES), f32),
        ],
        scratch_shapes=[
            pltpu.VMEM((2 * wide, 8, LANES), f32),
            pltpu.VMEM((2 * front, 4 * rows + 8, LANES), f32),
            pltpu.VMEM((2 * front, 4 * rows + 8, LANES), f32),
            pltpu.VMEM((4 * rows, LANES), jnp.int32),
            pltpu.VMEM((rows + 4, wide + 1, 16, LANES), bf16),
            pltpu.VMEM((wide * 16, 2 * LANES), f32),
            pltpu.VMEM((wide * 16, 2 * LANES), f32),
            pltpu.VMEM((2 * rows + 4, wide, 16, LANES), bf16),
            pltpu.VMEM((2 * rows + 4, front, 16, LANES), f32),
            pltpu.VMEM((4, front, 16, LANES), bf16),
            pltpu.VMEM((4, front, 16, LANES), bf16),
            pltpu.VMEM((4, front + 1, 16, LANES), bf16),
            pltpu.VMEM((4, front + 1, 16, LANES), bf16),
            pltpu.VMEM((front * 16, LANES), f32),
            pltpu.VMEM((48, LANES), f32),
            pltpu.VMEM((48 * rows, LANES), f32),
            pltpu.VMEM((256, 256), f32),
            pltpu.VMEM((2 * chan1, 256), f32),
            pltpu.VMEM((256, 256), f32),
            pltpu.VMEM((2 * chan2, 256), f32),
        ],
        compiler_params=params,
        name="band",
    )(
        member_seeds,
        noise_scale,
        channel_weight,
        source,
        above,
        below,
        targets,
        land_words,
        *bands,
    )
    one, two, three = (swapped(lat_grad, "mem", k) for k in range(1, 4))
    taps = taps.reshape(lat_count, tap_rows // lat_count, LANES)
    share = jnp.sum(lax.all_to_all(taps, "lat", 0, 0, tiled=True), axis=0)
    share = jnp.broadcast_to(share, (lax.axis_size("mem"),) + share.shape)
    share = jnp.sum(lax.all_to_all(share, "mem", 0, 0, tiled=True), axis=0)
    share = jnp.broadcast_to(share, (lat_count,) + share.shape)
    taps = lax.all_to_all(share, "lat", 0, 0, tiled=True).reshape(tap_rows, LANES)
    latent_grad = pl.pallas_call(
        functools.partial(place_kernel, own),
        in_specs=[vmem] * 4,
        out_specs=vmem,
        out_shape=jax.ShapeDtypeStruct((1, rows, span), f32),
        compiler_params=small,
        name="place",
    )(lat_grad, one, two, three)
    one, two = pl.pallas_call(
        taps_kernel,
        in_specs=[vmem],
        out_specs=[vmem] * 2,
        out_shape=[
            jax.ShapeDtypeStruct(kernel_one.shape, f32),
            jax.ShapeDtypeStruct(kernel_two.shape, f32),
        ],
        compiler_params=small,
        name="taps",
    )(taps)
    return (latent_grad, one.transpose(0, 1, 3, 2), two.transpose(0, 1, 3, 2))


def solution(mesh):
    in_specs = (P(None, "lat", None), P(), P(), P(), P(), P(None, "lat", None), P("lat", None), P())
    out_specs = (P(None, "lat", None), P(), P())
    return jax.shard_map(local, mesh=mesh, in_specs=in_specs, out_specs=out_specs, check_vma=False)
```

```python
import functools
import math

import jax
import jax.numpy as jnp
from jax import lax
from jax.experimental import pallas as pl
from jax.experimental.pallas import tpu as pltpu
from jax.sharding import PartitionSpec as P

SMOOTH = 0.01
HASH_CELL = 1103515245
HASH_SEED = 747796405
HASH_MIX = 277803737
LANES = 128
MEM = 8
GELU_A = math.sqrt(2.0 / math.pi)
GELU_B = 0.044715


def shifted(array, axis, by):
    peers = lax.axis_size(axis)
    pairs = [(i, i + by) for i in range(peers) if 0 <= i + by < peers]
    return lax.ppermute(array, axis, pairs)


def iota(shape, axis):
    return lax.broadcasted_iota(jnp.int32, shape, axis)


def lane_table(ref, count):
    lane = iota((8, LANES), 1) % count
    total = jnp.zeros((8, LANES), jnp.float32)
    for k in range(count):
        total = jnp.where(lane == k, ref[k], total)
    return total


def build_band(kernel_ref, band_ref):
    chan_out, chan_in = kernel_ref.shape[2], kernel_ref.shape[3]
    cells = LANES // chan_in
    repeat = (iota((chan_out, LANES), 1) % chan_out == iota((chan_out, LANES), 0)).astype(jnp.bfloat16)
    wide = {}
    for a in range(3):
        for b in range(3):
            wide[a, b] = lax.dot_general(
                kernel_ref[a, b], repeat, (((0,), (0,)), ((), ())), preferred_element_type=jnp.float32
            )
    column = iota((chan_in, LANES), 1) // chan_out
    zero = jnp.zeros((chan_in, LANES), jnp.float32)
    for block in range(2):
        for row in range(2):
            for cell in range(cells):
                at = block * 256 + row * LANES + cell * chan_in
                for sub in range(2):
                    a = sub - 2 * row + 1
                    part = zero
                    for q in range(2 * cells):
                        b = q - 2 * (cell + block * cells) + 1
                        if 0 <= a <= 2 and 0 <= b <= 2:
                            part = jnp.where(column == q, wide[a, b], part)
                    band_ref[at : at + chan_in, sub * LANES : (sub + 1) * LANES] = part.astype(jnp.bfloat16)


def build_back(kernel_ref, back_ref):
    chan_out, chan_in = kernel_ref.shape[2], kernel_ref.shape[3]
    cells = LANES // chan_in
    repeat = (iota((chan_in, LANES), 1) % chan_in == iota((chan_in, LANES), 0)).astype(jnp.bfloat16)
    flat = kernel_ref[...].reshape(9 * chan_out, chan_in)
    wide = jnp.dot(flat, repeat, preferred_element_type=jnp.float32)
    column = iota((chan_out, LANES), 1) // chan_in
    zero = jnp.zeros((chan_out, LANES), jnp.float32)
    for block in range(2):
        for sub in range(2):
            for q in range(2 * cells):
                at = block * 256 + sub * LANES + q * chan_out
                for row in range(2):
                    a = sub - 2 * row + 1
                    part = zero
                    for cell in range(cells):
                        b = q - 2 * (cell + block * cells) + 1
                        if 0 <= a <= 2 and 0 <= b <= 2:
                            tap = (3 * a + b) * chan_out
                            part = jnp.where(column == cell, wide[tap : tap + chan_out], part)
                    back_ref[at : at + chan_out, row * LANES : (row + 1) * LANES] = part.astype(jnp.bfloat16)


def pack_taps(acc_ref, next_ref, out_ref, first, chan_in, chan_out, norm):
    cells = LANES // chan_in
    group = iota((chan_out, LANES), 1) // chan_in
    packed = None
    for k in range(9):
        a, b = divmod(k, 3)
        row, sub = ((1, 1), (0, 0), (0, 1))[a]
        slot = k % cells
        part = None
        for reach in range(cells + 1):
            q = 2 * reach + b - 1
            if 0 <= q < 2 * cells:
                block, cell = reach // cells, reach % cells
                lines = sub * LANES + q * chan_out if block == 0 else sub * chan_out
                ref = acc_ref if block == 0 else next_ref
                piece = ref[lines : lines + chan_out, row * LANES : (row + 1) * LANES]
                turn = (slot - cell) % cells * chan_in
                piece = pltpu.roll(piece, turn, 1) if turn else piece
                part = piece if part is None else part + piece
        packed = part if slot == 0 else jnp.where(group == slot, part, packed)
        if slot == cells - 1 or k == 8:
            at = first + k // cells * chan_out
            out_ref[at : at + chan_out, :] = packed * norm


def spread_line(ref, slot, at):
    return jnp.broadcast_to(ref[slot, pl.ds(at, 1), :], (8, LANES))


def window_block(mem_pos, own, half, blocks, part, t):
    at = mem_pos * own + part * half + t + (blocks - 1)
    at = jnp.where(at >= blocks, at - blocks, at)
    return jnp.where(at >= blocks, at - blocks, at)


def land_of(words, block, chan):
    cell = block * (LANES // chan) + iota(words.shape, 1) // chan
    word = jnp.right_shift(cell * 2185, 16)
    picked = jnp.take_along_axis(words, word, axis=1, mode="promise_in_bounds")
    return jnp.bitwise_and(jnp.right_shift(picked, cell - 30 * word), 1).astype(jnp.float32)


def edge_kernel(half, chan, latent, targets, land, down, up, words):
    rows = latent.shape[1]
    blocks = latent.shape[2] // LANES
    own = blocks // lax.axis_size("mem")
    mem_pos = lax.axis_index("mem")
    words[...] = jnp.zeros(words.shape, jnp.int32)
    words[:, : land.shape[1]] = land[...]
    line = iota((8, LANES), 0)
    for t in range(half + 2):
        for part in range(2):
            block = window_block(mem_pos, own, half, blocks, part, t)
            off = pl.multiple_of(block * LANES, LANES)
            slot = t * 2 + part
            cells = latent[0, :, pl.ds(off, LANES)].astype(jnp.float32)
            aims = targets[0, :, pl.ds(off, LANES)].astype(jnp.float32)
            mask = land_of(words[...], block, chan)
            pack = pltpu.roll(cells, 1, 0)
            pack = jnp.where((line >= 1) & (line <= 3), pltpu.roll(aims, 4, 0), pack)
            pack = jnp.where((line >= 4) & (line <= 6), pltpu.roll(mask, 7, 0), pack)
            down[slot] = pack.astype(jnp.bfloat16)
            up[:, slot * LANES : (slot + 1) * LANES] = cells[0:1].astype(jnp.bfloat16)


def place_kernel(own, part0, part1, part2, part3, latent_grad):
    mem_pos = lax.axis_index("mem")
    for k, part in enumerate((part0, part1, part2, part3)):
        off = pl.multiple_of(jnp.bitwise_xor(mem_pos, k) * own * LANES, LANES)
        latent_grad[0, :, pl.ds(off, own * LANES)] = part[...].astype(jnp.float32)


def taps_kernel(mine, other, grad_one, grad_two, taps):
    count = mine.shape[0]
    odd = jnp.bitwise_and(lax.axis_index("lat"), 1)
    taps[pl.ds(pl.multiple_of(odd * count, 8), count), :] = mine[...]
    taps[pl.ds(pl.multiple_of((1 - odd) * count, 8), count), :] = other[...]
    first = 0
    for out in (grad_one, grad_two):
        chan_out, chan_in = out.shape[2], out.shape[3]
        cells = LANES // chan_in
        for k in range(9):
            at = first + k // cells * chan_out
            block = taps[at : at + chan_out, :]
            turn = (-(k % cells)) % cells * chan_in
            block = pltpu.roll(block, turn, 1) if turn else block
            out[k // 3, k % 3] = block[:, :chan_in]
        first += -(-9 // cells) * chan_out


def make_source(i, row, total_rows, span, own, half, seeds, scale, chan, line, store):
    blocks = span // LANES
    mem_pos = lax.axis_index("mem")
    sublane = iota((8, LANES), 0)
    seed_table = jnp.zeros((8, LANES), jnp.int32)
    for m in range(MEM):
        seed_table = jnp.where(sublane == m, seeds[m], seed_table)
    hash_table = iota((8, LANES), 1) * HASH_CELL + seed_table * HASH_SEED
    scale_table = lane_table(scale, chan)
    inside = jnp.where(row < total_rows, 1.0, 0.0).astype(jnp.float32)
    for t in range(half + 2):
        parts = []
        for part in range(2):
            first = (row * span + window_block(mem_pos, own, half, blocks, part, t) * LANES) * HASH_CELL
            h = hash_table + first
            h = jnp.bitwise_xor(h, jnp.right_shift(h, 15))
            h = h * HASH_MIX
            h = jnp.bitwise_xor(h, jnp.right_shift(h, 13))
            noise = jnp.bitwise_and(h, 65535).astype(jnp.float32) * (1.0 / 65536.0) - 0.5
            noise = noise * 3.4641016
            parts.append((line(t * 2 + part, i) + noise * scale_table) * inside)
        store(i, t, jnp.concatenate(parts, axis=0).astype(jnp.bfloat16))


def prepare_kernel(half, seeds, scale, latent, kernel_one, kernel_two, source, band_one, band_two, back_one, back_two, lines):
    rows, span = latent.shape[1], latent.shape[2]
    blocks = span // LANES
    own = blocks // lax.axis_size("mem")
    total_rows = rows * lax.axis_size("lat")
    lat_pos, mem_pos = lax.axis_index("lat"), lax.axis_index("mem")
    for t in range(half + 2):
        for part in range(2):
            off = pl.multiple_of(window_block(mem_pos, own, half, blocks, part, t) * LANES, LANES)
            lines[t * 2 + part] = latent[0, :, pl.ds(off, LANES)].astype(jnp.float32)

    def line(slot, i):
        return spread_line(lines, slot, i)

    def store(i, t, value):
        source[i, t] = value

    def step(i, _):
        make_source(
            i, lat_pos * rows + i, total_rows, span, own, half, seeds, scale, kernel_one.shape[3], line, store
        )
        return 0

    lax.fori_loop(0, rows, step, 0)
    build_band(kernel_one, band_one)
    build_band(kernel_two, band_two)
    build_back(kernel_one, back_one)
    build_back(kernel_two, back_two)


def band_kernel(
    half,
    chans,
    norm,
    seeds,
    scale,
    channel_weight,
    own_source,
    above,
    below,
    targets,
    land,
    band_one,
    band_two,
    back_one,
    back_two,
    out_lat,
    taps_keep,
    taps_send,
    lat_rows,
    tgt_rows,
    weight_rows,
    words,
    source,
    pre_even,
    pre_odd,
    act,
    slope,
    cast_even,
    cast_odd,
    fgrad_even,
    fgrad_odd,
    carry,
    carry_lat,
    lat_lines,
    taps,
    acc_one,
    acc_one_next,
    acc_two,
    acc_two_next,
):
    rows = own_source.shape[0]
    span = targets.shape[2]
    blocks = span // LANES
    lat_count = lax.axis_size("lat")
    own = blocks // lax.axis_size("mem")
    total_rows = rows * lat_count
    grid_rows = 4 * rows
    grid_total = grid_rows * lat_count
    lat_pos = lax.axis_index("lat")
    mem_pos = lax.axis_index("mem")
    wide = half + 2
    front = half + 1
    chan0, chan1, chan2 = chans
    f32, bf16 = jnp.float32, jnp.bfloat16

    def block_of(part, t):
        return window_block(mem_pos, own, half, blocks, part, t)

    pad_rows = grid_rows + 8
    grid_row = iota((pad_rows, LANES), 0)
    grid_row = jnp.where(grid_row < grid_rows, grid_row, grid_row - (grid_rows + 4)) + lat_pos * grid_rows
    latitude = math.pi / 2 - math.pi * (grid_row.astype(f32) + 0.5) / grid_total
    channels = lane_table(channel_weight, chan2)
    cosine = jnp.where(grid_row >= 0, jnp.cos(latitude), 0.0)
    base_rows = cosine * (jnp.tile(channels, (pad_rows // 8, 1)) * (1.0 / (MEM * (MEM - 1))))

    words[...] = jnp.zeros(words.shape, jnp.int32)
    words[:, : land.shape[1]] = land[...]
    for t in range(wide):
        for part in range(2):
            block = block_of(part, t)
            off = pl.multiple_of(block * LANES, LANES)
            slot = t * 2 + part
            edge = above[slot].astype(f32)
            lat_rows[slot, 0:1] = edge[0:1]
            lat_rows[slot, 1:2] = below[:, slot * LANES : (slot + 1) * LANES].astype(f32)
            if t < front:
                tgt_rows[slot, 0:grid_rows] = targets[0, :, pl.ds(off, LANES)].astype(f32)
                tgt_rows[slot, grid_rows:] = edge
                mask = jnp.concatenate([land_of(words[...], block, chan2), pltpu.roll(edge, 5, 0)], axis=0)
                weight_rows[slot] = base_rows + base_rows * mask

    source[rows + 2 :] = jnp.zeros((2,) + source.shape[1:], bf16)
    source[:, wide] = jnp.zeros((source.shape[0],) + source.shape[2:], bf16)
    fgrad_even[:, 0] = jnp.zeros((4,) + fgrad_even.shape[2:], bf16)
    fgrad_odd[...] = jnp.zeros(fgrad_odd.shape, bf16)
    carry[...] = jnp.zeros(carry.shape, f32)
    carry_lat[...] = jnp.zeros(carry_lat.shape, f32)
    for acc in (acc_one, acc_one_next, acc_two, acc_two_next):
        acc[...] = jnp.zeros(acc.shape, f32)

    def line(slot, i):
        return spread_line(lat_rows, slot, i)

    def store(i, t, value):
        source[i * (rows + 1), t] = value

    def edge_source(i, _):
        row = lat_pos * rows - 1 + i * (rows + 1)
        make_source(i, row, total_rows, span, own, half, seeds, scale, chan0, line, store)
        return 0

    lax.fori_loop(0, 2, edge_source, 0)
    source[1 : rows + 1, 0:wide] = own_source[...]

    def operand(ref, i, start, count):
        def piece(r, at):
            return ref[r, pl.ds(at, count)].reshape(count * 16, LANES)

        return jnp.concatenate(
            [piece(i, start), piece(i + 1, start), piece(i, start + 1), piece(i + 1, start + 1)], axis=1
        )

    def first_product(i, pre):
        pre[...] = jnp.dot(operand(source, i, 0, wide), band_one[...], preferred_element_type=f32)

    def first_gelu(i, pre):
        for t in range(wide):
            for sub in range(2):
                x = pre[t * 16 : (t + 1) * 16, sub * LANES : (sub + 1) * LANES]
                square = x * x
                th = jnp.tanh(x * (GELU_A + (GELU_A * GELU_B) * square))
                plus = 0.5 + 0.5 * th
                act[2 * i + sub, t] = (x * plus).astype(bf16)
                if t < front:
                    d = plus + (x * plus) * (1.0 - th) * (GELU_A + (3.0 * GELU_A * GELU_B) * square)
                    if t == half:
                        d = jnp.where(iota((16, LANES), 0) < 8, d, 0.0)
                    slope[2 * i + sub, t] = d

    def first_segment(m, _):
        first_product(2 * m + 1, pre_odd)
        first_gelu(2 * m, pre_even)
        first_product(2 * m + 2, pre_even)
        first_gelu(2 * m + 1, pre_odd)
        return 0

    first_product(0, pre_even)
    lax.fori_loop(0, rows // 2 + 1, first_segment, 0)

    members = front * 16
    owner = iota((48, members), 0)
    group = iota((48, members), 1) // 8
    place = (group % 2) * half + group // 2
    real = (group // 2 > 0) & (place - 1 < own)
    pick_own = (real & (place - 1 == owner)).astype(bf16)
    pick_prev = ((group // 2 < half) & (place == owner)).astype(bf16)
    pick = jnp.concatenate([pick_own, pick_prev], axis=0)

    def second_product(n, cast):
        taken = jnp.concatenate([operand(act, 2 * n + k, 0, front) for k in range(2)], axis=0)
        out = jnp.dot(taken, band_two[...], preferred_element_type=f32).astype(bf16)
        for k in range(2):
            for sub in range(2):
                part = out[k * members : (k + 1) * members, sub * LANES : (sub + 1) * LANES]
                cast[2 * k + sub] = part.reshape(front, 16, LANES)

    def loss_gradient(n, cast, fgrad):
        first = jnp.where(n >= 1, 4 * (n - 1), grid_rows)
        for line in range(4):
            for t in range(front):
                both = cast[line, t].astype(f32)
                parts = []
                for part in range(2):
                    if t == half and part == 1:
                        parts.append(jnp.zeros((8, LANES), f32))
                        continue
                    f = both[part * 8 : part * 8 + 8]
                    d = f - spread_line(tgt_rows, t * 2 + part, first + line)
                    goal = d * lax.rsqrt(d * d + SMOOTH)
                    gs = []
                    for k in range(1, 5):
                        d = f - pltpu.roll(f, k, 0)
                        gs.append(d * lax.rsqrt(d * d + SMOOTH))
                    back = gs[2]
                    for k in (1, 0):
                        back = gs[k] + pltpu.roll(back, MEM - 1, 0)
                    back = pltpu.roll(back, MEM - 1, 0)
                    spread = (gs[0] + gs[1]) + (gs[2] + gs[3]) - back
                    weight = spread_line(weight_rows, t * 2 + part, first + line)
                    parts.append(weight * ((MEM - 1.0) * goal - spread))
                fgrad[line, t + 1] = jnp.concatenate(parts, axis=0).astype(bf16)

    def pull_back(n, fgrad):
        at = jnp.maximum(n, 0)
        keep = jnp.where(n >= 1, 1.0, 0.0).astype(bf16)

        def flat(line, start, count):
            return fgrad[line, start : start + count].reshape(count * 16, LANES)

        def add_taps(g, x, acc, acc_next, chan_out):
            turned = g.T
            acc[...] += jnp.dot(turned, x[:, :256], preferred_element_type=f32)
            last = [turned[k * LANES - chan_out : k * LANES] for k in (1, 2)]
            last = jnp.concatenate(last, axis=0)
            acc_next[...] += jnp.dot(last, x[:, 256:], preferred_element_type=f32)

        g = [
            jnp.concatenate(
                [flat(2 * k, 1, front), flat(2 * k + 1, 1, front), flat(2 * k, 0, front), flat(2 * k + 1, 0, front)],
                axis=1,
            )
            for k in range(2)
        ]
        pulled = jnp.dot(jnp.concatenate(g, axis=0), back_two[...], preferred_element_type=f32)
        g = [jnp.concatenate([flat(2 * k, 2, half), flat(2 * k + 1, 2, half)], axis=1) for k in range(2)]
        x = [operand(act, 2 * at + k, 1, half) for k in range(2)]
        add_taps(jnp.concatenate(g, axis=0) * keep, jnp.concatenate(x, axis=0), acc_two, acc_two_next, chan2)
        grads = [
            pulled[:members, :LANES] + carry[...],
            pulled[members:, :LANES] + pulled[:members, LANES:],
        ]
        carry[...] = pulled[members:, LANES:]
        grads = [(grads[k] * slope[2 * at + k].reshape(members, LANES)).astype(bf16) for k in range(2)]
        grads = jnp.concatenate(grads, axis=1)
        z = jnp.dot(pick, grads, preferred_element_type=f32)
        z = jnp.concatenate([z[:48], z[48:]], axis=1)
        high = z.astype(bf16)
        z = jnp.concatenate([high, (z - high.astype(f32)).astype(bf16)], axis=0)
        z = jnp.dot(z, back_one[...], preferred_element_type=f32)
        z = z[:48] + z[48:]
        lat_lines[pl.ds(jnp.maximum(n - 1, 0), 48, stride=rows), :] = z[:, :LANES] + carry_lat[...]
        carry_lat[...] = z[:, LANES:]
        add_taps(grads[16:] * keep, operand(source, at, 1, half), acc_one, acc_one_next, chan1)

    def second_segment(m, _):
        second_product(2 * m + 1, cast_odd)
        loss_gradient(2 * m, cast_even, fgrad_even)
        pull_back(2 * m - 1, fgrad_odd)
        second_product(2 * m + 2, cast_even)
        loss_gradient(2 * m + 1, cast_odd, fgrad_odd)
        pull_back(2 * m, fgrad_even)
        return 0

    second_product(0, cast_even)
    lax.fori_loop(0, rows // 2, second_segment, 0)
    loss_gradient(rows, cast_even, fgrad_even)
    pull_back(rows - 1, fgrad_odd)
    pull_back(rows, fgrad_even)

    for t in range(own):
        out_lat[:, t * LANES : (t + 1) * LANES] = lat_lines[t * rows : (t + 1) * rows].astype(bf16)
    pack_taps(acc_one, acc_one_next, taps, 0, chan0, chan1, norm)
    pack_taps(acc_two, acc_two_next, taps, -(-9 // (LANES // chan0)) * chan1, chan1, chan2, norm)
    count = taps_keep.shape[0]
    odd = jnp.bitwise_and(lat_pos, 1)
    taps_keep[...] = taps[pl.ds(pl.multiple_of(odd * count, 8), count), :]
    taps_send[...] = taps[pl.ds(pl.multiple_of((1 - odd) * count, 8), count), :]


def swapped(array, axis, bit):
    return lax.ppermute(array, axis, [(i, i ^ bit) for i in range(lax.axis_size(axis))])


def total(array, axis, first, second):
    one, two, three = (swapped(array, axis, k) for k in (first, second, first ^ second))
    return (array + one) + (two + three)


def local(
    latent, member_seeds, noise_scale, kernel_one, kernel_two, targets, land_words, channel_weight
):
    sample_count, rows, span = latent.shape
    chan0, chan1, chan2 = kernel_one.shape[2], kernel_one.shape[3], kernel_two.shape[3]
    lat_count = lax.axis_size("lat")
    own = span // LANES // lax.axis_size("mem")
    half = (own + 1) // 2
    assert sample_count == 1 and member_seeds.shape[0] == MEM and rows % 2 == 0 and own % 2 == 1 and lax.axis_size("mem") == 4
    assert 4 * chan2 == 2 * chan1 == chan0 and chan0 == 64
    vmem = pl.BlockSpec(memory_space=pltpu.VMEM)
    smem = pl.BlockSpec(memory_space=pltpu.SMEM)
    f32, bf16 = jnp.float32, jnp.bfloat16
    wide, front = half + 2, half + 1
    params = pltpu.CompilerParams(vmem_limit_bytes=32 * 1024 * 1024)
    small = pltpu.CompilerParams(vmem_limit_bytes=8 * 1024 * 1024)
    kernel_one = kernel_one.transpose(0, 1, 3, 2)
    kernel_two = kernel_two.transpose(0, 1, 3, 2)
    down, up = pl.pallas_call(
        functools.partial(edge_kernel, half, chan2),
        grid=(1,),
        in_specs=[
            pl.BlockSpec((1, 8, span), lambda i: (0, 0, 0)),
            pl.BlockSpec((1, 8, span), lambda i: (0, rows // 2 - 1, 0)),
            pl.BlockSpec((8, land_words.shape[1]), lambda i: (rows // 2 - 1, 0)),
        ],
        out_specs=[
            pl.BlockSpec((2 * wide, 8, LANES), lambda i: (0, 0, 0)),
            pl.BlockSpec((1, 2 * wide * LANES), lambda i: (0, 0)),
        ],
        out_shape=[
            jax.ShapeDtypeStruct((2 * wide, 8, LANES), bf16),
            jax.ShapeDtypeStruct((1, 2 * wide * LANES), bf16),
        ],
        scratch_shapes=[pltpu.VMEM((8, LANES), jnp.int32)],
        compiler_params=pltpu.CompilerParams(vmem_limit_bytes=56 * 1024 * 1024),
        name="edges",
    )(latent, targets, land_words)
    above = shifted(down, "lat", 1)
    below = shifted(up, "lat", -1)
    band = jax.ShapeDtypeStruct((512, 256), bf16)
    source, *bands = pl.pallas_call(
        functools.partial(prepare_kernel, half),
        in_specs=[smem] * 2 + [vmem] * 3,
        out_specs=[vmem] * 5,
        out_shape=[jax.ShapeDtypeStruct((rows, wide, 16, LANES), bf16)] + [band] * 4,
        scratch_shapes=[pltpu.VMEM((2 * wide, rows, LANES), f32)],
        compiler_params=small,
        cost_estimate=pl.CostEstimate(flops=10**8, bytes_accessed=10**7, transcendentals=0),
        name="prepare",
    )(member_seeds, noise_scale, latent, kernel_one, kernel_two)
    norm = 1.0 / math.sqrt(sample_count * 4 * rows * lat_count * targets.shape[2])
    tap_rows = 5 * chan1 + 3 * chan2
    lat_grad, taps, taps_send = pl.pallas_call(
        functools.partial(band_kernel, half, (chan0, chan1, chan2), norm),
        in_specs=[smem] * 3 + [vmem] * 9,
        out_specs=[vmem] * 3,
        out_shape=[
            jax.ShapeDtypeStruct((rows, own * LANES), bf16),
            jax.ShapeDtypeStruct((tap_rows // 2, LANES), f32),
            jax.ShapeDtypeStruct((tap_rows // 2, LANES), f32),
        ],
        scratch_shapes=[
            pltpu.VMEM((2 * wide, 8, LANES), f32),
            pltpu.VMEM((2 * front, 4 * rows + 8, LANES), f32),
            pltpu.VMEM((2 * front, 4 * rows + 8, LANES), f32),
            pltpu.VMEM((4 * rows, LANES), jnp.int32),
            pltpu.VMEM((rows + 4, wide + 1, 16, LANES), bf16),
            pltpu.VMEM((wide * 16, 2 * LANES), f32),
            pltpu.VMEM((wide * 16, 2 * LANES), f32),
            pltpu.VMEM((2 * rows + 4, wide, 16, LANES), bf16),
            pltpu.VMEM((2 * rows + 4, front, 16, LANES), f32),
            pltpu.VMEM((4, front, 16, LANES), bf16),
            pltpu.VMEM((4, front, 16, LANES), bf16),
            pltpu.VMEM((4, front + 1, 16, LANES), bf16),
            pltpu.VMEM((4, front + 1, 16, LANES), bf16),
            pltpu.VMEM((front * 16, LANES), f32),
            pltpu.VMEM((48, LANES), f32),
            pltpu.VMEM((48 * rows, LANES), f32),
            pltpu.VMEM((tap_rows, LANES), f32),
            pltpu.VMEM((256, 256), f32),
            pltpu.VMEM((2 * chan1, 256), f32),
            pltpu.VMEM((256, 256), f32),
            pltpu.VMEM((2 * chan2, 256), f32),
        ],
        compiler_params=params,
        name="band",
    )(
        member_seeds,
        noise_scale,
        channel_weight,
        source,
        above,
        below,
        targets,
        land_words,
        *bands,
    )
    taps = taps + swapped(taps_send, "lat", 1)
    taps = total(taps, "mem", 1, 2)
    one, two, three = (swapped(lat_grad, "mem", k) for k in range(1, 4))
    bits = [1 << k for k in range(1, lat_count.bit_length() - 1)]
    taps, one = lax.optimization_barrier((taps, one))
    for bit in bits:
        if bit == bits[-1]:
            taps, three = lax.optimization_barrier((taps, three))
        taps = taps + swapped(taps, "lat", bit)
    taps, two = lax.optimization_barrier((taps, two))
    other = swapped(taps, "lat", 1)
    latent_grad = pl.pallas_call(
        functools.partial(place_kernel, own),
        in_specs=[vmem] * 4,
        out_specs=vmem,
        out_shape=jax.ShapeDtypeStruct((1, rows, span), f32),
        compiler_params=small,
        name="place",
    )(lat_grad, one, two, three)
    one, two = pl.pallas_call(
        taps_kernel,
        in_specs=[vmem] * 2,
        out_specs=[vmem] * 2,
        out_shape=[
            jax.ShapeDtypeStruct(kernel_one.shape, f32),
            jax.ShapeDtypeStruct(kernel_two.shape, f32),
        ],
        scratch_shapes=[pltpu.VMEM((tap_rows, LANES), f32)],
        compiler_params=small,
        name="taps",
    )(taps, other)
    return (latent_grad, one.transpose(0, 1, 3, 2), two.transpose(0, 1, 3, 2))


def solution(mesh):
    in_specs = (P(None, "lat", None), P(), P(), P(), P(), P(None, "lat", None), P("lat", None), P())
    out_specs = (P(None, "lat", None), P(), P())
    return jax.shard_map(local, mesh=mesh, in_specs=in_specs, out_specs=out_specs, check_vma=False)
```

```python
import functools
import math

import jax
import jax.numpy as jnp
from jax import lax
from jax.experimental import pallas as pl
from jax.experimental.pallas import tpu as pltpu
from jax.sharding import PartitionSpec as P

SMOOTH = 0.01
HASH_CELL = 1103515245
HASH_SEED = 747796405
HASH_MIX = 277803737
LANES = 128
MEM = 8
GELU_A = math.sqrt(2.0 / math.pi)
GELU_B = 0.044715


def shifted(array, axis, by):
    peers = lax.axis_size(axis)
    pairs = [(i, i + by) for i in range(peers) if 0 <= i + by < peers]
    return lax.ppermute(array, axis, pairs)


def iota(shape, axis):
    return lax.broadcasted_iota(jnp.int32, shape, axis)


def lane_table(ref, count):
    lane = iota((8, LANES), 1) % count
    total = jnp.zeros((8, LANES), jnp.float32)
    for k in range(count):
        total = jnp.where(lane == k, ref[k], total)
    return total


def build_band(kernel_ref, band_ref):
    chan_out, chan_in = kernel_ref.shape[2], kernel_ref.shape[3]
    cells = LANES // chan_in
    repeat = (iota((chan_out, LANES), 1) % chan_out == iota((chan_out, LANES), 0)).astype(jnp.bfloat16)
    wide = {}
    for a in range(3):
        for b in range(3):
            wide[a, b] = lax.dot_general(
                kernel_ref[a, b], repeat, (((0,), (0,)), ((), ())), preferred_element_type=jnp.float32
            )
    column = iota((chan_in, LANES), 1) // chan_out
    zero = jnp.zeros((chan_in, LANES), jnp.float32)
    for block in range(2):
        for row in range(2):
            for cell in range(cells):
                at = block * 256 + row * LANES + cell * chan_in
                for sub in range(2):
                    a = sub - 2 * row + 1
                    part = zero
                    for q in range(2 * cells):
                        b = q - 2 * (cell + block * cells) + 1
                        if 0 <= a <= 2 and 0 <= b <= 2:
                            part = jnp.where(column == q, wide[a, b], part)
                    band_ref[at : at + chan_in, sub * LANES : (sub + 1) * LANES] = part.astype(jnp.bfloat16)


def build_back(kernel_ref, back_ref):
    chan_out, chan_in = kernel_ref.shape[2], kernel_ref.shape[3]
    cells = LANES // chan_in
    repeat = (iota((chan_in, LANES), 1) % chan_in == iota((chan_in, LANES), 0)).astype(jnp.bfloat16)
    flat = kernel_ref[...].reshape(9 * chan_out, chan_in)
    wide = jnp.dot(flat, repeat, preferred_element_type=jnp.float32)
    column = iota((chan_out, LANES), 1) // chan_in
    zero = jnp.zeros((chan_out, LANES), jnp.float32)
    for block in range(2):
        for sub in range(2):
            for q in range(2 * cells):
                at = block * 256 + sub * LANES + q * chan_out
                for row in range(2):
                    a = sub - 2 * row + 1
                    part = zero
                    for cell in range(cells):
                        b = q - 2 * (cell + block * cells) + 1
                        if 0 <= a <= 2 and 0 <= b <= 2:
                            tap = (3 * a + b) * chan_out
                            part = jnp.where(column == cell, wide[tap : tap + chan_out], part)
                    back_ref[at : at + chan_out, row * LANES : (row + 1) * LANES] = part.astype(jnp.bfloat16)


def pack_taps(acc_ref, next_ref, out_ref, first, chan_in, chan_out, norm):
    cells = LANES // chan_in
    group = iota((chan_out, LANES), 1) // chan_in
    packed = None
    for k in range(9):
        a, b = divmod(k, 3)
        row, sub = ((1, 1), (0, 0), (0, 1))[a]
        slot = k % cells
        part = None
        for reach in range(cells + 1):
            q = 2 * reach + b - 1
            if 0 <= q < 2 * cells:
                block, cell = reach // cells, reach % cells
                lines = sub * LANES + q * chan_out if block == 0 else sub * chan_out
                ref = acc_ref if block == 0 else next_ref
                piece = ref[lines : lines + chan_out, row * LANES : (row + 1) * LANES]
                turn = (slot - cell) % cells * chan_in
                piece = pltpu.roll(piece, turn, 1) if turn else piece
                part = piece if part is None else part + piece
        packed = part if slot == 0 else jnp.where(group == slot, part, packed)
        if slot == cells - 1 or k == 8:
            at = first + k // cells * chan_out
            out_ref[at : at + chan_out, :] = packed * norm


def spread_line(ref, slot, at):
    return jnp.broadcast_to(ref[slot, pl.ds(at, 1), :], (8, LANES))


def window_block(mem_pos, own, half, blocks, part, t):
    at = mem_pos * own + part * half + t + (blocks - 1)
    at = jnp.where(at >= blocks, at - blocks, at)
    return jnp.where(at >= blocks, at - blocks, at)


def land_of(words, block, chan):
    cell = block * (LANES // chan) + iota(words.shape, 1) // chan
    word = jnp.right_shift(cell * 2185, 16)
    picked = jnp.take_along_axis(words, word, axis=1, mode="promise_in_bounds")
    return jnp.bitwise_and(jnp.right_shift(picked, cell - 30 * word), 1).astype(jnp.float32)


def edge_kernel(
    half,
    chan,
    latent_hbm,
    targets_hbm,
    land_hbm,
    down,
    up,
    latent,
    targets,
    land,
    words,
    sems,
):
    rows = latent.shape[1]
    blocks = latent.shape[2] // LANES
    edge = pl.ds(targets_hbm.shape[1] - 8, 8)
    copies = [
        pltpu.make_async_copy(latent_hbm, latent, sems.at[0]),
        pltpu.make_async_copy(targets_hbm.at[:, edge], targets, sems.at[1]),
        pltpu.make_async_copy(land_hbm.at[edge], land, sems.at[2]),
    ]
    for copy in copies:
        copy.start()
    for copy in copies:
        copy.wait()
    own = blocks // lax.axis_size("mem")
    mem_pos = lax.axis_index("mem")
    words[...] = jnp.zeros(words.shape, jnp.int32)
    words[:, : land.shape[1]] = land[...]
    line = iota((8, LANES), 0)
    for t in range(half + 2):
        for part in range(2):
            block = window_block(mem_pos, own, half, blocks, part, t)
            off = pl.multiple_of(block * LANES, LANES)
            slot = t * 2 + part
            cells = latent[0, :, pl.ds(off, LANES)].astype(jnp.float32)
            aims = targets[0, :, pl.ds(off, LANES)].astype(jnp.float32)
            mask = land_of(words[...], block, chan)
            pack = pltpu.roll(cells, 1, 0)
            pack = jnp.where((line >= 1) & (line <= 3), pltpu.roll(aims, 4, 0), pack)
            pack = jnp.where((line >= 4) & (line <= 6), pltpu.roll(mask, 7, 0), pack)
            down[slot] = pack.astype(jnp.bfloat16)
            up[:, slot * LANES : (slot + 1) * LANES] = cells[0:1].astype(jnp.bfloat16)


def place_kernel(own, part0, part1, part2, part3, latent_grad):
    mem_pos = lax.axis_index("mem")
    for k, part in enumerate((part0, part1, part2, part3)):
        off = pl.multiple_of(jnp.bitwise_xor(mem_pos, k) * own * LANES, LANES)
        latent_grad[0, :, pl.ds(off, own * LANES)] = part[...].astype(jnp.float32)


def taps_kernel(mine, other, grad_one, grad_two, taps):
    count = mine.shape[0]
    odd = jnp.bitwise_and(lax.axis_index("lat"), 1)
    taps[pl.ds(pl.multiple_of(odd * count, 8), count), :] = mine[...]
    taps[pl.ds(pl.multiple_of((1 - odd) * count, 8), count), :] = other[...]
    first = 0
    for out in (grad_one, grad_two):
        chan_out, chan_in = out.shape[2], out.shape[3]
        cells = LANES // chan_in
        for k in range(9):
            at = first + k // cells * chan_out
            block = taps[at : at + chan_out, :]
            turn = (-(k % cells)) % cells * chan_in
            block = pltpu.roll(block, turn, 1) if turn else block
            out[k // 3, k % 3] = block[:, :chan_in]
        first += -(-9 // cells) * chan_out


def make_source(i, row, total_rows, span, own, half, seeds, scale, chan, line, store):
    blocks = span // LANES
    mem_pos = lax.axis_index("mem")
    sublane = iota((8, LANES), 0)
    seed_table = jnp.zeros((8, LANES), jnp.int32)
    for m in range(MEM):
        seed_table = jnp.where(sublane == m, seeds[m], seed_table)
    hash_table = iota((8, LANES), 1) * HASH_CELL + seed_table * HASH_SEED
    scale_table = lane_table(scale, chan)
    inside = jnp.where(row < total_rows, 1.0, 0.0).astype(jnp.float32)
    for t in range(half + 2):
        parts = []
        for part in range(2):
            first = (row * span + window_block(mem_pos, own, half, blocks, part, t) * LANES) * HASH_CELL
            h = hash_table + first
            h = jnp.bitwise_xor(h, jnp.right_shift(h, 15))
            h = h * HASH_MIX
            h = jnp.bitwise_xor(h, jnp.right_shift(h, 13))
            noise = jnp.bitwise_and(h, 65535).astype(jnp.float32) * (1.0 / 65536.0) - 0.5
            noise = noise * 3.4641016
            parts.append((line(t * 2 + part, i) + noise * scale_table) * inside)
        store(i, t, jnp.concatenate(parts, axis=0).astype(jnp.bfloat16))


def prepare_kernel(half, chan, seeds, scale, latent, source, lines):
    rows, span = latent.shape[1], latent.shape[2]
    blocks = span // LANES
    own = blocks // lax.axis_size("mem")
    total_rows = rows * lax.axis_size("lat")
    lat_pos, mem_pos = lax.axis_index("lat"), lax.axis_index("mem")
    for t in range(half + 2):
        for part in range(2):
            off = pl.multiple_of(window_block(mem_pos, own, half, blocks, part, t) * LANES, LANES)
            lines[t * 2 + part] = latent[0, :, pl.ds(off, LANES)].astype(jnp.float32)

    def line(slot, i):
        return spread_line(lines, slot, i)

    def store(i, t, value):
        source[i, t] = value

    def step(i, _):
        make_source(
            i, lat_pos * rows + i, total_rows, span, own, half, seeds, scale, chan, line, store
        )
        return 0

    lax.fori_loop(0, rows, step, 0)


def bands_kernel(kernel_one, kernel_two, band_one, band_two, back_one, back_two):
    build_band(kernel_one, band_one)
    build_band(kernel_two, band_two)
    build_back(kernel_one, back_one)
    build_back(kernel_two, back_two)


def band_kernel(
    half,
    chans,
    norm,
    seeds,
    scale,
    channel_weight,
    own_source,
    above,
    below,
    targets,
    land,
    band_one,
    band_two,
    back_one,
    back_two,
    out_lat,
    taps_keep,
    taps_send,
    lat_rows,
    tgt_rows,
    weight_rows,
    words,
    source,
    pre_even,
    pre_odd,
    act,
    slope,
    cast_even,
    cast_odd,
    fgrad_even,
    fgrad_odd,
    carry,
    carry_lat,
    lat_lines,
    taps,
    acc_one,
    acc_one_next,
    acc_two,
    acc_two_next,
):
    rows = own_source.shape[0]
    span = targets.shape[2]
    blocks = span // LANES
    lat_count = lax.axis_size("lat")
    own = blocks // lax.axis_size("mem")
    total_rows = rows * lat_count
    grid_rows = 4 * rows
    grid_total = grid_rows * lat_count
    lat_pos = lax.axis_index("lat")
    mem_pos = lax.axis_index("mem")
    wide = half + 2
    front = half + 1
    chan0, chan1, chan2 = chans
    f32, bf16 = jnp.float32, jnp.bfloat16

    def block_of(part, t):
        return window_block(mem_pos, own, half, blocks, part, t)

    pad_rows = grid_rows + 8
    grid_row = iota((pad_rows, LANES), 0)
    grid_row = jnp.where(grid_row < grid_rows, grid_row, grid_row - (grid_rows + 4)) + lat_pos * grid_rows
    latitude = math.pi / 2 - math.pi * (grid_row.astype(f32) + 0.5) / grid_total
    channels = lane_table(channel_weight, chan2)
    cosine = jnp.where(grid_row >= 0, jnp.cos(latitude), 0.0)
    base_rows = cosine * (jnp.tile(channels, (pad_rows // 8, 1)) * (1.0 / (MEM * (MEM - 1))))

    words[...] = jnp.zeros(words.shape, jnp.int32)
    words[:, : land.shape[1]] = land[...]
    for t in range(wide):
        for part in range(2):
            block = block_of(part, t)
            off = pl.multiple_of(block * LANES, LANES)
            slot = t * 2 + part
            edge = above[slot].astype(f32)
            lat_rows[slot, 0:1] = edge[0:1]
            lat_rows[slot, 1:2] = below[:, slot * LANES : (slot + 1) * LANES].astype(f32)
            if t < front:
                tgt_rows[slot, 0:grid_rows] = targets[0, :, pl.ds(off, LANES)].astype(f32)
                tgt_rows[slot, grid_rows:] = edge
                mask = jnp.concatenate([land_of(words[...], block, chan2), pltpu.roll(edge, 5, 0)], axis=0)
                weight_rows[slot] = base_rows + base_rows * mask

    source[rows + 2 :] = jnp.zeros((2,) + source.shape[1:], bf16)
    source[:, wide] = jnp.zeros((source.shape[0],) + source.shape[2:], bf16)
    fgrad_even[:, 0] = jnp.zeros((4,) + fgrad_even.shape[2:], bf16)
    fgrad_odd[...] = jnp.zeros(fgrad_odd.shape, bf16)
    carry[...] = jnp.zeros(carry.shape, f32)
    carry_lat[...] = jnp.zeros(carry_lat.shape, f32)
    for acc in (acc_one, acc_one_next, acc_two, acc_two_next):
        acc[...] = jnp.zeros(acc.shape, f32)

    def line(slot, i):
        return spread_line(lat_rows, slot, i)

    def store(i, t, value):
        source[i * (rows + 1), t] = value

    def edge_source(i, _):
        row = lat_pos * rows - 1 + i * (rows + 1)
        make_source(i, row, total_rows, span, own, half, seeds, scale, chan0, line, store)
        return 0

    lax.fori_loop(0, 2, edge_source, 0)
    source[1 : rows + 1, 0:wide] = own_source[...]

    def operand(ref, i, start, count):
        def piece(r, at):
            return ref[r, pl.ds(at, count)].reshape(count * 16, LANES)

        return jnp.concatenate(
            [piece(i, start), piece(i + 1, start), piece(i, start + 1), piece(i + 1, start + 1)], axis=1
        )

    def first_product(i, pre):
        pre[...] = jnp.dot(operand(source, i, 0, wide), band_one[...], preferred_element_type=f32)

    def first_gelu(i, pre):
        for t in range(wide):
            for sub in range(2):
                x = pre[t * 16 : (t + 1) * 16, sub * LANES : (sub + 1) * LANES]
                square = x * x
                th = jnp.tanh(x * (GELU_A + (GELU_A * GELU_B) * square))
                plus = 0.5 + 0.5 * th
                act[2 * i + sub, t] = (x * plus).astype(bf16)
                if t < front:
                    d = plus + (x * plus) * (1.0 - th) * (GELU_A + (3.0 * GELU_A * GELU_B) * square)
                    if t == half:
                        d = jnp.where(iota((16, LANES), 0) < 8, d, 0.0)
                    slope[2 * i + sub, t] = d

    def first_segment(m, _):
        first_product(2 * m + 1, pre_odd)
        first_gelu(2 * m, pre_even)
        first_product(2 * m + 2, pre_even)
        first_gelu(2 * m + 1, pre_odd)
        return 0

    first_product(0, pre_even)
    lax.fori_loop(0, rows // 2 + 1, first_segment, 0)

    members = front * 16
    owner = iota((48, members), 0)
    group = iota((48, members), 1) // 8
    place = (group % 2) * half + group // 2
    real = (group // 2 > 0) & (place - 1 < own)
    pick_own = (real & (place - 1 == owner)).astype(bf16)
    pick_prev = ((group // 2 < half) & (place == owner)).astype(bf16)
    pick = jnp.concatenate([pick_own, pick_prev], axis=0)

    def second_product(n, cast):
        taken = jnp.concatenate([operand(act, 2 * n + k, 0, front) for k in range(2)], axis=0)
        out = jnp.dot(taken, band_two[...], preferred_element_type=f32).astype(bf16)
        for k in range(2):
            for sub in range(2):
                part = out[k * members : (k + 1) * members, sub * LANES : (sub + 1) * LANES]
                cast[2 * k + sub] = part.reshape(front, 16, LANES)

    def loss_gradient(n, cast, fgrad):
        first = jnp.where(n >= 1, 4 * (n - 1), grid_rows)
        for line in range(4):
            for t in range(front):
                both = cast[line, t].astype(f32)
                parts = []
                for part in range(2):
                    if t == half and part == 1:
                        parts.append(jnp.zeros((8, LANES), f32))
                        continue
                    f = both[part * 8 : part * 8 + 8]
                    d = f - spread_line(tgt_rows, t * 2 + part, first + line)
                    goal = d * lax.rsqrt(d * d + SMOOTH)
                    gs = []
                    for k in range(1, 5):
                        d = f - pltpu.roll(f, k, 0)
                        gs.append(d * lax.rsqrt(d * d + SMOOTH))
                    back = gs[2]
                    for k in (1, 0):
                        back = gs[k] + pltpu.roll(back, MEM - 1, 0)
                    back = pltpu.roll(back, MEM - 1, 0)
                    spread = (gs[0] + gs[1]) + (gs[2] + gs[3]) - back
                    weight = spread_line(weight_rows, t * 2 + part, first + line)
                    parts.append(weight * ((MEM - 1.0) * goal - spread))
                fgrad[line, t + 1] = jnp.concatenate(parts, axis=0).astype(bf16)

    def pull_back(n, fgrad):
        at = jnp.maximum(n, 0)
        keep = jnp.where(n >= 1, 1.0, 0.0).astype(bf16)

        def flat(line, start, count):
            return fgrad[line, start : start + count].reshape(count * 16, LANES)

        def add_taps(g, x, acc, acc_next, chan_out):
            turned = g.T
            acc[...] += jnp.dot(turned, x[:, :256], preferred_element_type=f32)
            last = [turned[k * LANES - chan_out : k * LANES] for k in (1, 2)]
            last = jnp.concatenate(last, axis=0)
            acc_next[...] += jnp.dot(last, x[:, 256:], preferred_element_type=f32)

        g = [
            jnp.concatenate(
                [flat(2 * k, 1, front), flat(2 * k + 1, 1, front), flat(2 * k, 0, front), flat(2 * k + 1, 0, front)],
                axis=1,
            )
            for k in range(2)
        ]
        pulled = jnp.dot(jnp.concatenate(g, axis=0), back_two[...], preferred_element_type=f32)
        g = [jnp.concatenate([flat(2 * k, 2, half), flat(2 * k + 1, 2, half)], axis=1) for k in range(2)]
        x = [operand(act, 2 * at + k, 1, half) for k in range(2)]
        add_taps(jnp.concatenate(g, axis=0) * keep, jnp.concatenate(x, axis=0), acc_two, acc_two_next, chan2)
        grads = [
            pulled[:members, :LANES] + carry[...],
            pulled[members:, :LANES] + pulled[:members, LANES:],
        ]
        carry[...] = pulled[members:, LANES:]
        grads = [(grads[k] * slope[2 * at + k].reshape(members, LANES)).astype(bf16) for k in range(2)]
        grads = jnp.concatenate(grads, axis=1)
        z = jnp.dot(pick, grads, preferred_element_type=f32)
        z = jnp.concatenate([z[:48], z[48:]], axis=1)
        high = z.astype(bf16)
        z = jnp.concatenate([high, (z - high.astype(f32)).astype(bf16)], axis=0)
        z = jnp.dot(z, back_one[...], preferred_element_type=f32)
        z = z[:48] + z[48:]
        lat_lines[pl.ds(jnp.maximum(n - 1, 0), 48, stride=rows), :] = z[:, :LANES] + carry_lat[...]
        carry_lat[...] = z[:, LANES:]
        add_taps(grads[16:] * keep, operand(source, at, 1, half), acc_one, acc_one_next, chan1)

    def second_segment(m, _):
        second_product(2 * m + 1, cast_odd)
        loss_gradient(2 * m, cast_even, fgrad_even)
        pull_back(2 * m - 1, fgrad_odd)
        second_product(2 * m + 2, cast_even)
        loss_gradient(2 * m + 1, cast_odd, fgrad_odd)
        pull_back(2 * m, fgrad_even)
        return 0

    second_product(0, cast_even)
    lax.fori_loop(0, rows // 2, second_segment, 0)
    loss_gradient(rows, cast_even, fgrad_even)
    pull_back(rows - 1, fgrad_odd)
    pull_back(rows, fgrad_even)

    for t in range(own):
        out_lat[:, t * LANES : (t + 1) * LANES] = lat_lines[t * rows : (t + 1) * rows].astype(bf16)
    pack_taps(acc_one, acc_one_next, taps, 0, chan0, chan1, norm)
    pack_taps(acc_two, acc_two_next, taps, -(-9 // (LANES // chan0)) * chan1, chan1, chan2, norm)
    count = taps_keep.shape[0]
    odd = jnp.bitwise_and(lat_pos, 1)
    taps_keep[...] = taps[pl.ds(pl.multiple_of(odd * count, 8), count), :]
    taps_send[...] = taps[pl.ds(pl.multiple_of((1 - odd) * count, 8), count), :]


def swapped(array, axis, bit):
    return lax.ppermute(array, axis, [(i, i ^ bit) for i in range(lax.axis_size(axis))])


def total(array, axis, first, second):
    one, two, three = (swapped(array, axis, k) for k in (first, second, first ^ second))
    return (array + one) + (two + three)


def local(
    latent, member_seeds, noise_scale, kernel_one, kernel_two, targets, land_words, channel_weight
):
    sample_count, rows, span = latent.shape
    chan0, chan1, chan2 = kernel_one.shape[2], kernel_one.shape[3], kernel_two.shape[3]
    lat_count = lax.axis_size("lat")
    own = span // LANES // lax.axis_size("mem")
    half = (own + 1) // 2
    assert sample_count == 1 and member_seeds.shape[0] == MEM and rows % 2 == 0 and own % 2 == 1 and lax.axis_size("mem") == 4
    assert 4 * chan2 == 2 * chan1 == chan0 and chan0 == 64
    vmem = pl.BlockSpec(memory_space=pltpu.VMEM)
    smem = pl.BlockSpec(memory_space=pltpu.SMEM)
    hbm = pl.BlockSpec(memory_space=pltpu.HBM)
    f32, bf16 = jnp.float32, jnp.bfloat16
    wide, front = half + 2, half + 1
    params = pltpu.CompilerParams(vmem_limit_bytes=32 * 1024 * 1024)
    small = pltpu.CompilerParams(vmem_limit_bytes=8 * 1024 * 1024)
    kernel_one = kernel_one.transpose(0, 1, 3, 2)
    kernel_two = kernel_two.transpose(0, 1, 3, 2)
    down, up = pl.pallas_call(
        functools.partial(edge_kernel, half, chan2),
        in_specs=[hbm] * 3,
        out_specs=[vmem] * 2,
        out_shape=[
            jax.ShapeDtypeStruct((2 * wide, 8, LANES), bf16),
            jax.ShapeDtypeStruct((1, 2 * wide * LANES), bf16),
        ],
        scratch_shapes=[
            pltpu.VMEM((1, 8, span), bf16),
            pltpu.VMEM((1, 8, span), bf16),
            pltpu.VMEM((8, land_words.shape[1]), jnp.int32),
            pltpu.VMEM((8, LANES), jnp.int32),
            pltpu.SemaphoreType.DMA((3,)),
        ],
        compiler_params=pltpu.CompilerParams(vmem_limit_bytes=56 * 1024 * 1024),
        name="edges",
    )(latent, targets, land_words)
    above = shifted(down, "lat", 1)
    below = shifted(up, "lat", -1)
    source = pl.pallas_call(
        functools.partial(prepare_kernel, half, chan0),
        in_specs=[smem] * 2 + [vmem],
        out_specs=vmem,
        out_shape=jax.ShapeDtypeStruct((rows, wide, 16, LANES), bf16),
        scratch_shapes=[pltpu.VMEM((2 * wide, rows, LANES), f32)],
        compiler_params=small,
        cost_estimate=pl.CostEstimate(flops=10**8, bytes_accessed=10**7, transcendentals=0),
        name="prepare",
    )(member_seeds, noise_scale, latent)
    bands = pl.pallas_call(
        bands_kernel,
        in_specs=[vmem] * 2,
        out_specs=[vmem] * 4,
        out_shape=[jax.ShapeDtypeStruct((512, 256), bf16)] * 4,
        compiler_params=small,
        cost_estimate=pl.CostEstimate(flops=10**8, bytes_accessed=10**7, transcendentals=0),
        name="bands",
    )(kernel_one, kernel_two)
    norm = 1.0 / math.sqrt(sample_count * 4 * rows * lat_count * targets.shape[2])
    tap_rows = 5 * chan1 + 3 * chan2
    lat_grad, taps, taps_send = pl.pallas_call(
        functools.partial(band_kernel, half, (chan0, chan1, chan2), norm),
        in_specs=[smem] * 3 + [vmem] * 9,
        out_specs=[vmem] * 3,
        out_shape=[
            jax.ShapeDtypeStruct((rows, own * LANES), bf16),
            jax.ShapeDtypeStruct((tap_rows // 2, LANES), f32),
            jax.ShapeDtypeStruct((tap_rows // 2, LANES), f32),
        ],
        scratch_shapes=[
            pltpu.VMEM((2 * wide, 8, LANES), f32),
            pltpu.VMEM((2 * front, 4 * rows + 8, LANES), f32),
            pltpu.VMEM((2 * front, 4 * rows + 8, LANES), f32),
            pltpu.VMEM((4 * rows, LANES), jnp.int32),
            pltpu.VMEM((rows + 4, wide + 1, 16, LANES), bf16),
            pltpu.VMEM((wide * 16, 2 * LANES), f32),
            pltpu.VMEM((wide * 16, 2 * LANES), f32),
            pltpu.VMEM((2 * rows + 4, wide, 16, LANES), bf16),
            pltpu.VMEM((2 * rows + 4, front, 16, LANES), f32),
            pltpu.VMEM((4, front, 16, LANES), bf16),
            pltpu.VMEM((4, front, 16, LANES), bf16),
            pltpu.VMEM((4, front + 1, 16, LANES), bf16),
            pltpu.VMEM((4, front + 1, 16, LANES), bf16),
            pltpu.VMEM((front * 16, LANES), f32),
            pltpu.VMEM((48, LANES), f32),
            pltpu.VMEM((48 * rows, LANES), f32),
            pltpu.VMEM((tap_rows, LANES), f32),
            pltpu.VMEM((256, 256), f32),
            pltpu.VMEM((2 * chan1, 256), f32),
            pltpu.VMEM((256, 256), f32),
            pltpu.VMEM((2 * chan2, 256), f32),
        ],
        compiler_params=params,
        name="band",
    )(
        member_seeds,
        noise_scale,
        channel_weight,
        source,
        above,
        below,
        targets,
        land_words,
        *bands,
    )
    taps = taps + swapped(taps_send, "lat", 1)
    taps = total(taps, "mem", 1, 2)
    one, two, three = (swapped(lat_grad, "mem", k) for k in range(1, 4))
    bits = [1 << k for k in range(1, lat_count.bit_length() - 1)]
    for bit in bits:
        if bit == bits[-1]:
            taps, three = lax.optimization_barrier((taps, three))
        taps = taps + swapped(taps, "lat", bit)
    taps, one, two = lax.optimization_barrier((taps, one, two))
    other = swapped(taps, "lat", 1)
    latent_grad = pl.pallas_call(
        functools.partial(place_kernel, own),
        in_specs=[vmem] * 4,
        out_specs=vmem,
        out_shape=jax.ShapeDtypeStruct((1, rows, span), f32),
        compiler_params=small,
        name="place",
    )(lat_grad, one, two, three)
    one, two = pl.pallas_call(
        taps_kernel,
        in_specs=[vmem] * 2,
        out_specs=[vmem] * 2,
        out_shape=[
            jax.ShapeDtypeStruct(kernel_one.shape, f32),
            jax.ShapeDtypeStruct(kernel_two.shape, f32),
        ],
        scratch_shapes=[pltpu.VMEM((tap_rows, LANES), f32)],
        compiler_params=small,
        name="taps",
    )(taps, other)
    return (latent_grad, one.transpose(0, 1, 3, 2), two.transpose(0, 1, 3, 2))


def solution(mesh):
    in_specs = (P(None, "lat", None), P(), P(), P(), P(), P(None, "lat", None), P("lat", None), P())
    out_specs = (P(None, "lat", None), P(), P())
    return jax.shard_map(local, mesh=mesh, in_specs=in_specs, out_specs=out_specs, check_vma=False)
```

```python
import functools
import math

import jax
import jax.numpy as jnp
from jax import lax
from jax.experimental import pallas as pl
from jax.experimental.pallas import tpu as pltpu
from jax.sharding import PartitionSpec as P

SMOOTH = 0.01
HASH_CELL = 1103515245
HASH_SEED = 747796405
HASH_MIX = 277803737
LANES = 128
MEM = 8
GELU_A = math.sqrt(2.0 / math.pi)
GELU_B = 0.044715


def shifted(array, axis, by):
    peers = lax.axis_size(axis)
    pairs = [(i, i + by) for i in range(peers) if 0 <= i + by < peers]
    return lax.ppermute(array, axis, pairs)


def iota(shape, axis):
    return lax.broadcasted_iota(jnp.int32, shape, axis)


def lane_table(ref, count):
    lane = iota((8, LANES), 1) % count
    total = jnp.zeros((8, LANES), jnp.float32)
    for k in range(count):
        total = jnp.where(lane == k, ref[k], total)
    return total


def build_band(kernel_ref, band_ref):
    chan_out, chan_in = kernel_ref.shape[2], kernel_ref.shape[3]
    cells = LANES // chan_in
    repeat = (iota((chan_out, LANES), 1) % chan_out == iota((chan_out, LANES), 0)).astype(jnp.bfloat16)
    wide = {}
    for a in range(3):
        for b in range(3):
            wide[a, b] = lax.dot_general(
                kernel_ref[a, b], repeat, (((0,), (0,)), ((), ())), preferred_element_type=jnp.float32
            )
    column = iota((chan_in, LANES), 1) // chan_out
    zero = jnp.zeros((chan_in, LANES), jnp.float32)
    for block in range(2):
        for row in range(2):
            for cell in range(cells):
                at = block * 256 + row * LANES + cell * chan_in
                for sub in range(2):
                    a = sub - 2 * row + 1
                    part = zero
                    for q in range(2 * cells):
                        b = q - 2 * (cell + block * cells) + 1
                        if 0 <= a <= 2 and 0 <= b <= 2:
                            part = jnp.where(column == q, wide[a, b], part)
                    band_ref[at : at + chan_in, sub * LANES : (sub + 1) * LANES] = part.astype(jnp.bfloat16)


def build_back(kernel_ref, back_ref):
    chan_out, chan_in = kernel_ref.shape[2], kernel_ref.shape[3]
    cells = LANES // chan_in
    repeat = (iota((chan_in, LANES), 1) % chan_in == iota((chan_in, LANES), 0)).astype(jnp.bfloat16)
    flat = kernel_ref[...].reshape(9 * chan_out, chan_in)
    wide = jnp.dot(flat, repeat, preferred_element_type=jnp.float32)
    column = iota((chan_out, LANES), 1) // chan_in
    zero = jnp.zeros((chan_out, LANES), jnp.float32)
    for block in range(2):
        for sub in range(2):
            for q in range(2 * cells):
                at = block * 256 + sub * LANES + q * chan_out
                for row in range(2):
                    a = sub - 2 * row + 1
                    part = zero
                    for cell in range(cells):
                        b = q - 2 * (cell + block * cells) + 1
                        if 0 <= a <= 2 and 0 <= b <= 2:
                            tap = (3 * a + b) * chan_out
                            part = jnp.where(column == cell, wide[tap : tap + chan_out], part)
                    back_ref[at : at + chan_out, row * LANES : (row + 1) * LANES] = part.astype(jnp.bfloat16)


def pack_taps(acc_ref, next_ref, out_ref, first, chan_in, chan_out, norm):
    cells = LANES // chan_in
    group = iota((chan_out, LANES), 1) // chan_in
    packed = None
    for k in range(9):
        a, b = divmod(k, 3)
        row, sub = ((1, 1), (0, 0), (0, 1))[a]
        slot = k % cells
        part = None
        for reach in range(cells + 1):
            q = 2 * reach + b - 1
            if 0 <= q < 2 * cells:
                block, cell = reach // cells, reach % cells
                lines = sub * LANES + q * chan_out if block == 0 else sub * chan_out
                ref = acc_ref if block == 0 else next_ref
                piece = ref[lines : lines + chan_out, row * LANES : (row + 1) * LANES]
                turn = (slot - cell) % cells * chan_in
                piece = pltpu.roll(piece, turn, 1) if turn else piece
                part = piece if part is None else part + piece
        packed = part if slot == 0 else jnp.where(group == slot, part, packed)
        if slot == cells - 1 or k == 8:
            at = first + k // cells * chan_out
            out_ref[at : at + chan_out, :] = packed * norm


def spread_line(ref, slot, at):
    return jnp.broadcast_to(ref[slot, pl.ds(at, 1), :], (8, LANES))


def window_block(mem_pos, own, half, blocks, part, t):
    at = mem_pos * own + part * half + t + (blocks - 1)
    at = jnp.where(at >= blocks, at - blocks, at)
    return jnp.where(at >= blocks, at - blocks, at)


def land_of(words, block, chan):
    cell = block * (LANES // chan) + iota(words.shape, 1) // chan
    word = jnp.right_shift(cell * 2185, 16)
    picked = jnp.take_along_axis(words, word, axis=1, mode="promise_in_bounds")
    return jnp.bitwise_and(jnp.right_shift(picked, cell - 30 * word), 1).astype(jnp.float32)


def edge_kernel(
    half,
    chan,
    latent_hbm,
    targets_hbm,
    land_hbm,
    down,
    up,
    latent,
    targets,
    land,
    words,
    sems,
):
    rows = latent.shape[1]
    blocks = latent.shape[2] // LANES
    edge = pl.ds(targets_hbm.shape[1] - 8, 8)
    copies = [
        pltpu.make_async_copy(latent_hbm, latent, sems.at[0]),
        pltpu.make_async_copy(targets_hbm.at[:, edge], targets, sems.at[1]),
        pltpu.make_async_copy(land_hbm.at[edge], land, sems.at[2]),
    ]
    for copy in copies:
        copy.start()
    for copy in copies:
        copy.wait()
    own = blocks // lax.axis_size("mem")
    mem_pos = lax.axis_index("mem")
    words[...] = jnp.zeros(words.shape, jnp.int32)
    words[:, : land.shape[1]] = land[...]
    line = iota((8, LANES), 0)
    for t in range(half + 2):
        for part in range(2):
            block = window_block(mem_pos, own, half, blocks, part, t)
            off = pl.multiple_of(block * LANES, LANES)
            slot = t * 2 + part
            cells = latent[0, :, pl.ds(off, LANES)].astype(jnp.float32)
            aims = targets[0, :, pl.ds(off, LANES)].astype(jnp.float32)
            mask = land_of(words[...], block, chan)
            pack = pltpu.roll(cells, 1, 0)
            pack = jnp.where((line >= 1) & (line <= 3), pltpu.roll(aims, 4, 0), pack)
            pack = jnp.where((line >= 4) & (line <= 6), pltpu.roll(mask, 7, 0), pack)
            down[slot] = pack.astype(jnp.bfloat16)
            up[:, slot * LANES : (slot + 1) * LANES] = cells[0:1].astype(jnp.bfloat16)


def place_kernel(own, part0, part1, part2, part3, latent_grad):
    mem_pos = lax.axis_index("mem")
    for k, part in enumerate((part0, part1, part2, part3)):
        off = pl.multiple_of(jnp.bitwise_xor(mem_pos, k) * own * LANES, LANES)
        latent_grad[0, :, pl.ds(off, own * LANES)] = part[...].astype(jnp.float32)


def taps_kernel(mine, other, grad_one, grad_two, taps):
    count = mine.shape[0]
    odd = jnp.bitwise_and(lax.axis_index("lat"), 1)
    taps[pl.ds(pl.multiple_of(odd * count, 8), count), :] = mine[...]
    taps[pl.ds(pl.multiple_of((1 - odd) * count, 8), count), :] = other[...]
    first = 0
    for out in (grad_one, grad_two):
        chan_out, chan_in = out.shape[2], out.shape[3]
        cells = LANES // chan_in
        for k in range(9):
            at = first + k // cells * chan_out
            block = taps[at : at + chan_out, :]
            turn = (-(k % cells)) % cells * chan_in
            block = pltpu.roll(block, turn, 1) if turn else block
            out[k // 3, k % 3] = block[:, :chan_in]
        first += -(-9 // cells) * chan_out


def make_source(i, row, total_rows, span, own, half, seeds, scale, chan, line, store):
    blocks = span // LANES
    mem_pos = lax.axis_index("mem")
    sublane = iota((8, LANES), 0)
    seed_table = jnp.zeros((8, LANES), jnp.int32)
    for m in range(MEM):
        seed_table = jnp.where(sublane == m, seeds[m], seed_table)
    hash_table = iota((8, LANES), 1) * HASH_CELL + seed_table * HASH_SEED
    scale_table = lane_table(scale, chan)
    inside = jnp.where(row < total_rows, 1.0, 0.0).astype(jnp.float32)
    for t in range(half + 2):
        parts = []
        for part in range(2):
            first = (row * span + window_block(mem_pos, own, half, blocks, part, t) * LANES) * HASH_CELL
            h = hash_table + first
            h = jnp.bitwise_xor(h, jnp.right_shift(h, 15))
            h = h * HASH_MIX
            h = jnp.bitwise_xor(h, jnp.right_shift(h, 13))
            noise = jnp.bitwise_and(h, 65535).astype(jnp.float32) * (1.0 / 65536.0) - 0.5
            noise = noise * 3.4641016
            parts.append((line(t * 2 + part, i) + noise * scale_table) * inside)
        store(i, t, jnp.concatenate(parts, axis=0).astype(jnp.bfloat16))


def weight_lines(grid_row, channel_weight, chan, grid_total):
    latitude = math.pi / 2 - math.pi * (grid_row.astype(jnp.float32) + 0.5) / grid_total
    cosine = jnp.where(grid_row >= 0, jnp.cos(latitude), 0.0)
    channels = jnp.tile(lane_table(channel_weight, chan), (grid_row.shape[0] // 8, 1))
    return cosine * (channels * (1.0 / (MEM * (MEM - 1))))


def prepare_kernel(
    half, chan, chan2, seeds, scale, channel_weight, latent, targets, land, source, aims, weights, lines, words
):
    rows, span = latent.shape[1], latent.shape[2]
    blocks = span // LANES
    own = blocks // lax.axis_size("mem")
    total_rows = rows * lax.axis_size("lat")
    lat_pos, mem_pos = lax.axis_index("lat"), lax.axis_index("mem")
    grid_row = iota((4 * rows, LANES), 0) + lat_pos * 4 * rows
    base = weight_lines(grid_row, channel_weight, chan2, 4 * total_rows)
    words[...] = jnp.zeros(words.shape, jnp.int32)
    words[:, : land.shape[1]] = land[...]
    for t in range(half + 2):
        for part in range(2):
            block = window_block(mem_pos, own, half, blocks, part, t)
            off = pl.multiple_of(block * LANES, LANES)
            slot = t * 2 + part
            lines[slot] = latent[0, :, pl.ds(off, LANES)].astype(jnp.float32)
            if t < half + 1:
                aims[slot] = targets[0, :, pl.ds(off, LANES)].astype(jnp.float32)
                weights[slot] = base + base * land_of(words[...], block, chan2)

    def line(slot, i):
        return spread_line(lines, slot, i)

    def store(i, t, value):
        source[i, t] = value

    def step(i, _):
        make_source(
            i, lat_pos * rows + i, total_rows, span, own, half, seeds, scale, chan, line, store
        )
        return 0

    lax.fori_loop(0, rows, step, 0)


def bands_kernel(kernel_one, kernel_two, band_one, band_two, back_one, back_two):
    build_band(kernel_one, band_one)
    build_band(kernel_two, band_two)
    build_back(kernel_one, back_one)
    build_back(kernel_two, back_two)


def take_turns(*parts):
    parts = list(parts)
    while parts:
        for part in tuple(parts):
            if next(part, part) is part:
                parts.remove(part)


def band_kernel(
    half,
    chans,
    span,
    norm,
    seeds,
    scale,
    channel_weight,
    own_source,
    aims,
    weights,
    above,
    below,
    band_one,
    band_two,
    back_one,
    back_two,
    out_lat,
    taps_keep,
    taps_send,
    lat_rows,
    edge_aims,
    edge_weights,
    source,
    pre_even,
    pre_odd,
    act,
    slope,
    cast_even,
    cast_odd,
    fgrad_even,
    fgrad_odd,
    carry,
    carry_lat,
    lat_lines,
    taps,
    acc_one,
    acc_one_next,
    acc_two,
    acc_two_next,
):
    rows = own_source.shape[0]
    blocks = span // LANES
    own = blocks // lax.axis_size("mem")
    total_rows = rows * lax.axis_size("lat")
    lat_pos = lax.axis_index("lat")
    wide = half + 2
    front = half + 1
    chan0, chan1, chan2 = chans
    f32, bf16 = jnp.float32, jnp.bfloat16

    grid_row = iota((8, LANES), 0) + (lat_pos * 4 * rows - 4)
    base = weight_lines(grid_row, channel_weight, chan2, 4 * total_rows)
    for slot in range(2 * wide):
        edge = above[slot].astype(f32)
        lat_rows[slot, 0:1] = edge[0:1]
        lat_rows[slot, 1:2] = below[:, slot * LANES : (slot + 1) * LANES].astype(f32)
        if slot < 2 * front:
            edge_aims[slot] = edge
            edge_weights[slot] = base + base * pltpu.roll(edge, 5, 0)

    source[rows + 2 :] = jnp.zeros((2,) + source.shape[1:], bf16)
    source[:, wide] = jnp.zeros((source.shape[0],) + source.shape[2:], bf16)
    fgrad_even[0] = jnp.zeros(fgrad_even.shape[1:], bf16)
    for fgrad in (fgrad_even, fgrad_odd):
        fgrad[:, 0] = jnp.zeros((4,) + fgrad.shape[2:], bf16)
    carry[...] = jnp.zeros(carry.shape, f32)
    carry_lat[...] = jnp.zeros(carry_lat.shape, f32)
    for acc in (acc_one, acc_one_next, acc_two, acc_two_next):
        acc[...] = jnp.zeros(acc.shape, f32)

    def line(slot, i):
        return spread_line(lat_rows, slot, i)

    def store(i, t, value):
        source[i * (rows + 1), t] = value

    def edge_source(i, _):
        row = lat_pos * rows - 1 + i * (rows + 1)
        make_source(i, row, total_rows, span, own, half, seeds, scale, chan0, line, store)
        return 0

    lax.fori_loop(0, 2, edge_source, 0)
    source[1 : rows + 1, 0:wide] = own_source[...]

    def operand(ref, i, start, count):
        def piece(r, at):
            return ref[r, pl.ds(at, count)].reshape(count * 16, LANES)

        return jnp.concatenate(
            [piece(i, start), piece(i + 1, start), piece(i, start + 1), piece(i + 1, start + 1)], axis=1
        )

    def first_product(i, pre):
        pre[...] = jnp.dot(operand(source, i, 0, wide), band_one[...], preferred_element_type=f32)

    def first_gelu(i, pre):
        for t in range(wide):
            for sub in range(2):
                x = pre[t * 16 : (t + 1) * 16, sub * LANES : (sub + 1) * LANES]
                square = x * x
                th = jnp.tanh(x * (GELU_A + (GELU_A * GELU_B) * square))
                plus = 0.5 + 0.5 * th
                act[2 * i + sub, t] = (x * plus).astype(bf16)
                if t < front:
                    d = plus + (x * plus) * (1.0 - th) * (GELU_A + (3.0 * GELU_A * GELU_B) * square)
                    if t == half:
                        d = jnp.where(iota((16, LANES), 0) < 8, d, 0.0)
                    slope[2 * i + sub, t] = d

    def first_segment(m, _):
        first_product(2 * m + 1, pre_odd)
        first_gelu(2 * m, pre_even)
        first_product(2 * m + 2, pre_even)
        first_gelu(2 * m + 1, pre_odd)
        return 0

    first_product(0, pre_even)
    lax.fori_loop(0, rows // 2 + 1, first_segment, 0)

    members = front * 16
    owner = iota((48, members), 0)
    group = iota((48, members), 1) // 8
    place = (group % 2) * half + group // 2
    real = (group // 2 > 0) & (place - 1 < own)
    pick_own = (real & (place - 1 == owner)).astype(bf16)
    pick_prev = ((group // 2 < half) & (place == owner)).astype(bf16)
    pick = jnp.concatenate([pick_own, pick_prev], axis=0)

    def second_product(n, cast):
        for k in range(2):
            out = jnp.dot(operand(act, 2 * n + k, 0, front), band_two[...], preferred_element_type=f32).astype(bf16)
            for sub in range(2):
                cast[2 * k + sub] = out[:, sub * LANES : (sub + 1) * LANES].reshape(front, 16, LANES)
            yield

    def loss_gradient(cast, fgrad, aim_ref, weight_ref, first, lines):
        for line in lines:
            for t in range(front):
                both = cast[line, t].astype(f32)
                parts = []
                for part in range(2):
                    if t == half and part == 1:
                        parts.append(jnp.zeros((8, LANES), f32))
                        continue
                    f = both[part * 8 : part * 8 + 8]
                    d = f - spread_line(aim_ref, t * 2 + part, first + line)
                    goal = d * lax.rsqrt(d * d + SMOOTH)
                    gs = []
                    for k in range(1, 5):
                        d = f - pltpu.roll(f, k, 0)
                        gs.append(d * lax.rsqrt(d * d + SMOOTH))
                    back = gs[2]
                    for k in (1, 0):
                        back = gs[k] + pltpu.roll(back, MEM - 1, 0)
                    back = pltpu.roll(back, MEM - 1, 0)
                    spread = (gs[0] + gs[1]) + (gs[2] + gs[3]) - back
                    weight = spread_line(weight_ref, t * 2 + part, first + line)
                    parts.append(weight * ((MEM - 1.0) * goal - spread))
                fgrad[line, t + 1] = jnp.concatenate(parts, axis=0).astype(bf16)
            yield

    def pull_back(n, fgrad):
        keep = jnp.where(n >= 1, 1.0, 0.0).astype(bf16)

        def flat(line, start, count):
            return fgrad[line, start : start + count].reshape(count * 16, LANES)

        def add_taps(g, x, acc, acc_next, chan_out):
            turned = g.T
            acc[...] += jnp.dot(turned, x[:, :256], preferred_element_type=f32)
            last = [turned[k * LANES - chan_out : k * LANES] for k in (1, 2)]
            last = jnp.concatenate(last, axis=0)
            acc_next[...] += jnp.dot(last, x[:, 256:], preferred_element_type=f32)

        grads = []
        for k in range(2):
            g = [flat(2 * k, 1, front), flat(2 * k + 1, 1, front), flat(2 * k, 0, front), flat(2 * k + 1, 0, front)]
            pulled = jnp.dot(jnp.concatenate(g, axis=1), back_two[...], preferred_element_type=f32)
            grad = pulled[:, :LANES] + carry[...]
            carry[...] = pulled[:, LANES:]
            grads.append((grad * slope[2 * n + k].reshape(members, LANES)).astype(bf16))
            yield
        grads = jnp.concatenate(grads, axis=1)
        g = [jnp.concatenate([flat(2 * k, 2, half), flat(2 * k + 1, 2, half)], axis=1) for k in range(2)]
        x = [operand(act, 2 * n + k, 1, half) for k in range(2)]
        add_taps(jnp.concatenate(g, axis=0) * keep, jnp.concatenate(x, axis=0), acc_two, acc_two_next, chan2)
        yield
        add_taps(grads[16:] * keep, operand(source, n, 1, half), acc_one, acc_one_next, chan1)
        yield
        z = jnp.dot(pick, grads, preferred_element_type=f32)
        z = jnp.concatenate([z[:48], z[48:]], axis=1)
        high = z.astype(bf16)
        z = jnp.concatenate([high, (z - high.astype(f32)).astype(bf16)], axis=0)
        z = jnp.dot(z, back_one[...], preferred_element_type=f32)
        z = z[:48] + z[48:]
        lat_lines[pl.ds(jnp.maximum(n - 1, 0), 48, stride=rows), :] = z[:, :LANES] + carry_lat[...]
        carry_lat[...] = z[:, LANES:]
        yield

    def own_gradient(n, cast, fgrad):
        return loss_gradient(cast, fgrad, aims, weights, 4 * (n - 1), range(4))

    def second_segment(m, _):
        take_turns(
            second_product(2 * m + 2, cast_even),
            own_gradient(2 * m + 1, cast_odd, fgrad_odd),
            pull_back(2 * m, fgrad_even),
        )
        take_turns(
            second_product(jnp.minimum(2 * m + 3, rows), cast_odd),
            own_gradient(2 * m + 2, cast_even, fgrad_even),
            pull_back(2 * m + 1, fgrad_odd),
        )
        return 0

    take_turns(second_product(0, cast_even))
    take_turns(
        second_product(1, cast_odd),
        loss_gradient(cast_even, fgrad_even, edge_aims, edge_weights, 0, range(1, 4)),
    )
    lax.fori_loop(0, rows // 2, second_segment, 0)
    take_turns(pull_back(rows, fgrad_even))

    for t in range(own):
        out_lat[:, t * LANES : (t + 1) * LANES] = lat_lines[t * rows : (t + 1) * rows].astype(bf16)
    pack_taps(acc_one, acc_one_next, taps, 0, chan0, chan1, norm)
    pack_taps(acc_two, acc_two_next, taps, -(-9 // (LANES // chan0)) * chan1, chan1, chan2, norm)
    count = taps_keep.shape[0]
    odd = jnp.bitwise_and(lat_pos, 1)
    taps_keep[...] = taps[pl.ds(pl.multiple_of(odd * count, 8), count), :]
    taps_send[...] = taps[pl.ds(pl.multiple_of((1 - odd) * count, 8), count), :]


def swapped(array, axis, bit):
    return lax.ppermute(array, axis, [(i, i ^ bit) for i in range(lax.axis_size(axis))])


def total(array, axis, first, second):
    one, two, three = (swapped(array, axis, k) for k in (first, second, first ^ second))
    return (array + one) + (two + three)


def local(
    latent, member_seeds, noise_scale, kernel_one, kernel_two, targets, land_words, channel_weight
):
    sample_count, rows, span = latent.shape
    chan0, chan1, chan2 = kernel_one.shape[2], kernel_one.shape[3], kernel_two.shape[3]
    lat_count = lax.axis_size("lat")
    own = span // LANES // lax.axis_size("mem")
    half = (own + 1) // 2
    assert sample_count == 1 and member_seeds.shape[0] == MEM and rows % 2 == 0 and own % 2 == 1 and lax.axis_size("mem") == 4
    assert 4 * chan2 == 2 * chan1 == chan0 and chan0 == 64
    vmem = pl.BlockSpec(memory_space=pltpu.VMEM)
    smem = pl.BlockSpec(memory_space=pltpu.SMEM)
    hbm = pl.BlockSpec(memory_space=pltpu.HBM)
    f32, bf16 = jnp.float32, jnp.bfloat16
    wide, front = half + 2, half + 1
    params = pltpu.CompilerParams(vmem_limit_bytes=32 * 1024 * 1024)
    small = pltpu.CompilerParams(vmem_limit_bytes=8 * 1024 * 1024)
    kernel_one = kernel_one.transpose(0, 1, 3, 2)
    kernel_two = kernel_two.transpose(0, 1, 3, 2)
    down, up = pl.pallas_call(
        functools.partial(edge_kernel, half, chan2),
        in_specs=[hbm] * 3,
        out_specs=[vmem] * 2,
        out_shape=[
            jax.ShapeDtypeStruct((2 * wide, 8, LANES), bf16),
            jax.ShapeDtypeStruct((1, 2 * wide * LANES), bf16),
        ],
        scratch_shapes=[
            pltpu.VMEM((1, 8, span), bf16),
            pltpu.VMEM((1, 8, span), bf16),
            pltpu.VMEM((8, land_words.shape[1]), jnp.int32),
            pltpu.VMEM((8, LANES), jnp.int32),
            pltpu.SemaphoreType.DMA((3,)),
        ],
        compiler_params=pltpu.CompilerParams(vmem_limit_bytes=56 * 1024 * 1024),
        name="edges",
    )(latent, targets, land_words)
    above = shifted(down, "lat", 1)
    below = shifted(up, "lat", -1)
    source, aims, weights = pl.pallas_call(
        functools.partial(prepare_kernel, half, chan0, chan2),
        in_specs=[smem] * 3 + [vmem] * 3,
        out_specs=[vmem] * 3,
        out_shape=[jax.ShapeDtypeStruct((rows, wide, 16, LANES), bf16)]
        + [jax.ShapeDtypeStruct((2 * front, 4 * rows, LANES), f32)] * 2,
        scratch_shapes=[pltpu.VMEM((2 * wide, rows, LANES), f32), pltpu.VMEM((4 * rows, LANES), jnp.int32)],
        compiler_params=small,
        cost_estimate=pl.CostEstimate(flops=10**8, bytes_accessed=10**7, transcendentals=0),
        name="prepare",
    )(member_seeds, noise_scale, channel_weight, latent, targets, land_words)
    one_late, two_late, source = lax.optimization_barrier((kernel_one, kernel_two, source))
    bands = pl.pallas_call(
        bands_kernel,
        in_specs=[vmem] * 2,
        out_specs=[vmem] * 4,
        out_shape=[jax.ShapeDtypeStruct((512, 256), bf16)] * 4,
        compiler_params=small,
        cost_estimate=pl.CostEstimate(flops=10**8, bytes_accessed=10**7, transcendentals=0),
        name="bands",
    )(one_late, two_late)
    norm = 1.0 / math.sqrt(sample_count * 4 * rows * lat_count * targets.shape[2])
    tap_rows = 5 * chan1 + 3 * chan2
    lat_grad, taps, taps_send = pl.pallas_call(
        functools.partial(band_kernel, half, (chan0, chan1, chan2), span, norm),
        in_specs=[smem] * 3 + [vmem] * 9,
        out_specs=[vmem] * 3,
        out_shape=[
            jax.ShapeDtypeStruct((rows, own * LANES), bf16),
            jax.ShapeDtypeStruct((tap_rows // 2, LANES), f32),
            jax.ShapeDtypeStruct((tap_rows // 2, LANES), f32),
        ],
        scratch_shapes=[
            pltpu.VMEM((2 * wide, 8, LANES), f32),
            pltpu.VMEM((2 * front, 8, LANES), f32),
            pltpu.VMEM((2 * front, 8, LANES), f32),
            pltpu.VMEM((rows + 4, wide + 1, 16, LANES), bf16),
            pltpu.VMEM((wide * 16, 2 * LANES), f32),
            pltpu.VMEM((wide * 16, 2 * LANES), f32),
            pltpu.VMEM((2 * rows + 4, wide, 16, LANES), bf16),
            pltpu.VMEM((2 * rows + 4, front, 16, LANES), f32),
            pltpu.VMEM((4, front, 16, LANES), bf16),
            pltpu.VMEM((4, front, 16, LANES), bf16),
            pltpu.VMEM((4, front + 1, 16, LANES), bf16),
            pltpu.VMEM((4, front + 1, 16, LANES), bf16),
            pltpu.VMEM((front * 16, LANES), f32),
            pltpu.VMEM((48, LANES), f32),
            pltpu.VMEM((48 * rows, LANES), f32),
            pltpu.VMEM((tap_rows, LANES), f32),
            pltpu.VMEM((256, 256), f32),
            pltpu.VMEM((2 * chan1, 256), f32),
            pltpu.VMEM((256, 256), f32),
            pltpu.VMEM((2 * chan2, 256), f32),
        ],
        compiler_params=params,
        name="band",
    )(
        member_seeds,
        noise_scale,
        channel_weight,
        source,
        aims,
        weights,
        above,
        below,
        *bands,
    )
    taps = taps + swapped(taps_send, "lat", 1)
    taps = total(taps, "mem", 1, 2)
    one, two, three = (swapped(lat_grad, "mem", k) for k in range(1, 4))
    bits = [1 << k for k in range(1, lat_count.bit_length() - 1)]
    for bit in bits:
        if bit == bits[-1]:
            taps, three = lax.optimization_barrier((taps, three))
        taps = taps + swapped(taps, "lat", bit)
    taps, one, two = lax.optimization_barrier((taps, one, two))
    other = swapped(taps, "lat", 1)
    latent_grad = pl.pallas_call(
        functools.partial(place_kernel, own),
        in_specs=[vmem] * 4,
        out_specs=vmem,
        out_shape=jax.ShapeDtypeStruct((1, rows, span), f32),
        compiler_params=small,
        name="place",
    )(lat_grad, one, two, three)
    one, two = pl.pallas_call(
        taps_kernel,
        in_specs=[vmem] * 2,
        out_specs=[vmem] * 2,
        out_shape=[
            jax.ShapeDtypeStruct(kernel_one.shape, f32),
            jax.ShapeDtypeStruct(kernel_two.shape, f32),
        ],
        scratch_shapes=[pltpu.VMEM((tap_rows, LANES), f32)],
        compiler_params=small,
        name="taps",
    )(taps, other)
    return (latent_grad, one.transpose(0, 1, 3, 2), two.transpose(0, 1, 3, 2))


def solution(mesh):
    in_specs = (P(None, "lat", None), P(), P(), P(), P(), P(None, "lat", None), P("lat", None), P())
    out_specs = (P(None, "lat", None), P(), P())
    return jax.shard_map(local, mesh=mesh, in_specs=in_specs, out_specs=out_specs, check_vma=False)
```

```python
import functools
import math

import jax
import jax.numpy as jnp
from jax import lax
from jax.experimental import pallas as pl
from jax.experimental.pallas import tpu as pltpu
from jax.sharding import PartitionSpec as P

SMOOTH = 0.01
HASH_CELL = 1103515245
HASH_SEED = 747796405
HASH_MIX = 277803737
LANES = 128
MEM = 8
GELU_A = math.sqrt(2.0 / math.pi)
GELU_B = 0.044715


def shifted(array, axis, by):
    peers = lax.axis_size(axis)
    pairs = [(i, i + by) for i in range(peers) if 0 <= i + by < peers]
    return lax.ppermute(array, axis, pairs)


def iota(shape, axis):
    return lax.broadcasted_iota(jnp.int32, shape, axis)


def lane_table(ref, count):
    lane = iota((8, LANES), 1) % count
    total = jnp.zeros((8, LANES), jnp.float32)
    for k in range(count):
        total = jnp.where(lane == k, ref[k], total)
    return total


def build_band(kernel_ref, band_ref):
    chan_out, chan_in = kernel_ref.shape[2], kernel_ref.shape[3]
    cells = LANES // chan_in
    repeat = (iota((chan_out, LANES), 1) % chan_out == iota((chan_out, LANES), 0)).astype(jnp.bfloat16)
    wide = {}
    for a in range(3):
        for b in range(3):
            wide[a, b] = lax.dot_general(
                kernel_ref[a, b], repeat, (((0,), (0,)), ((), ())), preferred_element_type=jnp.float32
            )
    column = iota((chan_in, LANES), 1) // chan_out
    zero = jnp.zeros((chan_in, LANES), jnp.float32)
    for block in range(2):
        for row in range(2):
            for cell in range(cells):
                at = block * 256 + row * LANES + cell * chan_in
                for sub in range(2):
                    a = sub - 2 * row + 1
                    part = zero
                    for q in range(2 * cells):
                        b = q - 2 * (cell + block * cells) + 1
                        if 0 <= a <= 2 and 0 <= b <= 2:
                            part = jnp.where(column == q, wide[a, b], part)
                    band_ref[at : at + chan_in, sub * LANES : (sub + 1) * LANES] = part.astype(jnp.bfloat16)


def build_back(kernel_ref, back_ref):
    chan_out, chan_in = kernel_ref.shape[2], kernel_ref.shape[3]
    cells = LANES // chan_in
    repeat = (iota((chan_in, LANES), 1) % chan_in == iota((chan_in, LANES), 0)).astype(jnp.bfloat16)
    flat = kernel_ref[...].reshape(9 * chan_out, chan_in)
    wide = jnp.dot(flat, repeat, preferred_element_type=jnp.float32)
    column = iota((chan_out, LANES), 1) // chan_in
    zero = jnp.zeros((chan_out, LANES), jnp.float32)
    for block in range(2):
        for sub in range(2):
            for q in range(2 * cells):
                at = block * 256 + sub * LANES + q * chan_out
                for row in range(2):
                    a = sub - 2 * row + 1
                    part = zero
                    for cell in range(cells):
                        b = q - 2 * (cell + block * cells) + 1
                        if 0 <= a <= 2 and 0 <= b <= 2:
                            tap = (3 * a + b) * chan_out
                            part = jnp.where(column == cell, wide[tap : tap + chan_out], part)
                    back_ref[at : at + chan_out, row * LANES : (row + 1) * LANES] = part.astype(jnp.bfloat16)


def pack_taps(acc_ref, next_ref, out_ref, first, chan_in, chan_out, norm):
    cells = LANES // chan_in
    group = iota((chan_out, LANES), 1) // chan_in
    packed = None
    for k in range(9):
        a, b = divmod(k, 3)
        row, sub = ((1, 1), (0, 0), (0, 1))[a]
        slot = k % cells
        part = None
        for reach in range(cells + 1):
            q = 2 * reach + b - 1
            if 0 <= q < 2 * cells:
                block, cell = reach // cells, reach % cells
                lines = sub * LANES + q * chan_out if block == 0 else sub * chan_out
                ref = acc_ref if block == 0 else next_ref
                piece = ref[lines : lines + chan_out, row * LANES : (row + 1) * LANES]
                turn = (slot - cell) % cells * chan_in
                piece = pltpu.roll(piece, turn, 1) if turn else piece
                part = piece if part is None else part + piece
        packed = part if slot == 0 else jnp.where(group == slot, part, packed)
        if slot == cells - 1 or k == 8:
            at = first + k // cells * chan_out
            out_ref[at : at + chan_out, :] = packed * norm


def spread_line(ref, slot, at):
    return jnp.broadcast_to(ref[slot, pl.ds(at, 1), :], (8, LANES))


def window_block(mem_pos, own, half, blocks, part, t):
    at = mem_pos * own + part * half + t + (blocks - 1)
    at = jnp.where(at >= blocks, at - blocks, at)
    return jnp.where(at >= blocks, at - blocks, at)


def land_of(words, block, chan):
    cell = block * (LANES // chan) + iota(words.shape, 1) // chan
    word = jnp.right_shift(cell * 2185, 16)
    picked = jnp.take_along_axis(words, word, axis=1, mode="promise_in_bounds")
    return jnp.bitwise_and(jnp.right_shift(picked, cell - 30 * word), 1).astype(jnp.float32)


def edge_kernel(
    half,
    chan,
    latent_hbm,
    targets_hbm,
    land_hbm,
    down,
    up,
    latent,
    targets,
    land,
    words,
    sems,
):
    rows = latent.shape[1]
    blocks = latent.shape[2] // LANES
    edge = pl.ds(targets_hbm.shape[1] - 8, 8)
    copies = [
        pltpu.make_async_copy(latent_hbm, latent, sems.at[0]),
        pltpu.make_async_copy(targets_hbm.at[:, edge], targets, sems.at[1]),
        pltpu.make_async_copy(land_hbm.at[edge], land, sems.at[2]),
    ]
    for copy in copies:
        copy.start()
    for copy in copies:
        copy.wait()
    own = blocks // lax.axis_size("mem")
    mem_pos = lax.axis_index("mem")
    words[...] = jnp.zeros(words.shape, jnp.int32)
    words[:, : land.shape[1]] = land[...]
    line = iota((8, LANES), 0)
    for t in range(half + 2):
        for part in range(2):
            block = window_block(mem_pos, own, half, blocks, part, t)
            off = pl.multiple_of(block * LANES, LANES)
            slot = t * 2 + part
            cells = latent[0, :, pl.ds(off, LANES)].astype(jnp.float32)
            aims = targets[0, :, pl.ds(off, LANES)].astype(jnp.float32)
            mask = land_of(words[...], block, chan)
            pack = pltpu.roll(cells, 1, 0)
            pack = jnp.where((line >= 1) & (line <= 3), pltpu.roll(aims, 4, 0), pack)
            pack = jnp.where((line >= 4) & (line <= 6), pltpu.roll(mask, 7, 0), pack)
            down[slot] = pack.astype(jnp.bfloat16)
            up[:, slot * LANES : (slot + 1) * LANES] = cells[0:1].astype(jnp.bfloat16)


def place_kernel(own, part0, part1, part2, part3, latent_grad):
    mem_pos = lax.axis_index("mem")
    for k, part in enumerate((part0, part1, part2, part3)):
        off = pl.multiple_of(jnp.bitwise_xor(mem_pos, k) * own * LANES, LANES)
        latent_grad[0, :, pl.ds(off, own * LANES)] = part[...].astype(jnp.float32)


def taps_kernel(mine, other, grad_one, grad_two, taps):
    count = mine.shape[0]
    odd = jnp.bitwise_and(lax.axis_index("lat"), 1)
    taps[pl.ds(pl.multiple_of(odd * count, 8), count), :] = mine[...]
    taps[pl.ds(pl.multiple_of((1 - odd) * count, 8), count), :] = other[...]
    first = 0
    for out in (grad_one, grad_two):
        chan_out, chan_in = out.shape[2], out.shape[3]
        cells = LANES // chan_in
        for k in range(9):
            at = first + k // cells * chan_out
            block = taps[at : at + chan_out, :]
            turn = (-(k % cells)) % cells * chan_in
            block = pltpu.roll(block, turn, 1) if turn else block
            out[k // 3, k % 3] = block[:, :chan_in]
        first += -(-9 // cells) * chan_out


def make_source(i, row, total_rows, span, own, half, seeds, scale, chan, line, store):
    blocks = span // LANES
    mem_pos = lax.axis_index("mem")
    sublane = iota((8, LANES), 0)
    seed_table = jnp.zeros((8, LANES), jnp.int32)
    for m in range(MEM):
        seed_table = jnp.where(sublane == m, seeds[m], seed_table)
    hash_table = iota((8, LANES), 1) * HASH_CELL + seed_table * HASH_SEED
    scale_table = lane_table(scale, chan)
    inside = jnp.where(row < total_rows, 1.0, 0.0).astype(jnp.float32)
    for t in range(half + 2):
        parts = []
        for part in range(2):
            first = (row * span + window_block(mem_pos, own, half, blocks, part, t) * LANES) * HASH_CELL
            h = hash_table + first
            h = jnp.bitwise_xor(h, jnp.right_shift(h, 15))
            h = h * HASH_MIX
            h = jnp.bitwise_xor(h, jnp.right_shift(h, 13))
            noise = jnp.bitwise_and(h, 65535).astype(jnp.float32) * (1.0 / 65536.0) - 0.5
            noise = noise * 3.4641016
            parts.append((line(t * 2 + part, i) + noise * scale_table) * inside)
        store(i, t, jnp.concatenate(parts, axis=0).astype(jnp.bfloat16))


def weight_lines(grid_row, channel_weight, chan, grid_total):
    latitude = math.pi / 2 - math.pi * (grid_row.astype(jnp.float32) + 0.5) / grid_total
    cosine = jnp.where(grid_row >= 0, jnp.cos(latitude), 0.0)
    channels = jnp.tile(lane_table(channel_weight, chan), (grid_row.shape[0] // 8, 1))
    return cosine * (channels * (1.0 / (MEM * (MEM - 1))))


def prepare_kernel(
    half, chan, chan2, seeds, scale, channel_weight, latent, targets, land, source, aims, weights, lines, words
):
    rows, span = latent.shape[1], latent.shape[2]
    blocks = span // LANES
    own = blocks // lax.axis_size("mem")
    total_rows = rows * lax.axis_size("lat")
    lat_pos, mem_pos = lax.axis_index("lat"), lax.axis_index("mem")
    grid_row = iota((4 * rows, LANES), 0) + lat_pos * 4 * rows
    base = weight_lines(grid_row, channel_weight, chan2, 4 * total_rows)
    words[...] = jnp.zeros(words.shape, jnp.int32)
    words[:, : land.shape[1]] = land[...]
    for t in range(half + 2):
        for part in range(2):
            block = window_block(mem_pos, own, half, blocks, part, t)
            off = pl.multiple_of(block * LANES, LANES)
            slot = t * 2 + part
            lines[slot] = latent[0, :, pl.ds(off, LANES)].astype(jnp.float32)
            if t < half + 1:
                aims[slot] = targets[0, :, pl.ds(off, LANES)].astype(jnp.float32)
                weights[slot] = base + base * land_of(words[...], block, chan2)

    def line(slot, i):
        return spread_line(lines, slot, i)

    def store(i, t, value):
        source[i, t] = value

    def step(i, _):
        make_source(
            i, lat_pos * rows + i, total_rows, span, own, half, seeds, scale, chan, line, store
        )
        return 0

    lax.fori_loop(0, rows, step, 0)


def bands_kernel(kernel_one, kernel_two, band_one, band_two, back_one, back_two):
    build_band(kernel_one, band_one)
    build_band(kernel_two, band_two)
    build_back(kernel_one, back_one)
    build_back(kernel_two, back_two)


def take_turns(*parts):
    parts = list(parts)
    while parts:
        for part in tuple(parts):
            if next(part, part) is part:
                parts.remove(part)


def band_kernel(
    half,
    chans,
    span,
    norm,
    seeds,
    scale,
    channel_weight,
    own_source,
    aims,
    weights,
    above,
    below,
    band_one,
    band_two,
    back_one,
    back_two,
    out_lat,
    taps_keep,
    taps_send,
    lat_rows,
    edge_aims,
    edge_weights,
    source,
    pre_even,
    pre_odd,
    act,
    slope,
    cast_even,
    cast_odd,
    fgrad_even,
    fgrad_odd,
    carry,
    carry_lat,
    lat_lines,
    taps,
    acc_one,
    acc_one_next,
    acc_two,
    acc_two_next,
):
    rows = own_source.shape[0]
    blocks = span // LANES
    own = blocks // lax.axis_size("mem")
    total_rows = rows * lax.axis_size("lat")
    lat_pos = lax.axis_index("lat")
    wide = half + 2
    front = half + 1
    chan0, chan1, chan2 = chans
    f32, bf16 = jnp.float32, jnp.bfloat16

    grid_row = iota((8, LANES), 0) + (lat_pos * 4 * rows - 4)
    base = weight_lines(grid_row, channel_weight, chan2, 4 * total_rows)
    for slot in range(2 * wide):
        edge = above[slot].astype(f32)
        lat_rows[slot, 0:1] = edge[0:1]
        lat_rows[slot, 1:2] = below[:, slot * LANES : (slot + 1) * LANES].astype(f32)
        if slot < 2 * front:
            edge_aims[slot] = edge
            edge_weights[slot] = base + base * pltpu.roll(edge, 5, 0)

    source[rows + 2 :] = jnp.zeros((2,) + source.shape[1:], bf16)
    source[:, wide] = jnp.zeros((source.shape[0],) + source.shape[2:], bf16)
    fgrad_even[0] = jnp.zeros(fgrad_even.shape[1:], bf16)
    for fgrad in (fgrad_even, fgrad_odd):
        fgrad[:, 0] = jnp.zeros((4,) + fgrad.shape[2:], bf16)
    carry[...] = jnp.zeros(carry.shape, f32)
    carry_lat[...] = jnp.zeros(carry_lat.shape, f32)
    for acc in (acc_one, acc_one_next, acc_two, acc_two_next):
        acc[...] = jnp.zeros(acc.shape, f32)

    def line(slot, i):
        return spread_line(lat_rows, slot, i)

    def store(i, t, value):
        source[i * (rows + 1), t] = value

    def edge_source(i, _):
        row = lat_pos * rows - 1 + i * (rows + 1)
        make_source(i, row, total_rows, span, own, half, seeds, scale, chan0, line, store)
        return 0

    lax.fori_loop(0, 2, edge_source, 0)
    source[1 : rows + 1, 0:wide] = own_source[...]

    def operand(ref, i, start, count):
        def piece(r, at):
            return ref[r, pl.ds(at, count)].reshape(count * 16, LANES)

        return jnp.concatenate(
            [piece(i, start), piece(i + 1, start), piece(i, start + 1), piece(i + 1, start + 1)], axis=1
        )

    def first_product(pair, pre):
        taken = jnp.concatenate([operand(source, 2 * pair + k, 0, wide) for k in range(2)], axis=0)
        pre[...] = jnp.dot(taken, band_one[...], preferred_element_type=f32)

    def first_gelu(pair, pre):
        for k in range(2):
            for t in range(wide):
                for sub in range(2):
                    at = (k * wide + t) * 16
                    x = pre[at : at + 16, sub * LANES : (sub + 1) * LANES]
                    square = x * x
                    th = jnp.tanh(x * (GELU_A + (GELU_A * GELU_B) * square))
                    plus = 0.5 + 0.5 * th
                    act[4 * pair + 2 * k + sub, t] = (x * plus).astype(bf16)
                    if t < front:
                        d = plus + (x * plus) * (1.0 - th) * (GELU_A + (3.0 * GELU_A * GELU_B) * square)
                        if t == half:
                            d = jnp.where(iota((16, LANES), 0) < 8, d, 0.0)
                        slope[4 * pair + 2 * k + sub, t] = d

    def first_segment(m, _):
        first_product(2 * m + 1, pre_odd)
        first_gelu(2 * m, pre_even)
        first_product(2 * m + 2, pre_even)
        first_gelu(2 * m + 1, pre_odd)
        return 0

    first_product(0, pre_even)
    lax.fori_loop(0, rows // 4, first_segment, 0)
    first_gelu(rows // 2, pre_even)

    members = front * 16
    owner = iota((48, members), 0)
    group = iota((48, members), 1) // 8
    place = (group % 2) * half + group // 2
    real = (group // 2 > 0) & (place - 1 < own)
    pick_own = (real & (place - 1 == owner)).astype(bf16)
    pick_prev = ((group // 2 < half) & (place == owner)).astype(bf16)
    pick = jnp.concatenate([pick_own, pick_prev], axis=0)

    def second_product(n, cast):
        taken = jnp.concatenate([operand(act, 2 * n + k, 0, front) for k in range(2)], axis=0)
        out = jnp.dot(taken, band_two[...], preferred_element_type=f32).astype(bf16)
        for k in range(2):
            for sub in range(2):
                part = out[k * members : (k + 1) * members, sub * LANES : (sub + 1) * LANES]
                cast[2 * k + sub] = part.reshape(front, 16, LANES)
        yield

    def loss_gradient(cast, fgrad, aim_ref, weight_ref, first, lines):
        for line in lines:
            for t in range(front):
                both = cast[line, t].astype(f32)
                parts = []
                for part in range(2):
                    if t == half and part == 1:
                        parts.append(jnp.zeros((8, LANES), f32))
                        continue
                    f = both[part * 8 : part * 8 + 8]
                    d = f - spread_line(aim_ref, t * 2 + part, first + line)
                    goal = d * lax.rsqrt(d * d + SMOOTH)
                    gs = []
                    for k in range(1, 5):
                        d = f - pltpu.roll(f, k, 0)
                        gs.append(d * lax.rsqrt(d * d + SMOOTH))
                    back = gs[2]
                    for k in (1, 0):
                        back = gs[k] + pltpu.roll(back, MEM - 1, 0)
                    back = pltpu.roll(back, MEM - 1, 0)
                    spread = (gs[0] + gs[1]) + (gs[2] + gs[3]) - back
                    weight = spread_line(weight_ref, t * 2 + part, first + line)
                    parts.append(weight * ((MEM - 1.0) * goal - spread))
                fgrad[line, t + 1] = jnp.concatenate(parts, axis=0).astype(bf16)
            yield

    def pull_back(n, fgrad):
        keep = jnp.where(n >= 1, 1.0, 0.0).astype(bf16)

        def flat(line, start, count):
            return fgrad[line, start : start + count].reshape(count * 16, LANES)

        def add_taps(g, x, acc, acc_next, chan_out):
            turned = g.T
            acc[...] += jnp.dot(turned, x[:, :256], preferred_element_type=f32)
            last = [turned[k * LANES - chan_out : k * LANES] for k in (1, 2)]
            last = jnp.concatenate(last, axis=0)
            acc_next[...] += jnp.dot(last, x[:, 256:], preferred_element_type=f32)

        g = [
            jnp.concatenate(
                [flat(2 * k, 1, front), flat(2 * k + 1, 1, front), flat(2 * k, 0, front), flat(2 * k + 1, 0, front)],
                axis=1,
            )
            for k in range(2)
        ]
        pulled = jnp.dot(jnp.concatenate(g, axis=0), back_two[...], preferred_element_type=f32)
        grads = [
            pulled[:members, :LANES] + carry[...],
            pulled[members:, :LANES] + pulled[:members, LANES:],
        ]
        carry[...] = pulled[members:, LANES:]
        grads = [(grads[k] * slope[2 * n + k].reshape(members, LANES)).astype(bf16) for k in range(2)]
        yield
        grads = jnp.concatenate(grads, axis=1)
        g = [jnp.concatenate([flat(2 * k, 2, half), flat(2 * k + 1, 2, half)], axis=1) for k in range(2)]
        x = [operand(act, 2 * n + k, 1, half) for k in range(2)]
        add_taps(jnp.concatenate(g, axis=0) * keep, jnp.concatenate(x, axis=0), acc_two, acc_two_next, chan2)
        yield
        add_taps(grads[16:] * keep, operand(source, n, 1, half), acc_one, acc_one_next, chan1)
        yield
        z = jnp.dot(pick, grads, preferred_element_type=f32)
        z = jnp.concatenate([z[:48], z[48:]], axis=1)
        high = z.astype(bf16)
        z = jnp.concatenate([high, (z - high.astype(f32)).astype(bf16)], axis=0)
        z = jnp.dot(z, back_one[...], preferred_element_type=f32)
        z = z[:48] + z[48:]
        lat_lines[pl.ds(jnp.maximum(n - 1, 0), 48, stride=rows), :] = z[:, :LANES] + carry_lat[...]
        carry_lat[...] = z[:, LANES:]
        yield

    def own_gradient(n, cast, fgrad):
        return loss_gradient(cast, fgrad, aims, weights, 4 * (n - 1), range(4))

    def second_segment(m, _):
        take_turns(
            second_product(2 * m + 2, cast_even),
            own_gradient(2 * m + 1, cast_odd, fgrad_odd),
            pull_back(2 * m, fgrad_even),
        )
        take_turns(
            second_product(jnp.minimum(2 * m + 3, rows), cast_odd),
            own_gradient(2 * m + 2, cast_even, fgrad_even),
            pull_back(2 * m + 1, fgrad_odd),
        )
        return 0

    take_turns(second_product(0, cast_even))
    take_turns(
        second_product(1, cast_odd),
        loss_gradient(cast_even, fgrad_even, edge_aims, edge_weights, 0, range(1, 4)),
    )
    lax.fori_loop(0, rows // 2, second_segment, 0)
    take_turns(pull_back(rows, fgrad_even))

    for t in range(own):
        out_lat[:, t * LANES : (t + 1) * LANES] = lat_lines[t * rows : (t + 1) * rows].astype(bf16)
    pack_taps(acc_one, acc_one_next, taps, 0, chan0, chan1, norm)
    pack_taps(acc_two, acc_two_next, taps, -(-9 // (LANES // chan0)) * chan1, chan1, chan2, norm)
    count = taps_keep.shape[0]
    odd = jnp.bitwise_and(lat_pos, 1)
    taps_keep[...] = taps[pl.ds(pl.multiple_of(odd * count, 8), count), :]
    taps_send[...] = taps[pl.ds(pl.multiple_of((1 - odd) * count, 8), count), :]


def swapped(array, axis, bit):
    return lax.ppermute(array, axis, [(i, i ^ bit) for i in range(lax.axis_size(axis))])


def total(array, axis, first, second):
    one, two, three = (swapped(array, axis, k).astype(jnp.float32) for k in (first, second, first ^ second))
    return (array.astype(jnp.float32) + one) + (two + three)


def local(
    latent, member_seeds, noise_scale, kernel_one, kernel_two, targets, land_words, channel_weight
):
    sample_count, rows, span = latent.shape
    chan0, chan1, chan2 = kernel_one.shape[2], kernel_one.shape[3], kernel_two.shape[3]
    lat_count = lax.axis_size("lat")
    own = span // LANES // lax.axis_size("mem")
    half = (own + 1) // 2
    assert sample_count == 1 and member_seeds.shape[0] == MEM and rows % 4 == 0 and own % 2 == 1 and lax.axis_size("mem") == 4
    assert 4 * chan2 == 2 * chan1 == chan0 and chan0 == 64
    vmem = pl.BlockSpec(memory_space=pltpu.VMEM)
    smem = pl.BlockSpec(memory_space=pltpu.SMEM)
    hbm = pl.BlockSpec(memory_space=pltpu.HBM)
    f32, bf16 = jnp.float32, jnp.bfloat16
    wide, front = half + 2, half + 1
    params = pltpu.CompilerParams(vmem_limit_bytes=32 * 1024 * 1024)
    small = pltpu.CompilerParams(vmem_limit_bytes=8 * 1024 * 1024)
    kernel_one = kernel_one.transpose(0, 1, 3, 2)
    kernel_two = kernel_two.transpose(0, 1, 3, 2)
    down, up = pl.pallas_call(
        functools.partial(edge_kernel, half, chan2),
        in_specs=[hbm] * 3,
        out_specs=[vmem] * 2,
        out_shape=[
            jax.ShapeDtypeStruct((2 * wide, 8, LANES), bf16),
            jax.ShapeDtypeStruct((1, 2 * wide * LANES), bf16),
        ],
        scratch_shapes=[
            pltpu.VMEM((1, 8, span), bf16),
            pltpu.VMEM((1, 8, span), bf16),
            pltpu.VMEM((8, land_words.shape[1]), jnp.int32),
            pltpu.VMEM((8, LANES), jnp.int32),
            pltpu.SemaphoreType.DMA((3,)),
        ],
        compiler_params=pltpu.CompilerParams(vmem_limit_bytes=56 * 1024 * 1024),
        name="edges",
    )(latent, targets, land_words)
    above = shifted(down, "lat", 1)
    below = shifted(up, "lat", -1)
    source, aims, weights = pl.pallas_call(
        functools.partial(prepare_kernel, half, chan0, chan2),
        in_specs=[smem] * 3 + [vmem] * 3,
        out_specs=[vmem] * 3,
        out_shape=[jax.ShapeDtypeStruct((rows, wide, 16, LANES), bf16)]
        + [jax.ShapeDtypeStruct((2 * front, 4 * rows, LANES), f32)] * 2,
        scratch_shapes=[pltpu.VMEM((2 * wide, rows, LANES), f32), pltpu.VMEM((4 * rows, LANES), jnp.int32)],
        compiler_params=small,
        cost_estimate=pl.CostEstimate(flops=10**8, bytes_accessed=10**7, transcendentals=0),
        name="prepare",
    )(member_seeds, noise_scale, channel_weight, latent, targets, land_words)
    one_late, two_late, source = lax.optimization_barrier((kernel_one, kernel_two, source))
    bands = pl.pallas_call(
        bands_kernel,
        in_specs=[vmem] * 2,
        out_specs=[vmem] * 4,
        out_shape=[jax.ShapeDtypeStruct((512, 256), bf16)] * 4,
        compiler_params=small,
        cost_estimate=pl.CostEstimate(flops=10**8, bytes_accessed=10**7, transcendentals=0),
        name="bands",
    )(one_late, two_late)
    norm = 1.0 / math.sqrt(sample_count * 4 * rows * lat_count * targets.shape[2])
    tap_rows = 5 * chan1 + 3 * chan2
    lat_grad, taps, taps_send = pl.pallas_call(
        functools.partial(band_kernel, half, (chan0, chan1, chan2), span, norm),
        in_specs=[smem] * 3 + [vmem] * 9,
        out_specs=[vmem] * 3,
        out_shape=[
            jax.ShapeDtypeStruct((rows, own * LANES), bf16),
            jax.ShapeDtypeStruct((tap_rows // 2, LANES), f32),
            jax.ShapeDtypeStruct((tap_rows // 2, LANES), f32),
        ],
        scratch_shapes=[
            pltpu.VMEM((2 * wide, 8, LANES), f32),
            pltpu.VMEM((2 * front, 8, LANES), f32),
            pltpu.VMEM((2 * front, 8, LANES), f32),
            pltpu.VMEM((rows + 4, wide + 1, 16, LANES), bf16),
            pltpu.VMEM((wide * 32, 2 * LANES), f32),
            pltpu.VMEM((wide * 32, 2 * LANES), f32),
            pltpu.VMEM((2 * rows + 4, wide, 16, LANES), bf16),
            pltpu.VMEM((2 * rows + 4, front, 16, LANES), f32),
            pltpu.VMEM((4, front, 16, LANES), bf16),
            pltpu.VMEM((4, front, 16, LANES), bf16),
            pltpu.VMEM((4, front + 1, 16, LANES), bf16),
            pltpu.VMEM((4, front + 1, 16, LANES), bf16),
            pltpu.VMEM((front * 16, LANES), f32),
            pltpu.VMEM((48, LANES), f32),
            pltpu.VMEM((48 * rows, LANES), f32),
            pltpu.VMEM((tap_rows, LANES), f32),
            pltpu.VMEM((256, 256), f32),
            pltpu.VMEM((2 * chan1, 256), f32),
            pltpu.VMEM((256, 256), f32),
            pltpu.VMEM((2 * chan2, 256), f32),
        ],
        compiler_params=params,
        name="band",
    )(
        member_seeds,
        noise_scale,
        channel_weight,
        source,
        aims,
        weights,
        above,
        below,
        *bands,
    )
    taps = (taps + swapped(taps_send, "lat", 1)).astype(bf16)
    taps = total(taps, "mem", 1, 2)
    one, two, three = (swapped(lat_grad, "mem", k) for k in range(1, 4))
    bits = [1 << k for k in range(1, lat_count.bit_length() - 1)]
    for bit in bits:
        if bit == bits[-1]:
            taps, three = lax.optimization_barrier((taps, three))
        taps = taps + swapped(taps, "lat", bit)
    taps, one, two = lax.optimization_barrier((taps, one, two))
    other = swapped(taps, "lat", 1)
    latent_grad = pl.pallas_call(
        functools.partial(place_kernel, own),
        in_specs=[vmem] * 4,
        out_specs=vmem,
        out_shape=jax.ShapeDtypeStruct((1, rows, span), f32),
        compiler_params=small,
        name="place",
    )(lat_grad, one, two, three)
    one, two = pl.pallas_call(
        taps_kernel,
        in_specs=[vmem] * 2,
        out_specs=[vmem] * 2,
        out_shape=[
            jax.ShapeDtypeStruct(kernel_one.shape, f32),
            jax.ShapeDtypeStruct(kernel_two.shape, f32),
        ],
        scratch_shapes=[pltpu.VMEM((tap_rows, LANES), f32)],
        compiler_params=small,
        name="taps",
    )(taps, other)
    return (latent_grad, one.transpose(0, 1, 3, 2), two.transpose(0, 1, 3, 2))


def solution(mesh):
    in_specs = (P(None, "lat", None), P(), P(), P(), P(), P(None, "lat", None), P("lat", None), P())
    out_specs = (P(None, "lat", None), P(), P())
    return jax.shard_map(local, mesh=mesh, in_specs=in_specs, out_specs=out_specs, check_vma=False)
```

```python
import functools
import math

import jax
import jax.numpy as jnp
from jax import lax
from jax.experimental import pallas as pl
from jax.experimental.pallas import tpu as pltpu
from jax.sharding import PartitionSpec as P

SMOOTH = 0.01
HASH_CELL = 1103515245
HASH_SEED = 747796405
HASH_MIX = 277803737
LANES = 128
MEM = 8
GELU_A = math.sqrt(2.0 / math.pi)
GELU_B = 0.044715


def shifted(array, axis, by):
    peers = lax.axis_size(axis)
    pairs = [(i, i + by) for i in range(peers) if 0 <= i + by < peers]
    return lax.ppermute(array, axis, pairs)


def iota(shape, axis):
    return lax.broadcasted_iota(jnp.int32, shape, axis)


def lane_table(ref, count):
    lane = iota((8, LANES), 1) % count
    total = jnp.zeros((8, LANES), jnp.float32)
    for k in range(count):
        total = jnp.where(lane == k, ref[k], total)
    return total


def build_band(kernel_ref, band_ref):
    chan_out, chan_in = kernel_ref.shape[2], kernel_ref.shape[3]
    cells = LANES // chan_in
    repeat = (iota((chan_out, LANES), 1) % chan_out == iota((chan_out, LANES), 0)).astype(jnp.bfloat16)
    wide = {}
    for a in range(3):
        for b in range(3):
            wide[a, b] = lax.dot_general(
                kernel_ref[a, b], repeat, (((0,), (0,)), ((), ())), preferred_element_type=jnp.float32
            )
    column = iota((chan_in, LANES), 1) // chan_out
    zero = jnp.zeros((chan_in, LANES), jnp.float32)
    for block in range(2):
        for row in range(2):
            for cell in range(cells):
                at = block * 256 + row * LANES + cell * chan_in
                for sub in range(2):
                    a = sub - 2 * row + 1
                    part = zero
                    for q in range(2 * cells):
                        b = q - 2 * (cell + block * cells) + 1
                        if 0 <= a <= 2 and 0 <= b <= 2:
                            part = jnp.where(column == q, wide[a, b], part)
                    band_ref[at : at + chan_in, sub * LANES : (sub + 1) * LANES] = part.astype(jnp.bfloat16)


def build_back(kernel_ref, back_ref):
    chan_out, chan_in = kernel_ref.shape[2], kernel_ref.shape[3]
    cells = LANES // chan_in
    repeat = (iota((chan_in, LANES), 1) % chan_in == iota((chan_in, LANES), 0)).astype(jnp.bfloat16)
    flat = kernel_ref[...].reshape(9 * chan_out, chan_in)
    wide = jnp.dot(flat, repeat, preferred_element_type=jnp.float32)
    column = iota((chan_out, LANES), 1) // chan_in
    zero = jnp.zeros((chan_out, LANES), jnp.float32)
    for block in range(2):
        for sub in range(2):
            for q in range(2 * cells):
                at = block * 256 + sub * LANES + q * chan_out
                for row in range(2):
                    a = sub - 2 * row + 1
                    part = zero
                    for cell in range(cells):
                        b = q - 2 * (cell + block * cells) + 1
                        if 0 <= a <= 2 and 0 <= b <= 2:
                            tap = (3 * a + b) * chan_out
                            part = jnp.where(column == cell, wide[tap : tap + chan_out], part)
                    back_ref[at : at + chan_out, row * LANES : (row + 1) * LANES] = part.astype(jnp.bfloat16)


def pack_taps(acc_ref, next_ref, out_ref, first, chan_in, chan_out, norm):
    cells = LANES // chan_in
    group = iota((chan_out, LANES), 1) // chan_in
    packed = None
    for k in range(9):
        a, b = divmod(k, 3)
        row, sub = ((1, 1), (0, 0), (0, 1))[a]
        slot = k % cells
        part = None
        for reach in range(cells + 1):
            q = 2 * reach + b - 1
            if 0 <= q < 2 * cells:
                block, cell = reach // cells, reach % cells
                lines = sub * LANES + q * chan_out if block == 0 else sub * chan_out
                ref = acc_ref if block == 0 else next_ref
                piece = ref[lines : lines + chan_out, row * LANES : (row + 1) * LANES]
                turn = (slot - cell) % cells * chan_in
                piece = pltpu.roll(piece, turn, 1) if turn else piece
                part = piece if part is None else part + piece
        packed = part if slot == 0 else jnp.where(group == slot, part, packed)
        if slot == cells - 1 or k == 8:
            at = first + k // cells * chan_out
            out_ref[at : at + chan_out, :] = packed * norm


def spread_line(ref, slot, at):
    return jnp.broadcast_to(ref[slot, pl.ds(at, 1), :], (8, LANES))


def window_block(mem_pos, own, half, blocks, part, t):
    at = mem_pos * own + part * half + t + (blocks - 1)
    at = jnp.where(at >= blocks, at - blocks, at)
    return jnp.where(at >= blocks, at - blocks, at)


def land_of(words, block, chan):
    cell = block * (LANES // chan) + iota(words.shape, 1) // chan
    word = jnp.right_shift(cell * 2185, 16)
    picked = jnp.take_along_axis(words, word, axis=1, mode="promise_in_bounds")
    return jnp.bitwise_and(jnp.right_shift(picked, cell - 30 * word), 1).astype(jnp.float32)


def edge_kernel(
    half,
    chan,
    latent_hbm,
    targets_hbm,
    land_hbm,
    down,
    up,
    latent,
    targets,
    land,
    words,
    sems,
):
    rows = latent.shape[1]
    blocks = latent.shape[2] // LANES
    edge = pl.ds(targets_hbm.shape[1] - 8, 8)
    copies = [
        pltpu.make_async_copy(latent_hbm, latent, sems.at[0]),
        pltpu.make_async_copy(targets_hbm.at[:, edge], targets, sems.at[1]),
        pltpu.make_async_copy(land_hbm.at[edge], land, sems.at[2]),
    ]
    for copy in copies:
        copy.start()
    for copy in copies:
        copy.wait()
    own = blocks // lax.axis_size("mem")
    mem_pos = lax.axis_index("mem")
    words[...] = jnp.zeros(words.shape, jnp.int32)
    words[:, : land.shape[1]] = land[...]
    line = iota((8, LANES), 0)
    for t in range(half + 2):
        for part in range(2):
            block = window_block(mem_pos, own, half, blocks, part, t)
            off = pl.multiple_of(block * LANES, LANES)
            slot = t * 2 + part
            cells = latent[0, :, pl.ds(off, LANES)].astype(jnp.float32)
            aims = targets[0, :, pl.ds(off, LANES)].astype(jnp.float32)
            mask = land_of(words[...], block, chan)
            pack = pltpu.roll(cells, 1, 0)
            pack = jnp.where((line >= 1) & (line <= 3), pltpu.roll(aims, 4, 0), pack)
            pack = jnp.where((line >= 4) & (line <= 6), pltpu.roll(mask, 7, 0), pack)
            down[slot] = pack.astype(jnp.bfloat16)
            up[:, slot * LANES : (slot + 1) * LANES] = cells[0:1].astype(jnp.bfloat16)


def place_kernel(own, part0, part1, part2, part3, latent_grad):
    mem_pos = lax.axis_index("mem")
    for k, part in enumerate((part0, part1, part2, part3)):
        off = pl.multiple_of(jnp.bitwise_xor(mem_pos, k) * own * LANES, LANES)
        latent_grad[0, :, pl.ds(off, own * LANES)] = part[...].astype(jnp.float32)


def taps_kernel(mine, other, grad_one, grad_two, taps):
    count = mine.shape[0]
    odd = jnp.bitwise_and(lax.axis_index("lat"), 1)
    taps[pl.ds(pl.multiple_of(odd * count, 8), count), :] = mine[...]
    taps[pl.ds(pl.multiple_of((1 - odd) * count, 8), count), :] = other[...]
    first = 0
    for out in (grad_one, grad_two):
        chan_out, chan_in = out.shape[2], out.shape[3]
        cells = LANES // chan_in
        for k in range(9):
            at = first + k // cells * chan_out
            block = taps[at : at + chan_out, :]
            turn = (-(k % cells)) % cells * chan_in
            block = pltpu.roll(block, turn, 1) if turn else block
            out[k // 3, k % 3] = block[:, :chan_in]
        first += -(-9 // cells) * chan_out


def make_source(i, row, total_rows, span, own, half, seeds, scale, chan, line, store):
    blocks = span // LANES
    mem_pos = lax.axis_index("mem")
    sublane = iota((8, LANES), 0)
    seed_table = jnp.zeros((8, LANES), jnp.int32)
    for m in range(MEM):
        seed_table = jnp.where(sublane == m, seeds[m], seed_table)
    hash_table = iota((8, LANES), 1) * HASH_CELL + seed_table * HASH_SEED
    scale_table = lane_table(scale, chan)
    inside = jnp.where(row < total_rows, 1.0, 0.0).astype(jnp.float32)
    for t in range(half + 2):
        parts = []
        for part in range(2):
            first = (row * span + window_block(mem_pos, own, half, blocks, part, t) * LANES) * HASH_CELL
            h = hash_table + first
            h = jnp.bitwise_xor(h, jnp.right_shift(h, 15))
            h = h * HASH_MIX
            h = jnp.bitwise_xor(h, jnp.right_shift(h, 13))
            noise = jnp.bitwise_and(h, 65535).astype(jnp.float32) * (1.0 / 65536.0) - 0.5
            noise = noise * 3.4641016
            parts.append((line(t * 2 + part, i) + noise * scale_table) * inside)
        store(i, t, jnp.concatenate(parts, axis=0).astype(jnp.bfloat16))


def weight_lines(grid_row, channel_weight, chan, grid_total):
    latitude = math.pi / 2 - math.pi * (grid_row.astype(jnp.float32) + 0.5) / grid_total
    cosine = jnp.where(grid_row >= 0, jnp.cos(latitude), 0.0)
    channels = jnp.tile(lane_table(channel_weight, chan), (grid_row.shape[0] // 8, 1))
    return cosine * (channels * (1.0 / (MEM * (MEM - 1))))


def prepare_kernel(
    half, chan, chan2, seeds, scale, channel_weight, latent, targets, land, source, aims, weights, lines, words
):
    rows, span = latent.shape[1], latent.shape[2]
    blocks = span // LANES
    own = blocks // lax.axis_size("mem")
    total_rows = rows * lax.axis_size("lat")
    lat_pos, mem_pos = lax.axis_index("lat"), lax.axis_index("mem")
    grid_row = iota((4 * rows, LANES), 0) + lat_pos * 4 * rows
    base = weight_lines(grid_row, channel_weight, chan2, 4 * total_rows)
    words[...] = jnp.zeros(words.shape, jnp.int32)
    words[:, : land.shape[1]] = land[...]
    for t in range(half + 2):
        for part in range(2):
            block = window_block(mem_pos, own, half, blocks, part, t)
            off = pl.multiple_of(block * LANES, LANES)
            slot = t * 2 + part
            lines[slot] = latent[0, :, pl.ds(off, LANES)].astype(jnp.float32)
            if t < half + 1:
                aims[slot] = targets[0, :, pl.ds(off, LANES)].astype(jnp.float32)
                weights[slot] = base + base * land_of(words[...], block, chan2)

    def line(slot, i):
        return spread_line(lines, slot, i)

    def store(i, t, value):
        source[i, t] = value

    def step(i, _):
        make_source(
            i, lat_pos * rows + i, total_rows, span, own, half, seeds, scale, chan, line, store
        )
        return 0

    lax.fori_loop(0, rows, step, 0)


def bands_kernel(kernel_one, kernel_two, band_one, band_two, back_one, back_two):
    build_band(kernel_one, band_one)
    build_band(kernel_two, band_two)
    build_back(kernel_one, back_one)
    build_back(kernel_two, back_two)


def take_turns(*parts):
    parts = list(parts)
    while parts:
        for part in tuple(parts):
            if next(part, part) is part:
                parts.remove(part)


def band_kernel(
    half,
    chans,
    span,
    norm,
    seeds,
    scale,
    channel_weight,
    own_source,
    aims,
    weights,
    above,
    below,
    band_one,
    band_two,
    back_one,
    back_two,
    out_lat,
    taps_keep,
    taps_send,
    lat_rows,
    edge_aims,
    edge_weights,
    source,
    pre_even,
    pre_odd,
    act,
    slope,
    cast_now,
    cast_next,
    fgrad_now,
    fgrad_next,
    carry,
    carry_lat,
    lat_lines,
    taps,
    acc_one,
    acc_one_next,
    acc_two,
    acc_two_next,
):
    rows = own_source.shape[0]
    blocks = span // LANES
    own = blocks // lax.axis_size("mem")
    total_rows = rows * lax.axis_size("lat")
    lat_pos = lax.axis_index("lat")
    wide = half + 2
    front = half + 1
    chan0, chan1, chan2 = chans
    f32, bf16 = jnp.float32, jnp.bfloat16

    grid_row = iota((8, LANES), 0) + (lat_pos * 4 * rows - 4)
    base = weight_lines(grid_row, channel_weight, chan2, 4 * total_rows)
    for slot in range(2 * wide):
        edge = above[slot].astype(f32)
        lat_rows[slot, 0:1] = edge[0:1]
        lat_rows[slot, 1:2] = below[:, slot * LANES : (slot + 1) * LANES].astype(f32)
        if slot < 2 * front:
            edge_aims[slot] = edge
            edge_weights[slot] = base + base * pltpu.roll(edge, 5, 0)

    source[rows + 2 :] = jnp.zeros((2,) + source.shape[1:], bf16)
    source[:, wide] = jnp.zeros((source.shape[0],) + source.shape[2:], bf16)
    fgrad_next[0] = jnp.zeros(fgrad_next.shape[1:], bf16)
    fgrad_next[:, 0] = jnp.zeros((4,) + fgrad_next.shape[2:], bf16)
    carry[...] = jnp.zeros(carry.shape, f32)
    carry_lat[...] = jnp.zeros(carry_lat.shape, f32)
    for acc in (acc_one, acc_one_next, acc_two, acc_two_next):
        acc[...] = jnp.zeros(acc.shape, f32)

    def line(slot, i):
        return spread_line(lat_rows, slot, i)

    def store(i, t, value):
        source[i * (rows + 1), t] = value

    def edge_source(i, _):
        row = lat_pos * rows - 1 + i * (rows + 1)
        make_source(i, row, total_rows, span, own, half, seeds, scale, chan0, line, store)
        return 0

    lax.fori_loop(0, 2, edge_source, 0)
    source[1 : rows + 1, 0:wide] = own_source[...]

    def operand(ref, i, start, count):
        def piece(r, at):
            return ref[r, pl.ds(at, count)].reshape(count * 16, LANES)

        return jnp.concatenate(
            [piece(i, start), piece(i + 1, start), piece(i, start + 1), piece(i + 1, start + 1)], axis=1
        )

    def first_product(i, pre):
        pre[...] = jnp.dot(operand(source, i, 0, wide), band_one[...], preferred_element_type=f32)

    def first_gelu(i, pre):
        for t in range(wide):
            for sub in range(2):
                x = pre[t * 16 : (t + 1) * 16, sub * LANES : (sub + 1) * LANES]
                square = x * x
                th = jnp.tanh(x * (GELU_A + (GELU_A * GELU_B) * square))
                plus = 0.5 + 0.5 * th
                act[2 * i + sub, t] = (x * plus).astype(bf16)
                if t < front:
                    d = plus + (x * plus) * (1.0 - th) * (GELU_A + (3.0 * GELU_A * GELU_B) * square)
                    if t == half:
                        d = jnp.where(iota((16, LANES), 0) < 8, d, 0.0)
                    slope[2 * i + sub, t] = d

    def first_segment(m, _):
        first_product(2 * m + 1, pre_odd)
        first_gelu(2 * m, pre_even)
        first_product(2 * m + 2, pre_even)
        first_gelu(2 * m + 1, pre_odd)
        return 0

    first_product(0, pre_even)
    lax.fori_loop(0, rows // 2 + 1, first_segment, 0)

    members = front * 16
    owner = iota((48, members), 0)
    group = iota((48, members), 1) // 8
    place = (group % 2) * half + group // 2
    real = (group // 2 > 0) & (place - 1 < own)
    pick_own = (real & (place - 1 == owner)).astype(bf16)
    pick_prev = ((group // 2 < half) & (place == owner)).astype(bf16)
    pick = jnp.concatenate([pick_own, pick_prev], axis=0)

    def second_product(n, cast):
        taken = jnp.concatenate([operand(act, 2 * n + k, 0, front) for k in range(2)], axis=0)
        out = jnp.dot(taken, band_two[...], preferred_element_type=f32).astype(bf16)
        for k in range(2):
            for sub in range(2):
                part = out[k * members : (k + 1) * members, sub * LANES : (sub + 1) * LANES]
                cast[2 * k + sub] = part.reshape(front, 16, LANES)
        yield

    def loss_gradient(cast, fgrad, aim_ref, weight_ref, first, lines):
        for line in lines:
            for t in range(front):
                both = cast[line, t].astype(f32)
                parts = []
                for part in range(2):
                    if t == half and part == 1:
                        parts.append(jnp.zeros((8, LANES), f32))
                        continue
                    f = both[part * 8 : part * 8 + 8]
                    d = f - spread_line(aim_ref, t * 2 + part, first + line)
                    goal = d * lax.rsqrt(d * d + SMOOTH)
                    gs = []
                    for k in range(1, 5):
                        d = f - pltpu.roll(f, k, 0)
                        gs.append(d * lax.rsqrt(d * d + SMOOTH))
                    back = gs[2]
                    for k in (1, 0):
                        back = gs[k] + pltpu.roll(back, MEM - 1, 0)
                    back = pltpu.roll(back, MEM - 1, 0)
                    spread = (gs[0] + gs[1]) + (gs[2] + gs[3]) - back
                    weight = spread_line(weight_ref, t * 2 + part, first + line)
                    parts.append(weight * ((MEM - 1.0) * goal - spread))
                fgrad[line, t + 1] = jnp.concatenate(parts, axis=0).astype(bf16)
            yield

    def pull_back(n, fgrad):
        keep = jnp.where(n >= 1, 1.0, 0.0).astype(bf16)

        def flat(line, start, count):
            return fgrad[line, start : start + count].reshape(count * 16, LANES)

        def add_taps(g, x, acc, acc_next, chan_out):
            turned = g.T
            acc[...] += jnp.dot(turned, x[:, :256], preferred_element_type=f32)
            last = [turned[k * LANES - chan_out : k * LANES] for k in (1, 2)]
            last = jnp.concatenate(last, axis=0)
            acc_next[...] += jnp.dot(last, x[:, 256:], preferred_element_type=f32)

        g = [
            jnp.concatenate(
                [flat(2 * k, 1, front), flat(2 * k + 1, 1, front), flat(2 * k, 0, front), flat(2 * k + 1, 0, front)],
                axis=1,
            )
            for k in range(2)
        ]
        pulled = jnp.dot(jnp.concatenate(g, axis=0), back_two[...], preferred_element_type=f32)
        grads = [
            pulled[:members, :LANES] + carry[...],
            pulled[members:, :LANES] + pulled[:members, LANES:],
        ]
        carry[...] = pulled[members:, LANES:]
        grads = [(grads[k] * slope[2 * n + k].reshape(members, LANES)).astype(bf16) for k in range(2)]
        yield
        grads = jnp.concatenate(grads, axis=1)
        g = [jnp.concatenate([flat(2 * k, 2, half), flat(2 * k + 1, 2, half)], axis=1) for k in range(2)]
        x = [operand(act, 2 * n + k, 1, half) for k in range(2)]
        add_taps(jnp.concatenate(g, axis=0) * keep, jnp.concatenate(x, axis=0), acc_two, acc_two_next, chan2)
        yield
        add_taps(grads[16:] * keep, operand(source, n, 1, half), acc_one, acc_one_next, chan1)
        yield
        z = jnp.dot(pick, grads, preferred_element_type=f32)
        z = jnp.concatenate([z[:48], z[48:]], axis=1)
        high = z.astype(bf16)
        z = jnp.concatenate([high, (z - high.astype(f32)).astype(bf16)], axis=0)
        z = jnp.dot(z, back_one[...], preferred_element_type=f32)
        z = z[:48] + z[48:]
        lat_lines[pl.ds(jnp.maximum(n - 1, 0), 48, stride=rows), :] = z[:, :LANES] + carry_lat[...]
        carry_lat[...] = z[:, LANES:]
        yield

    def second_segment(k, _):
        cast_now[...] = cast_next[...]
        fgrad_now[...] = fgrad_next[...]
        take_turns(
            second_product(jnp.minimum(k + 1, rows), cast_next),
            loss_gradient(cast_now, fgrad_next, aims, weights, 4 * (k - 1), range(4)),
            pull_back(k - 1, fgrad_now),
        )
        return 0

    take_turns(second_product(0, cast_now))
    take_turns(
        second_product(1, cast_next),
        loss_gradient(cast_now, fgrad_next, edge_aims, edge_weights, 0, range(1, 4)),
    )
    lax.fori_loop(1, rows + 1, second_segment, 0)
    take_turns(pull_back(rows, fgrad_next))

    for t in range(own):
        out_lat[:, t * LANES : (t + 1) * LANES] = lat_lines[t * rows : (t + 1) * rows].astype(bf16)
    pack_taps(acc_one, acc_one_next, taps, 0, chan0, chan1, norm)
    pack_taps(acc_two, acc_two_next, taps, -(-9 // (LANES // chan0)) * chan1, chan1, chan2, norm)
    count = taps_keep.shape[0]
    odd = jnp.bitwise_and(lat_pos, 1)
    taps_keep[...] = taps[pl.ds(pl.multiple_of(odd * count, 8), count), :]
    taps_send[...] = taps[pl.ds(pl.multiple_of((1 - odd) * count, 8), count), :]


def swapped(array, axis, bit):
    return lax.ppermute(array, axis, [(i, i ^ bit) for i in range(lax.axis_size(axis))])


def total(array, axis, first, second):
    one, two, three = (swapped(array, axis, k).astype(jnp.float32) for k in (first, second, first ^ second))
    return (array.astype(jnp.float32) + one) + (two + three)


def local(
    latent, member_seeds, noise_scale, kernel_one, kernel_two, targets, land_words, channel_weight
):
    sample_count, rows, span = latent.shape
    chan0, chan1, chan2 = kernel_one.shape[2], kernel_one.shape[3], kernel_two.shape[3]
    lat_count = lax.axis_size("lat")
    own = span // LANES // lax.axis_size("mem")
    half = (own + 1) // 2
    assert sample_count == 1 and member_seeds.shape[0] == MEM and rows % 4 == 0 and own % 2 == 1 and lax.axis_size("mem") == 4
    assert 4 * chan2 == 2 * chan1 == chan0 and chan0 == 64
    vmem = pl.BlockSpec(memory_space=pltpu.VMEM)
    smem = pl.BlockSpec(memory_space=pltpu.SMEM)
    hbm = pl.BlockSpec(memory_space=pltpu.HBM)
    f32, bf16 = jnp.float32, jnp.bfloat16
    wide, front = half + 2, half + 1
    params = pltpu.CompilerParams(vmem_limit_bytes=32 * 1024 * 1024)
    small = pltpu.CompilerParams(vmem_limit_bytes=8 * 1024 * 1024)
    kernel_one = kernel_one.transpose(0, 1, 3, 2)
    kernel_two = kernel_two.transpose(0, 1, 3, 2)
    down, up = pl.pallas_call(
        functools.partial(edge_kernel, half, chan2),
        in_specs=[hbm] * 3,
        out_specs=[vmem] * 2,
        out_shape=[
            jax.ShapeDtypeStruct((2 * wide, 8, LANES), bf16),
            jax.ShapeDtypeStruct((1, 2 * wide * LANES), bf16),
        ],
        scratch_shapes=[
            pltpu.VMEM((1, 8, span), bf16),
            pltpu.VMEM((1, 8, span), bf16),
            pltpu.VMEM((8, land_words.shape[1]), jnp.int32),
            pltpu.VMEM((8, LANES), jnp.int32),
            pltpu.SemaphoreType.DMA((3,)),
        ],
        compiler_params=pltpu.CompilerParams(vmem_limit_bytes=56 * 1024 * 1024),
        name="edges",
    )(latent, targets, land_words)
    above = shifted(down, "lat", 1)
    below = shifted(up, "lat", -1)
    source, aims, weights = pl.pallas_call(
        functools.partial(prepare_kernel, half, chan0, chan2),
        in_specs=[smem] * 3 + [vmem] * 3,
        out_specs=[vmem] * 3,
        out_shape=[jax.ShapeDtypeStruct((rows, wide, 16, LANES), bf16)]
        + [jax.ShapeDtypeStruct((2 * front, 4 * rows, LANES), f32)] * 2,
        scratch_shapes=[pltpu.VMEM((2 * wide, rows, LANES), f32), pltpu.VMEM((4 * rows, LANES), jnp.int32)],
        compiler_params=small,
        cost_estimate=pl.CostEstimate(flops=10**8, bytes_accessed=10**7, transcendentals=0),
        name="prepare",
    )(member_seeds, noise_scale, channel_weight, latent, targets, land_words)
    one_late, two_late, source = lax.optimization_barrier((kernel_one, kernel_two, source))
    bands = pl.pallas_call(
        bands_kernel,
        in_specs=[vmem] * 2,
        out_specs=[vmem] * 4,
        out_shape=[jax.ShapeDtypeStruct((512, 256), bf16)] * 4,
        compiler_params=small,
        cost_estimate=pl.CostEstimate(flops=10**8, bytes_accessed=10**7, transcendentals=0),
        name="bands",
    )(one_late, two_late)
    norm = 1.0 / math.sqrt(sample_count * 4 * rows * lat_count * targets.shape[2])
    tap_rows = 5 * chan1 + 3 * chan2
    lat_grad, taps, taps_send = pl.pallas_call(
        functools.partial(band_kernel, half, (chan0, chan1, chan2), span, norm),
        in_specs=[smem] * 3 + [vmem] * 9,
        out_specs=[vmem] * 3,
        out_shape=[
            jax.ShapeDtypeStruct((rows, own * LANES), bf16),
            jax.ShapeDtypeStruct((tap_rows // 2, LANES), f32),
            jax.ShapeDtypeStruct((tap_rows // 2, LANES), f32),
        ],
        scratch_shapes=[
            pltpu.VMEM((2 * wide, 8, LANES), f32),
            pltpu.VMEM((2 * front, 8, LANES), f32),
            pltpu.VMEM((2 * front, 8, LANES), f32),
            pltpu.VMEM((rows + 4, wide + 1, 16, LANES), bf16),
            pltpu.VMEM((wide * 16, 2 * LANES), f32),
            pltpu.VMEM((wide * 16, 2 * LANES), f32),
            pltpu.VMEM((2 * rows + 4, wide, 16, LANES), bf16),
            pltpu.VMEM((2 * rows + 4, front, 16, LANES), f32),
            pltpu.VMEM((4, front, 16, LANES), bf16),
            pltpu.VMEM((4, front, 16, LANES), bf16),
            pltpu.VMEM((4, front + 1, 16, LANES), bf16),
            pltpu.VMEM((4, front + 1, 16, LANES), bf16),
            pltpu.VMEM((front * 16, LANES), f32),
            pltpu.VMEM((48, LANES), f32),
            pltpu.VMEM((48 * rows, LANES), f32),
            pltpu.VMEM((tap_rows, LANES), f32),
            pltpu.VMEM((256, 256), f32),
            pltpu.VMEM((2 * chan1, 256), f32),
            pltpu.VMEM((256, 256), f32),
            pltpu.VMEM((2 * chan2, 256), f32),
        ],
        compiler_params=params,
        name="band",
    )(
        member_seeds,
        noise_scale,
        channel_weight,
        source,
        aims,
        weights,
        above,
        below,
        *bands,
    )
    taps = (taps + swapped(taps_send, "lat", 1)).astype(bf16)
    taps = total(taps, "mem", 1, 2)
    one, two, three = (swapped(lat_grad, "mem", k) for k in range(1, 4))
    bits = [1 << k for k in range(1, lat_count.bit_length() - 1)]
    for bit in bits:
        if bit == bits[-1]:
            taps, three = lax.optimization_barrier((taps, three))
        taps = taps + swapped(taps, "lat", bit)
    taps, one, two = lax.optimization_barrier((taps, one, two))
    other = swapped(taps, "lat", 1)
    latent_grad = pl.pallas_call(
        functools.partial(place_kernel, own),
        in_specs=[vmem] * 4,
        out_specs=vmem,
        out_shape=jax.ShapeDtypeStruct((1, rows, span), f32),
        compiler_params=small,
        name="place",
    )(lat_grad, one, two, three)
    one, two = pl.pallas_call(
        taps_kernel,
        in_specs=[vmem] * 2,
        out_specs=[vmem] * 2,
        out_shape=[
            jax.ShapeDtypeStruct(kernel_one.shape, f32),
            jax.ShapeDtypeStruct(kernel_two.shape, f32),
        ],
        scratch_shapes=[pltpu.VMEM((tap_rows, LANES), f32)],
        compiler_params=small,
        name="taps",
    )(taps, other)
    return (latent_grad, one.transpose(0, 1, 3, 2), two.transpose(0, 1, 3, 2))


def solution(mesh):
    in_specs = (P(None, "lat", None), P(), P(), P(), P(), P(None, "lat", None), P("lat", None), P())
    out_specs = (P(None, "lat", None), P(), P())
    return jax.shard_map(local, mesh=mesh, in_specs=in_specs, out_specs=out_specs, check_vma=False)
```

```python
import functools
import math

import jax
import jax.numpy as jnp
from jax import lax
from jax.experimental import pallas as pl
from jax.experimental.pallas import tpu as pltpu
from jax.sharding import PartitionSpec as P

SMOOTH = 0.01
HASH_CELL = 1103515245
HASH_SEED = 747796405
HASH_MIX = 277803737
LANES = 128
MEM = 8
GELU_A = math.sqrt(2.0 / math.pi)
GELU_B = 0.044715


def shifted(array, axis, by):
    peers = lax.axis_size(axis)
    pairs = [(i, i + by) for i in range(peers) if 0 <= i + by < peers]
    return lax.ppermute(array, axis, pairs)


def iota(shape, axis):
    return lax.broadcasted_iota(jnp.int32, shape, axis)


def lane_table(ref, count):
    lane = iota((8, LANES), 1) % count
    total = jnp.zeros((8, LANES), jnp.float32)
    for k in range(count):
        total = jnp.where(lane == k, ref[k], total)
    return total


def build_band(kernel_ref, band_ref):
    chan_out, chan_in = kernel_ref.shape[2], kernel_ref.shape[3]
    cells = LANES // chan_in
    repeat = (iota((chan_out, LANES), 1) % chan_out == iota((chan_out, LANES), 0)).astype(jnp.bfloat16)
    wide = {}
    for a in range(3):
        for b in range(3):
            wide[a, b] = lax.dot_general(
                kernel_ref[a, b], repeat, (((0,), (0,)), ((), ())), preferred_element_type=jnp.float32
            )
    column = iota((chan_in, LANES), 1) // chan_out
    zero = jnp.zeros((chan_in, LANES), jnp.float32)
    for block in range(2):
        for row in range(2):
            for cell in range(cells):
                at = block * 256 + row * LANES + cell * chan_in
                for sub in range(2):
                    a = sub - 2 * row + 1
                    part = zero
                    for q in range(2 * cells):
                        b = q - 2 * (cell + block * cells) + 1
                        if 0 <= a <= 2 and 0 <= b <= 2:
                            part = jnp.where(column == q, wide[a, b], part)
                    band_ref[at : at + chan_in, sub * LANES : (sub + 1) * LANES] = part.astype(jnp.bfloat16)


def build_back(kernel_ref, back_ref):
    chan_out, chan_in = kernel_ref.shape[2], kernel_ref.shape[3]
    cells = LANES // chan_in
    repeat = (iota((chan_in, LANES), 1) % chan_in == iota((chan_in, LANES), 0)).astype(jnp.bfloat16)
    flat = kernel_ref[...].reshape(9 * chan_out, chan_in)
    wide = jnp.dot(flat, repeat, preferred_element_type=jnp.float32)
    column = iota((chan_out, LANES), 1) // chan_in
    zero = jnp.zeros((chan_out, LANES), jnp.float32)
    for block in range(2):
        for sub in range(2):
            for q in range(2 * cells):
                at = block * 256 + sub * LANES + q * chan_out
                for row in range(2):
                    a = sub - 2 * row + 1
                    part = zero
                    for cell in range(cells):
                        b = q - 2 * (cell + block * cells) + 1
                        if 0 <= a <= 2 and 0 <= b <= 2:
                            tap = (3 * a + b) * chan_out
                            part = jnp.where(column == cell, wide[tap : tap + chan_out], part)
                    back_ref[at : at + chan_out, row * LANES : (row + 1) * LANES] = part.astype(jnp.bfloat16)


def pack_taps(acc_ref, next_ref, out_ref, first, chan_in, chan_out, norm):
    cells = LANES // chan_in
    group = iota((chan_out, LANES), 1) // chan_in
    packed = None
    for k in range(9):
        a, b = divmod(k, 3)
        row, sub = ((1, 1), (0, 0), (0, 1))[a]
        slot = k % cells
        part = None
        for reach in range(cells + 1):
            q = 2 * reach + b - 1
            if 0 <= q < 2 * cells:
                block, cell = reach // cells, reach % cells
                lines = sub * LANES + q * chan_out if block == 0 else sub * chan_out
                ref = acc_ref if block == 0 else next_ref
                piece = ref[lines : lines + chan_out, row * LANES : (row + 1) * LANES]
                turn = (slot - cell) % cells * chan_in
                piece = pltpu.roll(piece, turn, 1) if turn else piece
                part = piece if part is None else part + piece
        packed = part if slot == 0 else jnp.where(group == slot, part, packed)
        if slot == cells - 1 or k == 8:
            at = first + k // cells * chan_out
            out_ref[at : at + chan_out, :] = packed * norm


def spread_line(ref, slot, at):
    return jnp.broadcast_to(ref[slot, pl.ds(at, 1), :], (8, LANES))


def window_block(mem_pos, own, half, blocks, part, t):
    at = mem_pos * own + part * half + t + (blocks - 1)
    at = jnp.where(at >= blocks, at - blocks, at)
    return jnp.where(at >= blocks, at - blocks, at)


def land_of(words, block, chan):
    cell = block * (LANES // chan) + iota(words.shape, 1) // chan
    word = jnp.right_shift(cell * 2185, 16)
    picked = jnp.take_along_axis(words, word, axis=1, mode="promise_in_bounds")
    return jnp.bitwise_and(jnp.right_shift(picked, cell - 30 * word), 1).astype(jnp.float32)


def edge_kernel(
    half,
    chan,
    latent_hbm,
    targets_hbm,
    land_hbm,
    down,
    up,
    latent,
    targets,
    land,
    words,
    sems,
):
    rows = latent.shape[1]
    blocks = latent.shape[2] // LANES
    edge = pl.ds(targets_hbm.shape[1] - 8, 8)
    copies = [
        pltpu.make_async_copy(latent_hbm, latent, sems.at[0]),
        pltpu.make_async_copy(targets_hbm.at[:, edge], targets, sems.at[1]),
        pltpu.make_async_copy(land_hbm.at[edge], land, sems.at[2]),
    ]
    for copy in copies:
        copy.start()
    for copy in copies:
        copy.wait()
    own = blocks // lax.axis_size("mem")
    mem_pos = lax.axis_index("mem")
    words[...] = jnp.zeros(words.shape, jnp.int32)
    words[:, : land.shape[1]] = land[...]
    line = iota((8, LANES), 0)
    for t in range(half + 2):
        for part in range(2):
            block = window_block(mem_pos, own, half, blocks, part, t)
            off = pl.multiple_of(block * LANES, LANES)
            slot = t * 2 + part
            cells = latent[0, :, pl.ds(off, LANES)].astype(jnp.float32)
            aims = targets[0, :, pl.ds(off, LANES)].astype(jnp.float32)
            mask = land_of(words[...], block, chan)
            pack = pltpu.roll(cells, 1, 0)
            pack = jnp.where((line >= 1) & (line <= 3), pltpu.roll(aims, 4, 0), pack)
            pack = jnp.where((line >= 4) & (line <= 6), pltpu.roll(mask, 7, 0), pack)
            down[slot] = pack.astype(jnp.bfloat16)
            up[:, slot * LANES : (slot + 1) * LANES] = cells[0:1].astype(jnp.bfloat16)


def place_kernel(own, part0, part1, part2, part3, latent_grad):
    mem_pos = lax.axis_index("mem")
    for k, part in enumerate((part0, part1, part2, part3)):
        off = pl.multiple_of(jnp.bitwise_xor(mem_pos, k) * own * LANES, LANES)
        latent_grad[0, :, pl.ds(off, own * LANES)] = part[...].astype(jnp.float32)


def taps_kernel(mine, other, grad_one, grad_two, taps):
    count = mine.shape[0]
    odd = jnp.bitwise_and(lax.axis_index("lat"), 1)
    taps[pl.ds(pl.multiple_of(odd * count, 8), count), :] = mine[...]
    taps[pl.ds(pl.multiple_of((1 - odd) * count, 8), count), :] = other[...]
    first = 0
    for out in (grad_one, grad_two):
        chan_out, chan_in = out.shape[2], out.shape[3]
        cells = LANES // chan_in
        for k in range(9):
            at = first + k // cells * chan_out
            block = taps[at : at + chan_out, :]
            turn = (-(k % cells)) % cells * chan_in
            block = pltpu.roll(block, turn, 1) if turn else block
            out[k // 3, k % 3] = block[:, :chan_in]
        first += -(-9 // cells) * chan_out


def make_source(i, row, total_rows, span, own, half, seeds, scale, chan, line, store):
    blocks = span // LANES
    mem_pos = lax.axis_index("mem")
    sublane = iota((8, LANES), 0)
    seed_table = jnp.zeros((8, LANES), jnp.int32)
    for m in range(MEM):
        seed_table = jnp.where(sublane == m, seeds[m], seed_table)
    hash_table = iota((8, LANES), 1) * HASH_CELL + seed_table * HASH_SEED
    scale_table = lane_table(scale, chan)
    inside = jnp.where(row < total_rows, 1.0, 0.0).astype(jnp.float32)
    for t in range(half + 2):
        parts = []
        for part in range(2):
            first = (row * span + window_block(mem_pos, own, half, blocks, part, t) * LANES) * HASH_CELL
            h = hash_table + first
            h = jnp.bitwise_xor(h, jnp.right_shift(h, 15))
            h = h * HASH_MIX
            h = jnp.bitwise_xor(h, jnp.right_shift(h, 13))
            noise = jnp.bitwise_and(h, 65535).astype(jnp.float32) * (1.0 / 65536.0) - 0.5
            noise = noise * 3.4641016
            parts.append((line(t * 2 + part, i) + noise * scale_table) * inside)
        store(i, t, jnp.concatenate(parts, axis=0).astype(jnp.bfloat16))


def weight_lines(grid_row, channel_weight, chan, grid_total):
    latitude = math.pi / 2 - math.pi * (grid_row.astype(jnp.float32) + 0.5) / grid_total
    cosine = jnp.where(grid_row >= 0, jnp.cos(latitude), 0.0)
    channels = jnp.tile(lane_table(channel_weight, chan), (grid_row.shape[0] // 8, 1))
    return cosine * (channels * (1.0 / (MEM * (MEM - 1))))


def prepare_kernel(
    half, chan, chan2, seeds, scale, channel_weight, latent, targets, land, source, aims, weights, lines, words
):
    rows, span = latent.shape[1], latent.shape[2]
    blocks = span // LANES
    own = blocks // lax.axis_size("mem")
    total_rows = rows * lax.axis_size("lat")
    lat_pos, mem_pos = lax.axis_index("lat"), lax.axis_index("mem")
    grid_row = iota((4 * rows, LANES), 0) + lat_pos * 4 * rows
    base = weight_lines(grid_row, channel_weight, chan2, 4 * total_rows)
    words[...] = jnp.zeros(words.shape, jnp.int32)
    words[:, : land.shape[1]] = land[...]
    for t in range(half + 2):
        for part in range(2):
            block = window_block(mem_pos, own, half, blocks, part, t)
            off = pl.multiple_of(block * LANES, LANES)
            slot = t * 2 + part
            lines[slot] = latent[0, :, pl.ds(off, LANES)].astype(jnp.float32)
            if t < half + 1:
                aims[slot] = targets[0, :, pl.ds(off, LANES)].astype(jnp.float32)
                weights[slot] = base + base * land_of(words[...], block, chan2)

    def line(slot, i):
        return spread_line(lines, slot, i)

    def store(i, t, value):
        source[i, t] = value

    def step(i, _):
        make_source(
            i, lat_pos * rows + i, total_rows, span, own, half, seeds, scale, chan, line, store
        )
        return 0

    lax.fori_loop(0, rows, step, 0)


def bands_kernel(kernel_one, kernel_two, band_one, band_two, back_one, back_two):
    build_band(kernel_one, band_one)
    build_band(kernel_two, band_two)
    build_back(kernel_one, back_one)
    build_back(kernel_two, back_two)


def take_turns(*parts):
    parts = list(parts)
    while parts:
        for part in tuple(parts):
            if next(part, part) is part:
                parts.remove(part)


def band_kernel(
    half,
    chans,
    span,
    norm,
    seeds,
    scale,
    channel_weight,
    own_source,
    aims,
    weights,
    above,
    below,
    band_one,
    band_two,
    back_one,
    back_two,
    out_lat,
    taps_keep,
    taps_send,
    lat_rows,
    edge_aims,
    edge_weights,
    source,
    pre_even,
    pre_odd,
    act,
    slope,
    cast_even,
    cast_odd,
    fgrad_even,
    fgrad_odd,
    carry,
    carry_lat,
    lat_lines,
    taps,
    acc_one,
    acc_one_next,
    acc_two,
    acc_two_next,
):
    rows = own_source.shape[0]
    blocks = span // LANES
    own = blocks // lax.axis_size("mem")
    total_rows = rows * lax.axis_size("lat")
    lat_pos = lax.axis_index("lat")
    wide = half + 2
    front = half + 1
    chan0, chan1, chan2 = chans
    f32, bf16 = jnp.float32, jnp.bfloat16

    grid_row = iota((8, LANES), 0) + (lat_pos * 4 * rows - 4)
    base = weight_lines(grid_row, channel_weight, chan2, 4 * total_rows)
    for slot in range(2 * wide):
        edge = above[slot].astype(f32)
        lat_rows[slot, 0:1] = edge[0:1]
        lat_rows[slot, 1:2] = below[:, slot * LANES : (slot + 1) * LANES].astype(f32)
        if slot < 2 * front:
            edge_aims[slot] = edge
            edge_weights[slot] = base + base * pltpu.roll(edge, 5, 0)

    source[rows + 2 :] = jnp.zeros((2,) + source.shape[1:], bf16)
    source[:, wide] = jnp.zeros((source.shape[0],) + source.shape[2:], bf16)
    fgrad_even[0] = jnp.zeros(fgrad_even.shape[1:], bf16)
    for fgrad in (fgrad_even, fgrad_odd):
        fgrad[:, 0] = jnp.zeros((4,) + fgrad.shape[2:], bf16)
    carry[...] = jnp.zeros(carry.shape, f32)
    carry_lat[...] = jnp.zeros(carry_lat.shape, f32)
    for acc in (acc_one, acc_one_next, acc_two, acc_two_next):
        acc[...] = jnp.zeros(acc.shape, f32)

    def line(slot, i):
        return spread_line(lat_rows, slot, i)

    def store(i, t, value):
        source[i * (rows + 1), t] = value

    def edge_source(i, _):
        row = lat_pos * rows - 1 + i * (rows + 1)
        make_source(i, row, total_rows, span, own, half, seeds, scale, chan0, line, store)
        return 0

    lax.fori_loop(0, 2, edge_source, 0)
    source[1 : rows + 1, 0:wide] = own_source[...]

    def operand(ref, i, start, count):
        def piece(r, at):
            return ref[r, pl.ds(at, count)].reshape(count * 16, LANES)

        return jnp.concatenate(
            [piece(i, start), piece(i + 1, start), piece(i, start + 1), piece(i + 1, start + 1)], axis=1
        )

    def first_product(pair, pre):
        taken = jnp.concatenate([operand(source, 2 * pair + k, 0, wide) for k in range(2)], axis=0)
        pre[...] = jnp.dot(taken, band_one[...], preferred_element_type=f32)

    def first_gelu(pair, pre):
        for k in range(2):
            for t in range(wide):
                for sub in range(2):
                    at = (k * wide + t) * 16
                    x = pre[at : at + 16, sub * LANES : (sub + 1) * LANES]
                    square = x * x
                    th = jnp.tanh(x * (GELU_A + (GELU_A * GELU_B) * square))
                    plus = 0.5 + 0.5 * th
                    act[4 * pair + 2 * k + sub, t] = (x * plus).astype(bf16)
                    if t < front:
                        d = plus + (x * plus) * (1.0 - th) * (GELU_A + (3.0 * GELU_A * GELU_B) * square)
                        if t == half:
                            d = jnp.where(iota((16, LANES), 0) < 8, d, 0.0)
                        slope[4 * pair + 2 * k + sub, t] = d

    def first_segment(m, _):
        first_product(2 * m + 1, pre_odd)
        first_gelu(2 * m, pre_even)
        first_product(2 * m + 2, pre_even)
        first_gelu(2 * m + 1, pre_odd)
        return 0

    first_product(0, pre_even)
    lax.fori_loop(0, rows // 4, first_segment, 0)
    first_gelu(rows // 2, pre_even)

    members = front * 16
    owner = iota((48, members), 0)
    group = iota((48, members), 1) // 8
    place = (group % 2) * half + group // 2
    real = (group // 2 > 0) & (place - 1 < own)
    pick_own = (real & (place - 1 == owner)).astype(bf16)
    pick_prev = ((group // 2 < half) & (place == owner)).astype(bf16)
    pick = jnp.concatenate([pick_own, pick_prev], axis=0)

    def second_product(n, cast):
        taken = jnp.concatenate([operand(act, 2 * n + k, 0, front) for k in range(2)], axis=0)
        out = jnp.dot(taken, band_two[...], preferred_element_type=f32).astype(bf16)
        for k in range(2):
            for sub in range(2):
                part = out[k * members : (k + 1) * members, sub * LANES : (sub + 1) * LANES]
                cast[2 * k + sub] = part.reshape(front, 16, LANES)
        yield

    def loss_gradient(cast, fgrad, aim_ref, weight_ref, first, lines):
        for line in lines:
            for t in range(front):
                both = cast[line, t].astype(f32)
                parts = []
                for part in range(2):
                    if t == half and part == 1:
                        parts.append(jnp.zeros((8, LANES), f32))
                        continue
                    f = both[part * 8 : part * 8 + 8]
                    d = f - spread_line(aim_ref, t * 2 + part, first + line)
                    goal = d * lax.rsqrt(d * d + SMOOTH)
                    gs = []
                    for k in range(1, 5):
                        d = f - pltpu.roll(f, k, 0)
                        gs.append(d * lax.rsqrt(d * d + SMOOTH))
                    back = gs[2]
                    for k in (1, 0):
                        back = gs[k] + pltpu.roll(back, MEM - 1, 0)
                    back = pltpu.roll(back, MEM - 1, 0)
                    spread = (gs[0] + gs[1]) + (gs[2] + gs[3]) - back
                    weight = spread_line(weight_ref, t * 2 + part, first + line)
                    parts.append(weight * ((MEM - 1.0) * goal - spread))
                fgrad[line, t + 1] = jnp.concatenate(parts, axis=0).astype(bf16)
            yield

    def pull_back(n, fgrad, with_taps=True):
        def flat(line, start, count):
            return fgrad[line, start : start + count].reshape(count * 16, LANES)

        def add_taps(g, x, acc, acc_next, chan_out):
            turned = g.T
            acc[...] += jnp.dot(turned, x[:, :256], preferred_element_type=f32)
            last = [turned[k * LANES - chan_out : k * LANES] for k in (1, 2)]
            last = jnp.concatenate(last, axis=0)
            acc_next[...] += jnp.dot(last, x[:, 256:], preferred_element_type=f32)

        g = [
            jnp.concatenate(
                [flat(2 * k, 1, front), flat(2 * k + 1, 1, front), flat(2 * k, 0, front), flat(2 * k + 1, 0, front)],
                axis=1,
            )
            for k in range(2)
        ]
        pulled = jnp.dot(jnp.concatenate(g, axis=0), back_two[...], preferred_element_type=f32)
        grads = [
            pulled[:members, :LANES] + carry[...],
            pulled[members:, :LANES] + pulled[:members, LANES:],
        ]
        carry[...] = pulled[members:, LANES:]
        grads = [(grads[k] * slope[2 * n + k].reshape(members, LANES)).astype(bf16) for k in range(2)]
        yield
        grads = jnp.concatenate(grads, axis=1)
        g = [jnp.concatenate([flat(2 * k, 2, half), flat(2 * k + 1, 2, half)], axis=1) for k in range(2)]
        x = [operand(act, 2 * n + k, 1, half) for k in range(2)]
        if with_taps:
            add_taps(jnp.concatenate(g, axis=0), jnp.concatenate(x, axis=0), acc_two, acc_two_next, chan2)
            yield
            add_taps(grads[16:], operand(source, n, 1, half), acc_one, acc_one_next, chan1)
            yield
        z = jnp.dot(pick, grads, preferred_element_type=f32)
        z = jnp.concatenate([z[:48], z[48:]], axis=1)
        high = z.astype(bf16)
        z = jnp.concatenate([high, (z - high.astype(f32)).astype(bf16)], axis=0)
        z = jnp.dot(z, back_one[...], preferred_element_type=f32)
        z = z[:48] + z[48:]
        lat_lines[pl.ds(jnp.maximum(n - 1, 0), 48, stride=rows), :] = z[:, :LANES] + carry_lat[...]
        carry_lat[...] = z[:, LANES:]
        yield

    def own_gradient(n, cast, fgrad):
        return loss_gradient(cast, fgrad, aims, weights, 4 * (n - 1), range(4))

    def second_segment(m, _):
        take_turns(
            second_product(2 * m + 3, cast_odd),
            own_gradient(2 * m + 2, cast_even, fgrad_even),
            pull_back(2 * m + 1, fgrad_odd),
        )
        take_turns(
            second_product(2 * m + 4, cast_even),
            own_gradient(2 * m + 3, cast_odd, fgrad_odd),
            pull_back(2 * m + 2, fgrad_even),
        )
        return 0

    take_turns(second_product(0, cast_even))
    take_turns(
        second_product(1, cast_odd),
        loss_gradient(cast_even, fgrad_even, edge_aims, edge_weights, 0, range(1, 4)),
    )
    take_turns(
        second_product(2, cast_even),
        own_gradient(1, cast_odd, fgrad_odd),
        pull_back(0, fgrad_even, with_taps=False),
    )
    lax.fori_loop(0, rows // 2 - 1, second_segment, 0)
    take_turns(own_gradient(rows, cast_even, fgrad_even), pull_back(rows - 1, fgrad_odd))
    take_turns(pull_back(rows, fgrad_even))

    for t in range(own):
        out_lat[:, t * LANES : (t + 1) * LANES] = lat_lines[t * rows : (t + 1) * rows].astype(bf16)
    pack_taps(acc_one, acc_one_next, taps, 0, chan0, chan1, norm)
    pack_taps(acc_two, acc_two_next, taps, -(-9 // (LANES // chan0)) * chan1, chan1, chan2, norm)
    count = taps_keep.shape[0]
    odd = jnp.bitwise_and(lat_pos, 1)
    taps_keep[...] = taps[pl.ds(pl.multiple_of(odd * count, 8), count), :]
    taps_send[...] = taps[pl.ds(pl.multiple_of((1 - odd) * count, 8), count), :]


def swapped(array, axis, bit):
    return lax.ppermute(array, axis, [(i, i ^ bit) for i in range(lax.axis_size(axis))])


def total(array, axis, first, second):
    one, two, three = (swapped(array, axis, k).astype(jnp.float32) for k in (first, second, first ^ second))
    return (array.astype(jnp.float32) + one) + (two + three)


def local(
    latent, member_seeds, noise_scale, kernel_one, kernel_two, targets, land_words, channel_weight
):
    sample_count, rows, span = latent.shape
    chan0, chan1, chan2 = kernel_one.shape[2], kernel_one.shape[3], kernel_two.shape[3]
    lat_count = lax.axis_size("lat")
    own = span // LANES // lax.axis_size("mem")
    half = (own + 1) // 2
    assert sample_count == 1 and member_seeds.shape[0] == MEM and rows % 4 == 0 and own % 2 == 1 and lax.axis_size("mem") == 4
    assert 4 * chan2 == 2 * chan1 == chan0 and chan0 == 64
    vmem = pl.BlockSpec(memory_space=pltpu.VMEM)
    smem = pl.BlockSpec(memory_space=pltpu.SMEM)
    hbm = pl.BlockSpec(memory_space=pltpu.HBM)
    f32, bf16 = jnp.float32, jnp.bfloat16
    wide, front = half + 2, half + 1
    params = pltpu.CompilerParams(vmem_limit_bytes=32 * 1024 * 1024)
    small = pltpu.CompilerParams(vmem_limit_bytes=8 * 1024 * 1024)
    kernel_one = kernel_one.transpose(0, 1, 3, 2)
    kernel_two = kernel_two.transpose(0, 1, 3, 2)
    down, up = pl.pallas_call(
        functools.partial(edge_kernel, half, chan2),
        in_specs=[hbm] * 3,
        out_specs=[vmem] * 2,
        out_shape=[
            jax.ShapeDtypeStruct((2 * wide, 8, LANES), bf16),
            jax.ShapeDtypeStruct((1, 2 * wide * LANES), bf16),
        ],
        scratch_shapes=[
            pltpu.VMEM((1, 8, span), bf16),
            pltpu.VMEM((1, 8, span), bf16),
            pltpu.VMEM((8, land_words.shape[1]), jnp.int32),
            pltpu.VMEM((8, LANES), jnp.int32),
            pltpu.SemaphoreType.DMA((3,)),
        ],
        compiler_params=pltpu.CompilerParams(vmem_limit_bytes=56 * 1024 * 1024),
        name="edges",
    )(latent, targets, land_words)
    above = shifted(down, "lat", 1)
    below = shifted(up, "lat", -1)
    source, aims, weights = pl.pallas_call(
        functools.partial(prepare_kernel, half, chan0, chan2),
        in_specs=[smem] * 3 + [vmem] * 3,
        out_specs=[vmem] * 3,
        out_shape=[jax.ShapeDtypeStruct((rows, wide, 16, LANES), bf16)]
        + [jax.ShapeDtypeStruct((2 * front, 4 * rows, LANES), f32)] * 2,
        scratch_shapes=[pltpu.VMEM((2 * wide, rows, LANES), f32), pltpu.VMEM((4 * rows, LANES), jnp.int32)],
        compiler_params=small,
        cost_estimate=pl.CostEstimate(flops=10**8, bytes_accessed=10**7, transcendentals=0),
        name="prepare",
    )(member_seeds, noise_scale, channel_weight, latent, targets, land_words)
    one_late, two_late, source = lax.optimization_barrier((kernel_one, kernel_two, source))
    bands = pl.pallas_call(
        bands_kernel,
        in_specs=[vmem] * 2,
        out_specs=[vmem] * 4,
        out_shape=[jax.ShapeDtypeStruct((512, 256), bf16)] * 4,
        compiler_params=small,
        cost_estimate=pl.CostEstimate(flops=10**8, bytes_accessed=10**7, transcendentals=0),
        name="bands",
    )(one_late, two_late)
    norm = 1.0 / math.sqrt(sample_count * 4 * rows * lat_count * targets.shape[2])
    tap_rows = 5 * chan1 + 3 * chan2
    lat_grad, taps, taps_send = pl.pallas_call(
        functools.partial(band_kernel, half, (chan0, chan1, chan2), span, norm),
        in_specs=[smem] * 3 + [vmem] * 9,
        out_specs=[vmem] * 3,
        out_shape=[
            jax.ShapeDtypeStruct((rows, own * LANES), bf16),
            jax.ShapeDtypeStruct((tap_rows // 2, LANES), f32),
            jax.ShapeDtypeStruct((tap_rows // 2, LANES), f32),
        ],
        scratch_shapes=[
            pltpu.VMEM((2 * wide, 8, LANES), f32),
            pltpu.VMEM((2 * front, 8, LANES), f32),
            pltpu.VMEM((2 * front, 8, LANES), f32),
            pltpu.VMEM((rows + 4, wide + 1, 16, LANES), bf16),
            pltpu.VMEM((wide * 32, 2 * LANES), f32),
            pltpu.VMEM((wide * 32, 2 * LANES), f32),
            pltpu.VMEM((2 * rows + 4, wide, 16, LANES), bf16),
            pltpu.VMEM((2 * rows + 4, front, 16, LANES), f32),
            pltpu.VMEM((4, front, 16, LANES), bf16),
            pltpu.VMEM((4, front, 16, LANES), bf16),
            pltpu.VMEM((4, front + 1, 16, LANES), bf16),
            pltpu.VMEM((4, front + 1, 16, LANES), bf16),
            pltpu.VMEM((front * 16, LANES), f32),
            pltpu.VMEM((48, LANES), f32),
            pltpu.VMEM((48 * rows, LANES), f32),
            pltpu.VMEM((tap_rows, LANES), f32),
            pltpu.VMEM((256, 256), f32),
            pltpu.VMEM((2 * chan1, 256), f32),
            pltpu.VMEM((256, 256), f32),
            pltpu.VMEM((2 * chan2, 256), f32),
        ],
        compiler_params=params,
        name="band",
    )(
        member_seeds,
        noise_scale,
        channel_weight,
        source,
        aims,
        weights,
        above,
        below,
        *bands,
    )
    taps = (taps + swapped(taps_send, "lat", 1)).astype(bf16)
    taps = total(taps, "mem", 1, 2)
    one, two, three = (swapped(lat_grad, "mem", k) for k in range(1, 4))
    bits = [1 << k for k in range(1, lat_count.bit_length() - 1)]
    for bit in bits:
        if bit == bits[-1]:
            taps, one, three = lax.optimization_barrier((taps, one, three))
        taps = taps + swapped(taps, "lat", bit)
    taps, two = lax.optimization_barrier((taps, two))
    other = swapped(taps, "lat", 1)
    latent_grad = pl.pallas_call(
        functools.partial(place_kernel, own),
        in_specs=[vmem] * 4,
        out_specs=vmem,
        out_shape=jax.ShapeDtypeStruct((1, rows, span), f32),
        compiler_params=small,
        name="place",
    )(lat_grad, one, two, three)
    one, two = pl.pallas_call(
        taps_kernel,
        in_specs=[vmem] * 2,
        out_specs=[vmem] * 2,
        out_shape=[
            jax.ShapeDtypeStruct(kernel_one.shape, f32),
            jax.ShapeDtypeStruct(kernel_two.shape, f32),
        ],
        scratch_shapes=[pltpu.VMEM((tap_rows, LANES), f32)],
        compiler_params=small,
        name="taps",
    )(taps, other)
    return (latent_grad, one.transpose(0, 1, 3, 2), two.transpose(0, 1, 3, 2))


def solution(mesh):
    in_specs = (P(None, "lat", None), P(), P(), P(), P(), P(None, "lat", None), P("lat", None), P())
    out_specs = (P(None, "lat", None), P(), P())
    return jax.shard_map(local, mesh=mesh, in_specs=in_specs, out_specs=out_specs, check_vma=False)
```

```python
import functools
import math

import jax
import jax.numpy as jnp
from jax import lax
from jax.experimental import pallas as pl
from jax.experimental.pallas import tpu as pltpu
from jax.sharding import PartitionSpec as P

SMOOTH = 0.01
HASH_CELL = 1103515245
HASH_SEED = 747796405
HASH_MIX = 277803737
LANES = 128
MEM = 8
GELU_A = math.sqrt(2.0 / math.pi)
GELU_B = 0.044715


def shifted(array, axis, by):
    peers = lax.axis_size(axis)
    pairs = [(i, i + by) for i in range(peers) if 0 <= i + by < peers]
    return lax.ppermute(array, axis, pairs)


def iota(shape, axis):
    return lax.broadcasted_iota(jnp.int32, shape, axis)


def lane_table(ref, count):
    lane = iota((8, LANES), 1) % count
    total = jnp.zeros((8, LANES), jnp.float32)
    for k in range(count):
        total = jnp.where(lane == k, ref[k], total)
    return total


def build_band(kernel_ref, band_ref):
    chan_out, chan_in = kernel_ref.shape[2], kernel_ref.shape[3]
    cells = LANES // chan_in
    repeat = (iota((chan_out, LANES), 1) % chan_out == iota((chan_out, LANES), 0)).astype(jnp.bfloat16)
    wide = {}
    for a in range(3):
        for b in range(3):
            wide[a, b] = lax.dot_general(
                kernel_ref[a, b], repeat, (((0,), (0,)), ((), ())), preferred_element_type=jnp.float32
            )
    column = iota((chan_in, LANES), 1) // chan_out
    zero = jnp.zeros((chan_in, LANES), jnp.float32)
    for block in range(2):
        for row in range(2):
            for cell in range(cells):
                at = block * 256 + row * LANES + cell * chan_in
                for sub in range(2):
                    a = sub - 2 * row + 1
                    part = zero
                    for q in range(2 * cells):
                        b = q - 2 * (cell + block * cells) + 1
                        if 0 <= a <= 2 and 0 <= b <= 2:
                            part = jnp.where(column == q, wide[a, b], part)
                    band_ref[at : at + chan_in, sub * LANES : (sub + 1) * LANES] = part.astype(jnp.bfloat16)


def build_back(kernel_ref, back_ref):
    chan_out, chan_in = kernel_ref.shape[2], kernel_ref.shape[3]
    cells = LANES // chan_in
    repeat = (iota((chan_in, LANES), 1) % chan_in == iota((chan_in, LANES), 0)).astype(jnp.bfloat16)
    flat = kernel_ref[...].reshape(9 * chan_out, chan_in)
    wide = jnp.dot(flat, repeat, preferred_element_type=jnp.float32)
    column = iota((chan_out, LANES), 1) // chan_in
    zero = jnp.zeros((chan_out, LANES), jnp.float32)
    for block in range(2):
        for sub in range(2):
            for q in range(2 * cells):
                at = block * 256 + sub * LANES + q * chan_out
                for row in range(2):
                    a = sub - 2 * row + 1
                    part = zero
                    for cell in range(cells):
                        b = q - 2 * (cell + block * cells) + 1
                        if 0 <= a <= 2 and 0 <= b <= 2:
                            tap = (3 * a + b) * chan_out
                            part = jnp.where(column == cell, wide[tap : tap + chan_out], part)
                    back_ref[at : at + chan_out, row * LANES : (row + 1) * LANES] = part.astype(jnp.bfloat16)


def pack_taps(acc_ref, next_ref, out_ref, first, chan_in, chan_out, norm):
    cells = LANES // chan_in
    group = iota((chan_out, LANES), 1) // chan_in
    packed = None
    for k in range(9):
        a, b = divmod(k, 3)
        row, sub = ((1, 1), (0, 0), (0, 1))[a]
        slot = k % cells
        part = None
        for reach in range(cells + 1):
            q = 2 * reach + b - 1
            if 0 <= q < 2 * cells:
                block, cell = reach // cells, reach % cells
                lines = sub * LANES + q * chan_out if block == 0 else sub * chan_out
                ref = acc_ref if block == 0 else next_ref
                piece = ref[lines : lines + chan_out, row * LANES : (row + 1) * LANES]
                turn = (slot - cell) % cells * chan_in
                piece = pltpu.roll(piece, turn, 1) if turn else piece
                part = piece if part is None else part + piece
        packed = part if slot == 0 else jnp.where(group == slot, part, packed)
        if slot == cells - 1 or k == 8:
            at = first + k // cells * chan_out
            out_ref[at : at + chan_out, :] = packed * norm


def spread_line(ref, slot, at):
    return jnp.broadcast_to(ref[slot, pl.ds(at, 1), :], (8, LANES))


def window_block(mem_pos, own, half, blocks, part, t):
    at = mem_pos * own + part * half + t + (blocks - 1)
    at = jnp.where(at >= blocks, at - blocks, at)
    return jnp.where(at >= blocks, at - blocks, at)


def land_of(words, block, chan):
    cell = block * (LANES // chan) + iota(words.shape, 1) // chan
    word = jnp.right_shift(cell * 2185, 16)
    picked = jnp.take_along_axis(words, word, axis=1, mode="promise_in_bounds")
    return jnp.bitwise_and(jnp.right_shift(picked, cell - 30 * word), 1).astype(jnp.float32)


def edge_kernel(
    half,
    chan,
    latent_hbm,
    targets_hbm,
    land_hbm,
    down,
    up,
    latent,
    targets,
    land,
    words,
    sems,
):
    rows = latent.shape[1]
    blocks = latent.shape[2] // LANES
    edge = pl.ds(targets_hbm.shape[1] - 8, 8)
    copies = [
        pltpu.make_async_copy(latent_hbm, latent, sems.at[0]),
        pltpu.make_async_copy(targets_hbm.at[:, edge], targets, sems.at[1]),
        pltpu.make_async_copy(land_hbm.at[edge], land, sems.at[2]),
    ]
    for copy in copies:
        copy.start()
    for copy in copies:
        copy.wait()
    own = blocks // lax.axis_size("mem")
    mem_pos = lax.axis_index("mem")
    words[...] = jnp.zeros(words.shape, jnp.int32)
    words[:, : land.shape[1]] = land[...]
    line = iota((8, LANES), 0)
    for t in range(half + 2):
        for part in range(2):
            block = window_block(mem_pos, own, half, blocks, part, t)
            off = pl.multiple_of(block * LANES, LANES)
            slot = t * 2 + part
            cells = latent[0, :, pl.ds(off, LANES)].astype(jnp.float32)
            aims = targets[0, :, pl.ds(off, LANES)].astype(jnp.float32)
            mask = land_of(words[...], block, chan)
            pack = pltpu.roll(cells, 1, 0)
            pack = jnp.where((line >= 1) & (line <= 3), pltpu.roll(aims, 4, 0), pack)
            pack = jnp.where((line >= 4) & (line <= 6), pltpu.roll(mask, 7, 0), pack)
            down[slot] = pack.astype(jnp.bfloat16)
            up[:, slot * LANES : (slot + 1) * LANES] = cells[0:1].astype(jnp.bfloat16)


def place_kernel(own, part0, part1, part2, part3, latent_grad):
    mem_pos = lax.axis_index("mem")
    for k, part in enumerate((part0, part1, part2, part3)):
        off = pl.multiple_of(jnp.bitwise_xor(mem_pos, k) * own * LANES, LANES)
        latent_grad[0, :, pl.ds(off, own * LANES)] = part[...].astype(jnp.float32)


def taps_kernel(mine, other, grad_one, grad_two, taps):
    count = mine.shape[0]
    odd = jnp.bitwise_and(lax.axis_index("lat"), 1)
    taps[pl.ds(pl.multiple_of(odd * count, 8), count), :] = mine[...]
    taps[pl.ds(pl.multiple_of((1 - odd) * count, 8), count), :] = other[...]
    first = 0
    for out in (grad_one, grad_two):
        chan_out, chan_in = out.shape[2], out.shape[3]
        cells = LANES // chan_in
        for k in range(9):
            at = first + k // cells * chan_out
            block = taps[at : at + chan_out, :]
            turn = (-(k % cells)) % cells * chan_in
            block = pltpu.roll(block, turn, 1) if turn else block
            out[k // 3, k % 3] = block[:, :chan_in]
        first += -(-9 // cells) * chan_out


def make_source(i, row, total_rows, span, own, half, seeds, scale, chan, line, store):
    blocks = span // LANES
    mem_pos = lax.axis_index("mem")
    sublane = iota((8, LANES), 0)
    seed_table = jnp.zeros((8, LANES), jnp.int32)
    for m in range(MEM):
        seed_table = jnp.where(sublane == m, seeds[m], seed_table)
    hash_table = iota((8, LANES), 1) * HASH_CELL + seed_table * HASH_SEED
    scale_table = lane_table(scale, chan)
    inside = jnp.where(row < total_rows, 1.0, 0.0).astype(jnp.float32)
    for t in range(half + 2):
        parts = []
        for part in range(2):
            first = (row * span + window_block(mem_pos, own, half, blocks, part, t) * LANES) * HASH_CELL
            h = hash_table + first
            h = jnp.bitwise_xor(h, jnp.right_shift(h, 15))
            h = h * HASH_MIX
            h = jnp.bitwise_xor(h, jnp.right_shift(h, 13))
            noise = jnp.bitwise_and(h, 65535).astype(jnp.float32) * (1.0 / 65536.0) - 0.5
            noise = noise * 3.4641016
            parts.append((line(t * 2 + part, i) + noise * scale_table) * inside)
        store(i, t, jnp.concatenate(parts, axis=0).astype(jnp.bfloat16))


def weight_lines(grid_row, channel_weight, chan, grid_total):
    latitude = math.pi / 2 - math.pi * (grid_row.astype(jnp.float32) + 0.5) / grid_total
    cosine = jnp.where(grid_row >= 0, jnp.cos(latitude), 0.0)
    channels = jnp.tile(lane_table(channel_weight, chan), (grid_row.shape[0] // 8, 1))
    return cosine * (channels * (1.0 / (MEM * (MEM - 1))))


def prepare_kernel(
    half, chan, chan2, seeds, scale, channel_weight, latent, targets, land, source, aims, weights, lines, words
):
    rows, span = latent.shape[1], latent.shape[2]
    blocks = span // LANES
    own = blocks // lax.axis_size("mem")
    total_rows = rows * lax.axis_size("lat")
    lat_pos, mem_pos = lax.axis_index("lat"), lax.axis_index("mem")
    grid_row = iota((4 * rows, LANES), 0) + lat_pos * 4 * rows
    base = weight_lines(grid_row, channel_weight, chan2, 4 * total_rows)
    words[...] = jnp.zeros(words.shape, jnp.int32)
    words[:, : land.shape[1]] = land[...]
    for t in range(half + 2):
        for part in range(2):
            block = window_block(mem_pos, own, half, blocks, part, t)
            off = pl.multiple_of(block * LANES, LANES)
            slot = t * 2 + part
            lines[slot] = latent[0, :, pl.ds(off, LANES)].astype(jnp.float32)
            if t < half + 1:
                aims[slot] = targets[0, :, pl.ds(off, LANES)].astype(jnp.float32)
                weights[slot] = base + base * land_of(words[...], block, chan2)

    def line(slot, i):
        return spread_line(lines, slot, i)

    def store(i, t, value):
        source[i, t] = value

    def step(i, _):
        make_source(
            i, lat_pos * rows + i, total_rows, span, own, half, seeds, scale, chan, line, store
        )
        return 0

    lax.fori_loop(0, rows, step, 0)


def bands_kernel(kernel_one, kernel_two, band_one, band_two, back_one, back_two):
    build_band(kernel_one, band_one)
    build_band(kernel_two, band_two)
    build_back(kernel_one, back_one)
    build_back(kernel_two, back_two)


def take_turns(*parts):
    parts = list(parts)
    while parts:
        for part in tuple(parts):
            if next(part, part) is part:
                parts.remove(part)


def band_kernel(
    half,
    chans,
    span,
    norm,
    seeds,
    scale,
    channel_weight,
    own_source,
    aims,
    weights,
    above,
    below,
    band_one,
    band_two,
    back_one,
    back_two,
    out_lat,
    taps_keep,
    taps_send,
    lat_rows,
    edge_aims,
    edge_weights,
    source,
    pre_even,
    pre_odd,
    act,
    slope,
    cast_even,
    cast_odd,
    fgrad_even,
    fgrad_odd,
    carry,
    sums,
    lat_lines,
    taps,
    acc_one,
    acc_one_next,
    acc_two,
    acc_two_next,
):
    rows = own_source.shape[0]
    blocks = span // LANES
    own = blocks // lax.axis_size("mem")
    total_rows = rows * lax.axis_size("lat")
    lat_pos = lax.axis_index("lat")
    wide = half + 2
    front = half + 1
    chan0, chan1, chan2 = chans
    f32, bf16 = jnp.float32, jnp.bfloat16

    grid_row = iota((8, LANES), 0) + (lat_pos * 4 * rows - 4)
    base = weight_lines(grid_row, channel_weight, chan2, 4 * total_rows)
    for slot in range(2 * wide):
        edge = above[slot].astype(f32)
        lat_rows[slot, 0:1] = edge[0:1]
        lat_rows[slot, 1:2] = below[:, slot * LANES : (slot + 1) * LANES].astype(f32)
        if slot < 2 * front:
            edge_aims[slot] = edge
            edge_weights[slot] = base + base * pltpu.roll(edge, 5, 0)

    source[rows + 2 :] = jnp.zeros((2,) + source.shape[1:], bf16)
    source[:, wide] = jnp.zeros((source.shape[0],) + source.shape[2:], bf16)
    fgrad_even[0] = jnp.zeros(fgrad_even.shape[1:], bf16)
    for fgrad in (fgrad_even, fgrad_odd):
        fgrad[:, 0] = jnp.zeros((4,) + fgrad.shape[2:], bf16)
    carry[...] = jnp.zeros(carry.shape, f32)
    for acc in (acc_one, acc_one_next, acc_two, acc_two_next):
        acc[...] = jnp.zeros(acc.shape, f32)

    def line(slot, i):
        return spread_line(lat_rows, slot, i)

    def store(i, t, value):
        source[i * (rows + 1), t] = value

    def edge_source(i, _):
        row = lat_pos * rows - 1 + i * (rows + 1)
        make_source(i, row, total_rows, span, own, half, seeds, scale, chan0, line, store)
        return 0

    lax.fori_loop(0, 2, edge_source, 0)
    source[1 : rows + 1, 0:wide] = own_source[...]

    def operand(ref, i, start, count):
        def piece(r, at):
            return ref[r, pl.ds(at, count)].reshape(count * 16, LANES)

        return jnp.concatenate(
            [piece(i, start), piece(i + 1, start), piece(i, start + 1), piece(i + 1, start + 1)], axis=1
        )

    def first_product(pair, pre):
        taken = jnp.concatenate([operand(source, 2 * pair + k, 0, wide) for k in range(2)], axis=0)
        pre[...] = jnp.dot(taken, band_one[...], preferred_element_type=f32)

    def first_gelu(pair, pre):
        for k in range(2):
            for t in range(wide):
                for sub in range(2):
                    at = (k * wide + t) * 16
                    x = pre[at : at + 16, sub * LANES : (sub + 1) * LANES]
                    square = x * x
                    th = jnp.tanh(x * (GELU_A + (GELU_A * GELU_B) * square))
                    plus = 0.5 + 0.5 * th
                    act[4 * pair + 2 * k + sub, t] = (x * plus).astype(bf16)
                    if t < front:
                        d = plus + (x * plus) * (1.0 - th) * (GELU_A + (3.0 * GELU_A * GELU_B) * square)
                        if t == half:
                            d = jnp.where(iota((16, LANES), 0) < 8, d, 0.0)
                        slope[4 * pair + 2 * k + sub, t] = d

    def first_segment(m, _):
        first_product(2 * m + 1, pre_odd)
        first_gelu(2 * m, pre_even)
        first_product(2 * m + 2, pre_even)
        first_gelu(2 * m + 1, pre_odd)
        return 0

    first_product(0, pre_even)
    lax.fori_loop(0, rows // 4, first_segment, 0)
    first_gelu(rows // 2, pre_even)

    members = front * 16
    owner = iota((48, members), 0)
    group = iota((48, members), 1) // 8
    place = (group % 2) * half + group // 2
    real = (group // 2 > 0) & (place - 1 < own)
    pick_own = (real & (place - 1 == owner)).astype(bf16)
    pick_prev = ((group // 2 < half) & (place == owner)).astype(bf16)
    pick = jnp.concatenate([pick_own, pick_prev], axis=0)

    def second_product(n, cast):
        taken = jnp.concatenate([operand(act, 2 * n + k, 0, front) for k in range(2)], axis=0)
        out = jnp.dot(taken, band_two[...], preferred_element_type=f32).astype(bf16)
        for k in range(2):
            for sub in range(2):
                part = out[k * members : (k + 1) * members, sub * LANES : (sub + 1) * LANES]
                cast[2 * k + sub] = part.reshape(front, 16, LANES)
        yield

    def loss_gradient(cast, fgrad, aim_ref, weight_ref, first, lines):
        for line in lines:
            for t in range(front):
                both = cast[line, t].astype(f32)
                parts = []
                for part in range(2):
                    if t == half and part == 1:
                        parts.append(jnp.zeros((8, LANES), f32))
                        continue
                    f = both[part * 8 : part * 8 + 8]
                    d = f - spread_line(aim_ref, t * 2 + part, first + line)
                    goal = d * lax.rsqrt(d * d + SMOOTH)
                    gs = []
                    for k in range(1, 5):
                        d = f - pltpu.roll(f, k, 0)
                        gs.append(d * lax.rsqrt(d * d + SMOOTH))
                    back = gs[2]
                    for k in (1, 0):
                        back = gs[k] + pltpu.roll(back, MEM - 1, 0)
                    back = pltpu.roll(back, MEM - 1, 0)
                    spread = (gs[0] + gs[1]) + (gs[2] + gs[3]) - back
                    weight = spread_line(weight_ref, t * 2 + part, first + line)
                    parts.append(weight * ((MEM - 1.0) * goal - spread))
                fgrad[line, t + 1] = jnp.concatenate(parts, axis=0).astype(bf16)
            yield

    def pull_back(n, fgrad, with_taps=True):
        def flat(line, start, count):
            return fgrad[line, start : start + count].reshape(count * 16, LANES)

        def add_taps(g, x, acc, acc_next, chan_out):
            turned = g.T
            acc[...] += jnp.dot(turned, x[:, :256], preferred_element_type=f32)
            last = [turned[k * LANES - chan_out : k * LANES] for k in (1, 2)]
            last = jnp.concatenate(last, axis=0)
            acc_next[...] += jnp.dot(last, x[:, 256:], preferred_element_type=f32)

        g = [
            jnp.concatenate(
                [flat(2 * k, 1, front), flat(2 * k + 1, 1, front), flat(2 * k, 0, front), flat(2 * k + 1, 0, front)],
                axis=1,
            )
            for k in range(2)
        ]
        pulled = jnp.dot(jnp.concatenate(g, axis=0), back_two[...], preferred_element_type=f32)
        grads = [
            pulled[:members, :LANES] + carry[...],
            pulled[members:, :LANES] + pulled[:members, LANES:],
        ]
        carry[...] = pulled[members:, LANES:]
        grads = [(grads[k] * slope[2 * n + k].reshape(members, LANES)).astype(bf16) for k in range(2)]
        yield
        grads = jnp.concatenate(grads, axis=1)
        g = [jnp.concatenate([flat(2 * k, 2, half), flat(2 * k + 1, 2, half)], axis=1) for k in range(2)]
        x = [operand(act, 2 * n + k, 1, half) for k in range(2)]
        if with_taps:
            add_taps(jnp.concatenate(g, axis=0), jnp.concatenate(x, axis=0), acc_two, acc_two_next, chan2)
            yield
            add_taps(grads[16:], operand(source, n, 1, half), acc_one, acc_one_next, chan1)
            yield
        z = jnp.dot(pick, grads, preferred_element_type=f32)
        z = jnp.concatenate([z[:48], z[48:]], axis=1)
        high = z.astype(bf16)
        sums[0, n] = high
        sums[1, n] = (z - high.astype(f32)).astype(bf16)
        yield

    def own_gradient(n, cast, fgrad):
        return loss_gradient(cast, fgrad, aims, weights, 4 * (n - 1), range(4))

    def second_segment(m, _):
        take_turns(
            second_product(2 * m + 3, cast_odd),
            own_gradient(2 * m + 2, cast_even, fgrad_even),
            pull_back(2 * m + 1, fgrad_odd),
        )
        take_turns(
            second_product(2 * m + 4, cast_even),
            own_gradient(2 * m + 3, cast_odd, fgrad_odd),
            pull_back(2 * m + 2, fgrad_even),
        )
        return 0

    take_turns(second_product(0, cast_even))
    take_turns(
        second_product(1, cast_odd),
        loss_gradient(cast_even, fgrad_even, edge_aims, edge_weights, 0, range(1, 4)),
    )
    take_turns(
        second_product(2, cast_even),
        own_gradient(1, cast_odd, fgrad_odd),
        pull_back(0, fgrad_even, with_taps=False),
    )
    lax.fori_loop(0, rows // 2 - 1, second_segment, 0)
    take_turns(own_gradient(rows, cast_even, fgrad_even), pull_back(rows - 1, fgrad_odd))
    take_turns(pull_back(rows, fgrad_even))

    z = jnp.dot(sums[...].reshape(2 * (rows + 1) * 48, 512), back_one[...], preferred_element_type=f32)
    z = z.reshape(2, rows + 1, 48, 2 * LANES)
    z = z[0] + z[1]
    for n in range(rows):
        lat_lines[pl.ds(n, 48, stride=rows), :] = z[n + 1, :, :LANES] + z[n, :, LANES:]
    for t in range(own):
        out_lat[:, t * LANES : (t + 1) * LANES] = lat_lines[t * rows : (t + 1) * rows].astype(bf16)
    pack_taps(acc_one, acc_one_next, taps, 0, chan0, chan1, norm)
    pack_taps(acc_two, acc_two_next, taps, -(-9 // (LANES // chan0)) * chan1, chan1, chan2, norm)
    count = taps_keep.shape[0]
    odd = jnp.bitwise_and(lat_pos, 1)
    taps_keep[...] = taps[pl.ds(pl.multiple_of(odd * count, 8), count), :]
    taps_send[...] = taps[pl.ds(pl.multiple_of((1 - odd) * count, 8), count), :]


def swapped(array, axis, bit):
    return lax.ppermute(array, axis, [(i, i ^ bit) for i in range(lax.axis_size(axis))])


def total(array, axis, first, second):
    one, two, three = (swapped(array, axis, k).astype(jnp.float32) for k in (first, second, first ^ second))
    return (array.astype(jnp.float32) + one) + (two + three)


def local(
    latent, member_seeds, noise_scale, kernel_one, kernel_two, targets, land_words, channel_weight
):
    sample_count, rows, span = latent.shape
    chan0, chan1, chan2 = kernel_one.shape[2], kernel_one.shape[3], kernel_two.shape[3]
    lat_count = lax.axis_size("lat")
    own = span // LANES // lax.axis_size("mem")
    half = (own + 1) // 2
    assert sample_count == 1 and member_seeds.shape[0] == MEM and rows % 4 == 0 and own % 2 == 1 and lax.axis_size("mem") == 4
    assert 4 * chan2 == 2 * chan1 == chan0 and chan0 == 64
    vmem = pl.BlockSpec(memory_space=pltpu.VMEM)
    smem = pl.BlockSpec(memory_space=pltpu.SMEM)
    hbm = pl.BlockSpec(memory_space=pltpu.HBM)
    f32, bf16 = jnp.float32, jnp.bfloat16
    wide, front = half + 2, half + 1
    params = pltpu.CompilerParams(vmem_limit_bytes=32 * 1024 * 1024)
    small = pltpu.CompilerParams(vmem_limit_bytes=8 * 1024 * 1024)
    kernel_one = kernel_one.transpose(0, 1, 3, 2)
    kernel_two = kernel_two.transpose(0, 1, 3, 2)
    down, up = pl.pallas_call(
        functools.partial(edge_kernel, half, chan2),
        in_specs=[hbm] * 3,
        out_specs=[vmem] * 2,
        out_shape=[
            jax.ShapeDtypeStruct((2 * wide, 8, LANES), bf16),
            jax.ShapeDtypeStruct((1, 2 * wide * LANES), bf16),
        ],
        scratch_shapes=[
            pltpu.VMEM((1, 8, span), bf16),
            pltpu.VMEM((1, 8, span), bf16),
            pltpu.VMEM((8, land_words.shape[1]), jnp.int32),
            pltpu.VMEM((8, LANES), jnp.int32),
            pltpu.SemaphoreType.DMA((3,)),
        ],
        compiler_params=pltpu.CompilerParams(vmem_limit_bytes=56 * 1024 * 1024),
        name="edges",
    )(latent, targets, land_words)
    above = shifted(down, "lat", 1)
    below = shifted(up, "lat", -1)
    source, aims, weights = pl.pallas_call(
        functools.partial(prepare_kernel, half, chan0, chan2),
        in_specs=[smem] * 3 + [vmem] * 3,
        out_specs=[vmem] * 3,
        out_shape=[jax.ShapeDtypeStruct((rows, wide, 16, LANES), bf16)]
        + [jax.ShapeDtypeStruct((2 * front, 4 * rows, LANES), f32)] * 2,
        scratch_shapes=[pltpu.VMEM((2 * wide, rows, LANES), f32), pltpu.VMEM((4 * rows, LANES), jnp.int32)],
        compiler_params=small,
        cost_estimate=pl.CostEstimate(flops=10**8, bytes_accessed=10**7, transcendentals=0),
        name="prepare",
    )(member_seeds, noise_scale, channel_weight, latent, targets, land_words)
    one_late, two_late, source = lax.optimization_barrier((kernel_one, kernel_two, source))
    bands = pl.pallas_call(
        bands_kernel,
        in_specs=[vmem] * 2,
        out_specs=[vmem] * 4,
        out_shape=[jax.ShapeDtypeStruct((512, 256), bf16)] * 4,
        compiler_params=small,
        cost_estimate=pl.CostEstimate(flops=10**8, bytes_accessed=10**7, transcendentals=0),
        name="bands",
    )(one_late, two_late)
    norm = 1.0 / math.sqrt(sample_count * 4 * rows * lat_count * targets.shape[2])
    tap_rows = 5 * chan1 + 3 * chan2
    lat_grad, taps, taps_send = pl.pallas_call(
        functools.partial(band_kernel, half, (chan0, chan1, chan2), span, norm),
        in_specs=[smem] * 3 + [vmem] * 9,
        out_specs=[vmem] * 3,
        out_shape=[
            jax.ShapeDtypeStruct((rows, own * LANES), bf16),
            jax.ShapeDtypeStruct((tap_rows // 2, LANES), f32),
            jax.ShapeDtypeStruct((tap_rows // 2, LANES), f32),
        ],
        scratch_shapes=[
            pltpu.VMEM((2 * wide, 8, LANES), f32),
            pltpu.VMEM((2 * front, 8, LANES), f32),
            pltpu.VMEM((2 * front, 8, LANES), f32),
            pltpu.VMEM((rows + 4, wide + 1, 16, LANES), bf16),
            pltpu.VMEM((wide * 32, 2 * LANES), f32),
            pltpu.VMEM((wide * 32, 2 * LANES), f32),
            pltpu.VMEM((2 * rows + 4, wide, 16, LANES), bf16),
            pltpu.VMEM((2 * rows + 4, front, 16, LANES), f32),
            pltpu.VMEM((4, front, 16, LANES), bf16),
            pltpu.VMEM((4, front, 16, LANES), bf16),
            pltpu.VMEM((4, front + 1, 16, LANES), bf16),
            pltpu.VMEM((4, front + 1, 16, LANES), bf16),
            pltpu.VMEM((front * 16, LANES), f32),
            pltpu.VMEM((2, rows + 1, 48, 512), bf16),
            pltpu.VMEM((48 * rows, LANES), f32),
            pltpu.VMEM((tap_rows, LANES), f32),
            pltpu.VMEM((256, 256), f32),
            pltpu.VMEM((2 * chan1, 256), f32),
            pltpu.VMEM((256, 256), f32),
            pltpu.VMEM((2 * chan2, 256), f32),
        ],
        compiler_params=params,
        name="band",
    )(
        member_seeds,
        noise_scale,
        channel_weight,
        source,
        aims,
        weights,
        above,
        below,
        *bands,
    )
    taps = (taps + swapped(taps_send, "lat", 1)).astype(bf16)
    taps = total(taps, "mem", 1, 2)
    one, three = (swapped(lat_grad, "mem", k) for k in (1, 3))
    bits = [1 << k for k in range(1, lat_count.bit_length() - 1)]
    for bit in bits:
        if bit == bits[-1]:
            taps, one, three, late = lax.optimization_barrier((taps, one, three, lat_grad))
            two = swapped(late, "mem", 2)
        taps = taps + swapped(taps, "lat", bit)
    other = swapped(taps, "lat", 1)
    latent_grad = pl.pallas_call(
        functools.partial(place_kernel, own),
        in_specs=[vmem] * 4,
        out_specs=vmem,
        out_shape=jax.ShapeDtypeStruct((1, rows, span), f32),
        compiler_params=small,
        name="place",
    )(lat_grad, one, two, three)
    other, latent_grad = lax.optimization_barrier((other, latent_grad))
    one, two = pl.pallas_call(
        taps_kernel,
        in_specs=[vmem] * 2,
        out_specs=[vmem] * 2,
        out_shape=[
            jax.ShapeDtypeStruct(kernel_one.shape, f32),
            jax.ShapeDtypeStruct(kernel_two.shape, f32),
        ],
        scratch_shapes=[pltpu.VMEM((tap_rows, LANES), f32)],
        compiler_params=small,
        name="taps",
    )(taps, other)
    return (latent_grad, one.transpose(0, 1, 3, 2), two.transpose(0, 1, 3, 2))


def solution(mesh):
    in_specs = (P(None, "lat", None), P(), P(), P(), P(), P(None, "lat", None), P("lat", None), P())
    out_specs = (P(None, "lat", None), P(), P())
    return jax.shard_map(local, mesh=mesh, in_specs=in_specs, out_specs=out_specs, check_vma=False)
```

```python
import functools
import math

import jax
import jax.numpy as jnp
from jax import lax
from jax.experimental import pallas as pl
from jax.experimental.pallas import tpu as pltpu
from jax.sharding import PartitionSpec as P

SMOOTH = 0.01
HASH_CELL = 1103515245
HASH_SEED = 747796405
HASH_MIX = 277803737
LANES = 128
MEM = 8
GELU_A = math.sqrt(2.0 / math.pi)
GELU_B = 0.044715


def shifted(array, axis, by):
    peers = lax.axis_size(axis)
    pairs = [(i, i + by) for i in range(peers) if 0 <= i + by < peers]
    return lax.ppermute(array, axis, pairs)


def iota(shape, axis):
    return lax.broadcasted_iota(jnp.int32, shape, axis)


def lane_table(ref, count):
    lane = iota((8, LANES), 1) % count
    total = jnp.zeros((8, LANES), jnp.float32)
    for k in range(count):
        total = jnp.where(lane == k, ref[k], total)
    return total


def build_band(kernel_ref, band_ref):
    chan_out, chan_in = kernel_ref.shape[2], kernel_ref.shape[3]
    cells = LANES // chan_in
    repeat = (iota((chan_out, LANES), 1) % chan_out == iota((chan_out, LANES), 0)).astype(jnp.bfloat16)
    wide = {}
    for a in range(3):
        for b in range(3):
            wide[a, b] = lax.dot_general(
                kernel_ref[a, b], repeat, (((0,), (0,)), ((), ())), preferred_element_type=jnp.float32
            )
    column = iota((chan_in, LANES), 1) // chan_out
    zero = jnp.zeros((chan_in, LANES), jnp.float32)
    for block in range(2):
        for row in range(2):
            for cell in range(cells):
                at = block * 256 + row * LANES + cell * chan_in
                for sub in range(2):
                    a = sub - 2 * row + 1
                    part = zero
                    for q in range(2 * cells):
                        b = q - 2 * (cell + block * cells) + 1
                        if 0 <= a <= 2 and 0 <= b <= 2:
                            part = jnp.where(column == q, wide[a, b], part)
                    band_ref[at : at + chan_in, sub * LANES : (sub + 1) * LANES] = part.astype(jnp.bfloat16)


def build_back(kernel_ref, back_ref):
    chan_out, chan_in = kernel_ref.shape[2], kernel_ref.shape[3]
    cells = LANES // chan_in
    repeat = (iota((chan_in, LANES), 1) % chan_in == iota((chan_in, LANES), 0)).astype(jnp.bfloat16)
    flat = kernel_ref[...].reshape(9 * chan_out, chan_in)
    wide = jnp.dot(flat, repeat, preferred_element_type=jnp.float32)
    column = iota((chan_out, LANES), 1) // chan_in
    zero = jnp.zeros((chan_out, LANES), jnp.float32)
    for block in range(2):
        for sub in range(2):
            for q in range(2 * cells):
                at = block * 256 + sub * LANES + q * chan_out
                for row in range(2):
                    a = sub - 2 * row + 1
                    part = zero
                    for cell in range(cells):
                        b = q - 2 * (cell + block * cells) + 1
                        if 0 <= a <= 2 and 0 <= b <= 2:
                            tap = (3 * a + b) * chan_out
                            part = jnp.where(column == cell, wide[tap : tap + chan_out], part)
                    back_ref[at : at + chan_out, row * LANES : (row + 1) * LANES] = part.astype(jnp.bfloat16)


def pack_taps(acc_ref, out_ref, first, chan_in, chan_out, norm):
    acc = acc_ref[...].T
    cells = LANES // chan_in
    group = iota((chan_out, LANES), 1) // chan_in
    packed = None
    for k in range(9):
        a, b = divmod(k, 3)
        row, sub = ((1, 1), (0, 0), (0, 1))[a]
        slot = k % cells
        part = None
        for reach in range(cells + 1):
            q = 2 * reach + b - 1
            if 0 <= q < 2 * cells:
                block, cell = reach // cells, reach % cells
                lines = sub * LANES + q * chan_out
                lanes = row * LANES if block == 0 else 256
                piece = acc[lines : lines + chan_out, lanes : lanes + LANES]
                turn = (slot - (cell if block == 0 else row)) % cells * chan_in
                piece = pltpu.roll(piece, turn, 1) if turn else piece
                part = piece if part is None else part + piece
        packed = part if slot == 0 else jnp.where(group == slot, part, packed)
        if slot == cells - 1 or k == 8:
            at = first + k // cells * chan_out
            out_ref[at : at + chan_out, :] = packed * norm


def spread_line(ref, slot, at):
    return jnp.broadcast_to(ref[slot, pl.ds(at, 1), :], (8, LANES))


def window_block(mem_pos, own, half, blocks, part, t):
    at = mem_pos * own + part * half + t + (blocks - 1)
    at = jnp.where(at >= blocks, at - blocks, at)
    return jnp.where(at >= blocks, at - blocks, at)


def land_of(words, block, chan):
    cell = block * (LANES // chan) + iota(words.shape, 1) // chan
    word = jnp.right_shift(cell * 2185, 16)
    picked = jnp.take_along_axis(words, word, axis=1, mode="promise_in_bounds")
    return jnp.bitwise_and(jnp.right_shift(picked, cell - 30 * word), 1).astype(jnp.float32)


def edge_kernel(
    half,
    chan,
    latent_hbm,
    targets_hbm,
    land_hbm,
    down,
    up,
    latent,
    targets,
    land,
    words,
    sems,
):
    rows = latent.shape[1]
    blocks = latent.shape[2] // LANES
    edge = pl.ds(targets_hbm.shape[1] - 8, 8)
    copies = [
        pltpu.make_async_copy(latent_hbm, latent, sems.at[0]),
        pltpu.make_async_copy(targets_hbm.at[:, edge], targets, sems.at[1]),
        pltpu.make_async_copy(land_hbm.at[edge], land, sems.at[2]),
    ]
    for copy in copies:
        copy.start()
    for copy in copies:
        copy.wait()
    own = blocks // lax.axis_size("mem")
    mem_pos = lax.axis_index("mem")
    words[...] = jnp.zeros(words.shape, jnp.int32)
    words[:, : land.shape[1]] = land[...]
    line = iota((8, LANES), 0)
    for t in range(half + 2):
        for part in range(2):
            block = window_block(mem_pos, own, half, blocks, part, t)
            off = pl.multiple_of(block * LANES, LANES)
            slot = t * 2 + part
            cells = latent[0, :, pl.ds(off, LANES)].astype(jnp.float32)
            aims = targets[0, :, pl.ds(off, LANES)].astype(jnp.float32)
            mask = land_of(words[...], block, chan)
            pack = pltpu.roll(cells, 1, 0)
            pack = jnp.where((line >= 1) & (line <= 3), pltpu.roll(aims, 4, 0), pack)
            pack = jnp.where((line >= 4) & (line <= 6), pltpu.roll(mask, 7, 0), pack)
            down[slot] = pack.astype(jnp.bfloat16)
            up[:, slot * LANES : (slot + 1) * LANES] = cells[0:1].astype(jnp.bfloat16)


def place_kernel(own, part0, part1, part2, part3, latent_grad):
    mem_pos = lax.axis_index("mem")
    for k, part in enumerate((part0, part1, part2, part3)):
        off = pl.multiple_of(jnp.bitwise_xor(mem_pos, k) * own * LANES, LANES)
        latent_grad[0, :, pl.ds(off, own * LANES)] = part[...].astype(jnp.float32)


def taps_kernel(mine, other, grad_one, grad_two, taps):
    count = mine.shape[0]
    odd = jnp.bitwise_and(lax.axis_index("lat"), 1)
    taps[pl.ds(pl.multiple_of(odd * count, 8), count), :] = mine[...]
    taps[pl.ds(pl.multiple_of((1 - odd) * count, 8), count), :] = other[...]
    first = 0
    for out in (grad_one, grad_two):
        chan_out, chan_in = out.shape[2], out.shape[3]
        cells = LANES // chan_in
        for k in range(9):
            at = first + k // cells * chan_out
            block = taps[at : at + chan_out, :]
            turn = (-(k % cells)) % cells * chan_in
            block = pltpu.roll(block, turn, 1) if turn else block
            out[k // 3, k % 3] = block[:, :chan_in]
        first += -(-9 // cells) * chan_out


def make_source(i, row, total_rows, span, own, half, seeds, scale, chan, line, store):
    blocks = span // LANES
    mem_pos = lax.axis_index("mem")
    sublane = iota((8, LANES), 0)
    seed_table = jnp.zeros((8, LANES), jnp.int32)
    for m in range(MEM):
        seed_table = jnp.where(sublane == m, seeds[m], seed_table)
    hash_table = iota((8, LANES), 1) * HASH_CELL + seed_table * HASH_SEED
    scale_table = lane_table(scale, chan)
    inside = jnp.where(row < total_rows, 1.0, 0.0).astype(jnp.float32)
    for t in range(half + 2):
        parts = []
        for part in range(2):
            first = (row * span + window_block(mem_pos, own, half, blocks, part, t) * LANES) * HASH_CELL
            h = hash_table + first
            h = jnp.bitwise_xor(h, jnp.right_shift(h, 15))
            h = h * HASH_MIX
            h = jnp.bitwise_xor(h, jnp.right_shift(h, 13))
            noise = jnp.bitwise_and(h, 65535).astype(jnp.float32) * (1.0 / 65536.0) - 0.5
            noise = noise * 3.4641016
            parts.append((line(t * 2 + part, i) + noise * scale_table) * inside)
        store(i, t, jnp.concatenate(parts, axis=0).astype(jnp.bfloat16))


def weight_lines(grid_row, channel_weight, chan, grid_total):
    latitude = math.pi / 2 - math.pi * (grid_row.astype(jnp.float32) + 0.5) / grid_total
    cosine = jnp.where(grid_row >= 0, jnp.cos(latitude), 0.0)
    channels = jnp.tile(lane_table(channel_weight, chan), (grid_row.shape[0] // 8, 1))
    return cosine * (channels * (1.0 / (MEM * (MEM - 1))))


def prepare_kernel(
    half, chan, chan2, seeds, scale, channel_weight, latent, targets, land, source, aims, weights, lines, words
):
    rows, span = latent.shape[1], latent.shape[2]
    blocks = span // LANES
    own = blocks // lax.axis_size("mem")
    total_rows = rows * lax.axis_size("lat")
    lat_pos, mem_pos = lax.axis_index("lat"), lax.axis_index("mem")
    grid_row = iota((4 * rows, LANES), 0) + lat_pos * 4 * rows
    base = weight_lines(grid_row, channel_weight, chan2, 4 * total_rows)
    words[...] = jnp.zeros(words.shape, jnp.int32)
    words[:, : land.shape[1]] = land[...]
    for t in range(half + 2):
        for part in range(2):
            block = window_block(mem_pos, own, half, blocks, part, t)
            off = pl.multiple_of(block * LANES, LANES)
            slot = t * 2 + part
            lines[slot] = latent[0, :, pl.ds(off, LANES)].astype(jnp.float32)
            if t < half + 1:
                aims[slot] = targets[0, :, pl.ds(off, LANES)].astype(jnp.float32)
                weights[slot] = base + base * land_of(words[...], block, chan2)

    def line(slot, i):
        return spread_line(lines, slot, i)

    def store(i, t, value):
        source[i, t] = value

    def step(i, _):
        make_source(
            i, lat_pos * rows + i, total_rows, span, own, half, seeds, scale, chan, line, store
        )
        return 0

    lax.fori_loop(0, rows, step, 0)


def bands_kernel(kernel_one, kernel_two, band_one, band_two, back_one, back_two):
    build_band(kernel_one, band_one)
    build_band(kernel_two, band_two)
    build_back(kernel_one, back_one)
    build_back(kernel_two, back_two)


def take_turns(*parts):
    parts = list(parts)
    while parts:
        for part in tuple(parts):
            if next(part, part) is part:
                parts.remove(part)


def band_kernel(
    half,
    chans,
    span,
    norm,
    seeds,
    scale,
    channel_weight,
    own_source,
    aims,
    weights,
    above,
    below,
    band_one,
    band_two,
    back_one,
    back_two,
    out_lat,
    taps_keep,
    taps_send,
    lat_rows,
    edge_aims,
    edge_weights,
    source,
    pre_even,
    pre_odd,
    act,
    slope,
    cast_even,
    cast_odd,
    fgrad_even,
    fgrad_odd,
    carry,
    sums,
    lat_lines,
    taps,
    acc_one,
    acc_two,
):
    rows = own_source.shape[0]
    blocks = span // LANES
    own = blocks // lax.axis_size("mem")
    total_rows = rows * lax.axis_size("lat")
    lat_pos = lax.axis_index("lat")
    wide = half + 2
    front = half + 1
    chan0, chan1, chan2 = chans
    f32, bf16 = jnp.float32, jnp.bfloat16

    grid_row = iota((8, LANES), 0) + (lat_pos * 4 * rows - 4)
    base = weight_lines(grid_row, channel_weight, chan2, 4 * total_rows)
    for slot in range(2 * wide):
        edge = above[slot].astype(f32)
        lat_rows[slot, 0:1] = edge[0:1]
        lat_rows[slot, 1:2] = below[:, slot * LANES : (slot + 1) * LANES].astype(f32)
        if slot < 2 * front:
            edge_aims[slot] = edge
            edge_weights[slot] = base + base * pltpu.roll(edge, 5, 0)

    source[rows + 2 :] = jnp.zeros((2,) + source.shape[1:], bf16)
    source[:, wide] = jnp.zeros((source.shape[0],) + source.shape[2:], bf16)
    fgrad_even[0] = jnp.zeros(fgrad_even.shape[1:], bf16)
    for fgrad in (fgrad_even, fgrad_odd):
        fgrad[:, 0] = jnp.zeros((4,) + fgrad.shape[2:], bf16)
    carry[...] = jnp.zeros(carry.shape, f32)
    for acc in (acc_one, acc_two):
        acc[...] = jnp.zeros(acc.shape, f32)

    def line(slot, i):
        return spread_line(lat_rows, slot, i)

    def store(i, t, value):
        source[i * (rows + 1), t] = value

    def edge_source(i, _):
        row = lat_pos * rows - 1 + i * (rows + 1)
        make_source(i, row, total_rows, span, own, half, seeds, scale, chan0, line, store)
        return 0

    lax.fori_loop(0, 2, edge_source, 0)
    source[1 : rows + 1, 0:wide] = own_source[...]

    def operand(ref, i, start, count):
        def piece(r, at):
            return ref[r, pl.ds(at, count)].reshape(count * 16, LANES)

        return jnp.concatenate(
            [piece(i, start), piece(i + 1, start), piece(i, start + 1), piece(i + 1, start + 1)], axis=1
        )

    def first_product(pair, pre):
        taken = jnp.concatenate([operand(source, 2 * pair + k, 0, wide) for k in range(2)], axis=0)
        pre[...] = jnp.dot(taken, band_one[...], preferred_element_type=f32)

    def first_gelu(pair, pre):
        for k in range(2):
            for t in range(wide):
                for sub in range(2):
                    at = (k * wide + t) * 16
                    x = pre[at : at + 16, sub * LANES : (sub + 1) * LANES]
                    square = x * x
                    th = jnp.tanh(x * (GELU_A + (GELU_A * GELU_B) * square))
                    plus = 0.5 + 0.5 * th
                    act[4 * pair + 2 * k + sub, t] = (x * plus).astype(bf16)
                    if t < front:
                        d = plus + (x * plus) * (1.0 - th) * (GELU_A + (3.0 * GELU_A * GELU_B) * square)
                        if t == half:
                            d = jnp.where(iota((16, LANES), 0) < 8, d, 0.0)
                        slope[4 * pair + 2 * k + sub, t] = d

    def first_segment(m, _):
        first_product(2 * m + 1, pre_odd)
        first_gelu(2 * m, pre_even)
        first_product(2 * m + 2, pre_even)
        first_gelu(2 * m + 1, pre_odd)
        return 0

    first_product(0, pre_even)
    lax.fori_loop(0, rows // 4, first_segment, 0)
    first_gelu(rows // 2, pre_even)

    members = front * 16
    owner = iota((48, members), 0)
    group = iota((48, members), 1) // 8
    place = (group % 2) * half + group // 2
    real = (group // 2 > 0) & (place - 1 < own)
    pick_own = (real & (place - 1 == owner)).astype(bf16)
    pick_prev = ((group // 2 < half) & (place == owner)).astype(bf16)
    pick = jnp.concatenate([pick_own, pick_prev], axis=0)

    def second_product(n, cast):
        taken = jnp.concatenate([operand(act, 2 * n + k, 0, front) for k in range(2)], axis=0)
        out = jnp.dot(taken, band_two[...], preferred_element_type=f32).astype(bf16)
        for k in range(2):
            for sub in range(2):
                part = out[k * members : (k + 1) * members, sub * LANES : (sub + 1) * LANES]
                cast[2 * k + sub] = part.reshape(front, 16, LANES)
        yield

    def loss_gradient(cast, fgrad, aim_ref, weight_ref, first, lines):
        for line in lines:
            for t in range(front):
                both = cast[line, t].astype(f32)
                parts = []
                for part in range(2):
                    if t == half and part == 1:
                        parts.append(jnp.zeros((8, LANES), f32))
                        continue
                    f = both[part * 8 : part * 8 + 8]
                    d = f - spread_line(aim_ref, t * 2 + part, first + line)
                    goal = d * lax.rsqrt(d * d + SMOOTH)
                    gs = []
                    for k in range(1, 5):
                        d = f - pltpu.roll(f, k, 0)
                        gs.append(d * lax.rsqrt(d * d + SMOOTH))
                    back = gs[2]
                    for k in (1, 0):
                        back = gs[k] + pltpu.roll(back, MEM - 1, 0)
                    back = pltpu.roll(back, MEM - 1, 0)
                    spread = (gs[0] + gs[1]) + (gs[2] + gs[3]) - back
                    weight = spread_line(weight_ref, t * 2 + part, first + line)
                    parts.append(weight * ((MEM - 1.0) * goal - spread))
                fgrad[line, t + 1] = jnp.concatenate(parts, axis=0).astype(bf16)
            yield

    def pull_back(n, fgrad, with_taps=True):
        def flat(line, start, count):
            return fgrad[line, start : start + count].reshape(count * 16, LANES)

        def add_taps(g, x, acc, chan_in):
            beside = pltpu.roll(x[:, 384:], chan_in, 1)
            after = jnp.where(iota((x.shape[0], LANES), 1) < chan_in, x[:, 256:384], beside)
            turned = jnp.concatenate([x[:, :256].T, after.T[: 2 * chan_in]], axis=0)
            acc[: 256 + 2 * chan_in] += jnp.dot(turned, g, preferred_element_type=f32)

        g = [
            jnp.concatenate(
                [flat(2 * k, 1, front), flat(2 * k + 1, 1, front), flat(2 * k, 0, front), flat(2 * k + 1, 0, front)],
                axis=1,
            )
            for k in range(2)
        ]
        pulled = jnp.dot(jnp.concatenate(g, axis=0), back_two[...], preferred_element_type=f32)
        grads = [
            pulled[:members, :LANES] + carry[...],
            pulled[members:, :LANES] + pulled[:members, LANES:],
        ]
        carry[...] = pulled[members:, LANES:]
        grads = [(grads[k] * slope[2 * n + k].reshape(members, LANES)).astype(bf16) for k in range(2)]
        yield
        grads = jnp.concatenate(grads, axis=1)
        g = [jnp.concatenate([flat(2 * k, 2, half), flat(2 * k + 1, 2, half)], axis=1) for k in range(2)]
        x = [operand(act, 2 * n + k, 1, half) for k in range(2)]
        if with_taps:
            add_taps(jnp.concatenate(g, axis=0), jnp.concatenate(x, axis=0), acc_two, chan1)
            yield
            add_taps(grads[16:], operand(source, n, 1, half), acc_one, chan0)
            yield
        z = jnp.dot(pick, grads, preferred_element_type=f32)
        z = jnp.concatenate([z[:48], z[48:]], axis=1)
        high = z.astype(bf16)
        sums[0, n] = high
        sums[1, n] = (z - high.astype(f32)).astype(bf16)
        yield

    def own_gradient(n, cast, fgrad):
        return loss_gradient(cast, fgrad, aims, weights, 4 * (n - 1), range(4))

    def second_segment(m, _):
        take_turns(
            second_product(2 * m + 3, cast_odd),
            own_gradient(2 * m + 2, cast_even, fgrad_even),
            pull_back(2 * m + 1, fgrad_odd),
        )
        take_turns(
            second_product(2 * m + 4, cast_even),
            own_gradient(2 * m + 3, cast_odd, fgrad_odd),
            pull_back(2 * m + 2, fgrad_even),
        )
        return 0

    take_turns(second_product(0, cast_even))
    take_turns(
        second_product(1, cast_odd),
        loss_gradient(cast_even, fgrad_even, edge_aims, edge_weights, 0, range(1, 4)),
    )
    take_turns(
        second_product(2, cast_even),
        own_gradient(1, cast_odd, fgrad_odd),
        pull_back(0, fgrad_even, with_taps=False),
    )
    lax.fori_loop(0, rows // 2 - 1, second_segment, 0)
    take_turns(own_gradient(rows, cast_even, fgrad_even), pull_back(rows - 1, fgrad_odd))
    take_turns(pull_back(rows, fgrad_even))

    z = jnp.dot(sums[...].reshape(2 * (rows + 1) * 48, 512), back_one[...], preferred_element_type=f32)
    z = z.reshape(2, rows + 1, 48, 2 * LANES)
    z = z[0] + z[1]
    for n in range(rows):
        lat_lines[pl.ds(n, 48, stride=rows), :] = z[n + 1, :, :LANES] + z[n, :, LANES:]
    for t in range(own):
        out_lat[:, t * LANES : (t + 1) * LANES] = lat_lines[t * rows : (t + 1) * rows].astype(bf16)
    pack_taps(acc_one, taps, 0, chan0, chan1, norm)
    pack_taps(acc_two, taps, -(-9 // (LANES // chan0)) * chan1, chan1, chan2, norm)
    count = taps_keep.shape[0]
    odd = jnp.bitwise_and(lat_pos, 1)
    taps_keep[...] = taps[pl.ds(pl.multiple_of(odd * count, 8), count), :]
    taps_send[...] = taps[pl.ds(pl.multiple_of((1 - odd) * count, 8), count), :]


def swapped(array, axis, bit):
    return lax.ppermute(array, axis, [(i, i ^ bit) for i in range(lax.axis_size(axis))])


def total(array, axis, first, second):
    one, two, three = (swapped(array, axis, k).astype(jnp.float32) for k in (first, second, first ^ second))
    return (array.astype(jnp.float32) + one) + (two + three)


def local(
    latent, member_seeds, noise_scale, kernel_one, kernel_two, targets, land_words, channel_weight
):
    sample_count, rows, span = latent.shape
    chan0, chan1, chan2 = kernel_one.shape[2], kernel_one.shape[3], kernel_two.shape[3]
    lat_count = lax.axis_size("lat")
    own = span // LANES // lax.axis_size("mem")
    half = (own + 1) // 2
    assert sample_count == 1 and member_seeds.shape[0] == MEM and rows % 4 == 0 and own % 2 == 1 and lax.axis_size("mem") == 4
    assert 4 * chan2 == 2 * chan1 == chan0 and chan0 == 64
    vmem = pl.BlockSpec(memory_space=pltpu.VMEM)
    smem = pl.BlockSpec(memory_space=pltpu.SMEM)
    hbm = pl.BlockSpec(memory_space=pltpu.HBM)
    f32, bf16 = jnp.float32, jnp.bfloat16
    wide, front = half + 2, half + 1
    params = pltpu.CompilerParams(vmem_limit_bytes=32 * 1024 * 1024)
    small = pltpu.CompilerParams(vmem_limit_bytes=8 * 1024 * 1024)
    kernel_one = kernel_one.transpose(0, 1, 3, 2)
    kernel_two = kernel_two.transpose(0, 1, 3, 2)
    down, up = pl.pallas_call(
        functools.partial(edge_kernel, half, chan2),
        in_specs=[hbm] * 3,
        out_specs=[vmem] * 2,
        out_shape=[
            jax.ShapeDtypeStruct((2 * wide, 8, LANES), bf16),
            jax.ShapeDtypeStruct((1, 2 * wide * LANES), bf16),
        ],
        scratch_shapes=[
            pltpu.VMEM((1, 8, span), bf16),
            pltpu.VMEM((1, 8, span), bf16),
            pltpu.VMEM((8, land_words.shape[1]), jnp.int32),
            pltpu.VMEM((8, LANES), jnp.int32),
            pltpu.SemaphoreType.DMA((3,)),
        ],
        compiler_params=pltpu.CompilerParams(vmem_limit_bytes=56 * 1024 * 1024),
        name="edges",
    )(latent, targets, land_words)
    above = shifted(down, "lat", 1)
    below = shifted(up, "lat", -1)
    source, aims, weights = pl.pallas_call(
        functools.partial(prepare_kernel, half, chan0, chan2),
        in_specs=[smem] * 3 + [vmem] * 3,
        out_specs=[vmem] * 3,
        out_shape=[jax.ShapeDtypeStruct((rows, wide, 16, LANES), bf16)]
        + [jax.ShapeDtypeStruct((2 * front, 4 * rows, LANES), f32)] * 2,
        scratch_shapes=[pltpu.VMEM((2 * wide, rows, LANES), f32), pltpu.VMEM((4 * rows, LANES), jnp.int32)],
        compiler_params=small,
        cost_estimate=pl.CostEstimate(flops=10**8, bytes_accessed=10**7, transcendentals=0),
        name="prepare",
    )(member_seeds, noise_scale, channel_weight, latent, targets, land_words)
    one_late, two_late, source = lax.optimization_barrier((kernel_one, kernel_two, source))
    bands = pl.pallas_call(
        bands_kernel,
        in_specs=[vmem] * 2,
        out_specs=[vmem] * 4,
        out_shape=[jax.ShapeDtypeStruct((512, 256), bf16)] * 4,
        compiler_params=small,
        cost_estimate=pl.CostEstimate(flops=10**8, bytes_accessed=10**7, transcendentals=0),
        name="bands",
    )(one_late, two_late)
    norm = 1.0 / math.sqrt(sample_count * 4 * rows * lat_count * targets.shape[2])
    tap_rows = 5 * chan1 + 3 * chan2
    lat_grad, taps, taps_send = pl.pallas_call(
        functools.partial(band_kernel, half, (chan0, chan1, chan2), span, norm),
        in_specs=[smem] * 3 + [vmem] * 9,
        out_specs=[vmem] * 3,
        out_shape=[
            jax.ShapeDtypeStruct((rows, own * LANES), bf16),
            jax.ShapeDtypeStruct((tap_rows // 2, LANES), f32),
            jax.ShapeDtypeStruct((tap_rows // 2, LANES), f32),
        ],
        scratch_shapes=[
            pltpu.VMEM((2 * wide, 8, LANES), f32),
            pltpu.VMEM((2 * front, 8, LANES), f32),
            pltpu.VMEM((2 * front, 8, LANES), f32),
            pltpu.VMEM((rows + 4, wide + 1, 16, LANES), bf16),
            pltpu.VMEM((wide * 32, 2 * LANES), f32),
            pltpu.VMEM((wide * 32, 2 * LANES), f32),
            pltpu.VMEM((2 * rows + 4, wide, 16, LANES), bf16),
            pltpu.VMEM((2 * rows + 4, front, 16, LANES), f32),
            pltpu.VMEM((4, front, 16, LANES), bf16),
            pltpu.VMEM((4, front, 16, LANES), bf16),
            pltpu.VMEM((4, front + 1, 16, LANES), bf16),
            pltpu.VMEM((4, front + 1, 16, LANES), bf16),
            pltpu.VMEM((front * 16, LANES), f32),
            pltpu.VMEM((2, rows + 1, 48, 512), bf16),
            pltpu.VMEM((48 * rows, LANES), f32),
            pltpu.VMEM((tap_rows, LANES), f32),
            pltpu.VMEM((384, 256), f32),
            pltpu.VMEM((384, 256), f32),
        ],
        compiler_params=params,
        name="band",
    )(
        member_seeds,
        noise_scale,
        channel_weight,
        source,
        aims,
        weights,
        above,
        below,
        *bands,
    )
    taps = (taps + swapped(taps_send, "lat", 1)).astype(bf16)
    taps = total(taps, "mem", 1, 2)
    one, two, three = (swapped(lat_grad, "mem", k) for k in range(1, 4))
    bits = [1 << k for k in range(1, lat_count.bit_length() - 1)]
    for bit in bits:
        if bit == bits[-1]:
            taps, one, three = lax.optimization_barrier((taps, one, three))
        taps = taps + swapped(taps, "lat", bit)
    taps, two = lax.optimization_barrier((taps, two))
    other = swapped(taps, "lat", 1)
    latent_grad = pl.pallas_call(
        functools.partial(place_kernel, own),
        in_specs=[vmem] * 4,
        out_specs=vmem,
        out_shape=jax.ShapeDtypeStruct((1, rows, span), f32),
        compiler_params=small,
        name="place",
    )(lat_grad, one, two, three)
    one, two = pl.pallas_call(
        taps_kernel,
        in_specs=[vmem] * 2,
        out_specs=[vmem] * 2,
        out_shape=[
            jax.ShapeDtypeStruct(kernel_one.shape, f32),
            jax.ShapeDtypeStruct(kernel_two.shape, f32),
        ],
        scratch_shapes=[pltpu.VMEM((tap_rows, LANES), f32)],
        compiler_params=small,
        name="taps",
    )(taps, other)
    return (latent_grad, one.transpose(0, 1, 3, 2), two.transpose(0, 1, 3, 2))


def solution(mesh):
    in_specs = (P(None, "lat", None), P(), P(), P(), P(), P(None, "lat", None), P("lat", None), P())
    out_specs = (P(None, "lat", None), P(), P())
    return jax.shard_map(local, mesh=mesh, in_specs=in_specs, out_specs=out_specs, check_vma=False)
```

```python
import functools
import math

import jax
import jax.numpy as jnp
from jax import lax
from jax.experimental import pallas as pl
from jax.experimental.pallas import tpu as pltpu
from jax.sharding import PartitionSpec as P

SMOOTH = 0.01
HASH_CELL = 1103515245
HASH_SEED = 747796405
HASH_MIX = 277803737
LANES = 128
MEM = 8
GELU_A = math.sqrt(2.0 / math.pi)
GELU_B = 0.044715


def shifted(array, axis, by):
    peers = lax.axis_size(axis)
    pairs = [(i, i + by) for i in range(peers) if 0 <= i + by < peers]
    return lax.ppermute(array, axis, pairs)


def iota(shape, axis):
    return lax.broadcasted_iota(jnp.int32, shape, axis)


def lane_table(ref, count):
    lane = iota((8, LANES), 1) % count
    total = jnp.zeros((8, LANES), jnp.float32)
    for k in range(count):
        total = jnp.where(lane == k, ref[k], total)
    return total


def build_band(kernel_ref, band_ref):
    chan_out, chan_in = kernel_ref.shape[2], kernel_ref.shape[3]
    cells = LANES // chan_in
    repeat = (iota((chan_out, LANES), 1) % chan_out == iota((chan_out, LANES), 0)).astype(jnp.bfloat16)
    wide = {}
    for a in range(3):
        for b in range(3):
            wide[a, b] = lax.dot_general(
                kernel_ref[a, b], repeat, (((0,), (0,)), ((), ())), preferred_element_type=jnp.float32
            )
    column = iota((chan_in, LANES), 1) // chan_out
    zero = jnp.zeros((chan_in, LANES), jnp.float32)
    for block in range(2):
        for row in range(2):
            for cell in range(cells):
                at = block * 256 + row * LANES + cell * chan_in
                for sub in range(2):
                    a = sub - 2 * row + 1
                    part = zero
                    for q in range(2 * cells):
                        b = q - 2 * (cell + block * cells) + 1
                        if 0 <= a <= 2 and 0 <= b <= 2:
                            part = jnp.where(column == q, wide[a, b], part)
                    band_ref[at : at + chan_in, sub * LANES : (sub + 1) * LANES] = part.astype(jnp.bfloat16)


def build_back(kernel_ref, back_ref):
    chan_out, chan_in = kernel_ref.shape[2], kernel_ref.shape[3]
    cells = LANES // chan_in
    repeat = (iota((chan_in, LANES), 1) % chan_in == iota((chan_in, LANES), 0)).astype(jnp.bfloat16)
    flat = kernel_ref[...].reshape(9 * chan_out, chan_in)
    wide = jnp.dot(flat, repeat, preferred_element_type=jnp.float32)
    column = iota((chan_out, LANES), 1) // chan_in
    zero = jnp.zeros((chan_out, LANES), jnp.float32)
    for block in range(2):
        for sub in range(2):
            for q in range(2 * cells):
                at = block * 256 + sub * LANES + q * chan_out
                for row in range(2):
                    a = sub - 2 * row + 1
                    part = zero
                    for cell in range(cells):
                        b = q - 2 * (cell + block * cells) + 1
                        if 0 <= a <= 2 and 0 <= b <= 2:
                            tap = (3 * a + b) * chan_out
                            part = jnp.where(column == cell, wide[tap : tap + chan_out], part)
                    back_ref[at : at + chan_out, row * LANES : (row + 1) * LANES] = part.astype(jnp.bfloat16)


def pack_taps(acc_ref, next_ref, out_ref, first, chan_in, chan_out, norm):
    cells = LANES // chan_in
    group = iota((chan_out, LANES), 1) // chan_in
    packed = None
    for k in range(9):
        a, b = divmod(k, 3)
        row, sub = ((1, 1), (0, 0), (0, 1))[a]
        slot = k % cells
        part = None
        for reach in range(cells + 1):
            q = 2 * reach + b - 1
            if 0 <= q < 2 * cells:
                block, cell = reach // cells, reach % cells
                lines = sub * LANES + q * chan_out if block == 0 else sub * chan_out
                ref = acc_ref if block == 0 else next_ref
                piece = ref[lines : lines + chan_out, row * LANES : (row + 1) * LANES]
                turn = (slot - cell) % cells * chan_in
                piece = pltpu.roll(piece, turn, 1) if turn else piece
                part = piece if part is None else part + piece
        packed = part if slot == 0 else jnp.where(group == slot, part, packed)
        if slot == cells - 1 or k == 8:
            at = first + k // cells * chan_out
            out_ref[at : at + chan_out, :] = packed * norm


def spread_line(ref, slot, at):
    return jnp.broadcast_to(ref[slot, pl.ds(at, 1), :], (8, LANES))


def window_block(mem_pos, own, half, blocks, part, t):
    at = mem_pos * own + part * half + t + (blocks - 1)
    at = jnp.where(at >= blocks, at - blocks, at)
    return jnp.where(at >= blocks, at - blocks, at)


def land_of(words, block, chan):
    cell = block * (LANES // chan) + iota(words.shape, 1) // chan
    word = jnp.right_shift(cell * 2185, 16)
    picked = jnp.take_along_axis(words, word, axis=1, mode="promise_in_bounds")
    return jnp.bitwise_and(jnp.right_shift(picked, cell - 30 * word), 1).astype(jnp.float32)


def edge_kernel(
    half,
    chan,
    latent_hbm,
    targets_hbm,
    land_hbm,
    down,
    up,
    latent,
    targets,
    land,
    words,
    sems,
):
    rows = latent.shape[1]
    blocks = latent.shape[2] // LANES
    edge = pl.ds(targets_hbm.shape[1] - 8, 8)
    copies = [
        pltpu.make_async_copy(latent_hbm, latent, sems.at[0]),
        pltpu.make_async_copy(targets_hbm.at[:, edge], targets, sems.at[1]),
        pltpu.make_async_copy(land_hbm.at[edge], land, sems.at[2]),
    ]
    for copy in copies:
        copy.start()
    for copy in copies:
        copy.wait()
    own = blocks // lax.axis_size("mem")
    mem_pos = lax.axis_index("mem")
    words[...] = jnp.zeros(words.shape, jnp.int32)
    words[:, : land.shape[1]] = land[...]
    line = iota((8, LANES), 0)
    for t in range(half + 2):
        for part in range(2):
            block = window_block(mem_pos, own, half, blocks, part, t)
            off = pl.multiple_of(block * LANES, LANES)
            slot = t * 2 + part
            cells = latent[0, :, pl.ds(off, LANES)].astype(jnp.float32)
            aims = targets[0, :, pl.ds(off, LANES)].astype(jnp.float32)
            mask = land_of(words[...], block, chan)
            pack = pltpu.roll(cells, 1, 0)
            pack = jnp.where((line >= 1) & (line <= 3), pltpu.roll(aims, 4, 0), pack)
            pack = jnp.where((line >= 4) & (line <= 6), pltpu.roll(mask, 7, 0), pack)
            down[slot] = pack.astype(jnp.bfloat16)
            up[:, slot * LANES : (slot + 1) * LANES] = cells[0:1].astype(jnp.bfloat16)


def place_kernel(own, part0, part1, part2, part3, latent_grad):
    mem_pos = lax.axis_index("mem")
    for k, part in enumerate((part0, part1, part2, part3)):
        off = pl.multiple_of(jnp.bitwise_xor(mem_pos, k) * own * LANES, LANES)
        latent_grad[0, :, pl.ds(off, own * LANES)] = part[...].astype(jnp.float32)


def taps_kernel(mine, other, grad_one, grad_two, taps):
    count = mine.shape[0]
    odd = jnp.bitwise_and(lax.axis_index("lat"), 1)
    taps[pl.ds(pl.multiple_of(odd * count, 8), count), :] = mine[...]
    taps[pl.ds(pl.multiple_of((1 - odd) * count, 8), count), :] = other[...]
    first = 0
    for out in (grad_one, grad_two):
        chan_out, chan_in = out.shape[2], out.shape[3]
        cells = LANES // chan_in
        for k in range(9):
            at = first + k // cells * chan_out
            block = taps[at : at + chan_out, :]
            turn = (-(k % cells)) % cells * chan_in
            block = pltpu.roll(block, turn, 1) if turn else block
            out[k // 3, k % 3] = block[:, :chan_in]
        first += -(-9 // cells) * chan_out


def make_source(i, row, total_rows, span, own, half, seeds, scale, chan, line, store):
    blocks = span // LANES
    mem_pos = lax.axis_index("mem")
    sublane = iota((8, LANES), 0)
    seed_table = jnp.zeros((8, LANES), jnp.int32)
    for m in range(MEM):
        seed_table = jnp.where(sublane == m, seeds[m], seed_table)
    hash_table = iota((8, LANES), 1) * HASH_CELL + seed_table * HASH_SEED
    scale_table = lane_table(scale, chan)
    inside = jnp.where(row < total_rows, 1.0, 0.0).astype(jnp.float32)
    for t in range(half + 2):
        parts = []
        for part in range(2):
            first = (row * span + window_block(mem_pos, own, half, blocks, part, t) * LANES) * HASH_CELL
            h = hash_table + first
            h = jnp.bitwise_xor(h, jnp.right_shift(h, 15))
            h = h * HASH_MIX
            h = jnp.bitwise_xor(h, jnp.right_shift(h, 13))
            noise = jnp.bitwise_and(h, 65535).astype(jnp.float32) * (1.0 / 65536.0) - 0.5
            noise = noise * 3.4641016
            parts.append((line(t * 2 + part, i) + noise * scale_table) * inside)
        store(i, t, jnp.concatenate(parts, axis=0).astype(jnp.bfloat16))


def weight_lines(grid_row, channel_weight, chan, grid_total):
    latitude = math.pi / 2 - math.pi * (grid_row.astype(jnp.float32) + 0.5) / grid_total
    cosine = jnp.where(grid_row >= 0, jnp.cos(latitude), 0.0)
    channels = jnp.tile(lane_table(channel_weight, chan), (grid_row.shape[0] // 8, 1))
    return cosine * (channels * (1.0 / (MEM * (MEM - 1))))


def prepare_kernel(
    half, chan, chan2, seeds, scale, channel_weight, latent, targets, land, source, aims, weights, lines, words
):
    rows, span = latent.shape[1], latent.shape[2]
    blocks = span // LANES
    own = blocks // lax.axis_size("mem")
    total_rows = rows * lax.axis_size("lat")
    lat_pos, mem_pos = lax.axis_index("lat"), lax.axis_index("mem")
    grid_row = iota((4 * rows, LANES), 0) + lat_pos * 4 * rows
    base = weight_lines(grid_row, channel_weight, chan2, 4 * total_rows)
    words[...] = jnp.zeros(words.shape, jnp.int32)
    words[:, : land.shape[1]] = land[...]
    for t in range(half + 2):
        for part in range(2):
            block = window_block(mem_pos, own, half, blocks, part, t)
            off = pl.multiple_of(block * LANES, LANES)
            slot = t * 2 + part
            lines[slot] = latent[0, :, pl.ds(off, LANES)].astype(jnp.float32)
            if t < half + 1:
                aims[slot] = targets[0, :, pl.ds(off, LANES)].astype(jnp.float32)
                weights[slot] = base + base * land_of(words[...], block, chan2)

    def line(slot, i):
        return spread_line(lines, slot, i)

    def store(i, t, value):
        source[i, t] = value

    def step(i, _):
        make_source(
            i, lat_pos * rows + i, total_rows, span, own, half, seeds, scale, chan, line, store
        )
        return 0

    lax.fori_loop(0, rows, step, 0)


def bands_kernel(kernel_one, kernel_two, band_one, band_two, back_one, back_two):
    build_band(kernel_one, band_one)
    build_band(kernel_two, band_two)
    build_back(kernel_one, back_one)
    build_back(kernel_two, back_two)


def take_turns(*parts):
    parts = list(parts)
    while parts:
        for part in tuple(parts):
            if next(part, part) is part:
                parts.remove(part)


def band_kernel(
    half,
    chans,
    span,
    norm,
    seeds,
    scale,
    channel_weight,
    own_source,
    aims,
    weights,
    above,
    below,
    band_one,
    band_two,
    back_one,
    back_two,
    out_lat,
    taps_keep,
    taps_send,
    lat_rows,
    edge_aims,
    edge_weights,
    source,
    pre_even,
    pre_odd,
    act,
    slope,
    cast_even,
    cast_odd,
    fgrad_even,
    fgrad_odd,
    grads_even,
    grads_odd,
    carry,
    sums,
    lat_lines,
    taps,
    acc_one,
    acc_one_next,
    acc_two,
    acc_two_next,
):
    rows = own_source.shape[0]
    blocks = span // LANES
    own = blocks // lax.axis_size("mem")
    total_rows = rows * lax.axis_size("lat")
    lat_pos = lax.axis_index("lat")
    wide = half + 2
    front = half + 1
    chan0, chan1, chan2 = chans
    f32, bf16 = jnp.float32, jnp.bfloat16

    grid_row = iota((8, LANES), 0) + (lat_pos * 4 * rows - 4)
    base = weight_lines(grid_row, channel_weight, chan2, 4 * total_rows)
    for slot in range(2 * wide):
        edge = above[slot].astype(f32)
        lat_rows[slot, 0:1] = edge[0:1]
        lat_rows[slot, 1:2] = below[:, slot * LANES : (slot + 1) * LANES].astype(f32)
        if slot < 2 * front:
            edge_aims[slot] = edge
            edge_weights[slot] = base + base * pltpu.roll(edge, 5, 0)

    source[rows + 2 :] = jnp.zeros((2,) + source.shape[1:], bf16)
    source[:, wide] = jnp.zeros((source.shape[0],) + source.shape[2:], bf16)
    fgrad_even[0] = jnp.zeros(fgrad_even.shape[1:], bf16)
    for fgrad in (fgrad_even, fgrad_odd):
        fgrad[:, 0] = jnp.zeros((4,) + fgrad.shape[2:], bf16)
    carry[...] = jnp.zeros(carry.shape, f32)
    for acc in (acc_one, acc_one_next, acc_two, acc_two_next):
        acc[...] = jnp.zeros(acc.shape, f32)

    def line(slot, i):
        return spread_line(lat_rows, slot, i)

    def store(i, t, value):
        source[i * (rows + 1), t] = value

    def edge_source(i, _):
        row = lat_pos * rows - 1 + i * (rows + 1)
        make_source(i, row, total_rows, span, own, half, seeds, scale, chan0, line, store)
        return 0

    lax.fori_loop(0, 2, edge_source, 0)
    source[1 : rows + 1, 0:wide] = own_source[...]

    def operand(ref, i, start, count):
        def piece(r, at):
            return ref[r, pl.ds(at, count)].reshape(count * 16, LANES)

        return jnp.concatenate(
            [piece(i, start), piece(i + 1, start), piece(i, start + 1), piece(i + 1, start + 1)], axis=1
        )

    def first_product(pair, pre):
        taken = jnp.concatenate([operand(source, 2 * pair + k, 0, wide) for k in range(2)], axis=0)
        pre[...] = jnp.dot(taken, band_one[...], preferred_element_type=f32)

    def first_gelu(pair, pre):
        for k in range(2):
            for t in range(wide):
                for sub in range(2):
                    at = (k * wide + t) * 16
                    x = pre[at : at + 16, sub * LANES : (sub + 1) * LANES]
                    square = x * x
                    th = jnp.tanh(x * (GELU_A + (GELU_A * GELU_B) * square))
                    plus = 0.5 + 0.5 * th
                    act[4 * pair + 2 * k + sub, t] = (x * plus).astype(bf16)
                    if t < front:
                        d = plus + (x * plus) * (1.0 - th) * (GELU_A + (3.0 * GELU_A * GELU_B) * square)
                        if t == half:
                            d = jnp.where(iota((16, LANES), 0) < 8, d, 0.0)
                        slope[4 * pair + 2 * k + sub, t] = d

    def first_segment(m, _):
        first_product(2 * m + 1, pre_odd)
        first_gelu(2 * m, pre_even)
        first_product(2 * m + 2, pre_even)
        first_gelu(2 * m + 1, pre_odd)
        return 0

    first_product(0, pre_even)
    lax.fori_loop(0, rows // 4, first_segment, 0)
    first_gelu(rows // 2, pre_even)

    members = front * 16
    owner = iota((48, members), 0)
    group = iota((48, members), 1) // 8
    place = (group % 2) * half + group // 2
    real = (group // 2 > 0) & (place - 1 < own)
    pick_own = (real & (place - 1 == owner)).astype(bf16)
    pick_prev = ((group // 2 < half) & (place == owner)).astype(bf16)
    pick = jnp.concatenate([pick_own, pick_prev], axis=0)

    def second_product(n, cast):
        taken = jnp.concatenate([operand(act, 2 * n + k, 0, front) for k in range(2)], axis=0)
        out = jnp.dot(taken, band_two[...], preferred_element_type=f32).astype(bf16)
        for k in range(2):
            for sub in range(2):
                part = out[k * members : (k + 1) * members, sub * LANES : (sub + 1) * LANES]
                cast[2 * k + sub] = part.reshape(front, 16, LANES)
        yield

    def loss_gradient(cast, fgrad, aim_ref, weight_ref, first, lines):
        for line in lines:
            for t in range(front):
                both = cast[line, t].astype(f32)
                parts = []
                for part in range(2):
                    if t == half and part == 1:
                        parts.append(jnp.zeros((8, LANES), f32))
                        continue
                    f = both[part * 8 : part * 8 + 8]
                    d = f - spread_line(aim_ref, t * 2 + part, first + line)
                    goal = d * lax.rsqrt(d * d + SMOOTH)
                    gs = []
                    for k in range(1, 5):
                        d = f - pltpu.roll(f, k, 0)
                        gs.append(d * lax.rsqrt(d * d + SMOOTH))
                    back = gs[2]
                    for k in (1, 0):
                        back = gs[k] + pltpu.roll(back, MEM - 1, 0)
                    back = pltpu.roll(back, MEM - 1, 0)
                    spread = (gs[0] + gs[1]) + (gs[2] + gs[3]) - back
                    weight = spread_line(weight_ref, t * 2 + part, first + line)
                    parts.append(weight * ((MEM - 1.0) * goal - spread))
                fgrad[line, t + 1] = jnp.concatenate(parts, axis=0).astype(bf16)
            yield

    def add_taps(g, x, acc, acc_next, chan_out):
        turned = g.T
        acc[...] += jnp.dot(turned, x[:, :256], preferred_element_type=f32)
        last = [turned[k * LANES - chan_out : k * LANES] for k in (1, 2)]
        last = jnp.concatenate(last, axis=0)
        acc_next[...] += jnp.dot(last, x[:, 256:], preferred_element_type=f32)

    def pull_back(n, fgrad, grads_ref, with_taps=True):
        def flat(line, start, count):
            return fgrad[line, start : start + count].reshape(count * 16, LANES)

        g = [
            jnp.concatenate(
                [flat(2 * k, 1, front), flat(2 * k + 1, 1, front), flat(2 * k, 0, front), flat(2 * k + 1, 0, front)],
                axis=1,
            )
            for k in range(2)
        ]
        pulled = jnp.dot(jnp.concatenate(g, axis=0), back_two[...], preferred_element_type=f32)
        grads = [
            pulled[:members, :LANES] + carry[...],
            pulled[members:, :LANES] + pulled[:members, LANES:],
        ]
        carry[...] = pulled[members:, LANES:]
        grads = [(grads[k] * slope[2 * n + k].reshape(members, LANES)).astype(bf16) for k in range(2)]
        yield
        grads_ref[...] = jnp.concatenate(grads, axis=1)
        if with_taps:
            g = [jnp.concatenate([flat(2 * k, 2, half), flat(2 * k + 1, 2, half)], axis=1) for k in range(2)]
            x = [operand(act, 2 * n + k, 1, half) for k in range(2)]
            add_taps(jnp.concatenate(g, axis=0), jnp.concatenate(x, axis=0), acc_two, acc_two_next, chan2)
            yield

    def first_taps(n, grads_ref, keep=None):
        g = grads_ref[16:]
        g = g if keep is None else g * keep
        add_taps(g, operand(source, n, 1, half), acc_one, acc_one_next, chan1)
        yield
        z = jnp.dot(pick, grads_ref[...], preferred_element_type=f32)
        z = jnp.concatenate([z[:48], z[48:]], axis=1)
        high = z.astype(bf16)
        sums[0, n] = high
        sums[1, n] = (z - high.astype(f32)).astype(bf16)
        yield

    def own_gradient(n, cast, fgrad):
        return loss_gradient(cast, fgrad, aims, weights, 4 * (n - 1), range(4))

    def second_segment(m, _):
        take_turns(
            second_product(2 * m + 3, cast_odd),
            own_gradient(2 * m + 2, cast_even, fgrad_even),
            pull_back(2 * m + 1, fgrad_odd, grads_odd),
            first_taps(2 * m, grads_even, jnp.where(m >= 1, 1.0, 0.0).astype(bf16)),
        )
        take_turns(
            second_product(2 * m + 4, cast_even),
            own_gradient(2 * m + 3, cast_odd, fgrad_odd),
            pull_back(2 * m + 2, fgrad_even, grads_even),
            first_taps(2 * m + 1, grads_odd),
        )
        return 0

    take_turns(second_product(0, cast_even))
    take_turns(
        second_product(1, cast_odd),
        loss_gradient(cast_even, fgrad_even, edge_aims, edge_weights, 0, range(1, 4)),
    )
    take_turns(
        second_product(2, cast_even),
        own_gradient(1, cast_odd, fgrad_odd),
        pull_back(0, fgrad_even, grads_even, with_taps=False),
    )
    lax.fori_loop(0, rows // 2 - 1, second_segment, 0)
    take_turns(
        own_gradient(rows, cast_even, fgrad_even),
        pull_back(rows - 1, fgrad_odd, grads_odd),
        first_taps(rows - 2, grads_even),
    )
    take_turns(pull_back(rows, fgrad_even, grads_even), first_taps(rows - 1, grads_odd))
    take_turns(first_taps(rows, grads_even))

    z = jnp.dot(sums[...].reshape(2 * (rows + 1) * 48, 512), back_one[...], preferred_element_type=f32)
    z = z.reshape(2, rows + 1, 48, 2 * LANES)
    z = z[0] + z[1]
    for n in range(rows):
        lat_lines[pl.ds(n, 48, stride=rows), :] = z[n + 1, :, :LANES] + z[n, :, LANES:]
    for t in range(own):
        out_lat[:, t * LANES : (t + 1) * LANES] = lat_lines[t * rows : (t + 1) * rows].astype(bf16)
    pack_taps(acc_one, acc_one_next, taps, 0, chan0, chan1, norm)
    pack_taps(acc_two, acc_two_next, taps, -(-9 // (LANES // chan0)) * chan1, chan1, chan2, norm)
    count = taps_keep.shape[0]
    odd = jnp.bitwise_and(lat_pos, 1)
    taps_keep[...] = taps[pl.ds(pl.multiple_of(odd * count, 8), count), :]
    taps_send[...] = taps[pl.ds(pl.multiple_of((1 - odd) * count, 8), count), :]


def swapped(array, axis, bit):
    return lax.ppermute(array, axis, [(i, i ^ bit) for i in range(lax.axis_size(axis))])


def total(array, axis, first, second):
    one, two, three = (swapped(array, axis, k).astype(jnp.float32) for k in (first, second, first ^ second))
    return (array.astype(jnp.float32) + one) + (two + three)


def local(
    latent, member_seeds, noise_scale, kernel_one, kernel_two, targets, land_words, channel_weight
):
    sample_count, rows, span = latent.shape
    chan0, chan1, chan2 = kernel_one.shape[2], kernel_one.shape[3], kernel_two.shape[3]
    lat_count = lax.axis_size("lat")
    own = span // LANES // lax.axis_size("mem")
    half = (own + 1) // 2
    assert sample_count == 1 and member_seeds.shape[0] == MEM and rows % 4 == 0 and own % 2 == 1 and lax.axis_size("mem") == 4
    assert 4 * chan2 == 2 * chan1 == chan0 and chan0 == 64
    vmem = pl.BlockSpec(memory_space=pltpu.VMEM)
    smem = pl.BlockSpec(memory_space=pltpu.SMEM)
    hbm = pl.BlockSpec(memory_space=pltpu.HBM)
    f32, bf16 = jnp.float32, jnp.bfloat16
    wide, front = half + 2, half + 1
    params = pltpu.CompilerParams(vmem_limit_bytes=32 * 1024 * 1024)
    small = pltpu.CompilerParams(vmem_limit_bytes=8 * 1024 * 1024)
    kernel_one = kernel_one.transpose(0, 1, 3, 2)
    kernel_two = kernel_two.transpose(0, 1, 3, 2)
    down, up = pl.pallas_call(
        functools.partial(edge_kernel, half, chan2),
        in_specs=[hbm] * 3,
        out_specs=[vmem] * 2,
        out_shape=[
            jax.ShapeDtypeStruct((2 * wide, 8, LANES), bf16),
            jax.ShapeDtypeStruct((1, 2 * wide * LANES), bf16),
        ],
        scratch_shapes=[
            pltpu.VMEM((1, 8, span), bf16),
            pltpu.VMEM((1, 8, span), bf16),
            pltpu.VMEM((8, land_words.shape[1]), jnp.int32),
            pltpu.VMEM((8, LANES), jnp.int32),
            pltpu.SemaphoreType.DMA((3,)),
        ],
        compiler_params=pltpu.CompilerParams(vmem_limit_bytes=56 * 1024 * 1024),
        name="edges",
    )(latent, targets, land_words)
    above = shifted(down, "lat", 1)
    below = shifted(up, "lat", -1)
    source, aims, weights = pl.pallas_call(
        functools.partial(prepare_kernel, half, chan0, chan2),
        in_specs=[smem] * 3 + [vmem] * 3,
        out_specs=[vmem] * 3,
        out_shape=[jax.ShapeDtypeStruct((rows, wide, 16, LANES), bf16)]
        + [jax.ShapeDtypeStruct((2 * front, 4 * rows, LANES), f32)] * 2,
        scratch_shapes=[pltpu.VMEM((2 * wide, rows, LANES), f32), pltpu.VMEM((4 * rows, LANES), jnp.int32)],
        compiler_params=small,
        cost_estimate=pl.CostEstimate(flops=10**8, bytes_accessed=10**7, transcendentals=0),
        name="prepare",
    )(member_seeds, noise_scale, channel_weight, latent, targets, land_words)
    one_late, two_late, source = lax.optimization_barrier((kernel_one, kernel_two, source))
    bands = pl.pallas_call(
        bands_kernel,
        in_specs=[vmem] * 2,
        out_specs=[vmem] * 4,
        out_shape=[jax.ShapeDtypeStruct((512, 256), bf16)] * 4,
        compiler_params=small,
        cost_estimate=pl.CostEstimate(flops=10**8, bytes_accessed=10**7, transcendentals=0),
        name="bands",
    )(one_late, two_late)
    norm = 1.0 / math.sqrt(sample_count * 4 * rows * lat_count * targets.shape[2])
    tap_rows = 5 * chan1 + 3 * chan2
    lat_grad, taps, taps_send = pl.pallas_call(
        functools.partial(band_kernel, half, (chan0, chan1, chan2), span, norm),
        in_specs=[smem] * 3 + [vmem] * 9,
        out_specs=[vmem] * 3,
        out_shape=[
            jax.ShapeDtypeStruct((rows, own * LANES), bf16),
            jax.ShapeDtypeStruct((tap_rows // 2, LANES), f32),
            jax.ShapeDtypeStruct((tap_rows // 2, LANES), f32),
        ],
        scratch_shapes=[
            pltpu.VMEM((2 * wide, 8, LANES), f32),
            pltpu.VMEM((2 * front, 8, LANES), f32),
            pltpu.VMEM((2 * front, 8, LANES), f32),
            pltpu.VMEM((rows + 4, wide + 1, 16, LANES), bf16),
            pltpu.VMEM((wide * 32, 2 * LANES), f32),
            pltpu.VMEM((wide * 32, 2 * LANES), f32),
            pltpu.VMEM((2 * rows + 4, wide, 16, LANES), bf16),
            pltpu.VMEM((2 * rows + 4, front, 16, LANES), f32),
            pltpu.VMEM((4, front, 16, LANES), bf16),
            pltpu.VMEM((4, front, 16, LANES), bf16),
            pltpu.VMEM((4, front + 1, 16, LANES), bf16),
            pltpu.VMEM((4, front + 1, 16, LANES), bf16),
            pltpu.VMEM((front * 16, 2 * LANES), bf16),
            pltpu.VMEM((front * 16, 2 * LANES), bf16),
            pltpu.VMEM((front * 16, LANES), f32),
            pltpu.VMEM((2, rows + 1, 48, 512), bf16),
            pltpu.VMEM((48 * rows, LANES), f32),
            pltpu.VMEM((tap_rows, LANES), f32),
            pltpu.VMEM((256, 256), f32),
            pltpu.VMEM((2 * chan1, 256), f32),
            pltpu.VMEM((256, 256), f32),
            pltpu.VMEM((2 * chan2, 256), f32),
        ],
        compiler_params=params,
        name="band",
    )(
        member_seeds,
        noise_scale,
        channel_weight,
        source,
        aims,
        weights,
        above,
        below,
        *bands,
    )
    taps = (taps + swapped(taps_send, "lat", 1)).astype(bf16)
    taps = total(taps, "mem", 1, 2)
    one, two, three = (swapped(lat_grad, "mem", k) for k in range(1, 4))
    bits = [1 << k for k in range(1, lat_count.bit_length() - 1)]
    for bit in bits:
        if bit == bits[-1]:
            taps, one, three = lax.optimization_barrier((taps, one, three))
        taps = taps + swapped(taps, "lat", bit)
    taps, two = lax.optimization_barrier((taps, two))
    other = swapped(taps, "lat", 1)
    latent_grad = pl.pallas_call(
        functools.partial(place_kernel, own),
        in_specs=[vmem] * 4,
        out_specs=vmem,
        out_shape=jax.ShapeDtypeStruct((1, rows, span), f32),
        compiler_params=small,
        name="place",
    )(lat_grad, one, two, three)
    one, two = pl.pallas_call(
        taps_kernel,
        in_specs=[vmem] * 2,
        out_specs=[vmem] * 2,
        out_shape=[
            jax.ShapeDtypeStruct(kernel_one.shape, f32),
            jax.ShapeDtypeStruct(kernel_two.shape, f32),
        ],
        scratch_shapes=[pltpu.VMEM((tap_rows, LANES), f32)],
        compiler_params=small,
        name="taps",
    )(taps, other)
    return (latent_grad, one.transpose(0, 1, 3, 2), two.transpose(0, 1, 3, 2))


def solution(mesh):
    in_specs = (P(None, "lat", None), P(), P(), P(), P(), P(None, "lat", None), P("lat", None), P())
    out_specs = (P(None, "lat", None), P(), P())
    return jax.shard_map(local, mesh=mesh, in_specs=in_specs, out_specs=out_specs, check_vma=False)
```

```python
import functools
import math

import jax
import jax.numpy as jnp
from jax import lax
from jax.experimental import pallas as pl
from jax.experimental.pallas import tpu as pltpu
from jax.sharding import PartitionSpec as P

SMOOTH = 0.01
HASH_CELL = 1103515245
HASH_SEED = 747796405
HASH_MIX = 277803737
LANES = 128
MEM = 8
GELU_A = math.sqrt(2.0 / math.pi)
GELU_B = 0.044715


def shifted(array, axis, by):
    peers = lax.axis_size(axis)
    pairs = [(i, i + by) for i in range(peers) if 0 <= i + by < peers]
    return lax.ppermute(array, axis, pairs)


def iota(shape, axis):
    return lax.broadcasted_iota(jnp.int32, shape, axis)


def lane_table(ref, count):
    lane = iota((8, LANES), 1) % count
    total = jnp.zeros((8, LANES), jnp.float32)
    for k in range(count):
        total = jnp.where(lane == k, ref[k], total)
    return total


def build_band(kernel_ref, band_ref):
    chan_out, chan_in = kernel_ref.shape[2], kernel_ref.shape[3]
    cells = LANES // chan_in
    repeat = (iota((chan_out, LANES), 1) % chan_out == iota((chan_out, LANES), 0)).astype(jnp.bfloat16)
    wide = {}
    for a in range(3):
        for b in range(3):
            wide[a, b] = lax.dot_general(
                kernel_ref[a, b], repeat, (((0,), (0,)), ((), ())), preferred_element_type=jnp.float32
            )
    column = iota((chan_in, LANES), 1) // chan_out
    zero = jnp.zeros((chan_in, LANES), jnp.float32)
    for block in range(2):
        for row in range(2):
            for cell in range(cells):
                at = block * 256 + row * LANES + cell * chan_in
                for sub in range(2):
                    a = sub - 2 * row + 1
                    part = zero
                    for q in range(2 * cells):
                        b = q - 2 * (cell + block * cells) + 1
                        if 0 <= a <= 2 and 0 <= b <= 2:
                            part = jnp.where(column == q, wide[a, b], part)
                    band_ref[at : at + chan_in, sub * LANES : (sub + 1) * LANES] = part.astype(jnp.bfloat16)


def build_back(kernel_ref, back_ref):
    chan_out, chan_in = kernel_ref.shape[2], kernel_ref.shape[3]
    cells = LANES // chan_in
    repeat = (iota((chan_in, LANES), 1) % chan_in == iota((chan_in, LANES), 0)).astype(jnp.bfloat16)
    flat = kernel_ref[...].reshape(9 * chan_out, chan_in)
    wide = jnp.dot(flat, repeat, preferred_element_type=jnp.float32)
    column = iota((chan_out, LANES), 1) // chan_in
    zero = jnp.zeros((chan_out, LANES), jnp.float32)
    for block in range(2):
        for sub in range(2):
            for q in range(2 * cells):
                at = block * 256 + sub * LANES + q * chan_out
                for row in range(2):
                    a = sub - 2 * row + 1
                    part = zero
                    for cell in range(cells):
                        b = q - 2 * (cell + block * cells) + 1
                        if 0 <= a <= 2 and 0 <= b <= 2:
                            tap = (3 * a + b) * chan_out
                            part = jnp.where(column == cell, wide[tap : tap + chan_out], part)
                    back_ref[at : at + chan_out, row * LANES : (row + 1) * LANES] = part.astype(jnp.bfloat16)


def pack_taps(acc_ref, next_ref, out_ref, first, chan_in, chan_out, norm):
    cells = LANES // chan_in
    group = iota((chan_out, LANES), 1) // chan_in
    packed = None
    for k in range(9):
        a, b = divmod(k, 3)
        row, sub = ((1, 1), (0, 0), (0, 1))[a]
        slot = k % cells
        part = None
        for reach in range(cells + 1):
            q = 2 * reach + b - 1
            if 0 <= q < 2 * cells:
                block, cell = reach // cells, reach % cells
                lines = sub * LANES + q * chan_out if block == 0 else sub * chan_out
                ref = acc_ref if block == 0 else next_ref
                piece = ref[lines : lines + chan_out, row * LANES : (row + 1) * LANES]
                turn = (slot - cell) % cells * chan_in
                piece = pltpu.roll(piece, turn, 1) if turn else piece
                part = piece if part is None else part + piece
        packed = part if slot == 0 else jnp.where(group == slot, part, packed)
        if slot == cells - 1 or k == 8:
            at = first + k // cells * chan_out
            out_ref[at : at + chan_out, :] = packed * norm


def spread_line(ref, slot, at):
    return jnp.broadcast_to(ref[slot, pl.ds(at, 1), :], (8, LANES))


def window_block(mem_pos, own, half, blocks, part, t):
    at = mem_pos * own + part * half + t + (blocks - 1)
    at = jnp.where(at >= blocks, at - blocks, at)
    return jnp.where(at >= blocks, at - blocks, at)


def land_of(words, block, chan):
    cell = block * (LANES // chan) + iota(words.shape, 1) // chan
    word = jnp.right_shift(cell * 2185, 16)
    picked = jnp.take_along_axis(words, word, axis=1, mode="promise_in_bounds")
    return jnp.bitwise_and(jnp.right_shift(picked, cell - 30 * word), 1).astype(jnp.float32)


def edge_kernel(
    half,
    chan,
    latent_hbm,
    targets_hbm,
    land_hbm,
    down,
    up,
    latent,
    targets,
    land,
    words,
    sems,
):
    rows = latent.shape[1]
    blocks = latent.shape[2] // LANES
    edge = pl.ds(targets_hbm.shape[1] - 8, 8)
    copies = [
        pltpu.make_async_copy(latent_hbm, latent, sems.at[0]),
        pltpu.make_async_copy(targets_hbm.at[:, edge], targets, sems.at[1]),
        pltpu.make_async_copy(land_hbm.at[edge], land, sems.at[2]),
    ]
    for copy in copies:
        copy.start()
    for copy in copies:
        copy.wait()
    own = blocks // lax.axis_size("mem")
    mem_pos = lax.axis_index("mem")
    words[...] = jnp.zeros(words.shape, jnp.int32)
    words[:, : land.shape[1]] = land[...]
    line = iota((8, LANES), 0)
    for t in range(half + 2):
        for part in range(2):
            block = window_block(mem_pos, own, half, blocks, part, t)
            off = pl.multiple_of(block * LANES, LANES)
            slot = t * 2 + part
            cells = latent[0, :, pl.ds(off, LANES)].astype(jnp.float32)
            aims = targets[0, :, pl.ds(off, LANES)].astype(jnp.float32)
            mask = land_of(words[...], block, chan)
            pack = pltpu.roll(cells, 1, 0)
            pack = jnp.where((line >= 1) & (line <= 3), pltpu.roll(aims, 4, 0), pack)
            pack = jnp.where((line >= 4) & (line <= 6), pltpu.roll(mask, 7, 0), pack)
            down[slot] = pack.astype(jnp.bfloat16)
            up[:, slot * LANES : (slot + 1) * LANES] = cells[0:1].astype(jnp.bfloat16)


def place_kernel(own, part0, part1, part2, part3, latent_grad):
    mem_pos = lax.axis_index("mem")
    for k, part in enumerate((part0, part1, part2, part3)):
        off = pl.multiple_of(jnp.bitwise_xor(mem_pos, k) * own * LANES, LANES)
        latent_grad[0, :, pl.ds(off, own * LANES)] = part[...].astype(jnp.float32)


def taps_kernel(mine, other, grad_one, grad_two, taps):
    count = mine.shape[0]
    odd = jnp.bitwise_and(lax.axis_index("lat"), 1)
    taps[pl.ds(pl.multiple_of(odd * count, 8), count), :] = mine[...]
    taps[pl.ds(pl.multiple_of((1 - odd) * count, 8), count), :] = other[...]
    first = 0
    for out in (grad_one, grad_two):
        chan_out, chan_in = out.shape[2], out.shape[3]
        cells = LANES // chan_in
        for k in range(9):
            at = first + k // cells * chan_out
            block = taps[at : at + chan_out, :]
            turn = (-(k % cells)) % cells * chan_in
            block = pltpu.roll(block, turn, 1) if turn else block
            out[k // 3, k % 3] = block[:, :chan_in]
        first += -(-9 // cells) * chan_out


def make_source(i, row, total_rows, span, own, half, seeds, scale, chan, line, store):
    blocks = span // LANES
    mem_pos = lax.axis_index("mem")
    sublane = iota((8, LANES), 0)
    seed_table = jnp.zeros((8, LANES), jnp.int32)
    for m in range(MEM):
        seed_table = jnp.where(sublane == m, seeds[m], seed_table)
    hash_table = iota((8, LANES), 1) * HASH_CELL + seed_table * HASH_SEED
    scale_table = lane_table(scale, chan)
    inside = jnp.where(row < total_rows, 1.0, 0.0).astype(jnp.float32)
    for t in range(half + 2):
        parts = []
        for part in range(2):
            first = (row * span + window_block(mem_pos, own, half, blocks, part, t) * LANES) * HASH_CELL
            h = hash_table + first
            h = jnp.bitwise_xor(h, jnp.right_shift(h, 15))
            h = h * HASH_MIX
            h = jnp.bitwise_xor(h, jnp.right_shift(h, 13))
            noise = jnp.bitwise_and(h, 65535).astype(jnp.float32) * (1.0 / 65536.0) - 0.5
            noise = noise * 3.4641016
            parts.append((line(t * 2 + part, i) + noise * scale_table) * inside)
        store(i, t, jnp.concatenate(parts, axis=0).astype(jnp.bfloat16))


def weight_lines(grid_row, channel_weight, chan, grid_total):
    latitude = math.pi / 2 - math.pi * (grid_row.astype(jnp.float32) + 0.5) / grid_total
    cosine = jnp.where(grid_row >= 0, jnp.cos(latitude), 0.0)
    channels = jnp.tile(lane_table(channel_weight, chan), (grid_row.shape[0] // 8, 1))
    return cosine * (channels * (1.0 / (MEM * (MEM - 1))))


def prepare_kernel(
    half, chan, chan2, seeds, scale, channel_weight, latent, targets, land, source, aims, weights, lines, words
):
    rows, span = latent.shape[1], latent.shape[2]
    blocks = span // LANES
    own = blocks // lax.axis_size("mem")
    total_rows = rows * lax.axis_size("lat")
    lat_pos, mem_pos = lax.axis_index("lat"), lax.axis_index("mem")
    grid_row = iota((4 * rows, LANES), 0) + lat_pos * 4 * rows
    base = weight_lines(grid_row, channel_weight, chan2, 4 * total_rows)
    words[...] = jnp.zeros(words.shape, jnp.int32)
    words[:, : land.shape[1]] = land[...]
    for t in range(half + 2):
        for part in range(2):
            block = window_block(mem_pos, own, half, blocks, part, t)
            off = pl.multiple_of(block * LANES, LANES)
            slot = t * 2 + part
            lines[slot] = latent[0, :, pl.ds(off, LANES)].astype(jnp.float32)
            if t < half + 1:
                aims[slot] = targets[0, :, pl.ds(off, LANES)].astype(jnp.float32)
                weights[slot] = base + base * land_of(words[...], block, chan2)

    def line(slot, i):
        return spread_line(lines, slot, i)

    def store(i, t, value):
        source[i, t] = value

    def step(i, _):
        make_source(
            i, lat_pos * rows + i, total_rows, span, own, half, seeds, scale, chan, line, store
        )
        return 0

    lax.fori_loop(0, rows, step, 0)


def bands_kernel(kernel_one, kernel_two, band_one, band_two, back_one, back_two):
    build_band(kernel_one, band_one)
    build_band(kernel_two, band_two)
    build_back(kernel_one, back_one)
    build_back(kernel_two, back_two)


def take_turns(*parts):
    parts = list(parts)
    while parts:
        for part in tuple(parts):
            if next(part, part) is part:
                parts.remove(part)


def band_kernel(
    half,
    chans,
    span,
    norm,
    seeds,
    scale,
    channel_weight,
    own_source,
    aims,
    weights,
    above,
    below,
    band_one,
    band_two,
    back_one,
    back_two,
    out_lat,
    taps_keep,
    taps_send,
    lat_rows,
    edge_aims,
    edge_weights,
    source,
    pre_even,
    pre_odd,
    act,
    slope,
    cast_even,
    cast_odd,
    fgrad_even,
    fgrad_odd,
    twice,
    grads_even,
    grads_odd,
    carry,
    sums,
    lat_lines,
    taps,
    acc_one,
    acc_one_next,
    acc_two,
    acc_two_next,
):
    rows = own_source.shape[0]
    blocks = span // LANES
    own = blocks // lax.axis_size("mem")
    total_rows = rows * lax.axis_size("lat")
    lat_pos = lax.axis_index("lat")
    wide = half + 2
    front = half + 1
    chan0, chan1, chan2 = chans
    f32, bf16 = jnp.float32, jnp.bfloat16

    grid_row = iota((8, LANES), 0) + (lat_pos * 4 * rows - 4)
    base = weight_lines(grid_row, channel_weight, chan2, 4 * total_rows)
    for slot in range(2 * wide):
        edge = above[slot].astype(f32)
        lat_rows[slot, 0:1] = edge[0:1]
        lat_rows[slot, 1:2] = below[:, slot * LANES : (slot + 1) * LANES].astype(f32)
        if slot < 2 * front:
            edge_aims[slot] = edge
            edge_weights[slot] = base + base * pltpu.roll(edge, 5, 0)

    source[rows + 2 :] = jnp.zeros((2,) + source.shape[1:], bf16)
    source[:, wide] = jnp.zeros((source.shape[0],) + source.shape[2:], bf16)
    fgrad_even[0] = jnp.zeros(fgrad_even.shape[1:], bf16)
    for fgrad in (fgrad_even, fgrad_odd):
        fgrad[:, 0] = jnp.zeros((4,) + fgrad.shape[2:], bf16)
    carry[...] = jnp.zeros(carry.shape, f32)
    for acc in (acc_one, acc_one_next, acc_two, acc_two_next):
        acc[...] = jnp.zeros(acc.shape, f32)

    def line(slot, i):
        return spread_line(lat_rows, slot, i)

    def store(i, t, value):
        source[i * (rows + 1), t] = value

    def edge_source(i, _):
        row = lat_pos * rows - 1 + i * (rows + 1)
        make_source(i, row, total_rows, span, own, half, seeds, scale, chan0, line, store)
        return 0

    lax.fori_loop(0, 2, edge_source, 0)
    source[1 : rows + 1, 0:wide] = own_source[...]

    def operand(ref, i, start, count):
        def piece(r, at):
            return ref[r, pl.ds(at, count)].reshape(count * 16, LANES)

        return jnp.concatenate(
            [piece(i, start), piece(i + 1, start), piece(i, start + 1), piece(i + 1, start + 1)], axis=1
        )

    def first_product(pair, pre):
        taken = jnp.concatenate([operand(source, 2 * pair + k, 0, wide) for k in range(2)], axis=0)
        pre[...] = jnp.dot(taken, band_one[...], preferred_element_type=f32)

    def first_gelu(pair, pre):
        for k in range(2):
            for t in range(wide):
                for sub in range(2):
                    at = (k * wide + t) * 16
                    x = pre[at : at + 16, sub * LANES : (sub + 1) * LANES]
                    square = x * x
                    th = jnp.tanh(x * (GELU_A + (GELU_A * GELU_B) * square))
                    plus = 0.5 + 0.5 * th
                    act[4 * pair + 2 * k + sub, t] = (x * plus).astype(bf16)
                    if t < front:
                        d = plus + (x * plus) * (1.0 - th) * (GELU_A + (3.0 * GELU_A * GELU_B) * square)
                        if t == half:
                            d = jnp.where(iota((16, LANES), 0) < 8, d, 0.0)
                        slope[4 * pair + 2 * k + sub, t] = d

    def first_segment(m, _):
        first_product(2 * m + 1, pre_odd)
        first_gelu(2 * m, pre_even)
        first_product(2 * m + 2, pre_even)
        first_gelu(2 * m + 1, pre_odd)
        return 0

    first_product(0, pre_even)
    lax.fori_loop(0, rows // 4, first_segment, 0)
    first_gelu(rows // 2, pre_even)

    members = front * 16
    owner = iota((48, members), 0)
    group = iota((48, members), 1) // 8
    place = (group % 2) * half + group // 2
    real = (group // 2 > 0) & (place - 1 < own)
    pick_own = (real & (place - 1 == owner)).astype(bf16)
    pick_prev = ((group // 2 < half) & (place == owner)).astype(bf16)
    pick = jnp.concatenate([pick_own, pick_prev], axis=0)

    def second_product(n, cast):
        taken = jnp.concatenate([operand(act, 2 * n + k, 0, front) for k in range(2)], axis=0)
        out = jnp.dot(taken, band_two[...], preferred_element_type=f32).astype(bf16)
        for k in range(2):
            for sub in range(2):
                part = out[k * members : (k + 1) * members, sub * LANES : (sub + 1) * LANES]
                cast[2 * k + sub] = part.reshape(front, 16, LANES)
        yield

    def loss_gradient(cast, fgrad, aim_ref, weight_ref, first, lines):
        for line in lines:
            for t in range(front):
                both = cast[line, t].astype(f32)
                parts = []
                for part in range(2):
                    if t == half and part == 1:
                        parts.append(jnp.zeros((8, LANES), f32))
                        continue
                    f = both[part * 8 : part * 8 + 8]
                    d = f - spread_line(aim_ref, t * 2 + part, first + line)
                    goal = d * lax.rsqrt(d * d + SMOOTH)
                    for start in (0, 2 * MEM):
                        twice[line, t * 2 + part, pl.ds(start, MEM, stride=2), :] = f
                    gs = []
                    for k in range(1, 5):
                        d = f - twice[line, t * 2 + part, pl.ds(2 * (MEM - k), MEM, stride=2), :]
                        gs.append(d * lax.rsqrt(d * d + SMOOTH))
                    back = gs[2]
                    for k in (1, 0):
                        back = gs[k] + pltpu.roll(back, MEM - 1, 0)
                    back = pltpu.roll(back, MEM - 1, 0)
                    spread = (gs[0] + gs[1]) + (gs[2] + gs[3]) - back
                    weight = spread_line(weight_ref, t * 2 + part, first + line)
                    parts.append(weight * ((MEM - 1.0) * goal - spread))
                fgrad[line, t + 1] = jnp.concatenate(parts, axis=0).astype(bf16)
            yield

    def add_taps(g, x, acc, acc_next, chan_out):
        turned = g.T
        acc[...] += jnp.dot(turned, x[:, :256], preferred_element_type=f32)
        last = [turned[k * LANES - chan_out : k * LANES] for k in (1, 2)]
        last = jnp.concatenate(last, axis=0)
        acc_next[...] += jnp.dot(last, x[:, 256:], preferred_element_type=f32)

    def pull_back(n, fgrad, grads_ref, with_taps=True):
        def flat(line, start, count):
            return fgrad[line, start : start + count].reshape(count * 16, LANES)

        g = [
            jnp.concatenate(
                [flat(2 * k, 1, front), flat(2 * k + 1, 1, front), flat(2 * k, 0, front), flat(2 * k + 1, 0, front)],
                axis=1,
            )
            for k in range(2)
        ]
        pulled = jnp.dot(jnp.concatenate(g, axis=0), back_two[...], preferred_element_type=f32)
        grads = [
            pulled[:members, :LANES] + carry[...],
            pulled[members:, :LANES] + pulled[:members, LANES:],
        ]
        carry[...] = pulled[members:, LANES:]
        grads = [(grads[k] * slope[2 * n + k].reshape(members, LANES)).astype(bf16) for k in range(2)]
        yield
        grads_ref[...] = jnp.concatenate(grads, axis=1)
        if with_taps:
            g = [jnp.concatenate([flat(2 * k, 2, half), flat(2 * k + 1, 2, half)], axis=1) for k in range(2)]
            x = [operand(act, 2 * n + k, 1, half) for k in range(2)]
            add_taps(jnp.concatenate(g, axis=0), jnp.concatenate(x, axis=0), acc_two, acc_two_next, chan2)
            yield

    def first_taps(n, grads_ref, keep=None):
        g = grads_ref[16:]
        g = g if keep is None else g * keep
        add_taps(g, operand(source, n, 1, half), acc_one, acc_one_next, chan1)
        yield
        z = jnp.dot(pick, grads_ref[...], preferred_element_type=f32)
        z = jnp.concatenate([z[:48], z[48:]], axis=1)
        high = z.astype(bf16)
        sums[0, n] = high
        sums[1, n] = (z - high.astype(f32)).astype(bf16)
        yield

    def own_gradient(n, cast, fgrad):
        return loss_gradient(cast, fgrad, aims, weights, 4 * (n - 1), range(4))

    def second_segment(m, _):
        take_turns(
            second_product(2 * m + 3, cast_odd),
            own_gradient(2 * m + 2, cast_even, fgrad_even),
            pull_back(2 * m + 1, fgrad_odd, grads_odd),
            first_taps(2 * m, grads_even, jnp.where(m >= 1, 1.0, 0.0).astype(bf16)),
        )
        take_turns(
            second_product(2 * m + 4, cast_even),
            own_gradient(2 * m + 3, cast_odd, fgrad_odd),
            pull_back(2 * m + 2, fgrad_even, grads_even),
            first_taps(2 * m + 1, grads_odd),
        )
        return 0

    take_turns(second_product(0, cast_even))
    take_turns(
        second_product(1, cast_odd),
        loss_gradient(cast_even, fgrad_even, edge_aims, edge_weights, 0, range(1, 4)),
    )
    take_turns(
        second_product(2, cast_even),
        own_gradient(1, cast_odd, fgrad_odd),
        pull_back(0, fgrad_even, grads_even, with_taps=False),
    )
    lax.fori_loop(0, rows // 2 - 1, second_segment, 0)
    take_turns(
        own_gradient(rows, cast_even, fgrad_even),
        pull_back(rows - 1, fgrad_odd, grads_odd),
        first_taps(rows - 2, grads_even),
    )
    take_turns(pull_back(rows, fgrad_even, grads_even), first_taps(rows - 1, grads_odd))
    take_turns(first_taps(rows, grads_even))

    z = jnp.dot(sums[...].reshape(2 * (rows + 1) * 48, 512), back_one[...], preferred_element_type=f32)
    z = z.reshape(2, rows + 1, 48, 2 * LANES)
    z = z[0] + z[1]
    for n in range(rows):
        lat_lines[pl.ds(n, 48, stride=rows), :] = z[n + 1, :, :LANES] + z[n, :, LANES:]
    for t in range(own):
        out_lat[:, t * LANES : (t + 1) * LANES] = lat_lines[t * rows : (t + 1) * rows].astype(bf16)
    pack_taps(acc_one, acc_one_next, taps, 0, chan0, chan1, norm)
    pack_taps(acc_two, acc_two_next, taps, -(-9 // (LANES // chan0)) * chan1, chan1, chan2, norm)
    count = taps_keep.shape[0]
    odd = jnp.bitwise_and(lat_pos, 1)
    taps_keep[...] = taps[pl.ds(pl.multiple_of(odd * count, 8), count), :]
    taps_send[...] = taps[pl.ds(pl.multiple_of((1 - odd) * count, 8), count), :]


def swapped(array, axis, bit):
    return lax.ppermute(array, axis, [(i, i ^ bit) for i in range(lax.axis_size(axis))])


def total(array, axis, first, second):
    one, two, three = (swapped(array, axis, k).astype(jnp.float32) for k in (first, second, first ^ second))
    return (array.astype(jnp.float32) + one) + (two + three)


def local(
    latent, member_seeds, noise_scale, kernel_one, kernel_two, targets, land_words, channel_weight
):
    sample_count, rows, span = latent.shape
    chan0, chan1, chan2 = kernel_one.shape[2], kernel_one.shape[3], kernel_two.shape[3]
    lat_count = lax.axis_size("lat")
    own = span // LANES // lax.axis_size("mem")
    half = (own + 1) // 2
    assert sample_count == 1 and member_seeds.shape[0] == MEM and rows % 4 == 0 and own % 2 == 1 and lax.axis_size("mem") == 4
    assert 4 * chan2 == 2 * chan1 == chan0 and chan0 == 64
    vmem = pl.BlockSpec(memory_space=pltpu.VMEM)
    smem = pl.BlockSpec(memory_space=pltpu.SMEM)
    hbm = pl.BlockSpec(memory_space=pltpu.HBM)
    f32, bf16 = jnp.float32, jnp.bfloat16
    wide, front = half + 2, half + 1
    params = pltpu.CompilerParams(vmem_limit_bytes=32 * 1024 * 1024)
    small = pltpu.CompilerParams(vmem_limit_bytes=8 * 1024 * 1024)
    kernel_one = kernel_one.transpose(0, 1, 3, 2)
    kernel_two = kernel_two.transpose(0, 1, 3, 2)
    down, up = pl.pallas_call(
        functools.partial(edge_kernel, half, chan2),
        in_specs=[hbm] * 3,
        out_specs=[vmem] * 2,
        out_shape=[
            jax.ShapeDtypeStruct((2 * wide, 8, LANES), bf16),
            jax.ShapeDtypeStruct((1, 2 * wide * LANES), bf16),
        ],
        scratch_shapes=[
            pltpu.VMEM((1, 8, span), bf16),
            pltpu.VMEM((1, 8, span), bf16),
            pltpu.VMEM((8, land_words.shape[1]), jnp.int32),
            pltpu.VMEM((8, LANES), jnp.int32),
            pltpu.SemaphoreType.DMA((3,)),
        ],
        compiler_params=pltpu.CompilerParams(vmem_limit_bytes=56 * 1024 * 1024),
        name="edges",
    )(latent, targets, land_words)
    above = shifted(down, "lat", 1)
    below = shifted(up, "lat", -1)
    source, aims, weights = pl.pallas_call(
        functools.partial(prepare_kernel, half, chan0, chan2),
        in_specs=[smem] * 3 + [vmem] * 3,
        out_specs=[vmem] * 3,
        out_shape=[jax.ShapeDtypeStruct((rows, wide, 16, LANES), bf16)]
        + [jax.ShapeDtypeStruct((2 * front, 4 * rows, LANES), f32)] * 2,
        scratch_shapes=[pltpu.VMEM((2 * wide, rows, LANES), f32), pltpu.VMEM((4 * rows, LANES), jnp.int32)],
        compiler_params=small,
        cost_estimate=pl.CostEstimate(flops=10**8, bytes_accessed=10**7, transcendentals=0),
        name="prepare",
    )(member_seeds, noise_scale, channel_weight, latent, targets, land_words)
    one_late, two_late, source = lax.optimization_barrier((kernel_one, kernel_two, source))
    bands = pl.pallas_call(
        bands_kernel,
        in_specs=[vmem] * 2,
        out_specs=[vmem] * 4,
        out_shape=[jax.ShapeDtypeStruct((512, 256), bf16)] * 4,
        compiler_params=small,
        cost_estimate=pl.CostEstimate(flops=10**8, bytes_accessed=10**7, transcendentals=0),
        name="bands",
    )(one_late, two_late)
    norm = 1.0 / math.sqrt(sample_count * 4 * rows * lat_count * targets.shape[2])
    tap_rows = 5 * chan1 + 3 * chan2
    lat_grad, taps, taps_send = pl.pallas_call(
        functools.partial(band_kernel, half, (chan0, chan1, chan2), span, norm),
        in_specs=[smem] * 3 + [vmem] * 9,
        out_specs=[vmem] * 3,
        out_shape=[
            jax.ShapeDtypeStruct((rows, own * LANES), bf16),
            jax.ShapeDtypeStruct((tap_rows // 2, LANES), f32),
            jax.ShapeDtypeStruct((tap_rows // 2, LANES), f32),
        ],
        scratch_shapes=[
            pltpu.VMEM((2 * wide, 8, LANES), f32),
            pltpu.VMEM((2 * front, 8, LANES), f32),
            pltpu.VMEM((2 * front, 8, LANES), f32),
            pltpu.VMEM((rows + 4, wide + 1, 16, LANES), bf16),
            pltpu.VMEM((wide * 32, 2 * LANES), f32),
            pltpu.VMEM((wide * 32, 2 * LANES), f32),
            pltpu.VMEM((2 * rows + 4, wide, 16, LANES), bf16),
            pltpu.VMEM((2 * rows + 4, front, 16, LANES), f32),
            pltpu.VMEM((4, front, 16, LANES), bf16),
            pltpu.VMEM((4, front, 16, LANES), bf16),
            pltpu.VMEM((4, front + 1, 16, LANES), bf16),
            pltpu.VMEM((4, front + 1, 16, LANES), bf16),
            pltpu.VMEM((4, 2 * front, 4 * MEM, LANES), f32),
            pltpu.VMEM((front * 16, 2 * LANES), bf16),
            pltpu.VMEM((front * 16, 2 * LANES), bf16),
            pltpu.VMEM((front * 16, LANES), f32),
            pltpu.VMEM((2, rows + 1, 48, 512), bf16),
            pltpu.VMEM((48 * rows, LANES), f32),
            pltpu.VMEM((tap_rows, LANES), f32),
            pltpu.VMEM((256, 256), f32),
            pltpu.VMEM((2 * chan1, 256), f32),
            pltpu.VMEM((256, 256), f32),
            pltpu.VMEM((2 * chan2, 256), f32),
        ],
        compiler_params=params,
        name="band",
    )(
        member_seeds,
        noise_scale,
        channel_weight,
        source,
        aims,
        weights,
        above,
        below,
        *bands,
    )
    taps = (taps + swapped(taps_send, "lat", 1)).astype(bf16)
    taps = total(taps, "mem", 1, 2)
    one, two, three = (swapped(lat_grad, "mem", k) for k in range(1, 4))
    bits = [1 << k for k in range(1, lat_count.bit_length() - 1)]
    for bit in bits:
        if bit == bits[-1]:
            taps, one, three = lax.optimization_barrier((taps, one, three))
        taps = taps + swapped(taps, "lat", bit)
    taps, two = lax.optimization_barrier((taps, two))
    other = swapped(taps, "lat", 1)
    latent_grad = pl.pallas_call(
        functools.partial(place_kernel, own),
        in_specs=[vmem] * 4,
        out_specs=vmem,
        out_shape=jax.ShapeDtypeStruct((1, rows, span), f32),
        compiler_params=small,
        name="place",
    )(lat_grad, one, two, three)
    one, two = pl.pallas_call(
        taps_kernel,
        in_specs=[vmem] * 2,
        out_specs=[vmem] * 2,
        out_shape=[
            jax.ShapeDtypeStruct(kernel_one.shape, f32),
            jax.ShapeDtypeStruct(kernel_two.shape, f32),
        ],
        scratch_shapes=[pltpu.VMEM((tap_rows, LANES), f32)],
        compiler_params=small,
        name="taps",
    )(taps, other)
    return (latent_grad, one.transpose(0, 1, 3, 2), two.transpose(0, 1, 3, 2))


def solution(mesh):
    in_specs = (P(None, "lat", None), P(), P(), P(), P(), P(None, "lat", None), P("lat", None), P())
    out_specs = (P(None, "lat", None), P(), P())
    return jax.shard_map(local, mesh=mesh, in_specs=in_specs, out_specs=out_specs, check_vma=False)
```

```python
import functools
import math

import jax
import jax.numpy as jnp
from jax import lax
from jax.experimental import pallas as pl
from jax.experimental.pallas import tpu as pltpu
from jax.sharding import PartitionSpec as P

SMOOTH = 0.01
HASH_CELL = 1103515245
HASH_SEED = 747796405
HASH_MIX = 277803737
LANES = 128
MEM = 8
GELU_A = math.sqrt(2.0 / math.pi)
GELU_B = 0.044715


def shifted(array, axis, by):
    peers = lax.axis_size(axis)
    pairs = [(i, i + by) for i in range(peers) if 0 <= i + by < peers]
    return lax.ppermute(array, axis, pairs)


def iota(shape, axis):
    return lax.broadcasted_iota(jnp.int32, shape, axis)


def lane_table(ref, count):
    lane = iota((8, LANES), 1) % count
    total = jnp.zeros((8, LANES), jnp.float32)
    for k in range(count):
        total = jnp.where(lane == k, ref[k], total)
    return total


def build_band(kernel_ref, band_ref):
    chan_out, chan_in = kernel_ref.shape[2], kernel_ref.shape[3]
    cells = LANES // chan_in
    repeat = (iota((chan_out, LANES), 1) % chan_out == iota((chan_out, LANES), 0)).astype(jnp.bfloat16)
    wide = {}
    for a in range(3):
        for b in range(3):
            wide[a, b] = lax.dot_general(
                kernel_ref[a, b], repeat, (((0,), (0,)), ((), ())), preferred_element_type=jnp.float32
            )
    column = iota((chan_in, LANES), 1) // chan_out
    zero = jnp.zeros((chan_in, LANES), jnp.float32)
    for block in range(2):
        for row in range(2):
            for cell in range(cells):
                at = block * 256 + row * LANES + cell * chan_in
                for sub in range(2):
                    a = sub - 2 * row + 1
                    part = zero
                    for q in range(2 * cells):
                        b = q - 2 * (cell + block * cells) + 1
                        if 0 <= a <= 2 and 0 <= b <= 2:
                            part = jnp.where(column == q, wide[a, b], part)
                    band_ref[at : at + chan_in, sub * LANES : (sub + 1) * LANES] = part.astype(jnp.bfloat16)


def build_back(kernel_ref, back_ref):
    chan_out, chan_in = kernel_ref.shape[2], kernel_ref.shape[3]
    cells = LANES // chan_in
    repeat = (iota((chan_in, LANES), 1) % chan_in == iota((chan_in, LANES), 0)).astype(jnp.bfloat16)
    flat = kernel_ref[...].reshape(9 * chan_out, chan_in)
    wide = jnp.dot(flat, repeat, preferred_element_type=jnp.float32)
    column = iota((chan_out, LANES), 1) // chan_in
    zero = jnp.zeros((chan_out, LANES), jnp.float32)
    for block in range(2):
        for sub in range(2):
            for q in range(2 * cells):
                at = block * 256 + sub * LANES + q * chan_out
                for row in range(2):
                    a = sub - 2 * row + 1
                    part = zero
                    for cell in range(cells):
                        b = q - 2 * (cell + block * cells) + 1
                        if 0 <= a <= 2 and 0 <= b <= 2:
                            tap = (3 * a + b) * chan_out
                            part = jnp.where(column == cell, wide[tap : tap + chan_out], part)
                    back_ref[at : at + chan_out, row * LANES : (row + 1) * LANES] = part.astype(jnp.bfloat16)


def pack_taps(acc_ref, next_ref, out_ref, first, chan_in, chan_out, norm):
    cells = LANES // chan_in
    group = iota((chan_out, LANES), 1) // chan_in
    packed = None
    for k in range(9):
        a, b = divmod(k, 3)
        row, sub = ((1, 1), (0, 0), (0, 1))[a]
        slot = k % cells
        part = None
        for reach in range(cells + 1):
            q = 2 * reach + b - 1
            if 0 <= q < 2 * cells:
                block, cell = reach // cells, reach % cells
                lines = sub * LANES + q * chan_out if block == 0 else sub * chan_out
                ref = acc_ref if block == 0 else next_ref
                piece = ref[lines : lines + chan_out, row * LANES : (row + 1) * LANES]
                turn = (slot - cell) % cells * chan_in
                piece = pltpu.roll(piece, turn, 1) if turn else piece
                part = piece if part is None else part + piece
        packed = part if slot == 0 else jnp.where(group == slot, part, packed)
        if slot == cells - 1 or k == 8:
            at = first + k // cells * chan_out
            out_ref[at : at + chan_out, :] = packed * norm


def spread_line(ref, slot, at):
    return jnp.broadcast_to(ref[slot, pl.ds(at, 1), :], (8, LANES))


def window_block(mem_pos, own, half, blocks, part, t):
    at = mem_pos * own + part * half + t + (blocks - 1)
    at = jnp.where(at >= blocks, at - blocks, at)
    return jnp.where(at >= blocks, at - blocks, at)


def land_of(words, block, chan):
    cell = block * (LANES // chan) + iota(words.shape, 1) // chan
    word = jnp.right_shift(cell * 2185, 16)
    picked = jnp.take_along_axis(words, word, axis=1, mode="promise_in_bounds")
    return jnp.bitwise_and(jnp.right_shift(picked, cell - 30 * word), 1).astype(jnp.float32)


def edge_kernel(
    half,
    chan,
    latent_hbm,
    targets_hbm,
    land_hbm,
    down,
    up,
    latent,
    targets,
    land,
    words,
    sems,
):
    rows = latent.shape[1]
    blocks = latent.shape[2] // LANES
    edge = pl.ds(targets_hbm.shape[1] - 8, 8)
    copies = [
        pltpu.make_async_copy(latent_hbm, latent, sems.at[0]),
        pltpu.make_async_copy(targets_hbm.at[:, edge], targets, sems.at[1]),
        pltpu.make_async_copy(land_hbm.at[edge], land, sems.at[2]),
    ]
    for copy in copies:
        copy.start()
    for copy in copies:
        copy.wait()
    own = blocks // lax.axis_size("mem")
    mem_pos = lax.axis_index("mem")
    words[...] = jnp.zeros(words.shape, jnp.int32)
    words[:, : land.shape[1]] = land[...]
    line = iota((8, LANES), 0)
    for t in range(half + 2):
        for part in range(2):
            block = window_block(mem_pos, own, half, blocks, part, t)
            off = pl.multiple_of(block * LANES, LANES)
            slot = t * 2 + part
            cells = latent[0, :, pl.ds(off, LANES)].astype(jnp.float32)
            aims = targets[0, :, pl.ds(off, LANES)].astype(jnp.float32)
            mask = land_of(words[...], block, chan)
            pack = pltpu.roll(cells, 1, 0)
            pack = jnp.where((line >= 1) & (line <= 3), pltpu.roll(aims, 4, 0), pack)
            pack = jnp.where((line >= 4) & (line <= 6), pltpu.roll(mask, 7, 0), pack)
            down[slot] = pack.astype(jnp.bfloat16)
            up[:, slot * LANES : (slot + 1) * LANES] = cells[0:1].astype(jnp.bfloat16)


def place_kernel(own, part0, part1, part2, part3, latent_grad):
    mem_pos = lax.axis_index("mem")
    for k, part in enumerate((part0, part1, part2, part3)):
        off = pl.multiple_of(jnp.bitwise_xor(mem_pos, k) * own * LANES, LANES)
        latent_grad[0, :, pl.ds(off, own * LANES)] = part[...].astype(jnp.float32)


def taps_kernel(mine, other, grad_one, grad_two, taps):
    count = mine.shape[0]
    odd = jnp.bitwise_and(lax.axis_index("lat"), 1)
    taps[pl.ds(pl.multiple_of(odd * count, 8), count), :] = mine[...]
    taps[pl.ds(pl.multiple_of((1 - odd) * count, 8), count), :] = other[...]
    first = 0
    for out in (grad_one, grad_two):
        chan_out, chan_in = out.shape[2], out.shape[3]
        cells = LANES // chan_in
        for k in range(9):
            at = first + k // cells * chan_out
            block = taps[at : at + chan_out, :]
            turn = (-(k % cells)) % cells * chan_in
            block = pltpu.roll(block, turn, 1) if turn else block
            out[k // 3, k % 3] = block[:, :chan_in]
        first += -(-9 // cells) * chan_out


def make_source(i, row, total_rows, span, own, half, seeds, scale, chan, line, store):
    blocks = span // LANES
    mem_pos = lax.axis_index("mem")
    sublane = iota((8, LANES), 0)
    seed_table = jnp.zeros((8, LANES), jnp.int32)
    for m in range(MEM):
        seed_table = jnp.where(sublane == m, seeds[m], seed_table)
    hash_table = iota((8, LANES), 1) * HASH_CELL + seed_table * HASH_SEED
    scale_table = lane_table(scale, chan)
    inside = jnp.where(row < total_rows, 1.0, 0.0).astype(jnp.float32)
    for t in range(half + 2):
        parts = []
        for part in range(2):
            first = (row * span + window_block(mem_pos, own, half, blocks, part, t) * LANES) * HASH_CELL
            h = hash_table + first
            h = jnp.bitwise_xor(h, jnp.right_shift(h, 15))
            h = h * HASH_MIX
            h = jnp.bitwise_xor(h, jnp.right_shift(h, 13))
            noise = jnp.bitwise_and(h, 65535).astype(jnp.float32) * (1.0 / 65536.0) - 0.5
            noise = noise * 3.4641016
            parts.append((line(t * 2 + part, i) + noise * scale_table) * inside)
        store(i, t, jnp.concatenate(parts, axis=0).astype(jnp.bfloat16))


def weight_lines(grid_row, channel_weight, chan, grid_total):
    latitude = math.pi / 2 - math.pi * (grid_row.astype(jnp.float32) + 0.5) / grid_total
    cosine = jnp.where(grid_row >= 0, jnp.cos(latitude), 0.0)
    channels = jnp.tile(lane_table(channel_weight, chan), (grid_row.shape[0] // 8, 1))
    return cosine * (channels * (1.0 / (MEM * (MEM - 1))))


def prepare_kernel(
    half, chan, chan2, seeds, scale, channel_weight, latent, targets, land, source, aims, weights, lines, words
):
    rows, span = latent.shape[1], latent.shape[2]
    blocks = span // LANES
    own = blocks // lax.axis_size("mem")
    total_rows = rows * lax.axis_size("lat")
    lat_pos, mem_pos = lax.axis_index("lat"), lax.axis_index("mem")
    grid_row = iota((4 * rows, LANES), 0) + lat_pos * 4 * rows
    base = weight_lines(grid_row, channel_weight, chan2, 4 * total_rows)
    words[...] = jnp.zeros(words.shape, jnp.int32)
    words[:, : land.shape[1]] = land[...]
    for t in range(half + 2):
        for part in range(2):
            block = window_block(mem_pos, own, half, blocks, part, t)
            off = pl.multiple_of(block * LANES, LANES)
            slot = t * 2 + part
            lines[slot] = latent[0, :, pl.ds(off, LANES)].astype(jnp.float32)
            if t < half + 1:
                aims[slot] = targets[0, :, pl.ds(off, LANES)].astype(jnp.float32)
                weights[slot] = base + base * land_of(words[...], block, chan2)

    def line(slot, i):
        return spread_line(lines, slot, i)

    def store(i, t, value):
        source[i, t] = value

    def step(i, _):
        make_source(
            i, lat_pos * rows + i, total_rows, span, own, half, seeds, scale, chan, line, store
        )
        return 0

    lax.fori_loop(0, rows, step, 0)


def bands_kernel(kernel_one, kernel_two, band_one, band_two, back_one, back_two):
    build_band(kernel_one, band_one)
    build_band(kernel_two, band_two)
    build_back(kernel_one, back_one)
    build_back(kernel_two, back_two)


def in_order(*parts):
    for part in parts:
        for _ in part:
            pass


def band_kernel(
    half,
    chans,
    span,
    norm,
    seeds,
    scale,
    channel_weight,
    own_source,
    aims,
    weights,
    above,
    below,
    band_one,
    band_two,
    back_one,
    back_two,
    out_lat,
    taps_keep,
    taps_send,
    lat_rows,
    edge_aims,
    edge_weights,
    source,
    pre_even,
    pre_odd,
    act,
    slope,
    cast_even,
    cast_odd,
    fgrad_even,
    fgrad_odd,
    grads_even,
    grads_odd,
    carry,
    sums,
    lat_lines,
    taps,
    acc_one,
    acc_one_next,
    acc_two,
    acc_two_next,
):
    rows = own_source.shape[0]
    blocks = span // LANES
    own = blocks // lax.axis_size("mem")
    total_rows = rows * lax.axis_size("lat")
    lat_pos = lax.axis_index("lat")
    wide = half + 2
    front = half + 1
    chan0, chan1, chan2 = chans
    f32, bf16 = jnp.float32, jnp.bfloat16

    grid_row = iota((8, LANES), 0) + (lat_pos * 4 * rows - 4)
    base = weight_lines(grid_row, channel_weight, chan2, 4 * total_rows)
    for slot in range(2 * wide):
        edge = above[slot].astype(f32)
        lat_rows[slot, 0:1] = edge[0:1]
        lat_rows[slot, 1:2] = below[:, slot * LANES : (slot + 1) * LANES].astype(f32)
        if slot < 2 * front:
            edge_aims[slot] = edge
            edge_weights[slot] = base + base * pltpu.roll(edge, 5, 0)

    source[rows + 2 :] = jnp.zeros((2,) + source.shape[1:], bf16)
    source[:, wide] = jnp.zeros((source.shape[0],) + source.shape[2:], bf16)
    fgrad_even[0] = jnp.zeros(fgrad_even.shape[1:], bf16)
    for fgrad in (fgrad_even, fgrad_odd):
        fgrad[:, 0] = jnp.zeros((4,) + fgrad.shape[2:], bf16)
    carry[...] = jnp.zeros(carry.shape, f32)
    for acc in (acc_one, acc_one_next, acc_two, acc_two_next):
        acc[...] = jnp.zeros(acc.shape, f32)

    def line(slot, i):
        return spread_line(lat_rows, slot, i)

    def store(i, t, value):
        source[i * (rows + 1), t] = value

    def edge_source(i, _):
        row = lat_pos * rows - 1 + i * (rows + 1)
        make_source(i, row, total_rows, span, own, half, seeds, scale, chan0, line, store)
        return 0

    lax.fori_loop(0, 2, edge_source, 0)
    source[1 : rows + 1, 0:wide] = own_source[...]

    def operand(ref, i, start, count):
        def piece(r, at):
            return ref[r, pl.ds(at, count)].reshape(count * 16, LANES)

        return jnp.concatenate(
            [piece(i, start), piece(i + 1, start), piece(i, start + 1), piece(i + 1, start + 1)], axis=1
        )

    def first_product(pair, pre):
        taken = jnp.concatenate([operand(source, 2 * pair + k, 0, wide) for k in range(2)], axis=0)
        pre[...] = jnp.dot(taken, band_one[...], preferred_element_type=f32)

    def first_gelu(pair, pre, last=False):
        for k in range(2):
            for t in range(wide):
                for sub in range(1 if last and k == 1 else 2):
                    at = (k * wide + t) * 16
                    x = pre[at : at + 16, sub * LANES : (sub + 1) * LANES]
                    square = x * x
                    th = jnp.tanh(x * (GELU_A + (GELU_A * GELU_B) * square))
                    plus = 0.5 + 0.5 * th
                    act[4 * pair + 2 * k + sub, t] = (x * plus).astype(bf16)
                    if t < front and not (last and k == 1):
                        d = plus + (x * plus) * (1.0 - th) * (GELU_A + (3.0 * GELU_A * GELU_B) * square)
                        if t == half:
                            d = jnp.where(iota((16, LANES), 0) < 8, d, 0.0)
                        slope[4 * pair + 2 * k + sub, t] = d

    def first_segment(m, _):
        first_product(2 * m + 1, pre_odd)
        first_gelu(2 * m, pre_even)
        first_product(2 * m + 2, pre_even)
        first_gelu(2 * m + 1, pre_odd)
        return 0

    first_product(0, pre_even)
    lax.fori_loop(0, rows // 4, first_segment, 0)
    first_gelu(rows // 2, pre_even, last=True)

    members = front * 16
    owner = iota((48, members), 0)
    group = iota((48, members), 1) // 8
    place = (group % 2) * half + group // 2
    real = (group // 2 > 0) & (place - 1 < own)
    pick_own = (real & (place - 1 == owner)).astype(bf16)
    pick_prev = ((group // 2 < half) & (place == owner)).astype(bf16)
    pick = jnp.concatenate([pick_own, pick_prev], axis=0)

    def second_product(n, cast):
        taken = jnp.concatenate([operand(act, 2 * n + k, 0, front) for k in range(2)], axis=0)
        out = jnp.dot(taken, band_two[...], preferred_element_type=f32).astype(bf16)
        for k in range(2):
            for sub in range(2):
                part = out[k * members : (k + 1) * members, sub * LANES : (sub + 1) * LANES]
                cast[2 * k + sub] = part.reshape(front, 16, LANES)
        yield

    def loss_gradient(cast, fgrad, aim_ref, weight_ref, first, lines):
        for line in lines:
            for t in range(front):
                both = cast[line, t].astype(f32)
                parts = []
                for part in range(2):
                    if t == half and part == 1:
                        parts.append(jnp.zeros((8, LANES), f32))
                        continue
                    f = both[part * 8 : part * 8 + 8]
                    d = f - spread_line(aim_ref, t * 2 + part, first + line)
                    goal = d * lax.rsqrt(d * d + SMOOTH)
                    gs = []
                    for k in range(1, 5):
                        d = f - pltpu.roll(f, k, 0)
                        gs.append(d * lax.rsqrt(d * d + SMOOTH))
                    back = gs[2]
                    for k in (1, 0):
                        back = gs[k] + pltpu.roll(back, MEM - 1, 0)
                    back = pltpu.roll(back, MEM - 1, 0)
                    spread = (gs[0] + gs[1]) + (gs[2] + gs[3]) - back
                    weight = spread_line(weight_ref, t * 2 + part, first + line)
                    parts.append(weight * ((MEM - 1.0) * goal - spread))
                fgrad[line, t + 1] = jnp.concatenate(parts, axis=0).astype(bf16)
            yield

    def add_taps(g, x, acc, acc_next, chan_out):
        turned = g.T
        acc[...] += jnp.dot(turned, x[:, :256], preferred_element_type=f32)
        last = [turned[k * LANES - chan_out : k * LANES] for k in (1, 2)]
        last = jnp.concatenate(last, axis=0)
        acc_next[...] += jnp.dot(last, x[:, 256:], preferred_element_type=f32)

    def pull_back(n, fgrad, grads_ref, with_taps=True):
        def flat(line, start, count):
            return fgrad[line, start : start + count].reshape(count * 16, LANES)

        g = [
            jnp.concatenate(
                [flat(2 * k, 1, front), flat(2 * k + 1, 1, front), flat(2 * k, 0, front), flat(2 * k + 1, 0, front)],
                axis=1,
            )
            for k in range(2)
        ]
        pulled = jnp.dot(jnp.concatenate(g, axis=0), back_two[...], preferred_element_type=f32)
        grads = [
            pulled[:members, :LANES] + carry[...],
            pulled[members:, :LANES] + pulled[:members, LANES:],
        ]
        carry[...] = pulled[members:, LANES:]
        grads = [(grads[k] * slope[2 * n + k].reshape(members, LANES)).astype(bf16) for k in range(2)]
        yield
        grads_ref[...] = jnp.concatenate(grads, axis=1)
        if with_taps:
            g = [jnp.concatenate([flat(2 * k, 2, half), flat(2 * k + 1, 2, half)], axis=1) for k in range(2)]
            x = [operand(act, 2 * n + k, 1, half) for k in range(2)]
            add_taps(jnp.concatenate(g, axis=0), jnp.concatenate(x, axis=0), acc_two, acc_two_next, chan2)
            yield

    def first_taps(n, grads_ref, keep=None):
        g = grads_ref[16:]
        g = g if keep is None else g * keep
        add_taps(g, operand(source, n, 1, half), acc_one, acc_one_next, chan1)
        yield
        z = jnp.dot(pick, grads_ref[...], preferred_element_type=f32)
        z = jnp.concatenate([z[:48], z[48:]], axis=1)
        high = z.astype(bf16)
        sums[0, n] = high
        sums[1, n] = (z - high.astype(f32)).astype(bf16)
        yield

    def own_gradient(n, cast, fgrad):
        return loss_gradient(cast, fgrad, aims, weights, 4 * (n - 1), range(4))

    def second_segment(m, _):
        in_order(
            second_product(2 * m + 3, cast_odd),
            own_gradient(2 * m + 2, cast_even, fgrad_even),
            pull_back(2 * m + 1, fgrad_odd, grads_odd),
            first_taps(2 * m, grads_even, jnp.where(m >= 1, 1.0, 0.0).astype(bf16)),
        )
        in_order(
            second_product(2 * m + 4, cast_even),
            own_gradient(2 * m + 3, cast_odd, fgrad_odd),
            pull_back(2 * m + 2, fgrad_even, grads_even),
            first_taps(2 * m + 1, grads_odd),
        )
        return 0

    in_order(second_product(0, cast_even))
    in_order(
        second_product(1, cast_odd),
        loss_gradient(cast_even, fgrad_even, edge_aims, edge_weights, 0, range(1, 4)),
    )
    in_order(
        second_product(2, cast_even),
        own_gradient(1, cast_odd, fgrad_odd),
        pull_back(0, fgrad_even, grads_even, with_taps=False),
    )
    lax.fori_loop(0, rows // 2 - 1, second_segment, 0)
    in_order(
        own_gradient(rows, cast_even, fgrad_even),
        pull_back(rows - 1, fgrad_odd, grads_odd),
        first_taps(rows - 2, grads_even),
    )
    in_order(pull_back(rows, fgrad_even, grads_even), first_taps(rows - 1, grads_odd))
    in_order(first_taps(rows, grads_even))

    z = jnp.dot(sums[...].reshape(2 * (rows + 1) * 48, 512), back_one[...], preferred_element_type=f32)
    z = z.reshape(2, rows + 1, 48, 2 * LANES)
    z = z[0] + z[1]
    for n in range(rows):
        lat_lines[pl.ds(n, 48, stride=rows), :] = z[n + 1, :, :LANES] + z[n, :, LANES:]
    for t in range(own):
        out_lat[:, t * LANES : (t + 1) * LANES] = lat_lines[t * rows : (t + 1) * rows].astype(bf16)
    pack_taps(acc_one, acc_one_next, taps, 0, chan0, chan1, norm)
    pack_taps(acc_two, acc_two_next, taps, -(-9 // (LANES // chan0)) * chan1, chan1, chan2, norm)
    count = taps_keep.shape[0]
    odd = jnp.bitwise_and(lat_pos, 1)
    taps_keep[...] = taps[pl.ds(pl.multiple_of(odd * count, 8), count), :]
    taps_send[...] = taps[pl.ds(pl.multiple_of((1 - odd) * count, 8), count), :]


def swapped(array, axis, bit):
    return lax.ppermute(array, axis, [(i, i ^ bit) for i in range(lax.axis_size(axis))])


def total(array, axis, first, second):
    one, two, three = (swapped(array, axis, k).astype(jnp.float32) for k in (first, second, first ^ second))
    return (array.astype(jnp.float32) + one) + (two + three)


def local(
    latent, member_seeds, noise_scale, kernel_one, kernel_two, targets, land_words, channel_weight
):
    sample_count, rows, span = latent.shape
    chan0, chan1, chan2 = kernel_one.shape[2], kernel_one.shape[3], kernel_two.shape[3]
    lat_count = lax.axis_size("lat")
    own = span // LANES // lax.axis_size("mem")
    half = (own + 1) // 2
    assert sample_count == 1 and member_seeds.shape[0] == MEM and rows % 4 == 0 and own % 2 == 1 and lax.axis_size("mem") == 4
    assert 4 * chan2 == 2 * chan1 == chan0 and chan0 == 64
    vmem = pl.BlockSpec(memory_space=pltpu.VMEM)
    smem = pl.BlockSpec(memory_space=pltpu.SMEM)
    hbm = pl.BlockSpec(memory_space=pltpu.HBM)
    f32, bf16 = jnp.float32, jnp.bfloat16
    wide, front = half + 2, half + 1
    params = pltpu.CompilerParams(vmem_limit_bytes=32 * 1024 * 1024)
    small = pltpu.CompilerParams(vmem_limit_bytes=8 * 1024 * 1024)
    kernel_one = kernel_one.transpose(0, 1, 3, 2)
    kernel_two = kernel_two.transpose(0, 1, 3, 2)
    down, up = pl.pallas_call(
        functools.partial(edge_kernel, half, chan2),
        in_specs=[hbm] * 3,
        out_specs=[vmem] * 2,
        out_shape=[
            jax.ShapeDtypeStruct((2 * wide, 8, LANES), bf16),
            jax.ShapeDtypeStruct((1, 2 * wide * LANES), bf16),
        ],
        scratch_shapes=[
            pltpu.VMEM((1, 8, span), bf16),
            pltpu.VMEM((1, 8, span), bf16),
            pltpu.VMEM((8, land_words.shape[1]), jnp.int32),
            pltpu.VMEM((8, LANES), jnp.int32),
            pltpu.SemaphoreType.DMA((3,)),
        ],
        compiler_params=pltpu.CompilerParams(vmem_limit_bytes=56 * 1024 * 1024),
        name="edges",
    )(latent, targets, land_words)
    above = shifted(down, "lat", 1)
    below = shifted(up, "lat", -1)
    source, aims, weights = pl.pallas_call(
        functools.partial(prepare_kernel, half, chan0, chan2),
        in_specs=[smem] * 3 + [vmem] * 3,
        out_specs=[vmem] * 3,
        out_shape=[jax.ShapeDtypeStruct((rows, wide, 16, LANES), bf16)]
        + [jax.ShapeDtypeStruct((2 * front, 4 * rows, LANES), f32)] * 2,
        scratch_shapes=[pltpu.VMEM((2 * wide, rows, LANES), f32), pltpu.VMEM((4 * rows, LANES), jnp.int32)],
        compiler_params=small,
        cost_estimate=pl.CostEstimate(flops=10**8, bytes_accessed=10**7, transcendentals=0),
        name="prepare",
    )(member_seeds, noise_scale, channel_weight, latent, targets, land_words)
    one_late, two_late, source = lax.optimization_barrier((kernel_one, kernel_two, source))
    bands = pl.pallas_call(
        bands_kernel,
        in_specs=[vmem] * 2,
        out_specs=[vmem] * 4,
        out_shape=[jax.ShapeDtypeStruct((512, 256), bf16)] * 4,
        compiler_params=small,
        cost_estimate=pl.CostEstimate(flops=10**8, bytes_accessed=10**7, transcendentals=0),
        name="bands",
    )(one_late, two_late)
    norm = 1.0 / math.sqrt(sample_count * 4 * rows * lat_count * targets.shape[2])
    tap_rows = 5 * chan1 + 3 * chan2
    lat_grad, taps, taps_send = pl.pallas_call(
        functools.partial(band_kernel, half, (chan0, chan1, chan2), span, norm),
        in_specs=[smem] * 3 + [vmem] * 9,
        out_specs=[vmem] * 3,
        out_shape=[
            jax.ShapeDtypeStruct((rows, own * LANES), bf16),
            jax.ShapeDtypeStruct((tap_rows // 2, LANES), f32),
            jax.ShapeDtypeStruct((tap_rows // 2, LANES), f32),
        ],
        scratch_shapes=[
            pltpu.VMEM((2 * wide, 8, LANES), f32),
            pltpu.VMEM((2 * front, 8, LANES), f32),
            pltpu.VMEM((2 * front, 8, LANES), f32),
            pltpu.VMEM((rows + 4, wide + 1, 16, LANES), bf16),
            pltpu.VMEM((wide * 32, 2 * LANES), f32),
            pltpu.VMEM((wide * 32, 2 * LANES), f32),
            pltpu.VMEM((2 * rows + 4, wide, 16, LANES), bf16),
            pltpu.VMEM((2 * rows + 4, front, 16, LANES), f32),
            pltpu.VMEM((4, front, 16, LANES), bf16),
            pltpu.VMEM((4, front, 16, LANES), bf16),
            pltpu.VMEM((4, front + 1, 16, LANES), bf16),
            pltpu.VMEM((4, front + 1, 16, LANES), bf16),
            pltpu.VMEM((front * 16, 2 * LANES), bf16),
            pltpu.VMEM((front * 16, 2 * LANES), bf16),
            pltpu.VMEM((front * 16, LANES), f32),
            pltpu.VMEM((2, rows + 1, 48, 512), bf16),
            pltpu.VMEM((48 * rows, LANES), f32),
            pltpu.VMEM((tap_rows, LANES), f32),
            pltpu.VMEM((256, 256), f32),
            pltpu.VMEM((2 * chan1, 256), f32),
            pltpu.VMEM((256, 256), f32),
            pltpu.VMEM((2 * chan2, 256), f32),
        ],
        compiler_params=params,
        name="band",
    )(
        member_seeds,
        noise_scale,
        channel_weight,
        source,
        aims,
        weights,
        above,
        below,
        *bands,
    )
    taps = (taps + swapped(taps_send, "lat", 1)).astype(bf16)
    taps = total(taps, "mem", 1, 2)
    one, two, three = (swapped(lat_grad, "mem", k) for k in range(1, 4))
    bits = [1 << k for k in range(1, lat_count.bit_length() - 1)]
    for bit in bits:
        if bit == bits[-1]:
            taps, one, three = lax.optimization_barrier((taps, one, three))
        taps = taps + swapped(taps, "lat", bit)
    taps, two = lax.optimization_barrier((taps, two))
    other = swapped(taps, "lat", 1)
    latent_grad = pl.pallas_call(
        functools.partial(place_kernel, own),
        in_specs=[vmem] * 4,
        out_specs=vmem,
        out_shape=jax.ShapeDtypeStruct((1, rows, span), f32),
        compiler_params=small,
        name="place",
    )(lat_grad, one, two, three)
    one, two = pl.pallas_call(
        taps_kernel,
        in_specs=[vmem] * 2,
        out_specs=[vmem] * 2,
        out_shape=[
            jax.ShapeDtypeStruct(kernel_one.shape, f32),
            jax.ShapeDtypeStruct(kernel_two.shape, f32),
        ],
        scratch_shapes=[pltpu.VMEM((tap_rows, LANES), f32)],
        compiler_params=small,
        name="taps",
    )(taps, other)
    return (latent_grad, one.transpose(0, 1, 3, 2), two.transpose(0, 1, 3, 2))


def solution(mesh):
    in_specs = (P(None, "lat", None), P(), P(), P(), P(), P(None, "lat", None), P("lat", None), P())
    out_specs = (P(None, "lat", None), P(), P())
    return jax.shard_map(local, mesh=mesh, in_specs=in_specs, out_specs=out_specs, check_vma=False)
```

```python
import functools
import math

import jax
import jax.numpy as jnp
from jax import lax
from jax.experimental import pallas as pl
from jax.experimental.pallas import tpu as pltpu
from jax.sharding import PartitionSpec as P

SMOOTH = 0.01
HASH_CELL = 1103515245
HASH_SEED = 747796405
HASH_MIX = 277803737
LANES = 128
MEM = 8
GELU_A = math.sqrt(2.0 / math.pi)
GELU_B = 0.044715


def shifted(array, axis, by):
    peers = lax.axis_size(axis)
    pairs = [(i, i + by) for i in range(peers) if 0 <= i + by < peers]
    return lax.ppermute(array, axis, pairs)


def iota(shape, axis):
    return lax.broadcasted_iota(jnp.int32, shape, axis)


def lane_table(ref, count):
    lane = iota((8, LANES), 1) % count
    total = jnp.zeros((8, LANES), jnp.float32)
    for k in range(count):
        total = jnp.where(lane == k, ref[k], total)
    return total


def build_band(kernel_ref, band_ref):
    chan_out, chan_in = kernel_ref.shape[2], kernel_ref.shape[3]
    cells = LANES // chan_in
    repeat = (iota((chan_out, LANES), 1) % chan_out == iota((chan_out, LANES), 0)).astype(jnp.bfloat16)
    wide = {}
    for a in range(3):
        for b in range(3):
            wide[a, b] = lax.dot_general(
                kernel_ref[a, b], repeat, (((0,), (0,)), ((), ())), preferred_element_type=jnp.float32
            )
    column = iota((chan_in, LANES), 1) // chan_out
    zero = jnp.zeros((chan_in, LANES), jnp.float32)
    for block in range(2):
        for row in range(2):
            for cell in range(cells):
                at = block * 256 + row * LANES + cell * chan_in
                for sub in range(2):
                    a = sub - 2 * row + 1
                    part = zero
                    for q in range(2 * cells):
                        b = q - 2 * (cell + block * cells) + 1
                        if 0 <= a <= 2 and 0 <= b <= 2:
                            part = jnp.where(column == q, wide[a, b], part)
                    band_ref[at : at + chan_in, sub * LANES : (sub + 1) * LANES] = part.astype(jnp.bfloat16)


def build_back(kernel_ref, back_ref):
    chan_out, chan_in = kernel_ref.shape[2], kernel_ref.shape[3]
    cells = LANES // chan_in
    repeat = (iota((chan_in, LANES), 1) % chan_in == iota((chan_in, LANES), 0)).astype(jnp.bfloat16)
    flat = kernel_ref[...].reshape(9 * chan_out, chan_in)
    wide = jnp.dot(flat, repeat, preferred_element_type=jnp.float32)
    column = iota((chan_out, LANES), 1) // chan_in
    zero = jnp.zeros((chan_out, LANES), jnp.float32)
    for block in range(2):
        for sub in range(2):
            for q in range(2 * cells):
                at = block * 256 + sub * LANES + q * chan_out
                for row in range(2):
                    a = sub - 2 * row + 1
                    part = zero
                    for cell in range(cells):
                        b = q - 2 * (cell + block * cells) + 1
                        if 0 <= a <= 2 and 0 <= b <= 2:
                            tap = (3 * a + b) * chan_out
                            part = jnp.where(column == cell, wide[tap : tap + chan_out], part)
                    back_ref[at : at + chan_out, row * LANES : (row + 1) * LANES] = part.astype(jnp.bfloat16)


def pack_taps(acc_ref, next_ref, out_ref, first, chan_in, chan_out, norm):
    cells = LANES // chan_in
    group = iota((chan_out, LANES), 1) // chan_in
    packed = None
    for k in range(9):
        a, b = divmod(k, 3)
        row, sub = ((1, 1), (0, 0), (0, 1))[a]
        slot = k % cells
        part = None
        for reach in range(cells + 1):
            q = 2 * reach + b - 1
            if 0 <= q < 2 * cells:
                block, cell = reach // cells, reach % cells
                lines = sub * LANES + q * chan_out if block == 0 else sub * chan_out
                ref = acc_ref if block == 0 else next_ref
                piece = ref[lines : lines + chan_out, row * LANES : (row + 1) * LANES]
                turn = (slot - cell) % cells * chan_in
                piece = pltpu.roll(piece, turn, 1) if turn else piece
                part = piece if part is None else part + piece
        packed = part if slot == 0 else jnp.where(group == slot, part, packed)
        if slot == cells - 1 or k == 8:
            at = first + k // cells * chan_out
            out_ref[at : at + chan_out, :] = packed * norm


def spread_line(ref, slot, at):
    return jnp.broadcast_to(ref[slot, pl.ds(at, 1), :], (8, LANES))


def window_block(mem_pos, own, half, blocks, part, t):
    at = mem_pos * own + part * half + t + (blocks - 1)
    at = jnp.where(at >= blocks, at - blocks, at)
    return jnp.where(at >= blocks, at - blocks, at)


def land_of(words, block, chan):
    cell = block * (LANES // chan) + iota(words.shape, 1) // chan
    word = jnp.right_shift(cell * 2185, 16)
    picked = jnp.take_along_axis(words, word, axis=1, mode="promise_in_bounds")
    return jnp.bitwise_and(jnp.right_shift(picked, cell - 30 * word), 1).astype(jnp.float32)


def edge_kernel(
    half,
    chan,
    latent_hbm,
    targets_hbm,
    land_hbm,
    down,
    up,
    latent,
    targets,
    land,
    words,
    sems,
):
    rows = latent.shape[1]
    blocks = latent.shape[2] // LANES
    edge = pl.ds(targets_hbm.shape[1] - 8, 8)
    copies = [
        pltpu.make_async_copy(latent_hbm, latent, sems.at[0]),
        pltpu.make_async_copy(targets_hbm.at[:, edge], targets, sems.at[1]),
        pltpu.make_async_copy(land_hbm.at[edge], land, sems.at[2]),
    ]
    for copy in copies:
        copy.start()
    for copy in copies:
        copy.wait()
    own = blocks // lax.axis_size("mem")
    mem_pos = lax.axis_index("mem")
    words[...] = jnp.zeros(words.shape, jnp.int32)
    words[:, : land.shape[1]] = land[...]
    line = iota((8, LANES), 0)
    for t in range(half + 2):
        for part in range(2):
            block = window_block(mem_pos, own, half, blocks, part, t)
            off = pl.multiple_of(block * LANES, LANES)
            slot = t * 2 + part
            cells = latent[0, :, pl.ds(off, LANES)].astype(jnp.float32)
            aims = targets[0, :, pl.ds(off, LANES)].astype(jnp.float32)
            mask = land_of(words[...], block, chan)
            pack = pltpu.roll(cells, 1, 0)
            pack = jnp.where((line >= 1) & (line <= 3), pltpu.roll(aims, 4, 0), pack)
            pack = jnp.where((line >= 4) & (line <= 6), pltpu.roll(mask, 7, 0), pack)
            down[slot] = pack.astype(jnp.bfloat16)
            up[:, slot * LANES : (slot + 1) * LANES] = cells[0:1].astype(jnp.bfloat16)


def place_kernel(own, part0, part1, part2, part3, latent_grad):
    mem_pos = lax.axis_index("mem")
    for k, part in enumerate((part0, part1, part2, part3)):
        off = pl.multiple_of(jnp.bitwise_xor(mem_pos, k) * own * LANES, LANES)
        latent_grad[0, :, pl.ds(off, own * LANES)] = part[...].astype(jnp.float32)


def taps_kernel(mine, other, grad_one, grad_two, taps):
    count = mine.shape[0]
    odd = jnp.bitwise_and(lax.axis_index("lat"), 1)
    taps[pl.ds(pl.multiple_of(odd * count, 8), count), :] = mine[...]
    taps[pl.ds(pl.multiple_of((1 - odd) * count, 8), count), :] = other[...]
    first = 0
    for out in (grad_one, grad_two):
        chan_out, chan_in = out.shape[2], out.shape[3]
        cells = LANES // chan_in
        for k in range(9):
            at = first + k // cells * chan_out
            block = taps[at : at + chan_out, :]
            turn = (-(k % cells)) % cells * chan_in
            block = pltpu.roll(block, turn, 1) if turn else block
            out[k // 3, k % 3] = block[:, :chan_in]
        first += -(-9 // cells) * chan_out


def make_source(i, row, total_rows, span, own, half, seeds, scale, chan, line, store):
    blocks = span // LANES
    mem_pos = lax.axis_index("mem")
    sublane = iota((8, LANES), 0)
    seed_table = jnp.zeros((8, LANES), jnp.int32)
    for m in range(MEM):
        seed_table = jnp.where(sublane == m, seeds[m], seed_table)
    hash_table = iota((8, LANES), 1) * HASH_CELL + seed_table * HASH_SEED
    scale_table = lane_table(scale, chan)
    inside = jnp.where(row < total_rows, 1.0, 0.0).astype(jnp.float32)
    for t in range(half + 2):
        parts = []
        for part in range(2):
            first = (row * span + window_block(mem_pos, own, half, blocks, part, t) * LANES) * HASH_CELL
            h = hash_table + first
            h = jnp.bitwise_xor(h, jnp.right_shift(h, 15))
            h = h * HASH_MIX
            h = jnp.bitwise_xor(h, jnp.right_shift(h, 13))
            noise = jnp.bitwise_and(h, 65535).astype(jnp.float32) * (1.0 / 65536.0) - 0.5
            noise = noise * 3.4641016
            parts.append((line(t * 2 + part, i) + noise * scale_table) * inside)
        store(i, t, jnp.concatenate(parts, axis=0).astype(jnp.bfloat16))


def weight_lines(grid_row, channel_weight, chan, grid_total):
    latitude = math.pi / 2 - math.pi * (grid_row.astype(jnp.float32) + 0.5) / grid_total
    cosine = jnp.where(grid_row >= 0, jnp.cos(latitude), 0.0)
    channels = jnp.tile(lane_table(channel_weight, chan), (grid_row.shape[0] // 8, 1))
    return cosine * (channels * (1.0 / (MEM * (MEM - 1))))


def prepare_kernel(
    half, chan, chan2, seeds, scale, channel_weight, latent, targets, land, source, aims, weights, lines, words
):
    rows, span = latent.shape[1], latent.shape[2]
    blocks = span // LANES
    own = blocks // lax.axis_size("mem")
    total_rows = rows * lax.axis_size("lat")
    lat_pos, mem_pos = lax.axis_index("lat"), lax.axis_index("mem")
    grid_row = iota((4 * rows, LANES), 0) + lat_pos * 4 * rows
    base = weight_lines(grid_row, channel_weight, chan2, 4 * total_rows)
    words[...] = jnp.zeros(words.shape, jnp.int32)
    words[:, : land.shape[1]] = land[...]
    for t in range(half + 2):
        for part in range(2):
            block = window_block(mem_pos, own, half, blocks, part, t)
            off = pl.multiple_of(block * LANES, LANES)
            slot = t * 2 + part
            lines[slot] = latent[0, :, pl.ds(off, LANES)].astype(jnp.float32)
            if t < half + 1:
                aims[slot] = targets[0, :, pl.ds(off, LANES)].astype(jnp.float32)
                weights[slot] = base + base * land_of(words[...], block, chan2)

    def line(slot, i):
        return spread_line(lines, slot, i)

    def store(i, t, value):
        source[i, t] = value

    def step(i, _):
        make_source(
            i, lat_pos * rows + i, total_rows, span, own, half, seeds, scale, chan, line, store
        )
        return 0

    lax.fori_loop(0, rows, step, 0)


def bands_kernel(kernel_one, kernel_two, band_one, band_two, back_one, back_two):
    build_band(kernel_one, band_one)
    build_band(kernel_two, band_two)
    build_back(kernel_one, back_one)
    build_back(kernel_two, back_two)


def take_turns(*parts):
    parts = list(parts)
    while parts:
        for part in tuple(parts):
            if next(part, part) is part:
                parts.remove(part)


def band_kernel(
    half,
    chans,
    span,
    norm,
    seeds,
    scale,
    channel_weight,
    own_source,
    aims,
    weights,
    above,
    below,
    band_one,
    band_two,
    back_one,
    back_two,
    out_lat,
    taps_keep,
    taps_send,
    lat_rows,
    edge_aims,
    edge_weights,
    source,
    pre_even,
    pre_odd,
    act,
    slope,
    cast_even,
    cast_odd,
    fgrad_even,
    fgrad_odd,
    grads_even,
    grads_odd,
    carry,
    sums,
    lat_lines,
    taps,
    acc_one,
    acc_one_next,
    acc_two,
    acc_two_next,
):
    rows = own_source.shape[0]
    blocks = span // LANES
    own = blocks // lax.axis_size("mem")
    total_rows = rows * lax.axis_size("lat")
    lat_pos = lax.axis_index("lat")
    wide = half + 2
    front = half + 1
    chan0, chan1, chan2 = chans
    f32, bf16 = jnp.float32, jnp.bfloat16

    grid_row = iota((8, LANES), 0) + (lat_pos * 4 * rows - 4)
    base = weight_lines(grid_row, channel_weight, chan2, 4 * total_rows)
    for slot in range(2 * wide):
        edge = above[slot].astype(f32)
        lat_rows[slot, 0:1] = edge[0:1]
        lat_rows[slot, 1:2] = below[:, slot * LANES : (slot + 1) * LANES].astype(f32)
        if slot < 2 * front:
            edge_aims[slot] = edge
            edge_weights[slot] = base + base * pltpu.roll(edge, 5, 0)

    source[rows + 2 :] = jnp.zeros((2,) + source.shape[1:], bf16)
    source[:, wide] = jnp.zeros((source.shape[0],) + source.shape[2:], bf16)
    fgrad_even[0] = jnp.zeros(fgrad_even.shape[1:], bf16)
    for fgrad in (fgrad_even, fgrad_odd):
        fgrad[:, 0] = jnp.zeros((4,) + fgrad.shape[2:], bf16)
    carry[...] = jnp.zeros(carry.shape, f32)
    for acc in (acc_one, acc_one_next, acc_two, acc_two_next):
        acc[...] = jnp.zeros(acc.shape, f32)

    def line(slot, i):
        return spread_line(lat_rows, slot, i)

    def store(i, t, value):
        source[i * (rows + 1), t] = value

    def edge_source(i, _):
        row = lat_pos * rows - 1 + i * (rows + 1)
        make_source(i, row, total_rows, span, own, half, seeds, scale, chan0, line, store)
        return 0

    lax.fori_loop(0, 2, edge_source, 0)
    source[1 : rows + 1, 0:wide] = own_source[...]

    def operand(ref, i, start, count):
        def piece(r, at):
            return ref[r, pl.ds(at, count)].reshape(count * 16, LANES)

        return jnp.concatenate(
            [piece(i, start), piece(i + 1, start), piece(i, start + 1), piece(i + 1, start + 1)], axis=1
        )

    def first_product(pair, pre):
        taken = jnp.concatenate([operand(source, 2 * pair + k, 0, wide) for k in range(2)], axis=0)
        pre[...] = jnp.dot(taken, band_one[...], preferred_element_type=f32)

    def first_gelu(pair, pre, last=False):
        for k in range(2):
            for t in range(wide):
                for sub in range(1 if last and k == 1 else 2):
                    at = (k * wide + t) * 16
                    x = pre[at : at + 16, sub * LANES : (sub + 1) * LANES]
                    square = x * x
                    th = jnp.tanh(x * (GELU_A + (GELU_A * GELU_B) * square))
                    plus = 0.5 + 0.5 * th
                    act[4 * pair + 2 * k + sub, t] = (x * plus).astype(bf16)
                    if t < front and not (last and k == 1):
                        d = plus + (x * plus) * (1.0 - th) * (GELU_A + (3.0 * GELU_A * GELU_B) * square)
                        if t == half:
                            d = jnp.where(iota((16, LANES), 0) < 8, d, 0.0)
                        slope[4 * pair + 2 * k + sub, t] = d

    def first_segment(m, _):
        first_product(2 * m + 1, pre_odd)
        first_gelu(2 * m, pre_even)
        first_product(2 * m + 2, pre_even)
        first_gelu(2 * m + 1, pre_odd)
        return 0

    first_product(0, pre_even)
    lax.fori_loop(0, rows // 4, first_segment, 0)
    first_gelu(rows // 2, pre_even, last=True)

    members = front * 16
    owner = iota((48, members), 0)
    group = iota((48, members), 1) // 8
    place = (group % 2) * half + group // 2
    real = (group // 2 > 0) & (place - 1 < own)
    pick_own = (real & (place - 1 == owner)).astype(bf16)
    pick_prev = ((group // 2 < half) & (place == owner)).astype(bf16)
    pick = jnp.concatenate([pick_own, pick_prev], axis=0)

    def second_product(n, cast):
        taken = jnp.concatenate([operand(act, 2 * n + k, 0, front) for k in range(2)], axis=0)
        out = jnp.dot(taken, band_two[...], preferred_element_type=f32).astype(bf16)
        for k in range(2):
            for sub in range(2):
                part = out[k * members : (k + 1) * members, sub * LANES : (sub + 1) * LANES]
                cast[2 * k + sub] = part.reshape(front, 16, LANES)
        yield

    def loss_gradient(cast, fgrad, aim_ref, weight_ref, first, lines):
        for line in lines:
            for t in range(front):
                both = cast[line, t].astype(f32)
                parts = []
                for part in range(2):
                    if t == half and part == 1:
                        parts.append(jnp.zeros((8, LANES), f32))
                        continue
                    f = both[part * 8 : part * 8 + 8]
                    d = f - spread_line(aim_ref, t * 2 + part, first + line)
                    goal = d * lax.rsqrt(d * d + SMOOTH)
                    gs = []
                    for k in range(1, 5):
                        d = f - pltpu.roll(f, k, 0)
                        gs.append(d * lax.rsqrt(d * d + SMOOTH))
                    back = gs[2]
                    for k in (1, 0):
                        back = gs[k] + pltpu.roll(back, MEM - 1, 0)
                    back = pltpu.roll(back, MEM - 1, 0)
                    spread = (gs[0] + gs[1]) + (gs[2] + gs[3]) - back
                    weight = spread_line(weight_ref, t * 2 + part, first + line)
                    parts.append(weight * ((MEM - 1.0) * goal - spread))
                fgrad[line, t + 1] = jnp.concatenate(parts, axis=0).astype(bf16)
            yield

    def add_taps(g, x, acc, acc_next, chan_out):
        turned = g.T
        acc[...] += jnp.dot(turned, x[:, :256], preferred_element_type=f32)
        last = [turned[k * LANES - chan_out : k * LANES] for k in (1, 2)]
        last = jnp.concatenate(last, axis=0)
        acc_next[...] += jnp.dot(last, x[:, 256:], preferred_element_type=f32)

    def pull_back(n, fgrad, grads_ref, with_taps=True):
        def flat(line, start, count):
            return fgrad[line, start : start + count].reshape(count * 16, LANES)

        g = [
            jnp.concatenate(
                [flat(2 * k, 1, front), flat(2 * k + 1, 1, front), flat(2 * k, 0, front), flat(2 * k + 1, 0, front)],
                axis=1,
            )
            for k in range(2)
        ]
        pulled = jnp.dot(jnp.concatenate(g, axis=0), back_two[...], preferred_element_type=f32)
        grads = [
            pulled[:members, :LANES] + carry[...],
            pulled[members:, :LANES] + pulled[:members, LANES:],
        ]
        carry[...] = pulled[members:, LANES:]
        grads = [(grads[k] * slope[2 * n + k].reshape(members, LANES)).astype(bf16) for k in range(2)]
        yield
        grads_ref[...] = jnp.concatenate(grads, axis=1)
        if with_taps:
            g = [jnp.concatenate([flat(2 * k, 2, half), flat(2 * k + 1, 2, half)], axis=1) for k in range(2)]
            x = [operand(act, 2 * n + k, 1, half) for k in range(2)]
            add_taps(jnp.concatenate(g, axis=0), jnp.concatenate(x, axis=0), acc_two, acc_two_next, chan2)
            yield

    def first_taps(n, grads_ref, keep=None):
        g = grads_ref[16:]
        g = g if keep is None else g * keep
        add_taps(g, operand(source, n, 1, half), acc_one, acc_one_next, chan1)
        yield
        z = jnp.dot(pick, grads_ref[...], preferred_element_type=f32)
        z = jnp.concatenate([z[:48], z[48:]], axis=1)
        high = z.astype(bf16)
        sums[0, n] = high
        sums[1, n] = (z - high.astype(f32)).astype(bf16)
        yield

    def own_gradient(n, cast, fgrad):
        return loss_gradient(cast, fgrad, aims, weights, 4 * (n - 1), range(4))

    def second_segment(m, _):
        take_turns(
            second_product(2 * m + 3, cast_odd),
            own_gradient(2 * m + 2, cast_even, fgrad_even),
            pull_back(2 * m + 1, fgrad_odd, grads_odd),
            first_taps(2 * m, grads_even, jnp.where(m >= 1, 1.0, 0.0).astype(bf16)),
        )
        take_turns(
            second_product(2 * m + 4, cast_even),
            own_gradient(2 * m + 3, cast_odd, fgrad_odd),
            pull_back(2 * m + 2, fgrad_even, grads_even),
            first_taps(2 * m + 1, grads_odd),
        )
        return 0

    take_turns(second_product(0, cast_even))
    take_turns(
        second_product(1, cast_odd),
        loss_gradient(cast_even, fgrad_even, edge_aims, edge_weights, 0, range(1, 4)),
    )
    take_turns(
        second_product(2, cast_even),
        own_gradient(1, cast_odd, fgrad_odd),
        pull_back(0, fgrad_even, grads_even, with_taps=False),
    )
    lax.fori_loop(0, rows // 2 - 1, second_segment, 0)
    take_turns(
        own_gradient(rows, cast_even, fgrad_even),
        pull_back(rows - 1, fgrad_odd, grads_odd),
        first_taps(rows - 2, grads_even),
    )
    take_turns(pull_back(rows, fgrad_even, grads_even), first_taps(rows - 1, grads_odd))
    take_turns(first_taps(rows, grads_even))

    z = jnp.dot(sums[...].reshape(2 * (rows + 1) * 48, 512), back_one[...], preferred_element_type=f32)
    z = z.reshape(2, rows + 1, 48, 2 * LANES)
    z = z[0] + z[1]
    for n in range(rows):
        lat_lines[pl.ds(n, 48, stride=rows), :] = z[n + 1, :, :LANES] + z[n, :, LANES:]
    for t in range(own):
        out_lat[:, t * LANES : (t + 1) * LANES] = lat_lines[t * rows : (t + 1) * rows].astype(bf16)
    pack_taps(acc_one, acc_one_next, taps, 0, chan0, chan1, norm)
    pack_taps(acc_two, acc_two_next, taps, -(-9 // (LANES // chan0)) * chan1, chan1, chan2, norm)
    count = taps_keep.shape[0]
    odd = jnp.bitwise_and(lat_pos, 1)
    taps_keep[...] = taps[pl.ds(pl.multiple_of(odd * count, 8), count), :]
    taps_send[...] = taps[pl.ds(pl.multiple_of((1 - odd) * count, 8), count), :]


def swapped(array, axis, bit):
    return lax.ppermute(array, axis, [(i, i ^ bit) for i in range(lax.axis_size(axis))])


def total(array, axis, first, second):
    one, two, three = (swapped(array, axis, k).astype(jnp.float32) for k in (first, second, first ^ second))
    return (array.astype(jnp.float32) + one) + (two + three)


def local(
    latent, member_seeds, noise_scale, kernel_one, kernel_two, targets, land_words, channel_weight
):
    sample_count, rows, span = latent.shape
    chan0, chan1, chan2 = kernel_one.shape[2], kernel_one.shape[3], kernel_two.shape[3]
    lat_count = lax.axis_size("lat")
    own = span // LANES // lax.axis_size("mem")
    half = (own + 1) // 2
    assert sample_count == 1 and member_seeds.shape[0] == MEM and rows % 4 == 0 and own % 2 == 1 and lax.axis_size("mem") == 4
    assert 4 * chan2 == 2 * chan1 == chan0 and chan0 == 64
    vmem = pl.BlockSpec(memory_space=pltpu.VMEM)
    smem = pl.BlockSpec(memory_space=pltpu.SMEM)
    hbm = pl.BlockSpec(memory_space=pltpu.HBM)
    f32, bf16 = jnp.float32, jnp.bfloat16
    wide, front = half + 2, half + 1
    params = pltpu.CompilerParams(vmem_limit_bytes=32 * 1024 * 1024)
    small = pltpu.CompilerParams(vmem_limit_bytes=8 * 1024 * 1024)
    kernel_one = kernel_one.transpose(0, 1, 3, 2)
    kernel_two = kernel_two.transpose(0, 1, 3, 2)
    down, up = pl.pallas_call(
        functools.partial(edge_kernel, half, chan2),
        in_specs=[hbm] * 3,
        out_specs=[vmem] * 2,
        out_shape=[
            jax.ShapeDtypeStruct((2 * wide, 8, LANES), bf16),
            jax.ShapeDtypeStruct((1, 2 * wide * LANES), bf16),
        ],
        scratch_shapes=[
            pltpu.VMEM((1, 8, span), bf16),
            pltpu.VMEM((1, 8, span), bf16),
            pltpu.VMEM((8, land_words.shape[1]), jnp.int32),
            pltpu.VMEM((8, LANES), jnp.int32),
            pltpu.SemaphoreType.DMA((3,)),
        ],
        compiler_params=pltpu.CompilerParams(vmem_limit_bytes=56 * 1024 * 1024),
        name="edges",
    )(latent, targets, land_words)
    above = shifted(down, "lat", 1)
    below = shifted(up, "lat", -1)
    source, aims, weights = pl.pallas_call(
        functools.partial(prepare_kernel, half, chan0, chan2),
        in_specs=[smem] * 3 + [vmem] * 3,
        out_specs=[vmem] * 3,
        out_shape=[jax.ShapeDtypeStruct((rows, wide, 16, LANES), bf16)]
        + [jax.ShapeDtypeStruct((2 * front, 4 * rows, LANES), f32)] * 2,
        scratch_shapes=[pltpu.VMEM((2 * wide, rows, LANES), f32), pltpu.VMEM((4 * rows, LANES), jnp.int32)],
        compiler_params=small,
        cost_estimate=pl.CostEstimate(flops=10**8, bytes_accessed=10**7, transcendentals=0),
        name="prepare",
    )(member_seeds, noise_scale, channel_weight, latent, targets, land_words)
    one_late, two_late, source = lax.optimization_barrier((kernel_one, kernel_two, source))
    bands = pl.pallas_call(
        bands_kernel,
        in_specs=[vmem] * 2,
        out_specs=[vmem] * 4,
        out_shape=[jax.ShapeDtypeStruct((512, 256), bf16)] * 4,
        compiler_params=small,
        cost_estimate=pl.CostEstimate(flops=10**8, bytes_accessed=10**7, transcendentals=0),
        name="bands",
    )(one_late, two_late)
    norm = 1.0 / math.sqrt(sample_count * 4 * rows * lat_count * targets.shape[2])
    tap_rows = 5 * chan1 + 3 * chan2
    lat_grad, taps, taps_send = pl.pallas_call(
        functools.partial(band_kernel, half, (chan0, chan1, chan2), span, norm),
        in_specs=[smem] * 3 + [vmem] * 9,
        out_specs=[vmem] * 3,
        out_shape=[
            jax.ShapeDtypeStruct((rows, own * LANES), bf16),
            jax.ShapeDtypeStruct((tap_rows // 2, LANES), f32),
            jax.ShapeDtypeStruct((tap_rows // 2, LANES), f32),
        ],
        scratch_shapes=[
            pltpu.VMEM((2 * wide, 8, LANES), f32),
            pltpu.VMEM((2 * front, 8, LANES), f32),
            pltpu.VMEM((2 * front, 8, LANES), f32),
            pltpu.VMEM((rows + 4, wide + 1, 16, LANES), bf16),
            pltpu.VMEM((wide * 32, 2 * LANES), f32),
            pltpu.VMEM((wide * 32, 2 * LANES), f32),
            pltpu.VMEM((2 * rows + 4, wide, 16, LANES), bf16),
            pltpu.VMEM((2 * rows + 4, front, 16, LANES), f32),
            pltpu.VMEM((4, front, 16, LANES), bf16),
            pltpu.VMEM((4, front, 16, LANES), bf16),
            pltpu.VMEM((4, front + 1, 16, LANES), bf16),
            pltpu.VMEM((4, front + 1, 16, LANES), bf16),
            pltpu.VMEM((front * 16, 2 * LANES), bf16),
            pltpu.VMEM((front * 16, 2 * LANES), bf16),
            pltpu.VMEM((front * 16, LANES), f32),
            pltpu.VMEM((2, rows + 1, 48, 512), bf16),
            pltpu.VMEM((48 * rows, LANES), f32),
            pltpu.VMEM((tap_rows, LANES), f32),
            pltpu.VMEM((256, 256), f32),
            pltpu.VMEM((2 * chan1, 256), f32),
            pltpu.VMEM((256, 256), f32),
            pltpu.VMEM((2 * chan2, 256), f32),
        ],
        compiler_params=params,
        name="band",
    )(
        member_seeds,
        noise_scale,
        channel_weight,
        source,
        aims,
        weights,
        above,
        below,
        *bands,
    )
    taps = (taps + swapped(taps_send, "lat", 1)).astype(bf16)
    taps = total(taps, "mem", 1, 2)
    one, two, three = (swapped(lat_grad, "mem", k) for k in range(1, 4))
    bits = [1 << k for k in range(1, lat_count.bit_length() - 1)]
    for bit in bits:
        if bit == bits[-1]:
            taps, one, three = lax.optimization_barrier((taps, one, three))
        taps = taps + swapped(taps, "lat", bit)
    taps, two = lax.optimization_barrier((taps, two))
    other = swapped(taps, "lat", 1)
    latent_grad = pl.pallas_call(
        functools.partial(place_kernel, own),
        in_specs=[vmem] * 4,
        out_specs=vmem,
        out_shape=jax.ShapeDtypeStruct((1, rows, span), f32),
        compiler_params=small,
        name="place",
    )(lat_grad, one, two, three)
    one, two = pl.pallas_call(
        taps_kernel,
        in_specs=[vmem] * 2,
        out_specs=[vmem] * 2,
        out_shape=[
            jax.ShapeDtypeStruct(kernel_one.shape, f32),
            jax.ShapeDtypeStruct(kernel_two.shape, f32),
        ],
        scratch_shapes=[pltpu.VMEM((tap_rows, LANES), f32)],
        compiler_params=small,
        name="taps",
    )(taps, other)
    return (latent_grad, one.transpose(0, 1, 3, 2), two.transpose(0, 1, 3, 2))


def solution(mesh):
    in_specs = (P(None, "lat", None), P(), P(), P(), P(), P(None, "lat", None), P("lat", None), P())
    out_specs = (P(None, "lat", None), P(), P())
    return jax.shard_map(local, mesh=mesh, in_specs=in_specs, out_specs=out_specs, check_vma=False)
```
